32 devices in a mesh: seq: 2 (over x), ctx: 16 (over z, y, core).
Axes of the slice: x: 2, y: 2, z: 4, core: 2. Of those that a mesh axis runs over, the one named last changes fastest.
Arguments:
- tokens: bfloat16 [4096, 4, 768], P('ctx', 'seq'), may hold values from -6 to 6
- segment: int32 [4096, 4], P('ctx', 'seq'), may hold values from 0 to 4095, as said below
- ln1_gain: bfloat16 [768], P(('seq', 'ctx')), may hold values from 0.099609375 to 1.8984375
- ln1_bias: bfloat16 [768], P(('seq', 'ctx')), may hold values from -3 to 3
- ln2_gain: bfloat16 [768], P(('seq', 'ctx')), may hold values from 0.099609375 to 1.8984375
- ln2_bias: bfloat16 [768], P(('seq', 'ctx')), may hold values from -3 to 3
- qkv_weight: bfloat16 [768, 2304], P(('seq', 'ctx')), may hold values from -0.21875 to 0.21875
- qkv_bias: bfloat16 [2304], P(('seq', 'ctx')), may hold values from -3 to 3
- dense_weight: bfloat16 [768, 768], P(('seq', 'ctx')), may hold values from -1.75 to 1.75
- dense_bias: bfloat16 [768], P(('seq', 'ctx')), may hold values from -3 to 3
- fc1_weight: bfloat16 [768, 3072], P(('seq', 'ctx')), may hold values from -0.21875 to 0.21875
- fc1_bias: bfloat16 [3072], P(('seq', 'ctx')), may hold values from -3 to 3
- output_feed_weight: bfloat16 [3072, 768], P(('seq', 'ctx')), may hold values from -0.109375 to 0.109375
- output_feed_bias: bfloat16 [768], P(('seq', 'ctx')), may hold values from -3 to 3
- cotangent: bfloat16 [4096, 4, 768], P('ctx', 'seq'), may hold values from -6 to 6
Outputs:
- output: bfloat16 [4096, 4, 768], P('ctx', 'seq')
- tokens_grad: bfloat16 [4096, 4, 768], P('ctx', 'seq')
- ln1_gain_grad: float32 [768], P(('seq', 'ctx'))
- ln1_bias_grad: float32 [768], P(('seq', 'ctx'))
- ln2_gain_grad: float32 [768], P(('seq', 'ctx'))
- ln2_bias_grad: float32 [768], P(('seq', 'ctx'))
- qkv_weight_grad: float32 [768, 2304], P(('seq', 'ctx'))
- qkv_bias_grad: float32 [2304], P(('seq', 'ctx'))
- dense_weight_grad: float32 [768, 768], P(('seq', 'ctx'))
- dense_bias_grad: float32 [768], P(('seq', 'ctx'))
- fc1_weight_grad: float32 [768, 3072], P(('seq', 'ctx'))
- fc1_bias_grad: float32 [3072], P(('seq', 'ctx'))
- fc2_weight_grad: float32 [3072, 768], P(('seq', 'ctx'))
- fc2_bias_grad: float32 [768], P(('seq', 'ctx'))
The draws below stay inside these ranges and needn't reach their ends.
Inputs may be any that keep to these rules, and one draw needn't show every extreme that they name: segment[t, s] is the first position of the document holding token t of sequence s, so segment[t, s] <= t; it is the same for all tokens of one document and documents are contiguous; a sequence's last document may be cut short by the sequence's end.
All inputs are finite; a program needn't handle non-finite values.
Results may differ from the reference program's by a relative error of at most 0.013.
Values may be sent and summed in bfloat16 or wider, within the bound.
No kernel may reach another device: no remote copies, remote signals or barrier semaphores. Data moves between devices by JAX's collectives and lax.ppermute only.
A program may use at most 192 MiB of HBM per device.

```python
import math
import jax
import jax.numpy as jnp
from jax import lax

D = 768
HEADS = 12
HEAD_DIM = 64
FF = 3072
ROT = 16
LEN = 4096
SG = 2
NSEQ = 4
DOC_MIN = 204
N_CTX = 16


def draw_segment(key, part):
    key = jax.random.fold_in(key, 11)
    key_len, key_pick, key_end = jax.random.split(key, 3)
    doc_count = LEN // DOC_MIN + 1
    lengths = jax.random.randint(key_len, (NSEQ, doc_count), DOC_MIN, LEN - LEN // 40 + 1)
    picked = jax.random.randint(key_pick, (NSEQ // SG, 1), 0, SG)
    seq_index = jnp.arange(NSEQ, dtype=jnp.int32).reshape(NSEQ // SG, SG)
    spanning = (seq_index % SG == picked).reshape(NSEQ)
    ending = jax.random.randint(key_end, (NSEQ,), LEN - LEN // N_CTX + 1, LEN + 1)
    column = jnp.arange(doc_count, dtype=jnp.int32)[None, :]
    forced = jnp.where(column == 0, ending[:, None], LEN)
    lengths = jnp.where(spanning[:, None], forced, lengths)
    starts = jnp.cumsum(lengths, axis=1) - lengths
    positions = jnp.arange(LEN, dtype=jnp.int32)
    start_hit = jnp.where(starts[:, None, :] <= positions[None, :, None], starts[:, None, :], 0)
    return jnp.max(start_hit, axis=2).T.astype(jnp.int32)


def level_of(key, extent, pieces, least, top_value):
    def one(position, blocks):
        steps = jax.random.uniform(jax.random.fold_in(jax.random.fold_in(key, 6), position), (blocks,), jnp.float32, least / len(pieces), top_value / len(pieces))
        return jnp.repeat(jnp.exp(steps), extent[position] // blocks).reshape((-1,) + (1,) * (len(extent) - position - 1))

    factor_of = one(*pieces[0])
    for cut in pieces[1:]:
        factor_of = factor_of * one(*cut)
    return factor_of


def normal_values(rng, shape, width, reach, pieces=(), held_as=jnp.bfloat16):
    values = width * jax.random.normal(rng, shape, jnp.float32)
    if pieces:
        values = values * level_of(rng, shape, pieces, -0.22, 0.18)
    return jnp.clip(values, -reach, reach).astype(held_as)


def setup_inputs(seed: int = 0) -> dict:
    arg_keys = jax.random.split(jax.random.key(seed), 16)
    return {
        "tokens": normal_values(arg_keys[0], (LEN, NSEQ, D), 1.0, 6.0, ((0, 16), (1, 2))),
        "segment": draw_segment(jax.random.fold_in(arg_keys[15], 71), 0),
        "ln1_gain": jnp.clip(1.0 + 0.18 * jax.random.normal(arg_keys[2], (D,), jnp.float32), 0.099609375, 1.8984375).astype(jnp.bfloat16),
        "ln1_bias": normal_values(arg_keys[3], (D,), 0.5, 3.0, ((0, 32),)),
        "ln2_gain": jnp.clip(1.0 + 0.18 * jax.random.normal(arg_keys[4], (D,), jnp.float32), 0.099609375, 1.8984375).astype(jnp.bfloat16),
        "ln2_bias": normal_values(arg_keys[5], (D,), 0.5, 3.0, ((0, 32),)),
        "qkv_weight": normal_values(arg_keys[6], (D, 3 * D), D ** -0.5, 0.21875, ((0, 32),)),
        "qkv_bias": normal_values(arg_keys[7], (3 * D,), 0.5, 3.0, ((0, 32),)),
        "dense_weight": normal_values(arg_keys[8], (D, D), (D // 64) ** -0.5, 1.75, ((0, 32),)),
        "dense_bias": normal_values(arg_keys[9], (D,), 0.5, 3.0, ((0, 32),)),
        "fc1_weight": normal_values(arg_keys[10], (D, FF), D ** -0.5, 0.21875, ((0, 32),)),
        "fc1_bias": normal_values(arg_keys[11], (FF,), 0.5, 3.0, ((0, 32),)),
        "output_feed_weight": normal_values(arg_keys[12], (FF, D), FF ** -0.5, 0.109375, ((0, 32),)),
        "output_feed_bias": normal_values(arg_keys[13], (D,), 0.5, 3.0, ((0, 32),)),
        "cotangent": normal_values(arg_keys[14], (LEN, NSEQ, D), 1.0, 6.0, ((0, 16), (1, 2))),
    }


EPSILON = 1e-05
NEG_BIG = -1e+30
accurate_mode = lax.Precision.HIGHEST

@jax.custom_vjp
def low(v):
    return lax.optimization_barrier(v.astype(jnp.bfloat16)).astype(jnp.float32)

@jax.custom_vjp
def low_back(v):
    return v

def low_keep(v):
    return (low(v), None)

def low_pass(kept, grad):
    return (grad,)

def backward_retained(v):
    return (v, None)

def back_low(kept, grad):
    return (low(grad),)
low.defvjp(low_keep, low_pass)
low_back.defvjp(backward_retained, back_low)

def layer_norm(values, gain, offset):
    centre = values - lax.optimization_barrier(jnp.mean(values, -1, keepdims=True))
    spread = lax.optimization_barrier(jnp.mean(centre * centre, -1, keepdims=True))
    return centre * lax.rsqrt(spread + EPSILON) * gain + offset

def gelu_exact(pre_act):
    return jax.nn.gelu(pre_act, approximate=False)

def rotary_tables(positions):
    freq_index = jnp.arange(ROT // 2, dtype=jnp.float32)
    inverse = jnp.exp(freq_index * (-2.0 * math.log(10000.0) / ROT))
    angles = positions.astype(jnp.float32)[..., None] * inverse
    return (jnp.cos(angles), jnp.sin(angles))

def rotate(values, cos_table, sin_table):
    half_rot = ROT // 2
    first_half = values[..., :half_rot]
    second_half = values[..., half_rot:ROT]
    return jnp.concatenate([first_half * cos_table - second_half * sin_table, second_half * cos_table + first_half * sin_table, values[..., ROT:]], -1)

def query_block(block_item, keys_all, values_all):
    queries, query_pos, query_seg = block_item
    key_pos = jnp.arange(LEN, dtype=jnp.int32)
    scores = jnp.einsum('qha,kha->hqk', queries, keys_all, precision=accurate_mode) * HEAD_DIM ** (-0.5)
    scores = low_back(scores)
    allowed = (key_pos[None, :] <= query_pos[:, None]) & (key_pos[None, :] >= query_seg[:, None])
    scores = jnp.where(allowed[None], scores, NEG_BIG)
    peak_score = lax.optimization_barrier(jnp.max(scores, -1, keepdims=True))
    expo_terms = jnp.where(allowed[None], jnp.exp(scores - peak_score), 0.0)
    probs = expo_terms / lax.optimization_barrier(jnp.sum(expo_terms, -1, keepdims=True))
    return jnp.einsum('hqk,kha->qha', low(probs), values_all, precision=accurate_mode)

def attend_sequence(seq_item):
    queries, keys_all, values_all, seg_row = seq_item
    block_len = math.gcd(LEN, 512)
    block_count = LEN // block_len
    query_pos = jnp.arange(LEN, dtype=jnp.int32)
    blocks = (queries.reshape(block_count, block_len, HEADS, HEAD_DIM), query_pos.reshape(block_count, block_len), seg_row.reshape(block_count, block_len))
    block_fn = jax.checkpoint(lambda block_item: query_block(block_item, keys_all, values_all))
    return lax.map(block_fn, blocks).reshape(LEN, HEADS, HEAD_DIM)

def layer(params, segment):
    tokens, ln1_gain, ln1_bias, ln2_gain, ln2_bias, qkv_weight, qkv_bias, dense_weight, dense_bias, fc1_weight, fc1_bias, output_feed_weight, output_feed_bias = params
    normed_one = low(layer_norm(tokens, ln1_gain, ln1_bias))
    normed_two = low(layer_norm(tokens, ln2_gain, ln2_bias))
    projected = low_back(jnp.einsum('lsd,de->lse', normed_one, qkv_weight, precision=accurate_mode) + qkv_bias)
    shape_four = (LEN, NSEQ, HEADS, HEAD_DIM)
    positions = jnp.arange(LEN, dtype=jnp.int32)[:, None] - segment
    cos_table, sin_table = rotary_tables(positions)
    cos_table = cos_table[:, :, None, :]
    sin_table = sin_table[:, :, None, :]
    queries = low(rotate(projected[..., :D].reshape(shape_four), cos_table, sin_table))
    keys_rot = low(rotate(projected[..., D:2 * D].reshape(shape_four), cos_table, sin_table))
    values_all = low(projected[..., 2 * D:].reshape(shape_four))
    attended = lax.map(jax.checkpoint(attend_sequence), (jnp.moveaxis(queries, 1, 0), jnp.moveaxis(keys_rot, 1, 0), jnp.moveaxis(values_all, 1, 0), segment.T))
    attended = low_back(low(jnp.moveaxis(attended, 0, 1).reshape(LEN, NSEQ, D)))
    branch_one = jnp.einsum('lsd,de->lse', attended, dense_weight, precision=accurate_mode) + dense_bias
    hidden_pre = low_back(jnp.einsum('lsd,de->lse', normed_two, fc1_weight, precision=accurate_mode) + fc1_bias)
    hidden_reduced = low(gelu_exact(hidden_pre))
    second_branch = jnp.einsum('xpr,rm->xpm', hidden_reduced, output_feed_weight, precision=accurate_mode) + output_feed_bias
    return tokens + branch_one + second_branch

def reference(tokens, segment, ln1_gain, ln1_bias, ln2_gain, ln2_bias, qkv_weight, qkv_bias, dense_weight, dense_bias, fc1_weight, fc1_bias, output_feed_weight, output_feed_bias, cotangent):
    floats = tuple((item.astype(jnp.float32) for item in (tokens, ln1_gain, ln1_bias, ln2_gain, ln2_bias, qkv_weight, qkv_bias, dense_weight, dense_bias, fc1_weight, fc1_bias, output_feed_weight, output_feed_bias)))

    def forward(*params):
        return layer(params, segment)
    result, pullback = jax.vjp(forward, *floats)
    grads = pullback(cotangent.astype(jnp.float32))
    return (result.astype(jnp.bfloat16), grads[0].astype(jnp.bfloat16), grads[1], grads[2], grads[3], grads[4], grads[5], grads[6], grads[7], grads[8], grads[9], grads[10], grads[11], grads[12])
```

```python
import functools
import math

import jax
import jax.numpy as jnp
from jax import lax
from jax.experimental import pallas as pl
from jax.experimental.pallas import tpu as pltpu
from jax.sharding import Mesh, PartitionSpec as P

HEADS = 12
HEAD_DIM = 64
ROT = 16
TRIO = 3
TILE = 128
PACK = 5 * TILE
OPACK = 2 * TILE

EPSILON = 1e-05
NEG_BIG = -1e30
BF = jnp.bfloat16
F32 = jnp.float32
ALL_AXES = ("seq", "unit", "part")
VMEM_BYTES = 56 * 1024 * 1024


def params_of(*semantics):
    return pltpu.CompilerParams(
        dimension_semantics=semantics, vmem_limit_bytes=VMEM_BYTES
    )


def mm(a, b):
    return jnp.dot(a, b, preferred_element_type=F32)


def outer_sum(left_rows, right_rows):
    return lax.dot_general(
        left_rows, right_rows, (((0,), (0,)), ((), ())), preferred_element_type=F32
    )


def inner_back(grad_rows, weight):
    return lax.dot_general(
        grad_rows, weight, (((1,), (1,)), ((), ())), preferred_element_type=F32
    )


def lane_of(shape):
    return lax.broadcasted_iota(jnp.int32, shape, len(shape) - 1)


def turn(tile, cos, sin):
    partner = jnp.where(
        lane_of(tile.shape) % HEAD_DIM < ROT // 2,
        pltpu.roll(tile, TILE - ROT // 2, 1),
        pltpu.roll(tile, ROT // 2, 1),
    )
    return tile * cos + partner * sin


def project_kernel(x_ref, w_ref, b_ref, cos_ref, sin_ref, aux_ref, out_ref):
    y = mm(x_ref[...], w_ref[...]) + b_ref[...]
    cos = cos_ref[...]
    sin = sin_ref[...]
    for t in range(5):
        tile = y[:, t * TILE : (t + 1) * TILE]
        if t in (0, 1, 3):
            tile = turn(tile, cos, sin)
        if t == 4:
            tile = tile + aux_ref[...]
        out_ref[0, :, t * TILE : (t + 1) * TILE] = tile.astype(BF)


def project(xn, weight, bias, cos, sin, aux, rows, trios, groups):
    d = xn.shape[1]
    row_spec = pl.BlockSpec((rows, TILE), lambda g, s: (s, 0))
    return pl.pallas_call(
        project_kernel,
        grid=(trios, groups),
        in_specs=[
            pl.BlockSpec((rows, d), lambda g, s: (s, 0)),
            pl.BlockSpec((d, PACK), lambda g, s: (0, g)),
            pl.BlockSpec((1, PACK), lambda g, s: (0, g)),
            row_spec,
            row_spec,
            row_spec,
        ],
        out_specs=pl.BlockSpec((1, rows, PACK), lambda g, s: (g * groups + s, 0, 0)),
        out_shape=jax.ShapeDtypeStruct((trios * groups, rows, PACK), BF),
        compiler_params=params_of("arbitrary", "arbitrary"),
        name="project",
    )(xn, weight, bias, cos, sin, aux)


def unturn_kernel(in_ref, cos_ref, sin_ref, out_ref):
    cos = cos_ref[...]
    sin = sin_ref[...]
    for t in range(5):
        tile = in_ref[0, :, t * TILE : (t + 1) * TILE].astype(F32)
        if t in (0, 1, 3):
            tile = turn(tile, cos, -sin)
        out_ref[:, t * TILE : (t + 1) * TILE] = tile.astype(BF)


def unturn(packed, cos, sin, rows, trios, groups):
    row_spec = pl.BlockSpec((rows, TILE), lambda g, s: (s, 0))
    return pl.pallas_call(
        unturn_kernel,
        grid=(trios, groups),
        in_specs=[
            pl.BlockSpec((1, rows, PACK), lambda g, s: (g * groups + s, 0, 0)),
            row_spec,
            row_spec,
        ],
        out_specs=pl.BlockSpec((rows, PACK), lambda g, s: (s, g)),
        out_shape=jax.ShapeDtypeStruct((rows * groups, trios * PACK), BF),
        compiler_params=params_of("arbitrary", "arbitrary"),
        name="unturn",
    )(packed, cos, sin)


def flip(tile):
    return tile.astype(F32).T


def head_rows(flipped, low):
    row = lax.broadcasted_iota(jnp.int32, flipped.shape, 0)
    keep = row < HEAD_DIM if low else row >= HEAD_DIM
    return jnp.where(keep, flipped, 0.0)


def head_lanes(tile, low):
    lane = lane_of(tile.shape)
    keep = lane < HEAD_DIM if low else lane >= HEAD_DIM
    return jnp.where(keep, tile, 0.0)


def query_sides(q_ref, qb):
    scale = HEAD_DIM ** (-0.5)
    a = flip(q_ref[0, :, 0:TILE]) * scale
    d = flip(q_ref[0, :, 3 * TILE : 4 * TILE]) * scale
    qb[0] = head_rows(a, True).astype(BF)
    qb[1] = head_rows(a, False).astype(BF)
    qb[2] = jnp.concatenate(
        [jnp.zeros((HEAD_DIM, d.shape[1]), F32), d[:HEAD_DIM]], 0
    ).astype(BF)


def live_of(seg_row, key_start, query_start, rows):
    shape = (rows, rows)
    key_pos = key_start + lax.broadcasted_iota(jnp.int32, shape, 0)
    query_pos = query_start + lax.broadcasted_iota(jnp.int32, shape, 1)
    return (key_pos <= query_pos) & (key_pos >= seg_row)


def block_loop(meta, part, units, rows, step):
    j = pl.program_id(0)
    c = meta[2 * units]
    diag = j * part + c
    first = meta[j] // rows
    top_seg = meta[units + j]

    def one(kb, unused):
        where = (lax.rem(c - lax.rem(kb, part) + part, part), kb // part)
        masked = (kb == diag) | (top_seg > kb * rows)

        @pl.when(masked)
        def _():
            step(where, kb, diag, True)

        @pl.when(jnp.logical_not(masked))
        def _():
            step(where, kb, diag, False)

        return unused

    lax.fori_loop(first, diag + 1, one, 0)
    return diag


def forward_kernel(
    part, units, meta, q_ref, kv_ref, seg_ref, o_ref, ot_ref, lse_ref, qb, vt, top, total, acc
):
    rows = q_ref.shape[1]
    c = meta[2 * units]

    @pl.when(pl.program_id(0) == 0)
    def _():
        for i in range(part):
            p = lax.rem(c - i + part, part)
            for unit in range(units):
                kb = unit * part + p
                vt[kb, :TILE] = flip(kv_ref[i, unit, :, TILE : 2 * TILE]).astype(BF)
                vt[kb, TILE:] = flip(kv_ref[i, unit, :, 3 * TILE :])[:HEAD_DIM].astype(BF)

    query_sides(q_ref, qb)
    top[...] = jnp.full(top.shape, NEG_BIG, F32)
    total[...] = jnp.zeros(total.shape, F32)
    acc[...] = jnp.zeros(acc.shape, F32)
    seg_row = seg_ref[0]

    def step(where, kb, diag, masked):
        k01 = kv_ref[where[0], where[1], :, 0:TILE]
        k2 = kv_ref[where[0], where[1], :, 2 * TILE : 3 * TILE]
        if masked:
            live = live_of(seg_row, kb * rows, diag * rows, rows)
        for h in range(TRIO):
            score = mm(k2 if h == 2 else k01, qb[h])
            if masked:
                score = jnp.where(live, score, NEG_BIG)
            old = top[h : h + 1]
            new = jnp.maximum(old, jnp.max(score, 0, keepdims=True))
            weight = jnp.exp(score - new)
            if masked:
                weight = jnp.where(live, weight, 0.0)
            factor = jnp.exp(old - new)
            top[h : h + 1] = new
            total[h : h + 1] = total[h : h + 1] * factor + jnp.sum(weight, 0, keepdims=True)
            vth = vt[kb, h * HEAD_DIM : (h + 1) * HEAD_DIM]
            acc[h] = acc[h] * factor + mm(vth, weight.astype(BF))

    block_loop(meta, part, units, rows, step)
    out = [acc[h] / total[h : h + 1] for h in range(TRIO)]
    for h in range(TRIO):
        ot_ref[0, h * HEAD_DIM : (h + 1) * HEAD_DIM] = out[h]
    lse_ref[0, 0:TRIO] = top[0:TRIO] + jnp.log(total[0:TRIO])
    o_ref[0, :, :TILE] = jnp.concatenate(out[:2], 0).T.astype(BF)
    o_ref[0, :, TILE:] = jnp.concatenate([out[2], jnp.zeros_like(out[2])], 0).T.astype(BF)


def backward_kernel(
    part,
    units,
    meta,
    q_ref,
    do_ref,
    ot_ref,
    lse_ref,
    kv_ref,
    seg_ref,
    own_ref,
    oth_ref,
    qb,
    db,
    qn,
    dn,
    kt,
    delta,
    dqt,
    dk01,
    dv01,
    dk2,
    dv2,
):
    rows = q_ref.shape[1]
    c = meta[2 * units]
    j = pl.program_id(0)

    @pl.when(j == 0)
    def _():
        for i in range(part):
            p = lax.rem(c - i + part, part)
            for unit in range(units):
                kb = unit * part + p
                kt[kb, :TILE] = flip(kv_ref[i, unit, :, 0:TILE]).astype(BF)
                kt[kb, TILE:] = flip(kv_ref[i, unit, :, 2 * TILE : 3 * TILE])[HEAD_DIM:].astype(BF)
        for ref in (dk01, dv01, dk2, dv2):
            ref[...] = jnp.zeros(ref.shape, F32)

    query_sides(q_ref, qb)
    scale = HEAD_DIM ** (-0.5)
    q01 = q_ref[0, :, 0:TILE].astype(F32) * scale
    q2 = pltpu.roll(q_ref[0, :, 3 * TILE : 4 * TILE].astype(F32), HEAD_DIM, 1) * scale
    qn[0:rows] = head_lanes(q01, True).astype(BF)
    qn[rows : 2 * rows] = head_lanes(q01, False).astype(BF)
    qn[2 * rows :] = head_lanes(q2, False).astype(BF)
    do01 = do_ref[0, :, :TILE].astype(F32)
    do2 = do_ref[0, :, TILE:].astype(F32)
    dn[0:rows] = head_lanes(do01, True).astype(BF)
    dn[rows : 2 * rows] = head_lanes(do01, False).astype(BF)
    dn[2 * rows :] = do2.astype(BF)
    do01t = do01.T
    do2t = do2.T
    db[0] = head_rows(do01t, True).astype(BF)
    db[1] = head_rows(do01t, False).astype(BF)
    db[2] = do2t.astype(BF)
    for h in range(TRIO):
        dot = do2t[:HEAD_DIM] if h == 2 else do01t[h * HEAD_DIM : (h + 1) * HEAD_DIM]
        delta[h : h + 1] = jnp.sum(
            dot * ot_ref[0, h * HEAD_DIM : (h + 1) * HEAD_DIM], 0, keepdims=True
        )
    dqt[...] = jnp.zeros(dqt.shape, F32)
    seg_row = seg_ref[0]

    def step(where, kb, diag, masked):
        k01 = kv_ref[where[0], where[1], :, 0:TILE]
        v01 = kv_ref[where[0], where[1], :, TILE : 2 * TILE]
        k2 = kv_ref[where[0], where[1], :, 2 * TILE : 3 * TILE]
        v2 = kv_ref[where[0], where[1], :, 3 * TILE :]
        if masked:
            live = live_of(seg_row, kb * rows, diag * rows, rows)
        probs = []
        grads = []
        for h in range(TRIO):
            score = mm(k2 if h == 2 else k01, qb[h])
            if masked:
                score = jnp.where(live, score, NEG_BIG)
            prob = jnp.exp(score - lse_ref[0, h : h + 1])
            if masked:
                prob = jnp.where(live, prob, 0.0)
            dprob = mm(v2 if h == 2 else v01, db[h])
            ds = (prob * (dprob - delta[h : h + 1])).astype(BF)
            probs.append(prob.astype(BF))
            grads.append(ds)
            kth = kt[kb, h * HEAD_DIM : (h + 1) * HEAD_DIM]
            dqt[h * HEAD_DIM : (h + 1) * HEAD_DIM] += mm(kth, ds)
        dv01[kb] += mm(jnp.concatenate(probs[:2], 1), dn[: 2 * rows])
        dk01[kb] += mm(jnp.concatenate(grads[:2], 1), qn[: 2 * rows])
        dv2[kb] += mm(probs[2], dn[2 * rows :])
        dk2[kb] += mm(grads[2], qn[2 * rows :])

    diag = block_loop(meta, part, units, rows, step)
    own_ref[j, :, 0:TILE] = (dqt[:TILE] * scale).T.astype(BF)
    dq2 = dqt[TILE:] * scale
    dk2[diag] += jnp.concatenate([dq2, jnp.zeros_like(dq2)], 0).T

    @pl.when(j == units - 1)
    def _():
        for unit in range(units):
            for i in range(part):
                kb = unit * part + lax.rem(c + i, part)
                for t, ref in enumerate((dk01, dv01, dk2, dv2)):
                    tile = ref[kb].astype(BF)
                    if i == 0:
                        own_ref[unit, :, (t + 1) * TILE : (t + 2) * TILE] = tile
                    else:
                        oth_ref[i - 1, unit, :, t * TILE : (t + 1) * TILE] = tile


def attention_cost(products, units, rows, part):
    pairs = TRIO * rows * rows * units * units * part // 2
    return pl.CostEstimate(
        flops=2 * 64 * products * pairs, bytes_accessed=20_000_000, transcendentals=pairs
    )


def whole_spec(shape):
    zeros = (0,) * len(shape)
    return pl.BlockSpec(shape, lambda j, meta: zeros)


def attend_forward(meta, packed, kv, seg):
    units, rows, unused = packed.shape
    part = kv.shape[0]
    return pl.pallas_call(
        functools.partial(forward_kernel, part, units),
        grid_spec=pltpu.PrefetchScalarGridSpec(
            num_scalar_prefetch=1,
            grid=(units,),
            in_specs=[
                pl.BlockSpec((1, rows, PACK), lambda j, meta: (j, 0, 0)),
                whole_spec(kv.shape),
                pl.BlockSpec((1, 1, rows), lambda j, meta: (j, 0, 0)),
            ],
            out_specs=[
                pl.BlockSpec((1, rows, OPACK), lambda j, meta: (j, 0, 0)),
                pl.BlockSpec((1, TRIO * HEAD_DIM, rows), lambda j, meta: (j, 0, 0)),
                pl.BlockSpec((1, 8, rows), lambda j, meta: (j, 0, 0)),
            ],
            scratch_shapes=[
                pltpu.VMEM((TRIO, TILE, rows), BF),
                pltpu.VMEM((units * part, TRIO * HEAD_DIM, rows), BF),
                pltpu.VMEM((8, rows), F32),
                pltpu.VMEM((8, rows), F32),
                pltpu.VMEM((TRIO, HEAD_DIM, rows), F32),
            ],
        ),
        out_shape=[
            jax.ShapeDtypeStruct((units, rows, OPACK), BF),
            jax.ShapeDtypeStruct((units, TRIO * HEAD_DIM, rows), F32),
            jax.ShapeDtypeStruct((units, 8, rows), F32),
        ],
        compiler_params=params_of("arbitrary"),
        cost_estimate=attention_cost(8, units, rows, part),
        name="attend_forward",
    )(meta, packed, kv, seg)


def attend_backward(meta, packed, dout, out_t, lse, kv, seg):
    units, rows, unused = packed.shape
    part = kv.shape[0]
    others = (max(part - 1, 1), units, rows, 4 * TILE)
    grads = pltpu.VMEM((units * part, rows, TILE), F32)
    return pl.pallas_call(
        functools.partial(backward_kernel, part, units),
        grid_spec=pltpu.PrefetchScalarGridSpec(
            num_scalar_prefetch=1,
            grid=(units,),
            in_specs=[
                pl.BlockSpec((1, rows, PACK), lambda j, meta: (j, 0, 0)),
                pl.BlockSpec((1, rows, OPACK), lambda j, meta: (j, 0, 0)),
                pl.BlockSpec((1, TRIO * HEAD_DIM, rows), lambda j, meta: (j, 0, 0)),
                pl.BlockSpec((1, 8, rows), lambda j, meta: (j, 0, 0)),
                whole_spec(kv.shape),
                pl.BlockSpec((1, 1, rows), lambda j, meta: (j, 0, 0)),
            ],
            out_specs=[whole_spec(packed.shape), whole_spec(others)],
            scratch_shapes=[
                pltpu.VMEM((TRIO, TILE, rows), BF),
                pltpu.VMEM((TRIO, TILE, rows), BF),
                pltpu.VMEM((TRIO * rows, TILE), BF),
                pltpu.VMEM((TRIO * rows, TILE), BF),
                pltpu.VMEM((units * part, TRIO * HEAD_DIM, rows), BF),
                pltpu.VMEM((8, rows), F32),
                pltpu.VMEM((TRIO * HEAD_DIM, rows), F32),
                grads,
                grads,
                grads,
                grads,
            ],
        ),
        out_shape=[
            jax.ShapeDtypeStruct(packed.shape, BF),
            jax.ShapeDtypeStruct(others, BF),
        ],
        compiler_params=params_of("arbitrary"),
        cost_estimate=attention_cost(20, units, rows, part),
        name="attend_backward",
    )(meta, packed, dout, out_t, lse, kv, seg)


def pack_columns(matrix, trios):
    r = matrix.shape[0]
    q, k, v = (
        part.reshape(r, trios, TRIO * HEAD_DIM) for part in jnp.split(matrix, 3, axis=1)
    )
    zeros = jnp.zeros((r, trios, HEAD_DIM), matrix.dtype)
    pieces = [q[..., :TILE], k[..., :TILE], v[..., :TILE], q[..., TILE:], k[..., TILE:]]
    return jnp.concatenate(pieces + [v[..., TILE:], zeros], -1).reshape(r, trios * PACK)


def unpack_columns(matrix, trios):
    r = matrix.shape[0]
    m = matrix.reshape(r, trios, PACK)
    halves = [
        m[..., 3 * TILE : 3 * TILE + HEAD_DIM],
        m[..., 3 * TILE + HEAD_DIM : 4 * TILE],
        m[..., 4 * TILE : 4 * TILE + HEAD_DIM],
    ]
    return jnp.concatenate(
        [
            jnp.concatenate([m[..., i * TILE : (i + 1) * TILE], halves[i]], -1).reshape(r, -1)
            for i in range(3)
        ],
        -1,
    )


def split_hidden(matrix, count, r):
    lead = matrix.shape[0]
    return matrix.reshape(lead, count, -1, r).transpose(0, 2, 1, 3).reshape(lead, -1)


def join_hidden(matrix, count, r):
    lead = matrix.shape[0]
    return matrix.reshape(lead, -1, count, r).transpose(0, 2, 1, 3).reshape(lead, -1)


def on_device(
    tokens,
    segment,
    ln1_gain,
    ln1_bias,
    ln2_gain,
    ln2_bias,
    qkv_weight,
    qkv_bias,
    dense_weight,
    dense_bias,
    fc1_weight,
    fc1_bias,
    output_feed_weight,
    output_feed_bias,
    cotangent,
):
    rows, groups, d = tokens.shape
    units = lax.axis_size("unit")
    part = lax.axis_size("part")
    count = units * part * lax.axis_size("seq")
    trios = units // groups
    all_rows = rows * groups
    r = qkv_weight.shape[0]
    ff = fc1_weight.shape[1]
    blocks = ff // d
    c = lax.axis_index("part")
    unit = lax.axis_index("unit")

    vectors = (
        ln1_gain,
        ln1_bias,
        ln2_gain,
        ln2_bias,
        qkv_bias,
        dense_bias,
        fc1_bias,
        output_feed_bias,
    )
    widths = [v.shape[0] // r for v in vectors]
    held = sum(widths)
    vec = jnp.pad(jnp.concatenate(vectors), (0, r * (16 - held))).reshape(r, 16)
    vec = jnp.pad(vec, ((0, 0), (0, TILE - 16)))
    first_pack = jnp.concatenate([pack_columns(qkv_weight, trios), dense_weight, vec], 1)
    first = lax.all_gather(first_pack, ALL_AXES, axis=0, tiled=True)
    feed_blocks = output_feed_weight.reshape(blocks, r, d)
    second_pack = jnp.concatenate(
        [split_hidden(fc1_weight, count, r)] + [feed_blocks[b] for b in range(blocks)], 1
    )
    second = lax.all_gather(second_pack, ALL_AXES, axis=0, tiled=True)

    qkv_cols = trios * PACK
    qkv_full = first[:, :qkv_cols]
    dense_pad = jnp.pad(
        first[:, qkv_cols : qkv_cols + d].reshape(trios, d // trios, d),
        ((0, 0), (0, OPACK - d // trios), (0, 0)),
    )
    vec_full = first[:, qkv_cols + d : qkv_cols + d + 16].reshape(count, r * 16).astype(F32)
    vecs = []
    at = 0
    for w in widths:
        vecs.append(vec_full[:, at * r : (at + w) * r].reshape(1, count * w * r))
        at += w
    gain_one, bias_one, gain_two, bias_two, qkv_shift, dense_shift, up_shift, down_shift = vecs
    qkv_shift = pack_columns(qkv_shift, trios)
    up_shift = split_hidden(up_shift, count, r)

    x = tokens.transpose(1, 0, 2).reshape(all_rows, d).astype(F32)
    cot = cotangent.transpose(1, 0, 2).reshape(all_rows, d)
    cot_float = cot.astype(F32)
    centre = x - jnp.mean(x, -1, keepdims=True)
    spread = lax.rsqrt(jnp.mean(centre * centre, -1, keepdims=True) + EPSILON)
    xhat = centre * spread
    normed_one = (xhat * gain_one + bias_one).astype(BF)
    normed_two = (xhat * gain_two + bias_two).astype(BF)

    seg_rows = segment.T.reshape(all_rows, 1)
    token_pos = (unit * part + c) * rows + jnp.arange(rows, dtype=jnp.int32)
    token_pos = jnp.tile(token_pos, groups)[:, None]
    lane = jnp.arange(TILE, dtype=jnp.int32)[None, :]
    in_head = lane % HEAD_DIM
    freq = (in_head % (ROT // 2)).astype(F32)
    inverse = jnp.where(in_head < ROT, jnp.exp(freq * (-2.0 * math.log(10000.0) / ROT)), 0.0)
    angles = (token_pos - seg_rows).astype(F32) * inverse
    cos = jnp.cos(angles)
    sin = jnp.sin(angles) * jnp.where(in_head < ROT // 2, -1.0, 1.0)
    aux = jnp.where(lane == HEAD_DIM, seg_rows // 64, 0) + jnp.where(
        lane == HEAD_DIM + 1, seg_rows % 64, 0
    )

    packed = project(
        normed_one, qkv_full, qkv_shift, cos, sin, aux.astype(F32), rows, trios, groups
    )

    def exchange(blocks_out):
        width = blocks_out.shape[-1]
        return lax.all_to_all(
            blocks_out.reshape(units * rows, width), "unit", 0, 0, tiled=True
        ).reshape(units, rows, width)

    mine = exchange(packed)
    seg_mine = mine[:, :, 4 * TILE + HEAD_DIM : 4 * TILE + HEAD_DIM + 2].astype(jnp.int32)
    seg_mine = seg_mine[:, :, 0] * 64 + seg_mine[:, :, 1]
    meta = jnp.concatenate([seg_mine[:, 0], seg_mine[:, -1], c[None]])
    seg_mine = seg_mine[:, None, :]

    def shift_part(value, i):
        return lax.ppermute(value, "part", [(p, (p + i) % part) for p in range(part)])

    kv_own = mine[:, :, TILE:]
    kv = jnp.stack([kv_own] + [shift_part(kv_own, i) for i in range(1, part)])

    attended_grad = jnp.einsum(
        "sld,gkd->gslk", cot.reshape(groups, rows, d), dense_pad, preferred_element_type=F32
    ).astype(BF)
    dout = exchange(attended_grad)

    out_low, out_t, lse = attend_forward(meta, mine, kv, seg_mine)
    attended = exchange(out_low)

    up_full = second[:, :ff]
    down_full = jnp.concatenate(
        [second[:, ff + b * d : ff + (b + 1) * d] for b in range(blocks)], 0
    )
    hidden_pre = mm(normed_two, up_full) + up_shift
    cdf = 0.5 * (1.0 + lax.erf(hidden_pre * math.sqrt(0.5)))
    hidden_low = (hidden_pre * cdf).astype(BF)
    slope = cdf + hidden_pre * (
        jnp.exp(-0.5 * hidden_pre * hidden_pre) * (1.0 / math.sqrt(2.0 * math.pi))
    )
    pre_grad = (inner_back(cot, down_full) * slope).astype(BF)
    second_branch = mm(hidden_low, down_full) + down_shift
    down_grad = outer_sum(hidden_low, cot)
    up_grad = outer_sum(normed_two, pre_grad)
    up_shift_grad = jnp.sum(pre_grad.astype(F32), 0)
    normed_two_grad = inner_back(pre_grad, up_full)
    cot_sum = jnp.sum(cot_float, 0)

    mlp_grads = jnp.concatenate(
        [up_grad.astype(BF)] + [down_grad[b * d : (b + 1) * d].astype(BF) for b in range(blocks)],
        1,
    )
    mlp_sum = lax.psum_scatter(mlp_grads, ALL_AXES, scatter_dimension=0, tiled=True).astype(F32)

    attended = attended.reshape(trios, groups, rows, OPACK).transpose(1, 2, 0, 3)
    attended = attended.reshape(all_rows, trios * OPACK)
    branch_one = mm(attended, dense_pad.reshape(trios * OPACK, d)) + dense_shift
    output = (x + branch_one + second_branch).astype(BF)
    dense_grad = outer_sum(attended, cot).reshape(trios, OPACK, d)[:, : d // trios].reshape(d, d)

    own, others = attend_backward(meta, mine, dout, out_t, lse, kv, seg_mine)
    rest = own[:, :, TILE:].astype(F32)
    for i in range(1, part):
        rest = rest + shift_part(others[i - 1], i).astype(F32)
    back = exchange(jnp.concatenate([own[:, :, :TILE], rest.astype(BF)], -1))
    qkv_grad = unturn(back, cos, sin, rows, trios, groups)
    qkv_grad_w = outer_sum(normed_one, qkv_grad)
    qkv_shift_grad = unpack_columns(jnp.sum(qkv_grad.astype(F32), 0)[None], trios)
    normed_one_grad = inner_back(qkv_grad, qkv_full)

    def norm_back(grad, gain):
        gy = grad * gain
        part_in = spread * (
            gy - jnp.mean(gy, -1, keepdims=True) - xhat * jnp.mean(gy * xhat, -1, keepdims=True)
        )
        return part_in, jnp.sum(grad * xhat, 0), jnp.sum(grad, 0)

    in_one, gain_one_grad, bias_one_grad = norm_back(normed_one_grad, gain_one)
    in_two, gain_two_grad, bias_two_grad = norm_back(normed_two_grad, gain_two)
    tokens_grad = (cot_float + in_one + in_two).astype(BF)

    vec_grads = [
        gain_one_grad,
        bias_one_grad,
        gain_two_grad,
        bias_two_grad,
        qkv_shift_grad,
        cot_sum,
        join_hidden(up_shift_grad[None], count, r),
    ]
    vec_grads = jnp.concatenate([v.reshape(count, -1) for v in vec_grads], 1)
    vec_grads = jnp.pad(vec_grads, ((0, 0), (0, 16 * r - vec_grads.shape[1])))
    vec_grads = jnp.pad(vec_grads.reshape(d, 16), ((0, 0), (0, TILE - 16)))
    last = jnp.concatenate(
        [qkv_grad_w.astype(BF), dense_grad.astype(BF), vec_grads.astype(BF)], 1
    )
    last_sum = lax.psum_scatter(last, ALL_AXES, scatter_dimension=0, tiled=True).astype(F32)

    def natural(value):
        return value.reshape(groups, rows, d).transpose(1, 0, 2)

    vec_sum = last_sum[:, qkv_cols + d : qkv_cols + d + 16].reshape(-1)
    vec_out = []
    at = 0
    for w in widths[:7]:
        vec_out.append(vec_sum[at * r : (at + w) * r])
        at += w
    down_sum = jnp.concatenate(
        [mlp_sum[:, ff + b * d : ff + (b + 1) * d] for b in range(blocks)], 0
    )
    return (
        natural(output),
        natural(tokens_grad),
        vec_out[0],
        vec_out[1],
        vec_out[2],
        vec_out[3],
        unpack_columns(last_sum[:, :qkv_cols], trios),
        vec_out[4],
        last_sum[:, qkv_cols : qkv_cols + d],
        vec_out[5],
        join_hidden(mlp_sum[:, :ff], count, r),
        vec_out[6],
        down_sum,
        vec_out[5],
    )


def solution(mesh):
    devices = mesh.devices
    seq_size, ctx_size = devices.shape
    ctx = ("unit", "part")
    tok = P(ctx, "seq", None)
    vec = P(ALL_AXES)
    mat = P(ALL_AXES, None)
    pairs = (vec, vec, vec, vec, mat, vec, mat, vec, mat, vec, mat, vec)

    def run(tokens, *rest):
        units = HEADS // TRIO * (tokens.shape[1] // seq_size)
        split = Mesh(devices.reshape(seq_size, units, ctx_size // units), ALL_AXES)
        mapped = jax.shard_map(
            on_device,
            mesh=split,
            in_specs=(tok, P(ctx, "seq")) + pairs + (tok,),
            out_specs=(tok, tok) + pairs,
            check_vma=False,
        )
        return mapped(tokens, *rest)

    return run
```

```python
import functools
import math

import jax
import jax.numpy as jnp
from jax import lax
from jax.experimental import pallas as pl
from jax.experimental.pallas import tpu as pltpu
from jax.sharding import Mesh, PartitionSpec as P

HEADS = 12
HEAD_DIM = 64
ROT = 16
TRIO = 3
TILE = 128
PACK = 5 * TILE
OPACK = 2 * TILE

EPSILON = 1e-05
NEG_BIG = -1e30
BF = jnp.bfloat16
F32 = jnp.float32
ALL_AXES = ("seq", "unit", "part")
VMEM_BYTES = 56 * 1024 * 1024


def params_of(*semantics):
    return pltpu.CompilerParams(
        dimension_semantics=semantics, vmem_limit_bytes=VMEM_BYTES
    )


def mm(a, b):
    return jnp.dot(a, b, preferred_element_type=F32)


def outer_sum(left_rows, right_rows):
    return lax.dot_general(
        left_rows, right_rows, (((0,), (0,)), ((), ())), preferred_element_type=F32
    )


def inner_back(grad_rows, weight):
    return lax.dot_general(
        grad_rows, weight, (((1,), (1,)), ((), ())), preferred_element_type=F32
    )


def lane_of(shape):
    return lax.broadcasted_iota(jnp.int32, shape, len(shape) - 1)


def turn(tile, cos, sin):
    partner = jnp.where(
        lane_of(tile.shape) % HEAD_DIM < ROT // 2,
        pltpu.roll(tile, TILE - ROT // 2, 1),
        pltpu.roll(tile, ROT // 2, 1),
    )
    return tile * cos + partner * sin


def turn_tables(cos_rows, sin_rows):
    rows = cos_rows.shape[1]
    rest = HEAD_DIM - ROT
    cos_head = [cos_rows, cos_rows, jnp.ones((rest, rows), F32)]
    sin_head = [-sin_rows, sin_rows, jnp.zeros((rest, rows), F32)]
    return jnp.concatenate(cos_head * 2, 0).T, jnp.concatenate(sin_head * 2, 0).T


def project_kernel(
    tok_ref, w_ref, b_ref, gain_ref, bias_ref, cos_ref, sin_ref, out_ref, norm_ref, hat_ref
):
    x = tok_ref[0].astype(F32)
    centre = x - jnp.mean(x, -1, keepdims=True)
    spread = jnp.mean(centre * centre, -1, keepdims=True)
    hat = centre * lax.rsqrt(spread + EPSILON)
    normed = (hat * gain_ref[...] + bias_ref[...]).astype(BF)
    hat_ref[0] = hat.astype(BF)
    norm_ref[0] = normed
    y = mm(normed, w_ref[...]) + b_ref[...]
    cos, sin = turn_tables(cos_ref[0], sin_ref[0])
    for t in range(5):
        tile = y[:, t * TILE : (t + 1) * TILE]
        if t in (0, 1, 3):
            tile = turn(tile, cos, sin)
        out_ref[0, :, t * TILE : (t + 1) * TILE] = tile.astype(BF)


def project(toks, weight, bias, gain, offset, cos, sin):
    units, rows, d = toks.shape
    tok_spec = pl.BlockSpec((1, rows, d), lambda j: (j, 0, 0))
    row_spec = pl.BlockSpec((1, d), lambda j: (0, 0))
    turn_spec = pl.BlockSpec((1, ROT // 2, rows), lambda j: (j, 0, 0))
    return pl.pallas_call(
        project_kernel,
        grid=(units,),
        in_specs=[
            tok_spec,
            pl.BlockSpec((d, PACK), lambda j: (0, 0)),
            pl.BlockSpec((1, PACK), lambda j: (0, 0)),
            row_spec,
            row_spec,
            turn_spec,
            turn_spec,
        ],
        out_specs=[pl.BlockSpec((1, rows, PACK), lambda j: (j, 0, 0)), tok_spec, tok_spec],
        out_shape=[
            jax.ShapeDtypeStruct((units, rows, PACK), BF),
            jax.ShapeDtypeStruct((units, rows, d), BF),
            jax.ShapeDtypeStruct((units, rows, d), BF),
        ],
        compiler_params=params_of("arbitrary"),
        cost_estimate=pl.CostEstimate(
            flops=2 * units * rows * d * PACK,
            bytes_accessed=2 * units * rows * (3 * d + PACK),
            transcendentals=0,
        ),
        name="project",
    )(toks, weight, bias, gain, offset, cos, sin)


def unturn_kernel(*refs):
    own_ref, cos_ref, sin_ref, out_ref = refs[0], refs[-3], refs[-2], refs[-1]
    others = refs[1:-3]
    cos, sin = turn_tables(cos_ref[0], sin_ref[0])
    for t in range(5):
        tile = own_ref[0, :, t * TILE : (t + 1) * TILE].astype(F32)
        if t > 0:
            for other in others:
                tile = tile + other[0, :, (t - 1) * TILE : t * TILE].astype(F32)
        if t in (0, 1, 3):
            tile = turn(tile, cos, -sin)
        out_ref[0, :, t * TILE : (t + 1) * TILE] = tile.astype(BF)


def unturn(own, others, cos, sin):
    units, rows, unused = own.shape
    turn_spec = pl.BlockSpec((1, ROT // 2, rows), lambda j: (j, 0, 0))
    own_spec = pl.BlockSpec((1, rows, PACK), lambda j: (j, 0, 0))
    other_spec = pl.BlockSpec((1, rows, PACK - TILE), lambda j: (j, 0, 0))
    return pl.pallas_call(
        unturn_kernel,
        grid=(units,),
        in_specs=[own_spec] + [other_spec] * len(others) + [turn_spec, turn_spec],
        out_specs=own_spec,
        out_shape=jax.ShapeDtypeStruct(own.shape, BF),
        compiler_params=params_of("arbitrary"),
        name="unturn",
    )(own, *others, cos, sin)


def flip(tile):
    return tile.astype(F32).T


def head_rows(flipped, low):
    row = lax.broadcasted_iota(jnp.int32, flipped.shape, 0)
    keep = row < HEAD_DIM if low else row >= HEAD_DIM
    return jnp.where(keep, flipped, 0.0)


def head_lanes(tile, low):
    lane = lane_of(tile.shape)
    keep = lane < HEAD_DIM if low else lane >= HEAD_DIM
    return jnp.where(keep, tile, 0.0)


def query_sides(q_ref, qb):
    scale = HEAD_DIM ** (-0.5)
    a = flip(q_ref[0, :, 0:TILE]) * scale
    d = flip(q_ref[0, :, 3 * TILE : 4 * TILE]) * scale
    qb[0] = head_rows(a, True).astype(BF)
    qb[1] = head_rows(a, False).astype(BF)
    qb[2] = jnp.concatenate(
        [jnp.zeros((HEAD_DIM, d.shape[1]), F32), d[:HEAD_DIM]], 0
    ).astype(BF)


def live_of(seg_row, key_start, query_start, rows):
    shape = (rows, rows)
    key_pos = key_start + lax.broadcasted_iota(jnp.int32, shape, 0)
    query_pos = query_start + lax.broadcasted_iota(jnp.int32, shape, 1)
    return (key_pos <= query_pos) & (key_pos >= seg_row)


def block_loop(meta, part, units, rows, step):
    j = pl.program_id(0)
    c = meta[2 * units]
    diag = j * part + c
    first = meta[j] // rows
    top_seg = meta[units + j]

    def one(kb, unused):
        where = (lax.rem(c - lax.rem(kb, part) + part, part), kb // part)
        masked = (kb == diag) | (top_seg > kb * rows)

        @pl.when(masked)
        def _():
            step(where, kb, diag, True)

        @pl.when(jnp.logical_not(masked))
        def _():
            step(where, kb, diag, False)

        return unused

    lax.fori_loop(first, diag + 1, one, 0)
    return diag


def forward_kernel(
    part, units, meta, q_ref, kv_ref, seg_ref, o_ref, ot_ref, lse_ref, qb, vt, top, total, acc
):
    rows = q_ref.shape[1]
    c = meta[2 * units]

    @pl.when(pl.program_id(0) == 0)
    def _():
        for i in range(part):
            p = lax.rem(c - i + part, part)
            for unit in range(units):
                kb = unit * part + p
                vt[kb, :TILE] = flip(kv_ref[i, unit, :, TILE : 2 * TILE]).astype(BF)
                vt[kb, TILE:] = flip(kv_ref[i, unit, :, 3 * TILE :])[:HEAD_DIM].astype(BF)

    query_sides(q_ref, qb)
    top[...] = jnp.full(top.shape, NEG_BIG, F32)
    total[...] = jnp.zeros(total.shape, F32)
    acc[...] = jnp.zeros(acc.shape, F32)
    seg_row = seg_ref[0]

    def step(where, kb, diag, masked):
        k01 = kv_ref[where[0], where[1], :, 0:TILE]
        k2 = kv_ref[where[0], where[1], :, 2 * TILE : 3 * TILE]
        if masked:
            live = live_of(seg_row, kb * rows, diag * rows, rows)
        scores = [mm(k2 if h == 2 else k01, qb[h]) for h in range(TRIO)]
        if masked:
            scores = [jnp.where(live, score, NEG_BIG) for score in scores]
        old = top[0:TRIO]
        new = jnp.concatenate([jnp.max(score, 0, keepdims=True) for score in scores], 0)
        new = jnp.maximum(old, new)
        factor = jnp.exp(old - new)
        weights = [jnp.exp(scores[h] - new[h : h + 1]) for h in range(TRIO)]
        if masked:
            weights = [jnp.where(live, weight, 0.0) for weight in weights]
        sums = [jnp.sum(weight, 0, keepdims=True) for weight in weights]
        top[0:TRIO] = new
        total[0:TRIO] = total[0:TRIO] * factor + jnp.concatenate(sums, 0)
        for h in range(TRIO):
            vth = vt[kb, h * HEAD_DIM : (h + 1) * HEAD_DIM]
            acc[h] = acc[h] * factor[h : h + 1] + mm(vth, weights[h].astype(BF))

    block_loop(meta, part, units, rows, step)
    out = [acc[h] / total[h : h + 1] for h in range(TRIO)]
    for h in range(TRIO):
        ot_ref[0, h * HEAD_DIM : (h + 1) * HEAD_DIM] = out[h]
    lse_ref[0, 0:TRIO] = top[0:TRIO] + jnp.log(total[0:TRIO])
    o_ref[0, :, :TILE] = jnp.concatenate(out[:2], 0).T.astype(BF)
    o_ref[0, :, TILE:] = jnp.concatenate([out[2], jnp.zeros_like(out[2])], 0).T.astype(BF)


def backward_kernel(
    part,
    units,
    meta,
    q_ref,
    do_ref,
    ot_ref,
    lse_ref,
    kv_ref,
    seg_ref,
    own_ref,
    oth_ref,
    qb,
    db,
    qn,
    dn,
    kt,
    delta,
    dqt,
    dk01,
    dv01,
    dk2,
    dv2,
):
    rows = q_ref.shape[1]
    c = meta[2 * units]
    j = pl.program_id(0)

    @pl.when(j == 0)
    def _():
        for i in range(part):
            p = lax.rem(c - i + part, part)
            for unit in range(units):
                kb = unit * part + p
                kt[kb, :TILE] = flip(kv_ref[i, unit, :, 0:TILE]).astype(BF)
                kt[kb, TILE:] = flip(kv_ref[i, unit, :, 2 * TILE : 3 * TILE])[HEAD_DIM:].astype(BF)
        for ref in (dk01, dv01, dk2, dv2):
            ref[...] = jnp.zeros(ref.shape, F32)

    query_sides(q_ref, qb)
    scale = HEAD_DIM ** (-0.5)
    q01 = q_ref[0, :, 0:TILE].astype(F32) * scale
    q2 = pltpu.roll(q_ref[0, :, 3 * TILE : 4 * TILE].astype(F32), HEAD_DIM, 1) * scale
    qn[0:rows] = head_lanes(q01, True).astype(BF)
    qn[rows : 2 * rows] = head_lanes(q01, False).astype(BF)
    qn[2 * rows :] = head_lanes(q2, False).astype(BF)
    do01 = do_ref[0, :, :TILE].astype(F32)
    do2 = do_ref[0, :, TILE:].astype(F32)
    dn[0:rows] = head_lanes(do01, True).astype(BF)
    dn[rows : 2 * rows] = head_lanes(do01, False).astype(BF)
    dn[2 * rows :] = do2.astype(BF)
    do01t = do01.T
    do2t = do2.T
    db[0] = head_rows(do01t, True).astype(BF)
    db[1] = head_rows(do01t, False).astype(BF)
    db[2] = do2t.astype(BF)
    for h in range(TRIO):
        dot = do2t[:HEAD_DIM] if h == 2 else do01t[h * HEAD_DIM : (h + 1) * HEAD_DIM]
        delta[h : h + 1] = jnp.sum(
            dot * ot_ref[0, h * HEAD_DIM : (h + 1) * HEAD_DIM], 0, keepdims=True
        )
    dqt[...] = jnp.zeros(dqt.shape, F32)
    seg_row = seg_ref[0]

    def step(where, kb, diag, masked):
        k01 = kv_ref[where[0], where[1], :, 0:TILE]
        v01 = kv_ref[where[0], where[1], :, TILE : 2 * TILE]
        k2 = kv_ref[where[0], where[1], :, 2 * TILE : 3 * TILE]
        v2 = kv_ref[where[0], where[1], :, 3 * TILE :]
        if masked:
            live = live_of(seg_row, kb * rows, diag * rows, rows)
        probs = []
        grads = []
        for h in range(TRIO):
            score = mm(k2 if h == 2 else k01, qb[h])
            if masked:
                score = jnp.where(live, score, NEG_BIG)
            prob = jnp.exp(score - lse_ref[0, h : h + 1])
            if masked:
                prob = jnp.where(live, prob, 0.0)
            dprob = mm(v2 if h == 2 else v01, db[h])
            ds = (prob * (dprob - delta[h : h + 1])).astype(BF)
            probs.append(prob.astype(BF))
            grads.append(ds)
            kth = kt[kb, h * HEAD_DIM : (h + 1) * HEAD_DIM]
            dqt[h * HEAD_DIM : (h + 1) * HEAD_DIM] += mm(kth, ds)
        dv01[kb] += mm(jnp.concatenate(probs[:2], 1), dn[: 2 * rows])
        dk01[kb] += mm(jnp.concatenate(grads[:2], 1), qn[: 2 * rows])
        dv2[kb] += mm(probs[2], dn[2 * rows :])
        dk2[kb] += mm(grads[2], qn[2 * rows :])

    diag = block_loop(meta, part, units, rows, step)
    own_ref[j, :, 0:TILE] = (dqt[:TILE] * scale).T.astype(BF)
    dq2 = dqt[TILE:] * scale
    dk2[diag] += jnp.concatenate([dq2, jnp.zeros_like(dq2)], 0).T

    @pl.when(j == units - 1)
    def _():
        for unit in range(units):
            for i in range(part):
                kb = unit * part + lax.rem(c + i, part)
                for t, ref in enumerate((dk01, dv01, dk2, dv2)):
                    tile = ref[kb].astype(BF)
                    if i == 0:
                        own_ref[unit, :, (t + 1) * TILE : (t + 2) * TILE] = tile
                    else:
                        oth_ref[i - 1, unit, :, t * TILE : (t + 1) * TILE] = tile


def attention_cost(products, units, rows, part):
    pairs = TRIO * rows * rows * units * units * part // 2
    return pl.CostEstimate(
        flops=2 * 64 * products * pairs, bytes_accessed=20_000_000, transcendentals=pairs
    )


def whole_spec(shape):
    zeros = (0,) * len(shape)
    return pl.BlockSpec(shape, lambda j, meta: zeros)


def attend_forward(meta, packed, kv, seg):
    units, rows, unused = packed.shape
    part = kv.shape[0]
    return pl.pallas_call(
        functools.partial(forward_kernel, part, units),
        grid_spec=pltpu.PrefetchScalarGridSpec(
            num_scalar_prefetch=1,
            grid=(units,),
            in_specs=[
                pl.BlockSpec((1, rows, PACK), lambda j, meta: (j, 0, 0)),
                whole_spec(kv.shape),
                pl.BlockSpec((1, 1, rows), lambda j, meta: (j, 0, 0)),
            ],
            out_specs=[
                pl.BlockSpec((1, rows, OPACK), lambda j, meta: (j, 0, 0)),
                pl.BlockSpec((1, TRIO * HEAD_DIM, rows), lambda j, meta: (j, 0, 0)),
                pl.BlockSpec((1, 8, rows), lambda j, meta: (j, 0, 0)),
            ],
            scratch_shapes=[
                pltpu.VMEM((TRIO, TILE, rows), BF),
                pltpu.VMEM((units * part, TRIO * HEAD_DIM, rows), BF),
                pltpu.VMEM((8, rows), F32),
                pltpu.VMEM((8, rows), F32),
                pltpu.VMEM((TRIO, HEAD_DIM, rows), F32),
            ],
        ),
        out_shape=[
            jax.ShapeDtypeStruct((units, rows, OPACK), BF),
            jax.ShapeDtypeStruct((units, TRIO * HEAD_DIM, rows), F32),
            jax.ShapeDtypeStruct((units, 8, rows), F32),
        ],
        compiler_params=params_of("arbitrary"),
        cost_estimate=attention_cost(8, units, rows, part),
        name="attend_forward",
    )(meta, packed, kv, seg)


def attend_backward(meta, packed, dout, out_t, lse, kv, seg):
    units, rows, unused = packed.shape
    part = kv.shape[0]
    others = (max(part - 1, 1), units, rows, 4 * TILE)
    grads = pltpu.VMEM((units * part, rows, TILE), F32)
    return pl.pallas_call(
        functools.partial(backward_kernel, part, units),
        grid_spec=pltpu.PrefetchScalarGridSpec(
            num_scalar_prefetch=1,
            grid=(units,),
            in_specs=[
                pl.BlockSpec((1, rows, PACK), lambda j, meta: (j, 0, 0)),
                pl.BlockSpec((1, rows, OPACK), lambda j, meta: (j, 0, 0)),
                pl.BlockSpec((1, TRIO * HEAD_DIM, rows), lambda j, meta: (j, 0, 0)),
                pl.BlockSpec((1, 8, rows), lambda j, meta: (j, 0, 0)),
                whole_spec(kv.shape),
                pl.BlockSpec((1, 1, rows), lambda j, meta: (j, 0, 0)),
            ],
            out_specs=[whole_spec(packed.shape), whole_spec(others)],
            scratch_shapes=[
                pltpu.VMEM((TRIO, TILE, rows), BF),
                pltpu.VMEM((TRIO, TILE, rows), BF),
                pltpu.VMEM((TRIO * rows, TILE), BF),
                pltpu.VMEM((TRIO * rows, TILE), BF),
                pltpu.VMEM((units * part, TRIO * HEAD_DIM, rows), BF),
                pltpu.VMEM((8, rows), F32),
                pltpu.VMEM((TRIO * HEAD_DIM, rows), F32),
                grads,
                grads,
                grads,
                grads,
            ],
        ),
        out_shape=[
            jax.ShapeDtypeStruct(packed.shape, BF),
            jax.ShapeDtypeStruct(others, BF),
        ],
        compiler_params=params_of("arbitrary"),
        cost_estimate=attention_cost(20, units, rows, part),
        name="attend_backward",
    )(meta, packed, dout, out_t, lse, kv, seg)


def pack_columns(matrix, trios):
    r = matrix.shape[0]
    q, k, v = (
        part.reshape(r, trios, TRIO * HEAD_DIM) for part in jnp.split(matrix, 3, axis=1)
    )
    zeros = jnp.zeros((r, trios, HEAD_DIM), matrix.dtype)
    pieces = [q[..., :TILE], k[..., :TILE], v[..., :TILE], q[..., TILE:], k[..., TILE:]]
    return jnp.concatenate(pieces + [v[..., TILE:], zeros], -1).reshape(r, trios * PACK)


def unpack_columns(matrix, trios):
    r = matrix.shape[0]
    m = matrix.reshape(r, trios, PACK)
    halves = [
        m[..., 3 * TILE : 3 * TILE + HEAD_DIM],
        m[..., 3 * TILE + HEAD_DIM : 4 * TILE],
        m[..., 4 * TILE : 4 * TILE + HEAD_DIM],
    ]
    return jnp.concatenate(
        [
            jnp.concatenate([m[..., i * TILE : (i + 1) * TILE], halves[i]], -1).reshape(r, -1)
            for i in range(3)
        ],
        -1,
    )


def split_hidden(matrix, count, r):
    lead = matrix.shape[0]
    return matrix.reshape(lead, count, -1, r).transpose(0, 2, 1, 3).reshape(lead, -1)


def join_hidden(matrix, count, r):
    lead = matrix.shape[0]
    return matrix.reshape(lead, -1, count, r).transpose(0, 2, 1, 3).reshape(lead, -1)


def on_device(
    tokens,
    segment,
    ln1_gain,
    ln1_bias,
    ln2_gain,
    ln2_bias,
    qkv_weight,
    qkv_bias,
    dense_weight,
    dense_bias,
    fc1_weight,
    fc1_bias,
    output_feed_weight,
    output_feed_bias,
    cotangent,
):
    rows, groups, d = tokens.shape
    units = lax.axis_size("unit")
    part = lax.axis_size("part")
    count = units * part * lax.axis_size("seq")
    trios = units // groups
    all_rows = rows * groups
    r = qkv_weight.shape[0]
    ff = fc1_weight.shape[1]
    blocks = ff // d
    c = lax.axis_index("part")
    unit = lax.axis_index("unit")

    seq = lax.axis_index("seq")
    seqs = lax.axis_size("seq")
    place = (seq * units + unit) * part + c

    def exchange(blocks_out):
        width = blocks_out.shape[-1]
        return lax.all_to_all(
            blocks_out.reshape(-1, width), "unit", 0, 0, tiled=True
        ).reshape(blocks_out.shape)

    def shift(value, axis, i):
        n = lax.axis_size(axis)
        return lax.ppermute(value, axis, [(p, (p + i) % n) for p in range(n)])

    def gather_small(value, axis):
        n = lax.axis_size(axis)
        me = lax.axis_index(axis)
        got = [value] + [shift(value, axis, i) for i in range(1, n)]
        if n == 2:
            return jnp.where(me == 0, jnp.stack(got), jnp.stack(got[::-1]))
        got = jnp.stack(got)
        return jnp.stack(
            [lax.dynamic_index_in_dim(got, (me - k + n) % n, 0, False) for k in range(n)]
        )

    def scatter_small(value, axis):
        n = lax.axis_size(axis)
        me = lax.axis_index(axis)
        total = lax.dynamic_index_in_dim(value, me, 0, False).astype(F32)
        for i in range(1, n):
            piece = lax.dynamic_index_in_dim(value, (me + i) % n, 0, False)
            total = total + shift(piece, axis, i).astype(F32)
        return total.astype(BF)

    vectors = (ln1_gain, ln1_bias, ln2_gain, ln2_bias, dense_bias, output_feed_bias)
    vec = jnp.concatenate(
        [v.reshape(r, 1) for v in vectors] + [qkv_bias.reshape(r, 3), fc1_bias.reshape(r, blocks)],
        1,
    )
    vec = jnp.pad(vec, ((0, 0), (0, TILE - vec.shape[1])))
    qkv_local = pack_columns(qkv_weight, trios)
    seg_rows = segment.T
    seg_pack = jnp.concatenate([seg_rows // 64, seg_rows % 64], 1).astype(BF)
    seg_pack = jnp.pad(seg_pack[:, None, :], ((0, 0), (0, 7), (0, PACK + TILE - 2 * rows)))
    early = []
    for u in range(units):
        g = u // groups
        trio_cols = jnp.concatenate([qkv_local[:, g * PACK : (g + 1) * PACK], vec], 1)
        early += [trio_cols, seg_pack[u % groups]]
    early = exchange(jnp.concatenate(early, 0).reshape(units, r + 8, PACK + TILE))
    token_rows = tokens.transpose(1, 0, 2)
    toks = exchange(jnp.concatenate([token_rows] * trios, 0))

    seg_mine = early[:, r, : 2 * rows].astype(jnp.int32)
    seg_mine = seg_mine[:, :rows] * 64 + seg_mine[:, rows:]
    meta = jnp.concatenate([seg_mine[:, 0], seg_mine[:, -1], c[None]])
    seg_mine = seg_mine[:, None, :]
    trio_full = gather_small(gather_small(early[:, :r], "seq"), "part")
    trio_full = trio_full.transpose(1, 2, 0, 3, 4).reshape(d, PACK + TILE)
    vec_full = trio_full[:, PACK:].astype(F32)
    vec_rows = vec_full[:, :8].T
    gain_one, bias_one, gain_two, bias_two, dense_shift, down_shift = (
        vec_rows[i : i + 1] for i in range(6)
    )
    qkv_shift = pack_columns(vec_full[:, 6:9].reshape(1, 3 * d), trios).reshape(trios, PACK)
    qkv_shift = lax.dynamic_slice_in_dim(qkv_shift, unit // groups, 1, 0)
    up_shift = split_hidden(vec_full[:, 9 : 9 + blocks].reshape(1, ff), count, r)

    feed_blocks = output_feed_weight.reshape(blocks, r, d)
    second_pack = jnp.concatenate(
        [split_hidden(fc1_weight, count, r)]
        + [feed_blocks[b] for b in range(blocks)]
        + [dense_weight],
        1,
    )
    second = lax.all_gather(second_pack, ALL_AXES, axis=0, tiled=True)
    qkv_full = lax.all_gather(qkv_local, ALL_AXES, axis=0, tiled=True)
    dense_pad = jnp.pad(
        second[:, 2 * ff :].reshape(trios, d // trios, d),
        ((0, 0), (0, OPACK - d // trios), (0, 0)),
    )

    block_start = (jnp.arange(units, dtype=jnp.int32) * part + c) * rows
    positions = block_start[:, None, None] + jnp.arange(rows, dtype=jnp.int32) - seg_mine
    freq = jnp.arange(ROT // 2, dtype=F32)
    inverse = jnp.exp(freq * (-2.0 * math.log(10000.0) / ROT))
    angles = positions.astype(F32) * inverse[None, :, None]
    cos = jnp.cos(angles)
    sin = jnp.sin(angles)

    packed, normed_one, hat_one = project(
        toks, trio_full, qkv_shift, gain_one, bias_one, cos, sin
    )
    kv_own = packed[:, :, TILE:]
    kv = jnp.stack([kv_own] + [shift(kv_own, "part", i) for i in range(1, part)])
    out_low, out_t, lse = attend_forward(meta, packed, kv, seg_mine)
    attended = exchange(out_low)

    x = token_rows.reshape(all_rows, d).astype(F32)
    cot = cotangent.transpose(1, 0, 2).reshape(all_rows, d)
    cot_float = cot.astype(F32)
    centre = x - jnp.mean(x, -1, keepdims=True)
    spread = lax.rsqrt(jnp.mean(centre * centre, -1, keepdims=True) + EPSILON)
    xhat = centre * spread
    normed_two = (xhat * gain_two + bias_two).astype(BF)
    attended_grad = jnp.einsum(
        "sld,gkd->gslk", cot.reshape(groups, rows, d), dense_pad, preferred_element_type=F32
    ).astype(BF)
    dout = exchange(attended_grad.reshape(units, rows, OPACK))

    up_full = second[:, :ff]
    down_full = jnp.concatenate(
        [second[:, ff + b * d : ff + (b + 1) * d] for b in range(blocks)], 0
    )
    hidden_pre = mm(normed_two, up_full) + up_shift
    cdf = 0.5 * (1.0 + lax.erf(hidden_pre * math.sqrt(0.5)))
    hidden_low = (hidden_pre * cdf).astype(BF)
    slope = cdf + hidden_pre * (
        jnp.exp(-0.5 * hidden_pre * hidden_pre) * (1.0 / math.sqrt(2.0 * math.pi))
    )
    pre_grad = (inner_back(cot, down_full) * slope).astype(BF)
    second_branch = mm(hidden_low, down_full) + down_shift
    down_grad = outer_sum(hidden_low, cot)
    up_grad = outer_sum(normed_two, pre_grad)
    up_shift_grad = jnp.sum(pre_grad.astype(F32), 0)
    normed_two_grad = inner_back(pre_grad, up_full)
    cot_sum = jnp.sum(cot_float, 0)

    def norm_back(grad, gain):
        gy = grad * gain
        return spread * (
            gy - jnp.mean(gy, -1, keepdims=True) - xhat * jnp.mean(gy * xhat, -1, keepdims=True)
        )

    in_two = norm_back(normed_two_grad, gain_two)

    attended = attended.reshape(trios, groups, rows, OPACK).transpose(1, 2, 0, 3)
    attended = attended.reshape(all_rows, trios * OPACK)
    branch_one = mm(attended, dense_pad.reshape(trios * OPACK, d)) + dense_shift
    output = (x + branch_one + second_branch).astype(BF)
    dense_grad = outer_sum(attended, cot).reshape(trios, OPACK, d)[:, : d // trios].reshape(d, d)

    vec_grads = jnp.concatenate(
        [
            jnp.sum(normed_two_grad * xhat, 0)[None],
            jnp.sum(normed_two_grad, 0)[None],
            cot_sum[None],
            jnp.zeros((5, d), F32),
        ],
        0,
    ).T
    up_shift_grad = join_hidden(up_shift_grad[None], count, r).reshape(d, blocks)
    vec_grads = jnp.concatenate(
        [vec_grads, up_shift_grad, jnp.zeros((d, TILE - 8 - blocks), F32)], 1
    )
    mlp_grads = jnp.concatenate(
        [up_grad.astype(BF)]
        + [down_grad[b * d : (b + 1) * d].astype(BF) for b in range(blocks)]
        + [dense_grad.astype(BF), vec_grads.astype(BF)],
        1,
    )
    mlp_grads, kv = lax.optimization_barrier((mlp_grads, kv))
    mlp_sum = lax.psum_scatter(mlp_grads, ALL_AXES, scatter_dimension=0, tiled=True).astype(F32)

    own, others = attend_backward(meta, packed, dout, out_t, lse, kv, seg_mine)
    others = [shift(others[i - 1], "part", i) for i in range(1, part)]
    qkv_grad = unturn(own, others, cos, sin)
    back = exchange(qkv_grad)

    grad_rows = qkv_grad.reshape(units * rows, PACK)
    trio_weight = trio_full[:, :PACK].astype(F32)
    trio_grad = outer_sum(normed_one.reshape(units * rows, d), grad_rows)
    hat_grad = outer_sum(hat_one.reshape(units * rows, d), grad_rows)
    shift_grad = jnp.sum(grad_rows.astype(F32), 0)[None]
    late_vec = jnp.concatenate(
        [
            jnp.sum(trio_weight * hat_grad, 1, keepdims=True),
            jnp.sum(trio_weight * shift_grad, 1, keepdims=True),
            jnp.zeros((d, TILE - 2), F32),
        ],
        1,
    )
    late = jnp.concatenate([trio_grad.astype(BF), late_vec.astype(BF)], 1)
    late = late.reshape(seqs, units, part, r, PACK + TILE)
    shift_rows = jnp.pad(shift_grad.astype(BF), ((0, 7), (0, TILE)))
    late = jnp.concatenate(
        [late, jnp.broadcast_to(shift_rows, (seqs, units, part) + shift_rows.shape)], 3
    )
    late = scatter_small(late.transpose(2, 0, 1, 3, 4), "part")
    late = exchange(scatter_small(late, "seq")).astype(F32)
    late = jnp.sum(late.reshape(trios, groups, r + 8, PACK + TILE), 1)
    qkv_weight_grad = unpack_columns(
        late[:, :r, :PACK].transpose(1, 0, 2).reshape(r, trios * PACK), trios
    )
    late_vec = jnp.sum(late[:, :r, PACK : PACK + 2], 0)
    qkv_shift_grad = unpack_columns(late[:, r, :PACK].reshape(1, trios * PACK), trios)[0]
    qkv_shift_grad = lax.dynamic_slice_in_dim(qkv_shift_grad, place * 3 * r, 3 * r)

    back = back.reshape(trios, groups, rows, PACK).transpose(1, 2, 0, 3)
    normed_one_grad = inner_back(back.reshape(all_rows, trios * PACK), qkv_full)
    in_one = norm_back(normed_one_grad, gain_one)
    tokens_grad = (cot_float + in_one + in_two).astype(BF)

    def natural(value):
        return value.reshape(groups, rows, d).transpose(1, 0, 2)

    down_sum = jnp.concatenate(
        [mlp_sum[:, ff + b * d : ff + (b + 1) * d] for b in range(blocks)], 0
    )
    vec_sum = mlp_sum[:, 2 * ff + d :]
    cot_total = vec_sum[:, 2]
    return (
        natural(output),
        natural(tokens_grad),
        late_vec[:, 0],
        late_vec[:, 1],
        vec_sum[:, 0],
        vec_sum[:, 1],
        qkv_weight_grad,
        qkv_shift_grad,
        mlp_sum[:, 2 * ff : 2 * ff + d],
        cot_total,
        join_hidden(mlp_sum[:, :ff], count, r),
        vec_sum[:, 8 : 8 + blocks].reshape(-1),
        down_sum,
        cot_total,
    )


def solution(mesh):
    devices = mesh.devices
    seq_size, ctx_size = devices.shape
    ctx = ("unit", "part")
    tok = P(ctx, "seq", None)
    vec = P(ALL_AXES)
    mat = P(ALL_AXES, None)
    pairs = (vec, vec, vec, vec, mat, vec, mat, vec, mat, vec, mat, vec)

    def run(tokens, *rest):
        units = HEADS // TRIO * (tokens.shape[1] // seq_size)
        split = Mesh(devices.reshape(seq_size, units, ctx_size // units), ALL_AXES)
        mapped = jax.shard_map(
            on_device,
            mesh=split,
            in_specs=(tok, P(ctx, "seq")) + pairs + (tok,),
            out_specs=(tok, tok) + pairs,
            check_vma=False,
        )
        return mapped(tokens, *rest)

    return run
```

```python
import functools
import math

import jax
import jax.numpy as jnp
from jax import lax
from jax.experimental import pallas as pl
from jax.experimental.pallas import tpu as pltpu
from jax.sharding import Mesh, PartitionSpec as P

HEADS = 12
HEAD_DIM = 64
ROT = 16
TRIO = 3
TILE = 128
PACK = 5 * TILE
OPACK = 2 * TILE

EPSILON = 1e-05
NEG_BIG = -1e30
BF = jnp.bfloat16
F32 = jnp.float32
ALL_AXES = ("seq", "unit", "part")
VMEM_BYTES = 56 * 1024 * 1024


def params_of(*semantics):
    return pltpu.CompilerParams(
        dimension_semantics=semantics, vmem_limit_bytes=VMEM_BYTES
    )


def mm(a, b):
    return jnp.dot(a, b, preferred_element_type=F32)


def outer_sum(left_rows, right_rows):
    return lax.dot_general(
        left_rows, right_rows, (((0,), (0,)), ((), ())), preferred_element_type=F32
    )


def inner_back(grad_rows, weight):
    return lax.dot_general(
        grad_rows, weight, (((1,), (1,)), ((), ())), preferred_element_type=F32
    )


def lane_of(shape):
    return lax.broadcasted_iota(jnp.int32, shape, len(shape) - 1)


def turn(tile, cos, sin):
    partner = jnp.where(
        lane_of(tile.shape) % HEAD_DIM < ROT // 2,
        pltpu.roll(tile, TILE - ROT // 2, 1),
        pltpu.roll(tile, ROT // 2, 1),
    )
    return tile * cos + partner * sin


def turn_tables(cos_rows, sin_rows):
    rows = cos_rows.shape[1]
    rest = HEAD_DIM - ROT
    cos_head = [cos_rows, cos_rows, jnp.ones((rest, rows), F32)]
    sin_head = [-sin_rows, sin_rows, jnp.zeros((rest, rows), F32)]
    return jnp.concatenate(cos_head * 2, 0).T, jnp.concatenate(sin_head * 2, 0).T


def project_kernel(
    tok_ref, w_ref, b_ref, gain_ref, bias_ref, cos_ref, sin_ref, out_ref, norm_ref, hat_ref
):
    x = tok_ref[0].astype(F32)
    centre = x - jnp.mean(x, -1, keepdims=True)
    spread = jnp.mean(centre * centre, -1, keepdims=True)
    hat = centre * lax.rsqrt(spread + EPSILON)
    normed = (hat * gain_ref[...] + bias_ref[...]).astype(BF)
    hat_ref[0] = hat.astype(BF)
    norm_ref[0] = normed
    y = mm(normed, w_ref[...]) + b_ref[...]
    cos, sin = turn_tables(cos_ref[0], sin_ref[0])
    for t in range(5):
        tile = y[:, t * TILE : (t + 1) * TILE]
        if t in (0, 1, 3):
            tile = turn(tile, cos, sin)
        out_ref[0, :, t * TILE : (t + 1) * TILE] = tile.astype(BF)


def project(toks, weight, bias, gain, offset, cos, sin):
    units, rows, d = toks.shape
    tok_spec = pl.BlockSpec((1, rows, d), lambda j: (j, 0, 0))
    row_spec = pl.BlockSpec((1, d), lambda j: (0, 0))
    turn_spec = pl.BlockSpec((1, ROT // 2, rows), lambda j: (j, 0, 0))
    return pl.pallas_call(
        project_kernel,
        grid=(units,),
        in_specs=[
            tok_spec,
            pl.BlockSpec((d, PACK), lambda j: (0, 0)),
            pl.BlockSpec((1, PACK), lambda j: (0, 0)),
            row_spec,
            row_spec,
            turn_spec,
            turn_spec,
        ],
        out_specs=[pl.BlockSpec((1, rows, PACK), lambda j: (j, 0, 0)), tok_spec, tok_spec],
        out_shape=[
            jax.ShapeDtypeStruct((units, rows, PACK), BF),
            jax.ShapeDtypeStruct((units, rows, d), BF),
            jax.ShapeDtypeStruct((units, rows, d), BF),
        ],
        compiler_params=params_of("arbitrary"),
        cost_estimate=pl.CostEstimate(
            flops=2 * units * rows * d * PACK,
            bytes_accessed=2 * units * rows * (3 * d + PACK),
            transcendentals=0,
        ),
        name="project",
    )(toks, weight, bias, gain, offset, cos, sin)


def unturn_kernel(*refs):
    own_ref, cos_ref, sin_ref, out_ref = refs[0], refs[-3], refs[-2], refs[-1]
    others = refs[1:-3]
    cos, sin = turn_tables(cos_ref[0], sin_ref[0])
    for t in range(5):
        tile = own_ref[0, :, t * TILE : (t + 1) * TILE].astype(F32)
        if t > 0:
            for other in others:
                tile = tile + other[0, :, (t - 1) * TILE : t * TILE].astype(F32)
        if t in (0, 1, 3):
            tile = turn(tile, cos, -sin)
        out_ref[0, :, t * TILE : (t + 1) * TILE] = tile.astype(BF)


def unturn(own, others, cos, sin):
    units, rows, unused = own.shape
    turn_spec = pl.BlockSpec((1, ROT // 2, rows), lambda j: (j, 0, 0))
    own_spec = pl.BlockSpec((1, rows, PACK), lambda j: (j, 0, 0))
    other_spec = pl.BlockSpec((1, rows, PACK - TILE), lambda j: (j, 0, 0))
    return pl.pallas_call(
        unturn_kernel,
        grid=(units,),
        in_specs=[own_spec] + [other_spec] * len(others) + [turn_spec, turn_spec],
        out_specs=own_spec,
        out_shape=jax.ShapeDtypeStruct(own.shape, BF),
        compiler_params=params_of("arbitrary"),
        name="unturn",
    )(own, *others, cos, sin)


def flip(tile):
    return tile.astype(F32).T


def head_rows(flipped, low):
    row = lax.broadcasted_iota(jnp.int32, flipped.shape, 0)
    keep = row < HEAD_DIM if low else row >= HEAD_DIM
    return jnp.where(keep, flipped, 0.0)


def head_lanes(tile, low):
    lane = lane_of(tile.shape)
    keep = lane < HEAD_DIM if low else lane >= HEAD_DIM
    return jnp.where(keep, tile, 0.0)


def query_sides(q_ref, qb):
    scale = HEAD_DIM ** (-0.5)
    a = flip(q_ref[0, :, 0:TILE]) * scale
    d = flip(q_ref[0, :, 3 * TILE : 4 * TILE]) * scale
    qb[0] = head_rows(a, True).astype(BF)
    qb[1] = head_rows(a, False).astype(BF)
    qb[2] = jnp.concatenate(
        [jnp.zeros((HEAD_DIM, d.shape[1]), F32), d[:HEAD_DIM]], 0
    ).astype(BF)


def live_of(seg_row, unit, query_start, part, rows, c):
    shape = (rows, rows)
    query_pos = query_start + lax.broadcasted_iota(jnp.int32, shape, 1)
    row = lax.broadcasted_iota(jnp.int32, shape, 0)
    pieces = []
    for i in range(part):
        key_pos = (unit * part + lax.rem(c - i + part, part)) * rows + row
        pieces.append((key_pos <= query_pos) & (key_pos >= seg_row))
    return jnp.concatenate(pieces, 0)


def unit_loop(meta, part, units, rows, step):
    j = pl.program_id(0)
    first = meta[j] // (rows * part)
    top_seg = meta[units + j]

    def one(unit, unused):
        masked = (unit == j) | (top_seg > unit * (rows * part))

        @pl.when(masked)
        def _():
            step(unit, True)

        @pl.when(jnp.logical_not(masked))
        def _():
            step(unit, False)

        return unused

    lax.fori_loop(first, j + 1, one, 0)


def forward_kernel(
    part, units, meta, q_ref, kv_ref, seg_ref, o_ref, ot_ref, lse_ref, qb, vt, top, total, acc
):
    rows = q_ref.shape[1]
    c = meta[2 * units]
    j = pl.program_id(0)

    @pl.when(j == 0)
    def _():
        def turn_values(unit, unused):
            vt[unit, :TILE] = flip(kv_ref[unit, :, TILE : 2 * TILE]).astype(BF)
            vt[unit, TILE:] = flip(kv_ref[unit, :, 3 * TILE :])[:HEAD_DIM].astype(BF)
            return unused

        lax.fori_loop(0, units, turn_values, 0)

    query_sides(q_ref, qb)
    top[...] = jnp.full(top.shape, NEG_BIG, F32)
    total[...] = jnp.zeros(total.shape, F32)
    acc[...] = jnp.zeros(acc.shape, F32)
    seg_row = seg_ref[0]
    query_start = (j * part + c) * rows

    def step(unit, masked):
        k01 = kv_ref[unit, :, 0:TILE]
        k2 = kv_ref[unit, :, 2 * TILE : 3 * TILE]
        if masked:
            live = live_of(seg_row, unit, query_start, part, rows, c)
        scores = [mm(k2 if h == 2 else k01, qb[h]) for h in range(TRIO)]
        if masked:
            scores = [jnp.where(live, score, NEG_BIG) for score in scores]
        old = top[0:TRIO]
        new = jnp.concatenate([jnp.max(score, 0, keepdims=True) for score in scores], 0)
        new = jnp.maximum(old, new)
        factor = jnp.exp(old - new)
        weights = [jnp.exp(scores[h] - new[h : h + 1]) for h in range(TRIO)]
        if masked:
            weights = [jnp.where(live, weight, 0.0) for weight in weights]
        sums = [jnp.sum(weight, 0, keepdims=True) for weight in weights]
        top[0:TRIO] = new
        total[0:TRIO] = total[0:TRIO] * factor + jnp.concatenate(sums, 0)
        for h in range(TRIO):
            vth = vt[unit, h * HEAD_DIM : (h + 1) * HEAD_DIM]
            acc[h] = acc[h] * factor[h : h + 1] + mm(vth, weights[h].astype(BF))

    unit_loop(meta, part, units, rows, step)
    out = [acc[h] / total[h : h + 1] for h in range(TRIO)]
    for h in range(TRIO):
        ot_ref[0, h * HEAD_DIM : (h + 1) * HEAD_DIM] = out[h]
    lse_ref[0, 0:TRIO] = top[0:TRIO] + jnp.log(total[0:TRIO])
    o_ref[0, :, :TILE] = jnp.concatenate(out[:2], 0).T.astype(BF)
    o_ref[0, :, TILE:] = jnp.concatenate([out[2], jnp.zeros_like(out[2])], 0).T.astype(BF)


def backward_kernel(
    part,
    units,
    meta,
    q_ref,
    do_ref,
    ot_ref,
    lse_ref,
    kv_ref,
    seg_ref,
    own_ref,
    oth_ref,
    qb,
    db,
    qn,
    dn,
    kt,
    delta,
    dqt,
    dk01,
    dv01,
    dk2,
    dv2,
):
    rows = q_ref.shape[1]
    c = meta[2 * units]
    j = pl.program_id(0)

    @pl.when(j == 0)
    def _():
        def turn_keys(unit, unused):
            kt[unit, :TILE] = flip(kv_ref[unit, :, 0:TILE]).astype(BF)
            kt[unit, TILE:] = flip(kv_ref[unit, :, 2 * TILE : 3 * TILE])[HEAD_DIM:].astype(BF)
            return unused

        lax.fori_loop(0, units, turn_keys, 0)
        for ref in (dk01, dv01, dk2, dv2):
            ref[...] = jnp.zeros(ref.shape, F32)

    query_sides(q_ref, qb)
    scale = HEAD_DIM ** (-0.5)
    q01 = q_ref[0, :, 0:TILE].astype(F32) * scale
    q2 = pltpu.roll(q_ref[0, :, 3 * TILE : 4 * TILE].astype(F32), HEAD_DIM, 1) * scale
    qn[0:rows] = head_lanes(q01, True).astype(BF)
    qn[rows : 2 * rows] = head_lanes(q01, False).astype(BF)
    qn[2 * rows :] = head_lanes(q2, False).astype(BF)
    do01 = do_ref[0, :, :TILE].astype(F32)
    do2 = do_ref[0, :, TILE:].astype(F32)
    dn[0:rows] = head_lanes(do01, True).astype(BF)
    dn[rows : 2 * rows] = head_lanes(do01, False).astype(BF)
    dn[2 * rows :] = do2.astype(BF)
    do01t = do01.T
    do2t = do2.T
    db[0] = head_rows(do01t, True).astype(BF)
    db[1] = head_rows(do01t, False).astype(BF)
    db[2] = do2t.astype(BF)
    for h in range(TRIO):
        dot = do2t[:HEAD_DIM] if h == 2 else do01t[h * HEAD_DIM : (h + 1) * HEAD_DIM]
        delta[h : h + 1] = jnp.sum(
            dot * ot_ref[0, h * HEAD_DIM : (h + 1) * HEAD_DIM], 0, keepdims=True
        )
    dqt[...] = jnp.zeros(dqt.shape, F32)
    seg_row = seg_ref[0]
    query_start = (j * part + c) * rows

    def step(unit, masked):
        k01 = kv_ref[unit, :, 0:TILE]
        v01 = kv_ref[unit, :, TILE : 2 * TILE]
        k2 = kv_ref[unit, :, 2 * TILE : 3 * TILE]
        v2 = kv_ref[unit, :, 3 * TILE :]
        if masked:
            live = live_of(seg_row, unit, query_start, part, rows, c)
        scores = [mm(k2 if h == 2 else k01, qb[h]) for h in range(TRIO)]
        dprobs = [mm(v2 if h == 2 else v01, db[h]) for h in range(TRIO)]
        probs = []
        grads = []
        for h in range(TRIO):
            score = scores[h]
            if masked:
                score = jnp.where(live, score, NEG_BIG)
            prob = jnp.exp(score - lse_ref[0, h : h + 1])
            if masked:
                prob = jnp.where(live, prob, 0.0)
            probs.append(prob.astype(BF))
            grads.append((prob * (dprobs[h] - delta[h : h + 1])).astype(BF))
        dv01[unit] += mm(jnp.concatenate(probs[:2], 1), dn[: 2 * rows])
        dk01[unit] += mm(jnp.concatenate(grads[:2], 1), qn[: 2 * rows])
        dv2[unit] += mm(probs[2], dn[2 * rows :])
        dk2[unit] += mm(grads[2], qn[2 * rows :])
        for h in range(TRIO):
            kth = kt[unit, h * HEAD_DIM : (h + 1) * HEAD_DIM]
            dqt[h * HEAD_DIM : (h + 1) * HEAD_DIM] += mm(kth, grads[h])

    unit_loop(meta, part, units, rows, step)
    own_ref[j, :, 0:TILE] = (dqt[:TILE] * scale).T.astype(BF)
    dq2 = dqt[TILE:] * scale
    dk2[j, 0:rows] += jnp.concatenate([dq2, jnp.zeros_like(dq2)], 0).T

    @pl.when(j == units - 1)
    def _():
        for unit in range(units):
            for i in range(part):
                span = slice(i * rows, (i + 1) * rows)
                for t, ref in enumerate((dk01, dv01, dk2, dv2)):
                    tile = ref[unit, span].astype(BF)
                    if i == 0:
                        own_ref[unit, :, (t + 1) * TILE : (t + 2) * TILE] = tile
                    else:
                        oth_ref[i - 1, unit, :, t * TILE : (t + 1) * TILE] = tile


def attention_cost(products, units, rows, part):
    pairs = TRIO * rows * rows * units * units * part // 2
    return pl.CostEstimate(
        flops=2 * 64 * products * pairs, bytes_accessed=20_000_000, transcendentals=pairs
    )


def whole_spec(shape):
    zeros = (0,) * len(shape)
    return pl.BlockSpec(shape, lambda j, meta: zeros)


def attend_forward(meta, packed, kv, seg):
    units, rows, unused = packed.shape
    part = kv.shape[1] // rows
    return pl.pallas_call(
        functools.partial(forward_kernel, part, units),
        grid_spec=pltpu.PrefetchScalarGridSpec(
            num_scalar_prefetch=1,
            grid=(units,),
            in_specs=[
                pl.BlockSpec((1, rows, PACK), lambda j, meta: (j, 0, 0)),
                whole_spec(kv.shape),
                pl.BlockSpec((1, 1, rows), lambda j, meta: (j, 0, 0)),
            ],
            out_specs=[
                pl.BlockSpec((1, rows, OPACK), lambda j, meta: (j, 0, 0)),
                pl.BlockSpec((1, TRIO * HEAD_DIM, rows), lambda j, meta: (j, 0, 0)),
                pl.BlockSpec((1, 8, rows), lambda j, meta: (j, 0, 0)),
            ],
            scratch_shapes=[
                pltpu.VMEM((TRIO, TILE, rows), BF),
                pltpu.VMEM((units, TRIO * HEAD_DIM, part * rows), BF),
                pltpu.VMEM((8, rows), F32),
                pltpu.VMEM((8, rows), F32),
                pltpu.VMEM((TRIO, HEAD_DIM, rows), F32),
            ],
        ),
        out_shape=[
            jax.ShapeDtypeStruct((units, rows, OPACK), BF),
            jax.ShapeDtypeStruct((units, TRIO * HEAD_DIM, rows), F32),
            jax.ShapeDtypeStruct((units, 8, rows), F32),
        ],
        compiler_params=params_of("arbitrary"),
        cost_estimate=attention_cost(8, units, rows, part),
        name="attend_forward",
    )(meta, packed, kv, seg)


def attend_backward(meta, packed, dout, out_t, lse, kv, seg):
    units, rows, unused = packed.shape
    part = kv.shape[1] // rows
    others = (max(part - 1, 1), units, rows, 4 * TILE)
    grads = pltpu.VMEM((units, part * rows, TILE), F32)
    return pl.pallas_call(
        functools.partial(backward_kernel, part, units),
        grid_spec=pltpu.PrefetchScalarGridSpec(
            num_scalar_prefetch=1,
            grid=(units,),
            in_specs=[
                pl.BlockSpec((1, rows, PACK), lambda j, meta: (j, 0, 0)),
                pl.BlockSpec((1, rows, OPACK), lambda j, meta: (j, 0, 0)),
                pl.BlockSpec((1, TRIO * HEAD_DIM, rows), lambda j, meta: (j, 0, 0)),
                pl.BlockSpec((1, 8, rows), lambda j, meta: (j, 0, 0)),
                whole_spec(kv.shape),
                pl.BlockSpec((1, 1, rows), lambda j, meta: (j, 0, 0)),
            ],
            out_specs=[whole_spec(packed.shape), whole_spec(others)],
            scratch_shapes=[
                pltpu.VMEM((TRIO, TILE, rows), BF),
                pltpu.VMEM((TRIO, TILE, rows), BF),
                pltpu.VMEM((TRIO * rows, TILE), BF),
                pltpu.VMEM((TRIO * rows, TILE), BF),
                pltpu.VMEM((units, TRIO * HEAD_DIM, part * rows), BF),
                pltpu.VMEM((8, rows), F32),
                pltpu.VMEM((TRIO * HEAD_DIM, rows), F32),
                grads,
                grads,
                grads,
                grads,
            ],
        ),
        out_shape=[
            jax.ShapeDtypeStruct(packed.shape, BF),
            jax.ShapeDtypeStruct(others, BF),
        ],
        compiler_params=params_of("arbitrary"),
        cost_estimate=attention_cost(20, units, rows, part),
        name="attend_backward",
    )(meta, packed, dout, out_t, lse, kv, seg)


def pack_kernel(trios, groups, w_ref, vec_ref, early_ref, local_ref):
    d = w_ref.shape[1] // 3
    w = w_ref[...].astype(F32)
    width = TRIO * HEAD_DIM
    zeros = jnp.zeros((w.shape[0], HEAD_DIM), F32)
    for g in range(trios):
        q, k, v = (w[:, i * d + g * width : i * d + (g + 1) * width] for i in range(3))
        tiles = [q[:, :TILE], k[:, :TILE], v[:, :TILE]]
        tiles.append(jnp.concatenate([q[:, TILE:], k[:, TILE:]], 1))
        tiles.append(jnp.concatenate([v[:, TILE:], zeros], 1))
        for t, tile in enumerate(tiles):
            tile = tile.astype(BF)
            local_ref[:, g * PACK + t * TILE : g * PACK + (t + 1) * TILE] = tile
            for s in range(groups):
                early_ref[g * groups + s, :, t * TILE : (t + 1) * TILE] = tile
        for s in range(groups):
            early_ref[g * groups + s, :, PACK:] = vec_ref[s]


def pack_early(weight, vec, trios):
    r = weight.shape[0]
    groups = vec.shape[0]
    return pl.pallas_call(
        functools.partial(pack_kernel, trios, groups),
        out_shape=[
            jax.ShapeDtypeStruct((trios * groups, r, PACK + TILE), BF),
            jax.ShapeDtypeStruct((r, trios * PACK), BF),
        ],
        name="pack_early",
    )(weight, vec)


def gradient_kernel(
    trios, blocks, norm_ref, pre_ref, hidden_ref, cot_ref, att_ref, vec_ref, out_ref
):
    i = pl.program_id(0)
    d = cot_ref.shape[1]
    where = pl.ds(pl.multiple_of(i * d, d), d)

    @pl.when(i < blocks)
    def _():
        out_ref[:, where] = outer_sum(norm_ref[...], pre_ref[...]).astype(BF)

    @pl.when((i >= blocks) & (i < 2 * blocks))
    def _():
        out_ref[:, where] = outer_sum(hidden_ref[...], cot_ref[...]).astype(BF)

    @pl.when(i == 2 * blocks)
    def _():
        width = d // trios
        for g in range(trios):
            part = outer_sum(att_ref[:, g * OPACK : (g + 1) * OPACK], cot_ref[...])
            out_ref[g * width : (g + 1) * width, where] = part[:width].astype(BF)
        out_ref[:, (2 * blocks + 1) * d :] = vec_ref[...]


def gradients(normed, pre_grad, hidden, cot, attended, vec, trios):
    rows, d = normed.shape
    blocks = hidden.shape[1] // d
    width = (2 * blocks + 1) * d + TILE
    return pl.pallas_call(
        functools.partial(gradient_kernel, trios, blocks),
        grid=(2 * blocks + 1,),
        in_specs=[
            pl.BlockSpec((rows, d), lambda i: (0, 0)),
            pl.BlockSpec((rows, d), lambda i: (0, jnp.minimum(i, blocks - 1))),
            pl.BlockSpec((rows, d), lambda i: (0, jnp.clip(i - blocks, 0, blocks - 1))),
            pl.BlockSpec((rows, d), lambda i: (0, 0)),
            pl.BlockSpec(attended.shape, lambda i: (0, 0)),
            pl.BlockSpec((d, TILE), lambda i: (0, 0)),
        ],
        out_specs=pl.BlockSpec((d, width), lambda i: (0, 0)),
        out_shape=jax.ShapeDtypeStruct((d, width), BF),
        compiler_params=params_of("arbitrary"),
        cost_estimate=pl.CostEstimate(
            flops=2 * rows * d * width, bytes_accessed=4 * d * width, transcendentals=0
        ),
        name="gradients",
    )(normed, pre_grad, hidden, cot, attended, vec)


def pack_columns(matrix, trios):
    r = matrix.shape[0]
    q, k, v = (
        part.reshape(r, trios, TRIO * HEAD_DIM) for part in jnp.split(matrix, 3, axis=1)
    )
    zeros = jnp.zeros((r, trios, HEAD_DIM), matrix.dtype)
    pieces = [q[..., :TILE], k[..., :TILE], v[..., :TILE], q[..., TILE:], k[..., TILE:]]
    return jnp.concatenate(pieces + [v[..., TILE:], zeros], -1).reshape(r, trios * PACK)


def unpack_columns(matrix, trios):
    r = matrix.shape[0]
    m = matrix.reshape(r, trios, PACK)
    halves = [
        m[..., 3 * TILE : 3 * TILE + HEAD_DIM],
        m[..., 3 * TILE + HEAD_DIM : 4 * TILE],
        m[..., 4 * TILE : 4 * TILE + HEAD_DIM],
    ]
    return jnp.concatenate(
        [
            jnp.concatenate([m[..., i * TILE : (i + 1) * TILE], halves[i]], -1).reshape(r, -1)
            for i in range(3)
        ],
        -1,
    )


def split_hidden(matrix, count, r):
    lead = matrix.shape[0]
    return matrix.reshape(lead, count, -1, r).transpose(0, 2, 1, 3).reshape(lead, -1)


def join_hidden(matrix, count, r):
    lead = matrix.shape[0]
    return matrix.reshape(lead, -1, count, r).transpose(0, 2, 1, 3).reshape(lead, -1)


def on_device(
    tokens,
    segment,
    ln1_gain,
    ln1_bias,
    ln2_gain,
    ln2_bias,
    qkv_weight,
    qkv_bias,
    dense_weight,
    dense_bias,
    fc1_weight,
    fc1_bias,
    output_feed_weight,
    output_feed_bias,
    cotangent,
):
    rows, groups, d = tokens.shape
    units = lax.axis_size("unit")
    part = lax.axis_size("part")
    count = units * part * lax.axis_size("seq")
    trios = units // groups
    all_rows = rows * groups
    r = qkv_weight.shape[0]
    ff = fc1_weight.shape[1]
    blocks = ff // d
    c = lax.axis_index("part")
    unit = lax.axis_index("unit")

    seq = lax.axis_index("seq")
    seqs = lax.axis_size("seq")
    place = (seq * units + unit) * part + c

    def exchange(blocks_out):
        width = blocks_out.shape[-1]
        return lax.all_to_all(
            blocks_out.reshape(-1, width), "unit", 0, 0, tiled=True
        ).reshape(blocks_out.shape)

    def shift(value, axis, i):
        n = lax.axis_size(axis)
        return lax.ppermute(value, axis, [(p, (p + i) % n) for p in range(n)])

    def natural_order(got, me):
        n = len(got)
        if n == 2:
            return jnp.where(me == 0, jnp.stack(got), jnp.stack(got[::-1]))
        ring = jnp.stack((got + got)[::-1])
        return lax.dynamic_slice_in_dim(ring, n - 1 - me, n, 0)

    def gather_small(value, axis):
        n = lax.axis_size(axis)
        got = [value] + [shift(value, axis, i) for i in range(1, n)]
        return natural_order(got, lax.axis_index(axis))

    def exchange_small(value):
        got = []
        for i in range(units):
            piece = lax.dynamic_index_in_dim(value, (unit + i) % units, 0, False)
            got.append(shift(piece, "unit", i) if i else piece)
        return natural_order(got, unit)

    def scatter_small(value, axis):
        n = lax.axis_size(axis)
        me = lax.axis_index(axis)
        total = lax.dynamic_index_in_dim(value, me, 0, False).astype(F32)
        for i in range(1, n):
            piece = lax.dynamic_index_in_dim(value, (me + i) % n, 0, False)
            total = total + shift(piece, axis, i).astype(F32)
        return total.astype(BF)

    vectors = (ln1_gain, ln1_bias, ln2_gain, ln2_bias, dense_bias, output_feed_bias)
    vec = jnp.concatenate(
        [v.reshape(r, 1) for v in vectors] + [qkv_bias.reshape(r, 3), fc1_bias.reshape(r, blocks)],
        1,
    )
    token_rows = tokens.transpose(1, 0, 2)
    toks = exchange(jnp.concatenate([token_rows] * trios, 0))
    seg_rows = segment.T
    seg_lanes = -(-2 * rows // r)
    seg_pack = jnp.concatenate([seg_rows // 64, seg_rows % 64], 1).astype(BF)
    seg_pack = jnp.pad(seg_pack, ((0, 0), (0, seg_lanes * r - 2 * rows)))
    seg_pack = seg_pack.reshape(groups, r, seg_lanes)
    vec = jnp.pad(vec, ((0, 0), (0, 16 - vec.shape[1])))
    vec = jnp.concatenate(
        [
            jnp.broadcast_to(vec, (groups, r, 16)),
            seg_pack,
            jnp.zeros((groups, r, TILE - 16 - seg_lanes), BF),
        ],
        -1,
    )
    early, qkv_local = pack_early(qkv_weight, vec, trios)
    early = exchange_small(early)

    seg_mine = early[:, :, PACK + 16 : PACK + 16 + seg_lanes].astype(jnp.int32)
    seg_mine = seg_mine.reshape(units, r * seg_lanes)
    seg_mine = seg_mine[:, :rows] * 64 + seg_mine[:, rows : 2 * rows]
    meta = jnp.concatenate([seg_mine[:, 0], seg_mine[:, -1], c[None]])
    seg_mine = seg_mine[:, None, :]
    trio_full = gather_small(gather_small(early, "seq"), "part")
    trio_full = trio_full.transpose(1, 2, 0, 3, 4).reshape(d, PACK + TILE)
    vec_full = trio_full[:, PACK:].astype(F32)
    vec_rows = vec_full[:, :8].T
    gain_one, bias_one, gain_two, bias_two, dense_shift, down_shift = (
        vec_rows[i : i + 1] for i in range(6)
    )
    qkv_shift = pack_columns(vec_full[:, 6:9].reshape(1, 3 * d), trios).reshape(trios, PACK)
    qkv_shift = lax.dynamic_slice_in_dim(qkv_shift, unit // groups, 1, 0)
    up_shift = split_hidden(vec_full[:, 9 : 9 + blocks].reshape(1, ff), count, r)

    feed_blocks = output_feed_weight.reshape(blocks, r, d)
    second_pack = jnp.concatenate(
        [split_hidden(fc1_weight, count, r)]
        + [feed_blocks[b] for b in range(blocks)]
        + [dense_weight],
        1,
    )
    second = lax.all_gather(second_pack, ALL_AXES, axis=0, tiled=True)
    qkv_full = lax.all_gather(qkv_local, ALL_AXES, axis=0, tiled=True)
    dense_pad = jnp.pad(
        second[:, 2 * ff :].reshape(trios, d // trios, d),
        ((0, 0), (0, OPACK - d // trios), (0, 0)),
    )

    block_start = (jnp.arange(units, dtype=jnp.int32) * part + c) * rows
    positions = block_start[:, None, None] + jnp.arange(rows, dtype=jnp.int32) - seg_mine
    freq = jnp.arange(ROT // 2, dtype=F32)
    inverse = jnp.exp(freq * (-2.0 * math.log(10000.0) / ROT))
    angles = positions.astype(F32) * inverse[None, :, None]
    cos = jnp.cos(angles)
    sin = jnp.sin(angles)

    packed, normed_one, hat_one = project(
        toks, trio_full, qkv_shift, gain_one, bias_one, cos, sin
    )
    kv_own = packed[:, :, TILE:]
    kv = jnp.concatenate([kv_own] + [shift(kv_own, "part", i) for i in range(1, part)], 1)
    out_low, out_t, lse = attend_forward(meta, packed, kv, seg_mine)
    attended = exchange(out_low)

    x = token_rows.reshape(all_rows, d).astype(F32)
    cot = cotangent.transpose(1, 0, 2).reshape(all_rows, d)
    cot_float = cot.astype(F32)
    centre = x - jnp.mean(x, -1, keepdims=True)
    spread = lax.rsqrt(jnp.mean(centre * centre, -1, keepdims=True) + EPSILON)
    xhat = centre * spread
    normed_two = (xhat * gain_two + bias_two).astype(BF)
    attended_grad = jnp.einsum(
        "sld,gkd->gslk", cot.reshape(groups, rows, d), dense_pad, preferred_element_type=F32
    ).astype(BF)
    dout = exchange(attended_grad.reshape(units, rows, OPACK))

    up_full = second[:, :ff]
    down_full = jnp.concatenate(
        [second[:, ff + b * d : ff + (b + 1) * d] for b in range(blocks)], 0
    )
    hidden_pre = mm(normed_two, up_full) + up_shift
    cdf = 0.5 * (1.0 + lax.erf(hidden_pre * math.sqrt(0.5)))
    hidden_low = (hidden_pre * cdf).astype(BF)
    slope = cdf + hidden_pre * (
        jnp.exp(-0.5 * hidden_pre * hidden_pre) * (1.0 / math.sqrt(2.0 * math.pi))
    )
    pre_grad = (inner_back(cot, down_full) * slope).astype(BF)
    hidden_low, pre_grad, attended = lax.optimization_barrier((hidden_low, pre_grad, attended))
    second_branch = mm(hidden_low, down_full) + down_shift
    up_shift_grad = jnp.sum(pre_grad.astype(F32), 0)
    normed_two_grad = inner_back(pre_grad, up_full)
    cot_sum = jnp.sum(cot_float, 0)

    def norm_back(grad, gain):
        gy = grad * gain
        return spread * (
            gy - jnp.mean(gy, -1, keepdims=True) - xhat * jnp.mean(gy * xhat, -1, keepdims=True)
        )

    in_two = norm_back(normed_two_grad, gain_two)

    attended = attended.reshape(trios, groups, rows, OPACK).transpose(1, 2, 0, 3)
    attended = attended.reshape(all_rows, trios * OPACK)
    branch_one = mm(attended, dense_pad.reshape(trios * OPACK, d)) + dense_shift
    output = (x + branch_one + second_branch).astype(BF)

    vec_grads = jnp.concatenate(
        [
            jnp.sum(normed_two_grad * xhat, 0)[None],
            jnp.sum(normed_two_grad, 0)[None],
            cot_sum[None],
            jnp.zeros((5, d), F32),
        ],
        0,
    ).T
    up_shift_grad = join_hidden(up_shift_grad[None], count, r).reshape(d, blocks)
    vec_grads = jnp.concatenate(
        [vec_grads, up_shift_grad, jnp.zeros((d, TILE - 8 - blocks), F32)], 1
    )
    mlp_grads = gradients(
        normed_two, pre_grad, hidden_low, cot, attended, vec_grads.astype(BF), trios
    )
    mlp_grads, kv = lax.optimization_barrier((mlp_grads, kv))
    mlp_sum = lax.psum_scatter(mlp_grads, ALL_AXES, scatter_dimension=0, tiled=True).astype(F32)

    own, others = attend_backward(meta, packed, dout, out_t, lse, kv, seg_mine)
    others = [shift(others[i - 1], "part", part - i) for i in range(1, part)]
    qkv_grad = unturn(own, others, cos, sin)
    back = exchange(qkv_grad)

    grad_rows = qkv_grad.reshape(units * rows, PACK)
    trio_weight = trio_full[:, :PACK].astype(F32)
    trio_grad = outer_sum(normed_one.reshape(units * rows, d), grad_rows)
    hat_grad = outer_sum(hat_one.reshape(units * rows, d), grad_rows)
    shift_grad = jnp.sum(grad_rows.astype(F32), 0)[None]
    late_vec = jnp.concatenate(
        [
            jnp.sum(trio_weight * hat_grad, 1, keepdims=True),
            jnp.sum(trio_weight * shift_grad, 1, keepdims=True),
            jnp.zeros((d, TILE - 2), F32),
        ],
        1,
    )
    late = jnp.concatenate([trio_grad.astype(BF), late_vec.astype(BF)], 1)
    late = late.reshape(seqs, units, part, r, PACK + TILE)
    shift_rows = jnp.pad(shift_grad.astype(BF), ((0, 7), (0, TILE)))
    late = jnp.concatenate(
        [late, jnp.broadcast_to(shift_rows, (seqs, units, part) + shift_rows.shape)], 3
    )
    late = scatter_small(late.transpose(2, 0, 1, 3, 4), "part")
    late = exchange_small(scatter_small(late, "seq")).astype(F32)
    late = jnp.sum(late.reshape(trios, groups, r + 8, PACK + TILE), 1)
    qkv_weight_grad = unpack_columns(
        late[:, :r, :PACK].transpose(1, 0, 2).reshape(r, trios * PACK), trios
    )
    late_vec = jnp.sum(late[:, :r, PACK : PACK + 2], 0)
    qkv_shift_grad = unpack_columns(late[:, r, :PACK].reshape(1, trios * PACK), trios)[0]
    qkv_shift_grad = lax.dynamic_slice_in_dim(qkv_shift_grad, place * 3 * r, 3 * r)

    down_sum = jnp.concatenate(
        [mlp_sum[:, ff + b * d : ff + (b + 1) * d] for b in range(blocks)], 0
    )
    vec_sum = mlp_sum[:, 2 * ff + d :]
    cot_total = vec_sum[:, 2]
    param_grads = (
        late_vec[:, 0],
        late_vec[:, 1],
        vec_sum[:, 0],
        vec_sum[:, 1],
        qkv_weight_grad,
        qkv_shift_grad,
        mlp_sum[:, 2 * ff : 2 * ff + d],
        cot_total,
        join_hidden(mlp_sum[:, :ff], count, r),
        vec_sum[:, 8 : 8 + blocks].reshape(-1),
        down_sum,
        cot_total,
    )
    param_grads, back = lax.optimization_barrier((param_grads, back))

    back = back.reshape(trios, groups, rows, PACK).transpose(1, 2, 0, 3)
    normed_one_grad = inner_back(back.reshape(all_rows, trios * PACK), qkv_full)
    in_one = norm_back(normed_one_grad, gain_one)
    tokens_grad = (cot_float + in_one + in_two).astype(BF)

    def natural(value):
        return value.reshape(groups, rows, d).transpose(1, 0, 2)

    return (natural(output), natural(tokens_grad)) + tuple(param_grads)


def solution(mesh):
    devices = mesh.devices
    seq_size, ctx_size = devices.shape
    ctx = ("unit", "part")
    tok = P(ctx, "seq", None)
    vec = P(ALL_AXES)
    mat = P(ALL_AXES, None)
    pairs = (vec, vec, vec, vec, mat, vec, mat, vec, mat, vec, mat, vec)

    def run(tokens, *rest):
        units = HEADS // TRIO * (tokens.shape[1] // seq_size)
        split = Mesh(devices.reshape(seq_size, units, ctx_size // units), ALL_AXES)
        mapped = jax.shard_map(
            on_device,
            mesh=split,
            in_specs=(tok, P(ctx, "seq")) + pairs + (tok,),
            out_specs=(tok, tok) + pairs,
            check_vma=False,
        )
        return mapped(tokens, *rest)

    return run
```

```python
import functools
import math

import jax
import jax.numpy as jnp
from jax import lax
from jax.experimental import pallas as pl
from jax.experimental.pallas import tpu as pltpu
from jax.sharding import Mesh, PartitionSpec as P

HEADS = 12
HEAD_DIM = 64
ROT = 16
TRIO = 3
TILE = 128
PACK = 5 * TILE
OPACK = 2 * TILE

EPSILON = 1e-05
NEG_BIG = -1e30
BF = jnp.bfloat16
F32 = jnp.float32
ALL_AXES = ("seq", "unit", "part")
VMEM_BYTES = 56 * 1024 * 1024


def params_of(*semantics):
    return pltpu.CompilerParams(
        dimension_semantics=semantics, vmem_limit_bytes=VMEM_BYTES
    )


def mm(a, b):
    return jnp.dot(a, b, preferred_element_type=F32)


def outer_sum(left_rows, right_rows):
    return lax.dot_general(
        left_rows, right_rows, (((0,), (0,)), ((), ())), preferred_element_type=F32
    )


def inner_back(grad_rows, weight):
    return lax.dot_general(
        grad_rows, weight, (((1,), (1,)), ((), ())), preferred_element_type=F32
    )


def lane_of(shape):
    return lax.broadcasted_iota(jnp.int32, shape, len(shape) - 1)


def turn(tile, cos, sin):
    partner = jnp.where(
        lane_of(tile.shape) % HEAD_DIM < ROT // 2,
        pltpu.roll(tile, TILE - ROT // 2, 1),
        pltpu.roll(tile, ROT // 2, 1),
    )
    return tile * cos + partner * sin


def turn_tables(cos_rows, sin_rows):
    rows = cos_rows.shape[1]
    rest = HEAD_DIM - ROT
    cos_head = [cos_rows, cos_rows, jnp.ones((rest, rows), F32)]
    sin_head = [-sin_rows, sin_rows, jnp.zeros((rest, rows), F32)]
    return jnp.concatenate(cos_head * 2, 0).T, jnp.concatenate(sin_head * 2, 0).T


def project_kernel(
    tok_ref, w_ref, b_ref, gain_ref, bias_ref, cos_ref, sin_ref, out_ref, kv_ref, norm_ref, hat_ref
):
    x = tok_ref[0].astype(F32)
    centre = x - jnp.mean(x, -1, keepdims=True)
    spread = jnp.mean(centre * centre, -1, keepdims=True)
    hat = centre * lax.rsqrt(spread + EPSILON)
    normed = (hat * gain_ref[...] + bias_ref[...]).astype(BF)
    hat_ref[0] = hat.astype(BF)
    norm_ref[0] = normed
    y = mm(normed, w_ref[...]) + b_ref[...]
    cos, sin = turn_tables(cos_ref[0], sin_ref[0])
    for t in range(5):
        tile = y[:, t * TILE : (t + 1) * TILE]
        if t in (0, 1, 3):
            tile = turn(tile, cos, sin)
        tile = tile.astype(BF)
        out_ref[0, :, t * TILE : (t + 1) * TILE] = tile
        if t > 0:
            kv_ref[0, :, (t - 1) * TILE : t * TILE] = tile


def project(toks, weight, bias, gain, offset, cos, sin):
    units, unused, d = toks.shape
    rows = cos.shape[2]
    tok_spec = pl.BlockSpec((1, rows, d), lambda j: (j, 0, 0))
    row_spec = pl.BlockSpec((1, d), lambda j: (0, 0))
    turn_spec = pl.BlockSpec((1, ROT // 2, rows), lambda j: (j, 0, 0))
    return pl.pallas_call(
        project_kernel,
        grid=(units,),
        in_specs=[
            tok_spec,
            pl.BlockSpec((d, PACK), lambda j: (0, 0)),
            pl.BlockSpec((1, PACK), lambda j: (0, 0)),
            row_spec,
            row_spec,
            turn_spec,
            turn_spec,
        ],
        out_specs=[
            pl.BlockSpec((1, rows, PACK), lambda j: (j, 0, 0)),
            pl.BlockSpec((1, rows, PACK - TILE), lambda j: (j, 0, 0)),
            tok_spec,
            tok_spec,
        ],
        out_shape=[
            jax.ShapeDtypeStruct((units, rows, PACK), BF),
            jax.ShapeDtypeStruct((units, rows, PACK - TILE), BF),
            jax.ShapeDtypeStruct((units, rows, d), BF),
            jax.ShapeDtypeStruct((units, rows, d), BF),
        ],
        compiler_params=params_of("arbitrary"),
        cost_estimate=pl.CostEstimate(
            flops=2 * units * rows * d * PACK,
            bytes_accessed=2 * units * rows * (3 * d + PACK),
            transcendentals=0,
        ),
        name="project",
    )(toks, weight, bias, gain, offset, cos, sin)


def unturn_kernel(*refs):
    own_ref, cos_ref, sin_ref, out_ref = refs[0], refs[-3], refs[-2], refs[-1]
    others = refs[1:-3]
    cos, sin = turn_tables(cos_ref[0], sin_ref[0])
    for t in range(5):
        tile = own_ref[0, :, t * TILE : (t + 1) * TILE].astype(F32)
        if t > 0:
            for other in others:
                tile = tile + other[0, :, (t - 1) * TILE : t * TILE].astype(F32)
        if t in (0, 1, 3):
            tile = turn(tile, cos, -sin)
        out_ref[0, :, t * TILE : (t + 1) * TILE] = tile.astype(BF)


def unturn(own, others, cos, sin):
    units, rows, unused = own.shape
    turn_spec = pl.BlockSpec((1, ROT // 2, rows), lambda j: (j, 0, 0))
    own_spec = pl.BlockSpec((1, rows, PACK), lambda j: (j, 0, 0))
    other_spec = pl.BlockSpec((1, rows, PACK - TILE), lambda j: (j, 0, 0))
    return pl.pallas_call(
        unturn_kernel,
        grid=(units,),
        in_specs=[own_spec] + [other_spec] * len(others) + [turn_spec, turn_spec],
        out_specs=own_spec,
        out_shape=jax.ShapeDtypeStruct(own.shape, BF),
        compiler_params=params_of("arbitrary"),
        name="unturn",
    )(own, *others, cos, sin)


def flip(tile):
    return tile.astype(F32).T


def head_rows(flipped, low):
    row = lax.broadcasted_iota(jnp.int32, flipped.shape, 0)
    keep = row < HEAD_DIM if low else row >= HEAD_DIM
    return jnp.where(keep, flipped, 0.0)


def head_lanes(tile, low):
    lane = lane_of(tile.shape)
    keep = lane < HEAD_DIM if low else lane >= HEAD_DIM
    return jnp.where(keep, tile, 0.0)


def query_sides(q_ref, qb):
    scale = HEAD_DIM ** (-0.5)
    a = flip(q_ref[0, :, 0:TILE]) * scale
    d = flip(q_ref[0, :, 3 * TILE : 4 * TILE]) * scale
    qb[0] = head_rows(a, True).astype(BF)
    qb[1] = head_rows(a, False).astype(BF)
    qb[2] = jnp.concatenate(
        [jnp.zeros((HEAD_DIM, d.shape[1]), F32), d[:HEAD_DIM]], 0
    ).astype(BF)


def live_of(seg_row, unit, query_start, part, rows, c):
    shape = (rows, rows)
    query_pos = query_start + lax.broadcasted_iota(jnp.int32, shape, 1)
    row = lax.broadcasted_iota(jnp.int32, shape, 0)
    pieces = []
    for i in range(part):
        key_pos = (unit * part + lax.rem(c - i + part, part)) * rows + row
        pieces.append((key_pos <= query_pos) & (key_pos >= seg_row))
    return jnp.concatenate(pieces, 0)


def unit_loop(meta, part, units, rows, step):
    j = pl.program_id(0)
    first = meta[j] // (rows * part)
    top_seg = meta[units + j]

    def one(unit, unused):
        masked = (unit == j) | (top_seg > unit * (rows * part))

        @pl.when(masked)
        def _():
            step(unit, True)

        @pl.when(jnp.logical_not(masked))
        def _():
            step(unit, False)

        return unused

    lax.fori_loop(first, j + 1, one, 0)


def join_parts(part, refs, kv_ref):
    rows = refs[0].shape[1]

    def one(unit, unused):
        for i in range(part):
            kv_ref[unit, i * rows : (i + 1) * rows] = refs[i][unit]
        return unused

    lax.fori_loop(0, refs[0].shape[0], one, 0)


def forward_kernel(part, units, meta, q_ref, *refs):
    seg_ref, o_ref, ot_ref, lse_ref, kv_ref, qb, vt, top, total, acc = refs[part:]
    rows = q_ref.shape[1]
    c = meta[2 * units]
    j = pl.program_id(0)

    @pl.when(j == 0)
    def _():
        join_parts(part, refs[:part], kv_ref)

        def turn_values(unit, unused):
            vt[unit, :TILE] = flip(kv_ref[unit, :, TILE : 2 * TILE]).astype(BF)
            vt[unit, TILE:] = flip(kv_ref[unit, :, 3 * TILE :])[:HEAD_DIM].astype(BF)
            return unused

        lax.fori_loop(0, units, turn_values, 0)

    query_sides(q_ref, qb)
    top[...] = jnp.full(top.shape, NEG_BIG, F32)
    total[...] = jnp.zeros(total.shape, F32)
    acc[...] = jnp.zeros(acc.shape, F32)
    seg_row = seg_ref[0]
    query_start = (j * part + c) * rows

    def step(unit, masked):
        k01 = kv_ref[unit, :, 0:TILE]
        k2 = kv_ref[unit, :, 2 * TILE : 3 * TILE]
        if masked:
            live = live_of(seg_row, unit, query_start, part, rows, c)
        scores = [mm(k2 if h == 2 else k01, qb[h]) for h in range(TRIO)]
        if masked:
            scores = [jnp.where(live, score, NEG_BIG) for score in scores]
        old = top[0:TRIO]
        new = jnp.concatenate([jnp.max(score, 0, keepdims=True) for score in scores], 0)
        new = jnp.maximum(old, new)
        factor = jnp.exp(old - new)
        weights = [jnp.exp(scores[h] - new[h : h + 1]) for h in range(TRIO)]
        if masked:
            weights = [jnp.where(live, weight, 0.0) for weight in weights]
        sums = [jnp.sum(weight, 0, keepdims=True) for weight in weights]
        top[0:TRIO] = new
        total[0:TRIO] = total[0:TRIO] * factor + jnp.concatenate(sums, 0)
        for h in range(TRIO):
            vth = vt[unit, h * HEAD_DIM : (h + 1) * HEAD_DIM]
            acc[h] = acc[h] * factor[h : h + 1] + mm(vth, weights[h].astype(BF))

    unit_loop(meta, part, units, rows, step)
    out = [acc[h] / total[h : h + 1] for h in range(TRIO)]
    for h in range(TRIO):
        ot_ref[0, h * HEAD_DIM : (h + 1) * HEAD_DIM] = out[h]
    lse_ref[0, 0:TRIO] = top[0:TRIO] + jnp.log(total[0:TRIO])
    o_ref[0, :, :TILE] = jnp.concatenate(out[:2], 0).T.astype(BF)
    o_ref[0, :, TILE:] = jnp.concatenate([out[2], jnp.zeros_like(out[2])], 0).T.astype(BF)


def backward_kernel(part, units, meta, q_ref, do_ref, ot_ref, lse_ref, *refs):
    seg_ref, own_ref, oth_ref, kv_ref, qb, db, qn, dn, kt, delta, dqt = refs[part : part + 11]
    dk01, dv01, dk2, dv2 = refs[part + 11 :]
    rows = q_ref.shape[1]
    c = meta[2 * units]
    j = pl.program_id(0)

    @pl.when(j == 0)
    def _():
        join_parts(part, refs[:part], kv_ref)

        def turn_keys(unit, unused):
            kt[unit, :TILE] = flip(kv_ref[unit, :, 0:TILE]).astype(BF)
            kt[unit, TILE:] = flip(kv_ref[unit, :, 2 * TILE : 3 * TILE])[HEAD_DIM:].astype(BF)
            return unused

        lax.fori_loop(0, units, turn_keys, 0)
        for ref in (dk01, dv01, dk2, dv2):
            ref[...] = jnp.zeros(ref.shape, F32)

    query_sides(q_ref, qb)
    scale = HEAD_DIM ** (-0.5)
    q01 = q_ref[0, :, 0:TILE].astype(F32) * scale
    q2 = pltpu.roll(q_ref[0, :, 3 * TILE : 4 * TILE].astype(F32), HEAD_DIM, 1) * scale
    qn[0:rows] = head_lanes(q01, True).astype(BF)
    qn[rows : 2 * rows] = head_lanes(q01, False).astype(BF)
    qn[2 * rows :] = head_lanes(q2, False).astype(BF)
    do01 = do_ref[0, :, :TILE].astype(F32)
    do2 = do_ref[0, :, TILE:].astype(F32)
    dn[0:rows] = head_lanes(do01, True).astype(BF)
    dn[rows : 2 * rows] = head_lanes(do01, False).astype(BF)
    dn[2 * rows :] = do2.astype(BF)
    do01t = do01.T
    do2t = do2.T
    db[0] = head_rows(do01t, True).astype(BF)
    db[1] = head_rows(do01t, False).astype(BF)
    db[2] = do2t.astype(BF)
    for h in range(TRIO):
        dot = do2t[:HEAD_DIM] if h == 2 else do01t[h * HEAD_DIM : (h + 1) * HEAD_DIM]
        delta[h : h + 1] = jnp.sum(
            dot * ot_ref[0, h * HEAD_DIM : (h + 1) * HEAD_DIM], 0, keepdims=True
        )
    dqt[...] = jnp.zeros(dqt.shape, F32)
    seg_row = seg_ref[0]
    query_start = (j * part + c) * rows

    def step(unit, masked):
        k01 = kv_ref[unit, :, 0:TILE]
        v01 = kv_ref[unit, :, TILE : 2 * TILE]
        k2 = kv_ref[unit, :, 2 * TILE : 3 * TILE]
        v2 = kv_ref[unit, :, 3 * TILE :]
        if masked:
            live = live_of(seg_row, unit, query_start, part, rows, c)
        scores = [mm(k2 if h == 2 else k01, qb[h]) for h in range(TRIO)]
        dprobs = [mm(v2 if h == 2 else v01, db[h]) for h in range(TRIO)]
        probs = []
        grads = []
        for h in range(TRIO):
            score = scores[h]
            if masked:
                score = jnp.where(live, score, NEG_BIG)
            prob = jnp.exp(score - lse_ref[0, h : h + 1])
            if masked:
                prob = jnp.where(live, prob, 0.0)
            probs.append(prob.astype(BF))
            grads.append((prob * (dprobs[h] - delta[h : h + 1])).astype(BF))
        dv01[unit] += mm(jnp.concatenate(probs[:2], 1), dn[: 2 * rows])
        dk01[unit] += mm(jnp.concatenate(grads[:2], 1), qn[: 2 * rows])
        dv2[unit] += mm(probs[2], dn[2 * rows :])
        dk2[unit] += mm(grads[2], qn[2 * rows :])
        for h in range(TRIO):
            kth = kt[unit, h * HEAD_DIM : (h + 1) * HEAD_DIM]
            dqt[h * HEAD_DIM : (h + 1) * HEAD_DIM] += mm(kth, grads[h])

    unit_loop(meta, part, units, rows, step)
    own_ref[j, :, 0:TILE] = (dqt[:TILE] * scale).T.astype(BF)
    dq2 = dqt[TILE:] * scale
    dk2[j, 0:rows] += jnp.concatenate([dq2, jnp.zeros_like(dq2)], 0).T

    @pl.when(j == units - 1)
    def _():
        for unit in range(units):
            for i in range(part):
                span = slice(i * rows, (i + 1) * rows)
                for t, ref in enumerate((dk01, dv01, dk2, dv2)):
                    tile = ref[unit, span].astype(BF)
                    if i == 0:
                        own_ref[unit, :, (t + 1) * TILE : (t + 2) * TILE] = tile
                    else:
                        oth_ref[i - 1, unit, :, t * TILE : (t + 1) * TILE] = tile


def attention_cost(products, units, rows, part):
    pairs = TRIO * rows * rows * units * units * part // 2
    return pl.CostEstimate(
        flops=2 * 64 * products * pairs, bytes_accessed=20_000_000, transcendentals=pairs
    )


def whole_spec(shape):
    zeros = (0,) * len(shape)
    return pl.BlockSpec(shape, lambda j, meta: zeros)


def attend_forward(meta, packed, kv, seg):
    units, rows, unused = packed.shape
    part = len(kv)
    return pl.pallas_call(
        functools.partial(forward_kernel, part, units),
        grid_spec=pltpu.PrefetchScalarGridSpec(
            num_scalar_prefetch=1,
            grid=(units,),
            in_specs=[
                pl.BlockSpec((1, rows, PACK), lambda j, meta: (j, 0, 0)),
                *[whole_spec(piece.shape) for piece in kv],
                pl.BlockSpec((1, 1, rows), lambda j, meta: (j, 0, 0)),
            ],
            out_specs=[
                pl.BlockSpec((1, rows, OPACK), lambda j, meta: (j, 0, 0)),
                pl.BlockSpec((1, TRIO * HEAD_DIM, rows), lambda j, meta: (j, 0, 0)),
                pl.BlockSpec((1, 8, rows), lambda j, meta: (j, 0, 0)),
            ],
            scratch_shapes=[
                pltpu.VMEM((units, part * rows, PACK - TILE), BF),
                pltpu.VMEM((TRIO, TILE, rows), BF),
                pltpu.VMEM((units, TRIO * HEAD_DIM, part * rows), BF),
                pltpu.VMEM((8, rows), F32),
                pltpu.VMEM((8, rows), F32),
                pltpu.VMEM((TRIO, HEAD_DIM, rows), F32),
            ],
        ),
        out_shape=[
            jax.ShapeDtypeStruct((units, rows, OPACK), BF),
            jax.ShapeDtypeStruct((units, TRIO * HEAD_DIM, rows), F32),
            jax.ShapeDtypeStruct((units, 8, rows), F32),
        ],
        compiler_params=params_of("arbitrary"),
        cost_estimate=attention_cost(8, units, rows, part),
        name="attend_forward",
    )(meta, packed, *kv, seg)


def attend_backward(meta, packed, dout, out_t, lse, kv, seg):
    units, rows, unused = packed.shape
    part = len(kv)
    others = (max(part - 1, 1), units, rows, 4 * TILE)
    grads = pltpu.VMEM((units, part * rows, TILE), F32)
    return pl.pallas_call(
        functools.partial(backward_kernel, part, units),
        grid_spec=pltpu.PrefetchScalarGridSpec(
            num_scalar_prefetch=1,
            grid=(units,),
            in_specs=[
                pl.BlockSpec((1, rows, PACK), lambda j, meta: (j, 0, 0)),
                pl.BlockSpec((1, rows, OPACK), lambda j, meta: (j, 0, 0)),
                pl.BlockSpec((1, TRIO * HEAD_DIM, rows), lambda j, meta: (j, 0, 0)),
                pl.BlockSpec((1, 8, rows), lambda j, meta: (j, 0, 0)),
                *[whole_spec(piece.shape) for piece in kv],
                pl.BlockSpec((1, 1, rows), lambda j, meta: (j, 0, 0)),
            ],
            out_specs=[whole_spec(packed.shape), whole_spec(others)],
            scratch_shapes=[
                pltpu.VMEM((units, part * rows, PACK - TILE), BF),
                pltpu.VMEM((TRIO, TILE, rows), BF),
                pltpu.VMEM((TRIO, TILE, rows), BF),
                pltpu.VMEM((TRIO * rows, TILE), BF),
                pltpu.VMEM((TRIO * rows, TILE), BF),
                pltpu.VMEM((units, TRIO * HEAD_DIM, part * rows), BF),
                pltpu.VMEM((8, rows), F32),
                pltpu.VMEM((TRIO * HEAD_DIM, rows), F32),
                grads,
                grads,
                grads,
                grads,
            ],
        ),
        out_shape=[
            jax.ShapeDtypeStruct(packed.shape, BF),
            jax.ShapeDtypeStruct(others, BF),
        ],
        compiler_params=params_of("arbitrary"),
        cost_estimate=attention_cost(20, units, rows, part),
        name="attend_backward",
    )(meta, packed, dout, out_t, lse, *kv, seg)


def pack_kernel(trios, groups, w_ref, vec_ref, early_ref, local_ref):
    d = w_ref.shape[1] // 3
    w = w_ref[...].astype(F32)
    width = TRIO * HEAD_DIM
    zeros = jnp.zeros((w.shape[0], HEAD_DIM), F32)
    for g in range(trios):
        q, k, v = (w[:, i * d + g * width : i * d + (g + 1) * width] for i in range(3))
        tiles = [q[:, :TILE], k[:, :TILE], v[:, :TILE]]
        tiles.append(jnp.concatenate([q[:, TILE:], k[:, TILE:]], 1))
        tiles.append(jnp.concatenate([v[:, TILE:], zeros], 1))
        for t, tile in enumerate(tiles):
            tile = tile.astype(BF)
            local_ref[:, g * PACK + t * TILE : g * PACK + (t + 1) * TILE] = tile
            for s in range(groups):
                early_ref[g * groups + s, :, t * TILE : (t + 1) * TILE] = tile
        for s in range(groups):
            early_ref[g * groups + s, :, PACK:] = vec_ref[s]


def pack_early(weight, vec, trios):
    r = weight.shape[0]
    groups = vec.shape[0]
    return pl.pallas_call(
        functools.partial(pack_kernel, trios, groups),
        out_shape=[
            jax.ShapeDtypeStruct((trios * groups, r, PACK + TILE), BF),
            jax.ShapeDtypeStruct((r, trios * PACK), BF),
        ],
        name="pack_early",
    )(weight, vec)


def feed_kernel(
    x_ref, cot_ref, up_ref, down_ref, shift_ref, hid_ref, pre_ref, sum_ref, second_ref, back_ref
):
    pre = mm(x_ref[...], up_ref[...]) + shift_ref[...]
    grad = inner_back(cot_ref[...], down_ref[...])
    cdf = 0.5 * (1.0 + lax.erf(pre * math.sqrt(0.5)))
    hidden = (pre * cdf).astype(BF)
    slope = cdf + pre * (jnp.exp(-0.5 * pre * pre) * (1.0 / math.sqrt(2.0 * math.pi)))
    pre_grad = (grad * slope).astype(BF)
    hid_ref[...] = hidden
    pre_ref[...] = pre_grad
    sum_ref[...] = jnp.sum(pre_grad.astype(F32), 0, keepdims=True)
    second = mm(hidden, down_ref[...])
    back = inner_back(pre_grad, up_ref[...])

    @pl.when(pl.program_id(0) == 0)
    def _():
        second_ref[...] = second
        back_ref[...] = back

    @pl.when(pl.program_id(0) > 0)
    def _():
        second_ref[...] += second
        back_ref[...] += back


def feed_forward(x, cot, weights, shift, blocks):
    rows, d = x.shape
    ff = blocks * d
    half = d // 2
    wide = pl.BlockSpec((rows, d), lambda i: (0, 0))
    column = pl.BlockSpec((rows, half), lambda i: (0, i))
    line = pl.BlockSpec((1, half), lambda i: (0, i))
    return pl.pallas_call(
        feed_kernel,
        grid=(2 * blocks,),
        in_specs=[
            wide,
            wide,
            pl.BlockSpec((d, half), lambda i: (0, i)),
            pl.BlockSpec((half, d), lambda i: (i % 2, blocks + i // 2)),
            line,
        ],
        out_specs=[column, column, line, wide, wide],
        out_shape=[
            jax.ShapeDtypeStruct((rows, ff), BF),
            jax.ShapeDtypeStruct((rows, ff), BF),
            jax.ShapeDtypeStruct((1, ff), F32),
            jax.ShapeDtypeStruct((rows, d), F32),
            jax.ShapeDtypeStruct((rows, d), F32),
        ],
        compiler_params=params_of("arbitrary"),
        cost_estimate=pl.CostEstimate(
            flops=8 * rows * d * ff, bytes_accessed=4 * d * ff, transcendentals=2 * rows * ff
        ),
        name="feed_forward",
    )(x, cot, weights, weights, shift)


def gradient_kernel(
    trios, ups, per, norm_ref, pre_ref, hidden_ref, cot_ref, att_ref, cols_ref, out_ref
):
    i = pl.program_id(0)
    d = norm_ref.shape[1]

    @pl.when(i < ups)
    def _():
        out_ref[...] = outer_sum(norm_ref[...], pre_ref[...]).astype(BF)

    @pl.when((i >= ups) & (i < 2 * ups))
    def _():
        out_ref[...] = outer_sum(hidden_ref[...], cot_ref[...]).astype(BF)

    @pl.when(i == 2 * ups)
    def _():
        width = d // trios
        for g in range(trios):
            part = outer_sum(att_ref[:, g * OPACK : (g + 1) * OPACK], cols_ref[...])
            out_ref[g * width : (g + 1) * width] = part[:width].astype(BF)


def gradients(normed, pre_grad, hidden, cot, attended, cols, trios):
    rows, d = normed.shape
    width = cols.shape[1]
    per = d // width
    ups = hidden.shape[1] // width

    def down(i):
        return jnp.clip(i - ups, 0, ups - 1)

    return pl.pallas_call(
        functools.partial(gradient_kernel, trios, ups, per),
        grid=(2 * ups + 1,),
        in_specs=[
            pl.BlockSpec((rows, d), lambda i: (0, 0)),
            pl.BlockSpec((rows, width), lambda i: (0, jnp.minimum(i, ups - 1))),
            pl.BlockSpec((rows, d), lambda i: (0, down(i) // per)),
            pl.BlockSpec((rows, width), lambda i: (0, down(i) % per)),
            pl.BlockSpec(attended.shape, lambda i: (0, 0)),
            pl.BlockSpec((rows, width), lambda i: (0, 0)),
        ],
        out_specs=pl.BlockSpec((d, width), lambda i: (0, i)),
        out_shape=jax.ShapeDtypeStruct((d, (2 * ups + 1) * width), BF),
        compiler_params=params_of("arbitrary"),
        cost_estimate=pl.CostEstimate(
            flops=2 * rows * d * (2 * ups + 1) * width, bytes_accessed=0, transcendentals=0
        ),
        name="gradients",
    )(normed, pre_grad, hidden, cot, attended, cols)


def trio_kernel(norm_ref, hat_ref, grad_ref, w_ref, vec_ref, late_ref, shift_ref, own, hat):
    j = pl.program_id(0)
    d = norm_ref.shape[2]
    grad = grad_ref[...].reshape(-1, PACK)
    own_part = outer_sum(norm_ref[...].reshape(-1, d), grad)
    hat_part = outer_sum(hat_ref[...].reshape(-1, d), grad)
    sums = jnp.sum(grad.astype(F32), 0, keepdims=True)

    @pl.when(j == 0)
    def _():
        own[...] = own_part
        hat[...] = hat_part
        shift_ref[...] = sums

    @pl.when(j > 0)
    def _():
        own[...] += own_part
        hat[...] += hat_part
        shift_ref[...] += sums

    @pl.when(j == pl.num_programs(0) - 1)
    def _():
        late_ref[:, :PACK] = own[...].astype(BF)
        weight = w_ref[...].astype(F32)
        lane = lane_of(vec_ref.shape)
        vec = vec_ref[...]
        vec = jnp.where(lane == 0, jnp.sum(weight * hat[...], 1, keepdims=True), vec)
        vec = jnp.where(lane == 1, jnp.sum(weight * shift_ref[...], 1, keepdims=True), vec)
        late_ref[:, PACK:] = vec.astype(BF)


def trio_gradient(normed, hat, grad, weight, vec):
    units, rows, d = normed.shape
    tok_spec = pl.BlockSpec((2, rows, d), lambda j: (j, 0, 0))
    return pl.pallas_call(
        trio_kernel,
        grid=(units // 2,),
        in_specs=[
            tok_spec,
            tok_spec,
            pl.BlockSpec((2, rows, PACK), lambda j: (j, 0, 0)),
            pl.BlockSpec((d, PACK), lambda j: (0, 0)),
            pl.BlockSpec((d, TILE), lambda j: (0, 0)),
        ],
        out_specs=[
            pl.BlockSpec((d, PACK + TILE), lambda j: (0, 0)),
            pl.BlockSpec((1, PACK), lambda j: (0, 0)),
        ],
        scratch_shapes=[pltpu.VMEM((d, PACK), F32), pltpu.VMEM((d, PACK), F32)],
        out_shape=[
            jax.ShapeDtypeStruct((d, PACK + TILE), BF),
            jax.ShapeDtypeStruct((1, PACK), F32),
        ],
        compiler_params=params_of("arbitrary"),
        cost_estimate=pl.CostEstimate(flops=0, bytes_accessed=0, transcendentals=0),
        name="trio_gradient",
    )(normed, hat, grad, weight, vec)


def pack_columns(matrix, trios):
    r = matrix.shape[0]
    q, k, v = (
        part.reshape(r, trios, TRIO * HEAD_DIM) for part in jnp.split(matrix, 3, axis=1)
    )
    zeros = jnp.zeros((r, trios, HEAD_DIM), matrix.dtype)
    pieces = [q[..., :TILE], k[..., :TILE], v[..., :TILE], q[..., TILE:], k[..., TILE:]]
    return jnp.concatenate(pieces + [v[..., TILE:], zeros], -1).reshape(r, trios * PACK)


def unpack_columns(matrix, trios):
    r = matrix.shape[0]
    m = matrix.reshape(r, trios, PACK)
    halves = [
        m[..., 3 * TILE : 3 * TILE + HEAD_DIM],
        m[..., 3 * TILE + HEAD_DIM : 4 * TILE],
        m[..., 4 * TILE : 4 * TILE + HEAD_DIM],
    ]
    return jnp.concatenate(
        [
            jnp.concatenate([m[..., i * TILE : (i + 1) * TILE], halves[i]], -1).reshape(r, -1)
            for i in range(3)
        ],
        -1,
    )


def split_hidden(matrix, count, r):
    lead = matrix.shape[0]
    return matrix.reshape(lead, count, -1, r).transpose(0, 2, 1, 3).reshape(lead, -1)


def join_hidden(matrix, count, r):
    lead = matrix.shape[0]
    return matrix.reshape(lead, -1, count, r).transpose(0, 2, 1, 3).reshape(lead, -1)


def on_device(
    tokens,
    segment,
    ln1_gain,
    ln1_bias,
    ln2_gain,
    ln2_bias,
    qkv_weight,
    qkv_bias,
    dense_weight,
    dense_bias,
    fc1_weight,
    fc1_bias,
    output_feed_weight,
    output_feed_bias,
    cotangent,
):
    rows, groups, d = tokens.shape
    units = lax.axis_size("unit")
    part = lax.axis_size("part")
    count = units * part * lax.axis_size("seq")
    trios = units // groups
    all_rows = rows * groups
    r = qkv_weight.shape[0]
    ff = fc1_weight.shape[1]
    blocks = ff // d
    c = lax.axis_index("part")
    unit = lax.axis_index("unit")

    seq = lax.axis_index("seq")
    seqs = lax.axis_size("seq")
    place = (seq * units + unit) * part + c

    def exchange(blocks_out):
        width = blocks_out.shape[-1]
        return lax.all_to_all(
            blocks_out.reshape(-1, width), "unit", 0, 0, tiled=True
        ).reshape(blocks_out.shape)

    def shift(value, axis, i):
        n = lax.axis_size(axis)
        return lax.ppermute(value, axis, [(p, (p + i) % n) for p in range(n)])

    def natural_order(got, me):
        n = len(got)
        if n == 2:
            return jnp.where(me == 0, jnp.stack(got), jnp.stack(got[::-1]))
        ring = jnp.stack((got + got)[::-1])
        return lax.dynamic_slice_in_dim(ring, n - 1 - me, n, 0)

    def gather_small(value, axis):
        n = lax.axis_size(axis)
        got = [value] + [shift(value, axis, i) for i in range(1, n)]
        return natural_order(got, lax.axis_index(axis))

    def swap_parts(value):
        got = [lax.dynamic_index_in_dim(value, c, 0, False)]
        for i in range(1, part):
            piece = lax.dynamic_index_in_dim(value, (c + i) % part, 0, False)
            got.append(shift(piece, "part", i))
        return natural_order(got, c)

    def all_parts(value):
        return jnp.concatenate([value] + [shift(value, "part", i) for i in range(1, part)], 0)

    def sum_parts(value):
        n = value.shape[0] // part
        total = value[:n]
        for i in range(1, part):
            total = total + shift(value[i * n : (i + 1) * n], "part", part - i)
        return total

    def scatter_small(value, axis):
        n = lax.axis_size(axis)
        me = lax.axis_index(axis)
        total = lax.dynamic_index_in_dim(value, me, 0, False).astype(F32)
        for i in range(1, n):
            piece = lax.dynamic_index_in_dim(value, (me + i) % n, 0, False)
            total = total + shift(piece, axis, i).astype(F32)
        return total.astype(BF)

    vectors = (ln1_gain, ln1_bias, ln2_gain, ln2_bias, dense_bias, output_feed_bias)
    vec = jnp.concatenate(
        [v.reshape(r, 1) for v in vectors] + [qkv_bias.reshape(r, 3), fc1_bias.reshape(r, blocks)],
        1,
    )
    token_rows = tokens.transpose(1, 0, 2)
    seg_rows = segment.T
    seg_lanes = -(-2 * rows // r)
    seg_pack = jnp.concatenate([seg_rows // 64, seg_rows % 64], 1).astype(BF)
    seg_pack = jnp.pad(seg_pack, ((0, 0), (0, seg_lanes * r - 2 * rows)))
    seg_pack = seg_pack.reshape(groups, r, seg_lanes)
    vec = jnp.pad(vec, ((0, 0), (0, 16 - vec.shape[1])))
    vec = jnp.concatenate(
        [
            jnp.broadcast_to(vec, (groups, r, 16)),
            seg_pack,
            jnp.zeros((groups, r, TILE - 16 - seg_lanes), BF),
        ],
        -1,
    )
    early, qkv_local = pack_early(qkv_weight, vec, trios)
    toks = jnp.concatenate([jnp.concatenate([token_rows] * trios, 0), early], 1)
    toks = exchange(toks)
    early = toks[:, rows:]

    seg_mine = early[:, :, PACK + 16 : PACK + 16 + seg_lanes].astype(jnp.int32)
    seg_mine = seg_mine.reshape(units, r * seg_lanes)
    seg_mine = seg_mine[:, :rows] * 64 + seg_mine[:, rows : 2 * rows]
    meta = jnp.concatenate([seg_mine[:, 0], seg_mine[:, -1], c[None]])
    seg_mine = seg_mine[:, None, :]
    trio_full = gather_small(gather_small(early, "seq"), "part")
    trio_full = trio_full.transpose(1, 2, 0, 3, 4).reshape(d, PACK + TILE)
    vec_full = trio_full[:, PACK:].astype(F32)
    vec_rows = vec_full[:, :8].T
    gain_one, bias_one, gain_two, bias_two, dense_shift, down_shift = (
        vec_rows[i : i + 1] for i in range(6)
    )
    qkv_shift = pack_columns(vec_full[:, 6:9].reshape(1, 3 * d), trios).reshape(trios, PACK)
    qkv_shift = lax.dynamic_slice_in_dim(qkv_shift, unit // groups, 1, 0)
    up_shift = split_hidden(vec_full[:, 9 : 9 + blocks].reshape(1, ff), count, r)

    feed_blocks = output_feed_weight.reshape(blocks, r, d)
    first_pack = jnp.concatenate([qkv_local, dense_weight], 1)
    first = lax.all_gather(first_pack, ALL_AXES, axis=0, tiled=True)
    half = blocks // part
    up_local = split_hidden(fc1_weight, count, r)
    second_pack = jnp.stack(
        [
            jnp.concatenate(
                [up_local[:, p * half * d : (p + 1) * half * d]]
                + [feed_blocks[b] for b in range(p * half, (p + 1) * half)],
                1,
            )
            for p in range(part)
        ]
    )
    second_pack = swap_parts(second_pack).reshape(part * r, 2 * half * d)
    second_pack, toks = lax.optimization_barrier((second_pack, toks))
    second = lax.all_gather(second_pack, ("seq", "unit"), axis=0, tiled=True)
    qkv_full = first[:, : trios * PACK]
    dense_pad = jnp.pad(
        first[:, trios * PACK :].reshape(trios, d // trios, d),
        ((0, 0), (0, OPACK - d // trios), (0, 0)),
    )

    block_start = (jnp.arange(units, dtype=jnp.int32) * part + c) * rows
    positions = block_start[:, None, None] + jnp.arange(rows, dtype=jnp.int32) - seg_mine
    freq = jnp.arange(ROT // 2, dtype=F32)
    inverse = jnp.exp(freq * (-2.0 * math.log(10000.0) / ROT))
    angles = positions.astype(F32) * inverse[None, :, None]
    cos = jnp.cos(angles)
    sin = jnp.sin(angles)

    packed, kv_own, normed_one, hat_one = project(
        toks, trio_full, qkv_shift, gain_one, bias_one, cos, sin
    )
    kv = [kv_own] + [shift(kv_own, "part", i) for i in range(1, part)]

    x = token_rows.reshape(all_rows, d).astype(F32)
    cot = cotangent.transpose(1, 0, 2).reshape(all_rows, d)
    cot_float = cot.astype(F32)
    centre = x - jnp.mean(x, -1, keepdims=True)
    spread = lax.rsqrt(jnp.mean(centre * centre, -1, keepdims=True) + EPSILON)
    xhat = centre * spread
    normed_two = (xhat * gain_two + bias_two).astype(BF)
    attended_grad = jnp.einsum(
        "sld,gkd->gslk", cot.reshape(groups, rows, d), dense_pad, preferred_element_type=F32
    ).astype(BF)
    attended_grad, meta = lax.optimization_barrier((attended_grad, meta))
    dout = exchange(attended_grad.reshape(units, rows, OPACK))
    out_low, out_t, lse = attend_forward(meta, packed, kv, seg_mine)
    dout, out_low = lax.optimization_barrier((dout, out_low))
    attended = exchange(out_low)

    normed_two, dout = lax.optimization_barrier((normed_two, dout))
    normed_all = all_parts(normed_two)
    cot_all = all_parts(cot)
    up_shift = lax.dynamic_slice_in_dim(up_shift, c * half * d, half * d, 1)
    hidden_low, pre_grad, up_shift_grad, second_branch, normed_two_grad = feed_forward(
        normed_all, cot_all, second, up_shift, half
    )
    hidden_low, pre_grad, attended = lax.optimization_barrier((hidden_low, pre_grad, attended))
    second_branch = sum_parts(second_branch)
    normed_two_grad = sum_parts(normed_two_grad)
    up_shift_grad = lax.dynamic_update_slice_in_dim(
        jnp.zeros((1, ff), F32), up_shift_grad, c * half * d, 1
    )

    def norm_back(grad, gain):
        gy = grad * gain
        return spread * (
            gy - jnp.mean(gy, -1, keepdims=True) - xhat * jnp.mean(gy * xhat, -1, keepdims=True)
        )

    attended = attended.reshape(trios, groups, rows, OPACK).transpose(1, 2, 0, 3)
    attended = attended.reshape(all_rows, trios * OPACK)
    dense_cols = d // part
    cols = lax.dynamic_slice_in_dim(cot_all, c * dense_cols, dense_cols, 1)
    cols = jnp.pad(cols, ((0, 0), (0, -dense_cols % TILE)))
    mlp_grads = gradients(
        normed_all, pre_grad, hidden_low, cot_all, all_parts(attended), cols, trios
    )
    mlp_grads, dout = lax.optimization_barrier((mlp_grads, dout))
    mlp_sum = lax.psum_scatter(mlp_grads, ("seq", "unit"), scatter_dimension=0, tiled=True)

    own, others = attend_backward(meta, packed, dout, out_t, lse, kv, seg_mine)
    others = [shift(others[i - 1], "part", part - i) for i in range(1, part)]
    qkv_grad = unturn(own, others, cos, sin)
    back = exchange(qkv_grad)

    attended, second_branch, normed_two_grad, qkv_grad = lax.optimization_barrier(
        (attended, second_branch, normed_two_grad, qkv_grad)
    )
    branch_one = mm(attended, dense_pad.reshape(trios * OPACK, d)) + dense_shift
    output = (x + branch_one + second_branch + down_shift).astype(BF)
    in_two = norm_back(normed_two_grad, gain_two)
    vec_grads = jnp.concatenate(
        [
            jnp.zeros((2, d), F32),
            jnp.sum(normed_two_grad * xhat, 0)[None],
            jnp.sum(normed_two_grad, 0)[None],
            jnp.sum(cot_float, 0)[None],
            jnp.zeros((3, d), F32),
        ],
        0,
    ).T
    up_shift_grad = join_hidden(up_shift_grad, count, r).reshape(d, blocks)

    vec_grads = jnp.concatenate(
        [vec_grads, up_shift_grad, jnp.zeros((d, TILE - 8 - blocks), F32)], 1
    )
    late, shift_grad = trio_gradient(normed_one, hat_one, qkv_grad, trio_full, vec_grads)
    late = late.reshape(seqs, units, part, r, PACK + TILE)
    shift_rows = jnp.pad(shift_grad.astype(BF), ((0, 7), (0, TILE)))
    late = jnp.concatenate(
        [late, jnp.broadcast_to(shift_rows, (seqs, units, part) + shift_rows.shape)], 3
    )
    late = scatter_small(late.transpose(2, 0, 1, 3, 4), "part")
    late = scatter_small(late, "seq")
    late, back, mlp_sum = lax.optimization_barrier((late, back, mlp_sum))
    late = exchange(late).astype(F32)
    late = jnp.sum(late.reshape(trios, groups, r + 8, PACK + TILE), 1)
    qkv_weight_grad = unpack_columns(
        late[:, :r, :PACK].transpose(1, 0, 2).reshape(r, trios * PACK), trios
    )
    late_vec = jnp.sum(late[:, :r, PACK:], 0)
    qkv_shift_grad = unpack_columns(late[:, r, :PACK].reshape(1, trios * PACK), trios)[0]
    qkv_shift_grad = lax.dynamic_slice_in_dim(qkv_shift_grad, place * 3 * r, 3 * r)

    mlp_sum = swap_parts(mlp_sum.reshape(part, r, -1)).astype(F32)
    up_sum = jnp.concatenate([mlp_sum[p, :, : half * d] for p in range(part)], 1)
    down_sum = jnp.concatenate(
        [
            mlp_sum[p, :, (half + b) * d : (half + b + 1) * d]
            for p in range(part)
            for b in range(half)
        ],
        0,
    )
    dense_sum = jnp.concatenate(
        [mlp_sum[p, :, 2 * half * d : 2 * half * d + dense_cols] for p in range(part)], 1
    )
    param_grads = (
        late_vec[:, 0],
        late_vec[:, 1],
        late_vec[:, 2],
        late_vec[:, 3],
        qkv_weight_grad,
        qkv_shift_grad,
        dense_sum,
        late_vec[:, 4],
        join_hidden(up_sum, count, r),
        late_vec[:, 8 : 8 + blocks].reshape(-1),
        down_sum,
        late_vec[:, 4],
    )

    back = back.reshape(trios, groups, rows, PACK).transpose(1, 2, 0, 3)
    normed_one_grad = inner_back(back.reshape(all_rows, trios * PACK), qkv_full)
    in_one = norm_back(normed_one_grad, gain_one)
    tokens_grad = (cot_float + in_one + in_two).astype(BF)

    def natural(value):
        return value.reshape(groups, rows, d).transpose(1, 0, 2)

    return (natural(output), natural(tokens_grad)) + tuple(param_grads)


def solution(mesh):
    devices = mesh.devices
    seq_size, ctx_size = devices.shape
    ctx = ("unit", "part")
    tok = P(ctx, "seq", None)
    vec = P(ALL_AXES)
    mat = P(ALL_AXES, None)
    pairs = (vec, vec, vec, vec, mat, vec, mat, vec, mat, vec, mat, vec)

    def run(tokens, *rest):
        units = HEADS // TRIO * (tokens.shape[1] // seq_size)
        split = Mesh(devices.reshape(seq_size, units, ctx_size // units), ALL_AXES)
        mapped = jax.shard_map(
            on_device,
            mesh=split,
            in_specs=(tok, P(ctx, "seq")) + pairs + (tok,),
            out_specs=(tok, tok) + pairs,
            check_vma=False,
        )
        return mapped(tokens, *rest)

    return run
```

```python
import functools
import math

import jax
import jax.numpy as jnp
from jax import lax
from jax.experimental import pallas as pl
from jax.experimental.pallas import tpu as pltpu
from jax.sharding import Mesh, PartitionSpec as P

HEADS = 12
HEAD_DIM = 64
ROT = 16
TRIO = 3
TILE = 128
PACK = 5 * TILE
OPACK = 2 * TILE

EPSILON = 1e-05
NEG_BIG = -1e30
BF = jnp.bfloat16
F32 = jnp.float32
ALL_AXES = ("seq", "unit", "part")
VMEM_BYTES = 56 * 1024 * 1024


def params_of(*semantics):
    return pltpu.CompilerParams(
        dimension_semantics=semantics, vmem_limit_bytes=VMEM_BYTES
    )


def mm(a, b):
    return jnp.dot(a, b, preferred_element_type=F32)


def outer_sum(left_rows, right_rows):
    return lax.dot_general(
        left_rows, right_rows, (((0,), (0,)), ((), ())), preferred_element_type=F32
    )


def inner_back(grad_rows, weight):
    return lax.dot_general(
        grad_rows, weight, (((1,), (1,)), ((), ())), preferred_element_type=F32
    )


def lane_of(shape):
    return lax.broadcasted_iota(jnp.int32, shape, len(shape) - 1)


def turn(tile, cos, sin):
    partner = jnp.where(
        lane_of(tile.shape) % HEAD_DIM < ROT // 2,
        pltpu.roll(tile, TILE - ROT // 2, 1),
        pltpu.roll(tile, ROT // 2, 1),
    )
    return tile * cos + partner * sin


def turn_tables(cos_rows, sin_rows):
    rows = cos_rows.shape[1]
    rest = HEAD_DIM - ROT
    cos_head = [cos_rows, cos_rows, jnp.ones((rest, rows), F32)]
    sin_head = [-sin_rows, sin_rows, jnp.zeros((rest, rows), F32)]
    return jnp.concatenate(cos_head * 2, 0).T, jnp.concatenate(sin_head * 2, 0).T


def first_place(rel):
    return rel % 2 * 4 + rel // 2 % 2 * 2 + rel // 4


def second_place(rel):
    return rel // 2 % 2 * 4 + rel % 2 * 2 + rel // 4


def project_kernel(
    place_ref,
    one_ref,
    two_ref,
    w_ref,
    b_ref,
    gain_ref,
    bias_ref,
    cos_ref,
    sin_ref,
    out_ref,
    kv_ref,
    norm_ref,
    hat_ref,
):
    x = jnp.concatenate([one_ref[0], two_ref[0]], 0).astype(F32)
    centre = x - jnp.mean(x, -1, keepdims=True)
    spread = jnp.mean(centre * centre, -1, keepdims=True)
    hat = centre * lax.rsqrt(spread + EPSILON)
    normed = (hat * gain_ref[...] + bias_ref[...]).astype(BF)
    hat_ref[0] = hat.astype(BF)
    norm_ref[0] = normed
    y = mm(normed, w_ref[...]) + b_ref[...]
    cos, sin = turn_tables(cos_ref[0], sin_ref[0])
    for t in range(5):
        tile = y[:, t * TILE : (t + 1) * TILE]
        if t in (0, 1, 3):
            tile = turn(tile, cos, sin)
        tile = tile.astype(BF)
        out_ref[0, :, t * TILE : (t + 1) * TILE] = tile
        if t > 0:
            kv_ref[0, :, (t - 1) * TILE : t * TILE] = tile


def half_specs(rows, d):
    return [
        pl.BlockSpec((1, rows // 2, d), lambda j, place: (first_place(j ^ place[0]), 0, 0)),
        pl.BlockSpec((1, rows // 2, d), lambda j, place: (second_place(j ^ place[0]), 0, 0)),
    ]


def project(place, toks, weight, bias, gain, offset, cos, sin):
    units, unused, rows = cos.shape
    d = toks[0].shape[2]
    tok_spec = pl.BlockSpec((1, rows, d), lambda j, place: (j, 0, 0))
    row_spec = pl.BlockSpec((1, d), lambda j, place: (0, 0))
    turn_spec = pl.BlockSpec((1, ROT // 2, rows), lambda j, place: (j, 0, 0))
    return pl.pallas_call(
        project_kernel,
        grid_spec=pltpu.PrefetchScalarGridSpec(
            num_scalar_prefetch=1,
            grid=(units,),
            in_specs=half_specs(rows, d)
            + [
                pl.BlockSpec((d, PACK), lambda j, place: (0, 0)),
                pl.BlockSpec((1, PACK), lambda j, place: (0, 0)),
                row_spec,
                row_spec,
                turn_spec,
                turn_spec,
            ],
            out_specs=[
                pl.BlockSpec((1, rows, PACK), lambda j, place: (j, 0, 0)),
                pl.BlockSpec((1, rows, PACK - TILE), lambda j, place: (j, 0, 0)),
                tok_spec,
                tok_spec,
            ],
        ),
        out_shape=[
            jax.ShapeDtypeStruct((units, rows, PACK), BF),
            jax.ShapeDtypeStruct((units, rows, PACK - TILE), BF),
            jax.ShapeDtypeStruct((units, rows, d), BF),
            jax.ShapeDtypeStruct((units, rows, d), BF),
        ],
        compiler_params=params_of("arbitrary"),
        cost_estimate=pl.CostEstimate(
            flops=2 * units * rows * d * PACK,
            bytes_accessed=2 * units * rows * (3 * d + PACK),
            transcendentals=0,
        ),
        name="project",
    )(place, *toks, weight, bias, gain, offset, cos, sin)


def unturn_kernel(place_ref, own_ref, *refs):
    w_ref, cos_ref, sin_ref, out_ref, one_ref, two_ref = refs[-6:]
    others = refs[:-6]
    cos, sin = turn_tables(cos_ref[0], sin_ref[0])
    for t in range(5):
        tile = own_ref[0, :, t * TILE : (t + 1) * TILE].astype(F32)
        if t > 0:
            for other in others:
                tile = tile + other[0, :, (t - 1) * TILE : t * TILE].astype(F32)
        if t in (0, 1, 3):
            tile = turn(tile, cos, -sin)
        out_ref[0, :, t * TILE : (t + 1) * TILE] = tile.astype(BF)
    back = inner_back(out_ref[0], w_ref[...]).astype(BF)
    rows = back.shape[0] // 2
    one_ref[0] = back[:rows]
    two_ref[0] = back[rows:]


def unturn(place, own, others, weight, cos, sin):
    units, rows, unused = own.shape
    d = weight.shape[0]
    turn_spec = pl.BlockSpec((1, ROT // 2, rows), lambda j, place: (j, 0, 0))
    own_spec = pl.BlockSpec((1, rows, PACK), lambda j, place: (j, 0, 0))
    other_spec = pl.BlockSpec((1, rows, PACK - TILE), lambda j, place: (j, 0, 0))
    half = jax.ShapeDtypeStruct((units, rows // 2, d), BF)
    return pl.pallas_call(
        unturn_kernel,
        grid_spec=pltpu.PrefetchScalarGridSpec(
            num_scalar_prefetch=1,
            grid=(units,),
            in_specs=[own_spec]
            + [other_spec] * len(others)
            + [pl.BlockSpec((d, PACK), lambda j, place: (0, 0)), turn_spec, turn_spec],
            out_specs=[own_spec] + half_specs(rows, d),
        ),
        out_shape=[jax.ShapeDtypeStruct(own.shape, BF), half, half],
        compiler_params=params_of("arbitrary"),
        name="unturn",
    )(place, own, *others, weight, cos, sin)


def flip(tile):
    return tile.astype(F32).T


def head_rows(flipped, low):
    row = lax.broadcasted_iota(jnp.int32, flipped.shape, 0)
    keep = row < HEAD_DIM if low else row >= HEAD_DIM
    return jnp.where(keep, flipped, 0.0)


def head_lanes(tile, low):
    lane = lane_of(tile.shape)
    keep = lane < HEAD_DIM if low else lane >= HEAD_DIM
    return jnp.where(keep, tile, 0.0)


def query_sides(q_ref, qb):
    scale = HEAD_DIM ** (-0.5)
    a = flip(q_ref[0, :, 0:TILE]) * scale
    d = flip(q_ref[0, :, 3 * TILE : 4 * TILE]) * scale
    qb[0] = head_rows(a, True).astype(BF)
    qb[1] = head_rows(a, False).astype(BF)
    qb[2] = jnp.concatenate(
        [jnp.zeros((HEAD_DIM, d.shape[1]), F32), d[:HEAD_DIM]], 0
    ).astype(BF)


def live_of(seg_row, unit, query_start, part, rows, c):
    shape = (rows, rows)
    query_pos = query_start + lax.broadcasted_iota(jnp.int32, shape, 1)
    row = lax.broadcasted_iota(jnp.int32, shape, 0)
    pieces = []
    for i in range(part):
        key_pos = (unit * part + lax.rem(c - i + part, part)) * rows + row
        pieces.append((key_pos <= query_pos) & (key_pos >= seg_row))
    return jnp.concatenate(pieces, 0)


def unit_loop(meta, part, units, rows, step):
    j = pl.program_id(0)
    first = meta[j] // (rows * part)
    top_seg = meta[units + j]

    def one(unit, unused):
        masked = (unit == j) | (top_seg > unit * (rows * part))

        @pl.when(masked)
        def _():
            step(unit, True)

        @pl.when(jnp.logical_not(masked))
        def _():
            step(unit, False)

        return unused

    lax.fori_loop(first, j + 1, one, 0)


def join_parts(part, refs, kv_ref):
    rows = refs[0].shape[1]

    def one(unit, unused):
        for i in range(part):
            kv_ref[unit, i * rows : (i + 1) * rows] = refs[i][unit]
        return unused

    lax.fori_loop(0, refs[0].shape[0], one, 0)


def forward_kernel(part, units, meta, q_ref, *refs):
    seg_ref, o_ref, ot_ref, lse_ref, kv_ref, qb, vt, top, total, acc = refs[part:]
    rows = q_ref.shape[1]
    c = meta[2 * units]
    j = pl.program_id(0)

    @pl.when(j == 0)
    def _():
        join_parts(part, refs[:part], kv_ref)

        def turn_values(unit, unused):
            vt[unit, :TILE] = flip(kv_ref[unit, :, TILE : 2 * TILE]).astype(BF)
            vt[unit, TILE:] = flip(kv_ref[unit, :, 3 * TILE :])[:HEAD_DIM].astype(BF)
            return unused

        lax.fori_loop(0, units, turn_values, 0)

    query_sides(q_ref, qb)
    top[...] = jnp.full(top.shape, NEG_BIG, F32)
    total[...] = jnp.zeros(total.shape, F32)
    acc[...] = jnp.zeros(acc.shape, F32)
    seg_row = seg_ref[0]
    query_start = (j * part + c) * rows

    def step(unit, masked):
        k01 = kv_ref[unit, :, 0:TILE]
        k2 = kv_ref[unit, :, 2 * TILE : 3 * TILE]
        if masked:
            live = live_of(seg_row, unit, query_start, part, rows, c)
        scores = [mm(k2 if h == 2 else k01, qb[h]) for h in range(TRIO)]
        if masked:
            scores = [jnp.where(live, score, NEG_BIG) for score in scores]
        old = top[0:TRIO]
        new = jnp.concatenate([jnp.max(score, 0, keepdims=True) for score in scores], 0)
        new = jnp.maximum(old, new)
        factor = jnp.exp(old - new)
        weights = [jnp.exp(scores[h] - new[h : h + 1]) for h in range(TRIO)]
        if masked:
            weights = [jnp.where(live, weight, 0.0) for weight in weights]
        sums = [jnp.sum(weight, 0, keepdims=True) for weight in weights]
        top[0:TRIO] = new
        total[0:TRIO] = total[0:TRIO] * factor + jnp.concatenate(sums, 0)
        for h in range(TRIO):
            vth = vt[unit, h * HEAD_DIM : (h + 1) * HEAD_DIM]
            acc[h] = acc[h] * factor[h : h + 1] + mm(vth, weights[h].astype(BF))

    unit_loop(meta, part, units, rows, step)
    out = [acc[h] / total[h : h + 1] for h in range(TRIO)]
    for h in range(TRIO):
        ot_ref[0, h * HEAD_DIM : (h + 1) * HEAD_DIM] = out[h]
    lse_ref[0, 0:TRIO] = top[0:TRIO] + jnp.log(total[0:TRIO])
    o_ref[0, :, :TILE] = jnp.concatenate(out[:2], 0).T.astype(BF)
    o_ref[0, :, TILE:] = jnp.concatenate([out[2], jnp.zeros_like(out[2])], 0).T.astype(BF)


def backward_kernel(part, units, meta, q_ref, do_ref, ot_ref, lse_ref, *refs):
    seg_ref, own_ref, oth_ref, kv_ref, qb, db, qn, dn, kt, delta, dqt = refs[part : part + 11]
    dk01, dv01, dk2, dv2 = refs[part + 11 :]
    rows = q_ref.shape[1]
    c = meta[2 * units]
    j = pl.program_id(0)

    @pl.when(j == 0)
    def _():
        join_parts(part, refs[:part], kv_ref)

        def turn_keys(unit, unused):
            kt[unit, :TILE] = flip(kv_ref[unit, :, 0:TILE]).astype(BF)
            kt[unit, TILE:] = flip(kv_ref[unit, :, 2 * TILE : 3 * TILE])[HEAD_DIM:].astype(BF)
            return unused

        lax.fori_loop(0, units, turn_keys, 0)
        for ref in (dk01, dv01, dk2, dv2):
            ref[...] = jnp.zeros(ref.shape, F32)

    query_sides(q_ref, qb)
    scale = HEAD_DIM ** (-0.5)
    q01 = q_ref[0, :, 0:TILE].astype(F32) * scale
    q2 = pltpu.roll(q_ref[0, :, 3 * TILE : 4 * TILE].astype(F32), HEAD_DIM, 1) * scale
    qn[0:rows] = head_lanes(q01, True).astype(BF)
    qn[rows : 2 * rows] = head_lanes(q01, False).astype(BF)
    qn[2 * rows :] = head_lanes(q2, False).astype(BF)
    do01 = do_ref[0, :, :TILE].astype(F32)
    do2 = do_ref[0, :, TILE:].astype(F32)
    dn[0:rows] = head_lanes(do01, True).astype(BF)
    dn[rows : 2 * rows] = head_lanes(do01, False).astype(BF)
    dn[2 * rows :] = do2.astype(BF)
    do01t = do01.T
    do2t = do2.T
    db[0] = head_rows(do01t, True).astype(BF)
    db[1] = head_rows(do01t, False).astype(BF)
    db[2] = do2t.astype(BF)
    for h in range(TRIO):
        dot = do2t[:HEAD_DIM] if h == 2 else do01t[h * HEAD_DIM : (h + 1) * HEAD_DIM]
        delta[h : h + 1] = jnp.sum(
            dot * ot_ref[0, h * HEAD_DIM : (h + 1) * HEAD_DIM], 0, keepdims=True
        )
    dqt[...] = jnp.zeros(dqt.shape, F32)
    seg_row = seg_ref[0]
    query_start = (j * part + c) * rows

    def step(unit, masked):
        k01 = kv_ref[unit, :, 0:TILE]
        v01 = kv_ref[unit, :, TILE : 2 * TILE]
        k2 = kv_ref[unit, :, 2 * TILE : 3 * TILE]
        v2 = kv_ref[unit, :, 3 * TILE :]
        if masked:
            live = live_of(seg_row, unit, query_start, part, rows, c)
        scores = [mm(k2 if h == 2 else k01, qb[h]) for h in range(TRIO)]
        dprobs = [mm(v2 if h == 2 else v01, db[h]) for h in range(TRIO)]
        probs = []
        grads = []
        for h in range(TRIO):
            score = scores[h]
            if masked:
                score = jnp.where(live, score, NEG_BIG)
            prob = jnp.exp(score - lse_ref[0, h : h + 1])
            if masked:
                prob = jnp.where(live, prob, 0.0)
            probs.append(prob.astype(BF))
            grads.append((prob * (dprobs[h] - delta[h : h + 1])).astype(BF))
        dv01[unit] += mm(jnp.concatenate(probs[:2], 1), dn[: 2 * rows])
        dk01[unit] += mm(jnp.concatenate(grads[:2], 1), qn[: 2 * rows])
        dv2[unit] += mm(probs[2], dn[2 * rows :])
        dk2[unit] += mm(grads[2], qn[2 * rows :])
        for h in range(TRIO):
            kth = kt[unit, h * HEAD_DIM : (h + 1) * HEAD_DIM]
            dqt[h * HEAD_DIM : (h + 1) * HEAD_DIM] += mm(kth, grads[h])

    unit_loop(meta, part, units, rows, step)
    own_ref[j, :, 0:TILE] = (dqt[:TILE] * scale).T.astype(BF)
    dq2 = dqt[TILE:] * scale
    dk2[j, 0:rows] += jnp.concatenate([dq2, jnp.zeros_like(dq2)], 0).T

    @pl.when(j == units - 1)
    def _():
        for unit in range(units):
            for i in range(part):
                span = slice(i * rows, (i + 1) * rows)
                for t, ref in enumerate((dk01, dv01, dk2, dv2)):
                    tile = ref[unit, span].astype(BF)
                    if i == 0:
                        own_ref[unit, :, (t + 1) * TILE : (t + 2) * TILE] = tile
                    else:
                        oth_ref[i - 1, unit, :, t * TILE : (t + 1) * TILE] = tile


def attention_cost(products, units, rows, part):
    pairs = TRIO * rows * rows * units * units * part // 2
    return pl.CostEstimate(
        flops=2 * 64 * products * pairs, bytes_accessed=20_000_000, transcendentals=pairs
    )


def whole_spec(shape):
    zeros = (0,) * len(shape)
    return pl.BlockSpec(shape, lambda j, meta: zeros)


def attend_forward(meta, packed, kv, seg):
    units, rows, unused = packed.shape
    part = len(kv)
    return pl.pallas_call(
        functools.partial(forward_kernel, part, units),
        grid_spec=pltpu.PrefetchScalarGridSpec(
            num_scalar_prefetch=1,
            grid=(units,),
            in_specs=[
                pl.BlockSpec((1, rows, PACK), lambda j, meta: (j, 0, 0)),
                *[whole_spec(piece.shape) for piece in kv],
                pl.BlockSpec((1, 1, rows), lambda j, meta: (j, 0, 0)),
            ],
            out_specs=[
                pl.BlockSpec((1, rows, OPACK), lambda j, meta: (j, 0, 0)),
                pl.BlockSpec((1, TRIO * HEAD_DIM, rows), lambda j, meta: (j, 0, 0)),
                pl.BlockSpec((1, 8, rows), lambda j, meta: (j, 0, 0)),
            ],
            scratch_shapes=[
                pltpu.VMEM((units, part * rows, PACK - TILE), BF),
                pltpu.VMEM((TRIO, TILE, rows), BF),
                pltpu.VMEM((units, TRIO * HEAD_DIM, part * rows), BF),
                pltpu.VMEM((8, rows), F32),
                pltpu.VMEM((8, rows), F32),
                pltpu.VMEM((TRIO, HEAD_DIM, rows), F32),
            ],
        ),
        out_shape=[
            jax.ShapeDtypeStruct((units, rows, OPACK), BF),
            jax.ShapeDtypeStruct((units, TRIO * HEAD_DIM, rows), F32),
            jax.ShapeDtypeStruct((units, 8, rows), F32),
        ],
        compiler_params=params_of("arbitrary"),
        cost_estimate=attention_cost(8, units, rows, part),
        name="attend_forward",
    )(meta, packed, *kv, seg)


def attend_backward(meta, packed, dout, out_t, lse, kv, seg):
    units, rows, unused = packed.shape
    part = len(kv)
    others = (max(part - 1, 1), units, rows, 4 * TILE)
    grads = pltpu.VMEM((units, part * rows, TILE), F32)
    return pl.pallas_call(
        functools.partial(backward_kernel, part, units),
        grid_spec=pltpu.PrefetchScalarGridSpec(
            num_scalar_prefetch=1,
            grid=(units,),
            in_specs=[
                pl.BlockSpec((1, rows, PACK), lambda j, meta: (j, 0, 0)),
                pl.BlockSpec((1, rows, OPACK), lambda j, meta: (j, 0, 0)),
                pl.BlockSpec((1, TRIO * HEAD_DIM, rows), lambda j, meta: (j, 0, 0)),
                pl.BlockSpec((1, 8, rows), lambda j, meta: (j, 0, 0)),
                *[whole_spec(piece.shape) for piece in kv],
                pl.BlockSpec((1, 1, rows), lambda j, meta: (j, 0, 0)),
            ],
            out_specs=[whole_spec(packed.shape), whole_spec(others)],
            scratch_shapes=[
                pltpu.VMEM((units, part * rows, PACK - TILE), BF),
                pltpu.VMEM((TRIO, TILE, rows), BF),
                pltpu.VMEM((TRIO, TILE, rows), BF),
                pltpu.VMEM((TRIO * rows, TILE), BF),
                pltpu.VMEM((TRIO * rows, TILE), BF),
                pltpu.VMEM((units, TRIO * HEAD_DIM, part * rows), BF),
                pltpu.VMEM((8, rows), F32),
                pltpu.VMEM((TRIO * HEAD_DIM, rows), F32),
                grads,
                grads,
                grads,
                grads,
            ],
        ),
        out_shape=[
            jax.ShapeDtypeStruct(packed.shape, BF),
            jax.ShapeDtypeStruct(others, BF),
        ],
        compiler_params=params_of("arbitrary"),
        cost_estimate=attention_cost(20, units, rows, part),
        name="attend_backward",
    )(meta, packed, dout, out_t, lse, *kv, seg)


def pack_kernel(trios, groups, w_ref, vec_ref, early_ref, local_ref):
    d = w_ref.shape[1] // 3
    w = w_ref[...].astype(F32)
    width = TRIO * HEAD_DIM
    zeros = jnp.zeros((w.shape[0], HEAD_DIM), F32)
    for g in range(trios):
        q, k, v = (w[:, i * d + g * width : i * d + (g + 1) * width] for i in range(3))
        tiles = [q[:, :TILE], k[:, :TILE], v[:, :TILE]]
        tiles.append(jnp.concatenate([q[:, TILE:], k[:, TILE:]], 1))
        tiles.append(jnp.concatenate([v[:, TILE:], zeros], 1))
        for t, tile in enumerate(tiles):
            tile = tile.astype(BF)
            local_ref[:, g * PACK + t * TILE : g * PACK + (t + 1) * TILE] = tile
            for s in range(groups):
                early_ref[s * trios + g, :, t * TILE : (t + 1) * TILE] = tile
        for s in range(groups):
            early_ref[s * trios + g, :, PACK:] = vec_ref[s]


def pack_early(weight, vec, trios):
    r = weight.shape[0]
    groups = vec.shape[0]
    return pl.pallas_call(
        functools.partial(pack_kernel, trios, groups),
        out_shape=[
            jax.ShapeDtypeStruct((trios * groups, r, PACK + TILE), BF),
            jax.ShapeDtypeStruct((r, trios * PACK), BF),
        ],
        name="pack_early",
    )(weight, vec)


def feed_kernel(
    x_ref, cot_ref, up_ref, down_ref, shift_ref, hid_ref, pre_ref, sum_ref, second_ref, back_ref
):
    pre = mm(x_ref[...], up_ref[...]) + shift_ref[...]
    grad = inner_back(cot_ref[...], down_ref[...])
    cdf = 0.5 * (1.0 + lax.erf(pre * math.sqrt(0.5)))
    hidden = (pre * cdf).astype(BF)
    slope = cdf + pre * (jnp.exp(-0.5 * pre * pre) * (1.0 / math.sqrt(2.0 * math.pi)))
    pre_grad = (grad * slope).astype(BF)
    hid_ref[...] = hidden
    pre_ref[...] = pre_grad
    sum_ref[...] = jnp.sum(pre_grad.astype(F32), 0, keepdims=True)
    second = mm(hidden, down_ref[...])
    back = inner_back(pre_grad, up_ref[...])

    @pl.when(pl.program_id(0) == 0)
    def _():
        second_ref[...] = second
        back_ref[...] = back

    @pl.when(pl.program_id(0) > 0)
    def _():
        second_ref[...] += second
        back_ref[...] += back


def feed_forward(x, cot, weights, shift, blocks):
    rows, d = x.shape
    ff = blocks * d
    half = d // 2
    wide = pl.BlockSpec((rows, d), lambda i: (0, 0))
    column = pl.BlockSpec((rows, half), lambda i: (0, i))
    line = pl.BlockSpec((1, half), lambda i: (0, i))
    return pl.pallas_call(
        feed_kernel,
        grid=(2 * blocks,),
        in_specs=[
            wide,
            wide,
            pl.BlockSpec((d, half), lambda i: (0, i)),
            pl.BlockSpec((half, d), lambda i: (i % 2, blocks + i // 2)),
            line,
        ],
        out_specs=[column, column, line, wide, wide],
        out_shape=[
            jax.ShapeDtypeStruct((rows, ff), BF),
            jax.ShapeDtypeStruct((rows, ff), BF),
            jax.ShapeDtypeStruct((1, ff), F32),
            jax.ShapeDtypeStruct((rows, d), F32),
            jax.ShapeDtypeStruct((rows, d), F32),
        ],
        compiler_params=params_of("arbitrary"),
        cost_estimate=pl.CostEstimate(
            flops=8 * rows * d * ff, bytes_accessed=4 * d * ff, transcendentals=2 * rows * ff
        ),
        name="feed_forward",
    )(x, cot, weights, weights, shift)


def gradient_kernel(ups, norm_ref, pre_ref, hidden_ref, cot_ref, out_ref):
    i = pl.program_id(0)

    @pl.when(i < ups)
    def _():
        out_ref[...] = outer_sum(norm_ref[...], pre_ref[...]).astype(BF)

    @pl.when(i >= ups)
    def _():
        out_ref[...] = outer_sum(hidden_ref[...], cot_ref[...]).astype(BF)


def gradients(normed, pre_grad, hidden, cot):
    rows, d = normed.shape
    width = d // 2
    ups = hidden.shape[1] // width

    def down(i):
        return jnp.clip(i - ups, 0, ups - 1)

    return pl.pallas_call(
        functools.partial(gradient_kernel, ups),
        grid=(2 * ups,),
        in_specs=[
            pl.BlockSpec((rows, d), lambda i: (0, 0)),
            pl.BlockSpec((rows, width), lambda i: (0, jnp.minimum(i, ups - 1))),
            pl.BlockSpec((rows, d), lambda i: (0, down(i) // 2)),
            pl.BlockSpec((rows, width), lambda i: (0, down(i) % 2)),
        ],
        out_specs=pl.BlockSpec((d, width), lambda i: (0, i)),
        out_shape=jax.ShapeDtypeStruct((d, 2 * ups * width), BF),
        compiler_params=params_of("arbitrary"),
        cost_estimate=pl.CostEstimate(
            flops=4 * rows * d * ups * width, bytes_accessed=0, transcendentals=0
        ),
        name="gradients",
    )(normed, pre_grad, hidden, cot)


def trio_kernel(norm_ref, hat_ref, grad_ref, w_ref, vec_ref, late_ref, shift_ref, own, hat):
    j = pl.program_id(0)
    d = norm_ref.shape[2]
    grad = grad_ref[...].reshape(-1, PACK)
    own_part = outer_sum(norm_ref[...].reshape(-1, d), grad)
    hat_part = outer_sum(hat_ref[...].reshape(-1, d), grad)
    sums = jnp.sum(grad.astype(F32), 0, keepdims=True)

    @pl.when(j == 0)
    def _():
        own[...] = own_part
        hat[...] = hat_part
        shift_ref[...] = sums

    @pl.when(j > 0)
    def _():
        own[...] += own_part
        hat[...] += hat_part
        shift_ref[...] += sums

    @pl.when(j == pl.num_programs(0) - 1)
    def _():
        late_ref[:, :PACK] = own[...].astype(BF)
        weight = w_ref[...].astype(F32)
        lane = lane_of(vec_ref.shape)
        vec = vec_ref[...]
        vec = jnp.where(lane == 0, jnp.sum(weight * hat[...], 1, keepdims=True), vec)
        vec = jnp.where(lane == 1, jnp.sum(weight * shift_ref[...], 1, keepdims=True), vec)
        late_ref[:, PACK:] = vec.astype(BF)


def trio_gradient(normed, hat, grad, weight, vec):
    units, rows, d = normed.shape
    tok_spec = pl.BlockSpec((2, rows, d), lambda j: (j, 0, 0))
    return pl.pallas_call(
        trio_kernel,
        grid=(units // 2,),
        in_specs=[
            tok_spec,
            tok_spec,
            pl.BlockSpec((2, rows, PACK), lambda j: (j, 0, 0)),
            pl.BlockSpec((d, PACK), lambda j: (0, 0)),
            pl.BlockSpec((d, TILE), lambda j: (0, 0)),
        ],
        out_specs=[
            pl.BlockSpec((d, PACK + TILE), lambda j: (0, 0)),
            pl.BlockSpec((1, PACK), lambda j: (0, 0)),
        ],
        scratch_shapes=[pltpu.VMEM((d, PACK), F32), pltpu.VMEM((d, PACK), F32)],
        out_shape=[
            jax.ShapeDtypeStruct((d, PACK + TILE), BF),
            jax.ShapeDtypeStruct((1, PACK), F32),
        ],
        compiler_params=params_of("arbitrary"),
        cost_estimate=pl.CostEstimate(flops=0, bytes_accessed=0, transcendentals=0),
        name="trio_gradient",
    )(normed, hat, grad, weight, vec)


def pack_columns(matrix, trios):
    r = matrix.shape[0]
    q, k, v = (
        part.reshape(r, trios, TRIO * HEAD_DIM) for part in jnp.split(matrix, 3, axis=1)
    )
    zeros = jnp.zeros((r, trios, HEAD_DIM), matrix.dtype)
    pieces = [q[..., :TILE], k[..., :TILE], v[..., :TILE], q[..., TILE:], k[..., TILE:]]
    return jnp.concatenate(pieces + [v[..., TILE:], zeros], -1).reshape(r, trios * PACK)


def unpack_columns(matrix, trios):
    r = matrix.shape[0]
    m = matrix.reshape(r, trios, PACK)
    halves = [
        m[..., 3 * TILE : 3 * TILE + HEAD_DIM],
        m[..., 3 * TILE + HEAD_DIM : 4 * TILE],
        m[..., 4 * TILE : 4 * TILE + HEAD_DIM],
    ]
    return jnp.concatenate(
        [
            jnp.concatenate([m[..., i * TILE : (i + 1) * TILE], halves[i]], -1).reshape(r, -1)
            for i in range(3)
        ],
        -1,
    )


def split_hidden(matrix, count, r):
    lead = matrix.shape[0]
    return matrix.reshape(lead, count, -1, r).transpose(0, 2, 1, 3).reshape(lead, -1)


def join_hidden(matrix, count, r):
    lead = matrix.shape[0]
    return matrix.reshape(lead, -1, count, r).transpose(0, 2, 1, 3).reshape(lead, -1)


def on_device(
    tokens,
    segment,
    ln1_gain,
    ln1_bias,
    ln2_gain,
    ln2_bias,
    qkv_weight,
    qkv_bias,
    dense_weight,
    dense_bias,
    fc1_weight,
    fc1_bias,
    output_feed_weight,
    output_feed_bias,
    cotangent,
):
    rows, groups, d = tokens.shape
    units = lax.axis_size("unit")
    part = lax.axis_size("part")
    count = units * part * lax.axis_size("seq")
    trios = units // groups
    all_rows = rows * groups
    r = qkv_weight.shape[0]
    ff = fc1_weight.shape[1]
    blocks = ff // d
    c = lax.axis_index("part")
    unit = lax.axis_index("unit")

    seq = lax.axis_index("seq")
    seqs = lax.axis_size("seq")
    place = (seq * units + unit) * part + c

    def exchange(blocks_out):
        width = blocks_out.shape[-1]
        return lax.all_to_all(
            blocks_out.reshape(-1, width), "unit", 0, 0, tiled=True
        ).reshape(blocks_out.shape)

    def shift(value, axis, i):
        n = lax.axis_size(axis)
        return lax.ppermute(value, axis, [(p, (p + i) % n) for p in range(n)])

    def flip_unit(value, bit):
        return lax.ppermute(value, "unit", [(u, u ^ bit) for u in range(units)])

    def pick(value, index, axis):
        return lax.dynamic_index_in_dim(value, index, axis, False)

    bits = (unit // trios, unit // 2 % 2, unit % 2)

    def exchange_small(value):
        shape = value.shape
        value = value.reshape((2, 2, 2) + shape[1:])
        for axis, bit in enumerate((trios, 2, 1)):
            keep = pick(value, bits[axis], axis)
            value = jnp.stack([keep, flip_unit(pick(value, 1 - bits[axis], axis), bit)], axis)
        for axis in range(3):
            value = jnp.where(bits[axis] == 0, value, jnp.flip(value, axis))
        return value.reshape(shape)

    def spread_tokens(value):
        keep = pick(value, bits[0], 0)
        both = jnp.stack([keep, flip_unit(pick(value, 1 - bits[0], 0), trios)])
        one, two = both[:, : rows // 2], both[:, rows // 2 :]
        one = jnp.stack([one, flip_unit(one, 2)])
        two = jnp.stack([two, flip_unit(two, 1)])
        one = jnp.stack([one, flip_unit(one, 1)])
        two = jnp.stack([two, flip_unit(two, 2)])
        return one.reshape(units, rows // 2, d), two.reshape(units, rows // 2, d)

    def add(a, b):
        return (a.astype(F32) + b.astype(F32)).astype(BF)

    def collect_tokens(one, two):
        one = one.reshape(2, 2, 2, rows // 2, d)
        two = two.reshape(2, 2, 2, rows // 2, d)
        one = add(one[0], flip_unit(one[1], 1))
        two = add(two[0], flip_unit(two[1], 2))
        one = add(one[0], flip_unit(one[1], 2))
        two = add(two[0], flip_unit(two[1], 1))
        both = jnp.concatenate([one, two], 1)
        other = flip_unit(both[1], trios)
        return jnp.where(
            bits[0] == 0, jnp.stack([both[0], other]), jnp.stack([other, both[0]])
        )

    def natural_order(got, me):
        n = len(got)
        if n == 2:
            return jnp.where(me == 0, jnp.stack(got), jnp.stack(got[::-1]))
        ring = jnp.stack((got + got)[::-1])
        return lax.dynamic_slice_in_dim(ring, n - 1 - me, n, 0)

    def gather_small(value, axis):
        n = lax.axis_size(axis)
        got = [value] + [shift(value, axis, i) for i in range(1, n)]
        return natural_order(got, lax.axis_index(axis))

    def swap_parts(value):
        got = [lax.dynamic_index_in_dim(value, c, 0, False)]
        for i in range(1, part):
            piece = lax.dynamic_index_in_dim(value, (c + i) % part, 0, False)
            got.append(shift(piece, "part", i))
        return natural_order(got, c)

    def all_parts(value):
        return jnp.concatenate([value] + [shift(value, "part", i) for i in range(1, part)], 0)

    def sum_parts(value):
        n = value.shape[0] // part
        total = value[:n]
        for i in range(1, part):
            total = total + shift(value[i * n : (i + 1) * n], "part", part - i)
        return total

    def scatter_small(value, axis):
        n = lax.axis_size(axis)
        me = lax.axis_index(axis)
        total = lax.dynamic_index_in_dim(value, me, 0, False).astype(F32)
        for i in range(1, n):
            piece = lax.dynamic_index_in_dim(value, (me + i) % n, 0, False)
            total = total + shift(piece, axis, i).astype(F32)
        return total.astype(BF)

    vectors = (ln1_gain, ln1_bias, ln2_gain, ln2_bias, dense_bias, output_feed_bias)
    vec = jnp.concatenate(
        [v.reshape(r, 1) for v in vectors] + [qkv_bias.reshape(r, 3), fc1_bias.reshape(r, blocks)],
        1,
    )
    token_rows = tokens.transpose(1, 0, 2)
    seg_rows = segment.T
    seg_lanes = -(-2 * rows // r)
    seg_pack = jnp.concatenate([seg_rows // 64, seg_rows % 64], 1).astype(BF)
    seg_pack = jnp.pad(seg_pack, ((0, 0), (0, seg_lanes * r - 2 * rows)))
    seg_pack = seg_pack.reshape(groups, r, seg_lanes)
    vec = jnp.pad(vec, ((0, 0), (0, 16 - vec.shape[1])))
    vec = jnp.concatenate(
        [
            jnp.broadcast_to(vec, (groups, r, 16)),
            seg_pack,
            jnp.zeros((groups, r, TILE - 16 - seg_lanes), BF),
        ],
        -1,
    )
    early, qkv_local = pack_early(qkv_weight, vec, trios)
    early = exchange_small(early)
    toks = spread_tokens(token_rows)

    seg_mine = early[:, :, PACK + 16 : PACK + 16 + seg_lanes].astype(jnp.int32)
    seg_mine = seg_mine.reshape(units, r * seg_lanes)
    seg_mine = seg_mine[:, :rows] * 64 + seg_mine[:, rows : 2 * rows]
    meta = jnp.concatenate([seg_mine[:, 0], seg_mine[:, -1], c[None]])
    seg_mine = seg_mine[:, None, :]
    trio_full = gather_small(gather_small(early, "seq"), "part")
    trio_full = trio_full.transpose(1, 2, 0, 3, 4).reshape(d, PACK + TILE)
    vec_full = trio_full[:, PACK:].astype(F32)
    vec_rows = vec_full[:, :8].T
    gain_one, bias_one, gain_two, bias_two, dense_shift, down_shift = (
        vec_rows[i : i + 1] for i in range(6)
    )
    qkv_shift = pack_columns(vec_full[:, 6:9].reshape(1, 3 * d), trios).reshape(trios, PACK)
    qkv_shift = lax.dynamic_slice_in_dim(qkv_shift, unit % trios, 1, 0)
    up_shift = split_hidden(vec_full[:, 9 : 9 + blocks].reshape(1, ff), count, r)

    feed_blocks = output_feed_weight.reshape(blocks, r, d)
    half = blocks // part
    dense_cols = d // part
    up_local = split_hidden(fc1_weight, count, r)
    second_pack = jnp.stack(
        [
            jnp.concatenate(
                [up_local[:, p * half * d : (p + 1) * half * d]]
                + [feed_blocks[b] for b in range(p * half, (p + 1) * half)]
                + [dense_weight[:, p * dense_cols : (p + 1) * dense_cols]],
                1,
            )
            for p in range(part)
        ]
    )
    second_pack = swap_parts(second_pack).reshape(part * r, -1)
    second = lax.all_gather(second_pack, ("seq", "unit"), axis=0, tiled=True)
    dense_full = gather_small(second[:, 2 * half * d :], "part").transpose(1, 0, 2)
    dense_pad = jnp.pad(
        dense_full.reshape(trios, d // trios, d), ((0, 0), (0, OPACK - d // trios), (0, 0))
    )

    block_start = (jnp.arange(units, dtype=jnp.int32) * part + c) * rows
    positions = block_start[:, None, None] + jnp.arange(rows, dtype=jnp.int32) - seg_mine
    freq = jnp.arange(ROT // 2, dtype=F32)
    inverse = jnp.exp(freq * (-2.0 * math.log(10000.0) / ROT))
    angles = positions.astype(F32) * inverse[None, :, None]
    cos = jnp.cos(angles)
    sin = jnp.sin(angles)

    place_unit = unit[None]
    packed, kv_own, normed_one, hat_one = project(
        place_unit, toks, trio_full, qkv_shift, gain_one, bias_one, cos, sin
    )
    kv = [kv_own] + [shift(kv_own, "part", i) for i in range(1, part)]

    x = token_rows.reshape(all_rows, d).astype(F32)
    cot = cotangent.transpose(1, 0, 2).reshape(all_rows, d)
    cot_float = cot.astype(F32)
    centre = x - jnp.mean(x, -1, keepdims=True)
    spread = lax.rsqrt(jnp.mean(centre * centre, -1, keepdims=True) + EPSILON)
    xhat = centre * spread
    normed_two = (xhat * gain_two + bias_two).astype(BF)
    attended_grad = jnp.einsum(
        "sld,gkd->sglk", cot.reshape(groups, rows, d), dense_pad, preferred_element_type=F32
    ).astype(BF)
    dout = exchange(attended_grad.reshape(units, rows, OPACK))
    out_low, out_t, lse = attend_forward(meta, packed, kv, seg_mine)
    normed_two, out_low = lax.optimization_barrier((normed_two, out_low))
    attended = exchange(out_low)

    normed_all = all_parts(normed_two)
    cot_all = all_parts(cot)
    up_shift = lax.dynamic_slice_in_dim(up_shift, c * half * d, half * d, 1)
    hidden_low, pre_grad, up_shift_grad, second_branch, normed_two_grad = feed_forward(
        normed_all, cot_all, second, up_shift, half
    )
    hidden_low, pre_grad, dout = lax.optimization_barrier((hidden_low, pre_grad, dout))
    second_branch = sum_parts(second_branch)
    normed_two_grad = sum_parts(normed_two_grad)
    up_shift_grad = lax.dynamic_update_slice_in_dim(
        jnp.zeros((1, ff), F32), up_shift_grad, c * half * d, 1
    )

    def norm_back(grad, gain):
        gy = grad * gain
        return spread * (
            gy - jnp.mean(gy, -1, keepdims=True) - xhat * jnp.mean(gy * xhat, -1, keepdims=True)
        )

    mlp_grads = gradients(normed_all, pre_grad, hidden_low, cot_all)
    mlp_grads, dout = lax.optimization_barrier((mlp_grads, dout))
    mlp_sum = lax.psum_scatter(mlp_grads, ("seq", "unit"), scatter_dimension=0, tiled=True)

    own, others = attend_backward(meta, packed, dout, out_t, lse, kv, seg_mine)
    others = [shift(others[i - 1], "part", part - i) for i in range(1, part)]
    own, attended = lax.optimization_barrier((own, attended))
    qkv_grad, back_one, back_two = unturn(place_unit, own, others, trio_full, cos, sin)
    back = collect_tokens(back_one, back_two)

    attended, second_branch, normed_two_grad, qkv_grad = lax.optimization_barrier(
        (attended, second_branch, normed_two_grad, qkv_grad)
    )
    attended = attended.reshape(groups, trios, rows, OPACK).transpose(0, 2, 1, 3)
    attended = attended.reshape(all_rows, trios * OPACK)
    dense_grad = outer_sum(attended, cot).reshape(trios, OPACK, d)[:, : d // trios].reshape(d, d)
    branch_one = mm(attended, dense_pad.reshape(trios * OPACK, d)) + dense_shift
    output = (x + branch_one + second_branch + down_shift).astype(BF)
    in_two = norm_back(normed_two_grad, gain_two)
    vec_grads = jnp.concatenate(
        [
            jnp.zeros((2, d), F32),
            jnp.sum(normed_two_grad * xhat, 0)[None],
            jnp.sum(normed_two_grad, 0)[None],
            jnp.sum(cot_float, 0)[None],
            jnp.zeros((3, d), F32),
        ],
        0,
    ).T
    up_shift_grad = join_hidden(up_shift_grad, count, r).reshape(d, blocks)

    vec_grads = jnp.concatenate(
        [vec_grads, up_shift_grad, jnp.zeros((d, TILE - 8 - blocks), F32)], 1
    )
    late, shift_grad = trio_gradient(normed_one, hat_one, qkv_grad, trio_full, vec_grads)
    late = jnp.concatenate([late, dense_grad.astype(BF)], 1)
    late = late.reshape(seqs, units, part, r, -1)
    width = late.shape[-1]
    shift_rows = jnp.pad(shift_grad.astype(BF), ((0, 7), (0, width - PACK)))
    late = jnp.concatenate(
        [late, jnp.broadcast_to(shift_rows, (seqs, units, part) + shift_rows.shape)], 3
    )
    late = scatter_small(late.transpose(2, 0, 1, 3, 4), "part")
    late = exchange_small(scatter_small(late, "seq")).astype(F32)
    late = jnp.sum(late.reshape(groups, trios, r + 8, width), 0)
    qkv_weight_grad = unpack_columns(
        late[:, :r, :PACK].transpose(1, 0, 2).reshape(r, trios * PACK), trios
    )
    late_rest = jnp.sum(late[:, :r, PACK:], 0)
    late_vec = late_rest[:, :TILE]
    dense_sum = late_rest[:, TILE:]
    qkv_shift_grad = unpack_columns(late[:, r, :PACK].reshape(1, trios * PACK), trios)[0]
    qkv_shift_grad = lax.dynamic_slice_in_dim(qkv_shift_grad, place * 3 * r, 3 * r)

    mlp_sum = swap_parts(mlp_sum.reshape(part, r, -1)).astype(F32)
    up_sum = jnp.concatenate([mlp_sum[p, :, : half * d] for p in range(part)], 1)
    down_sum = jnp.concatenate(
        [
            mlp_sum[p, :, (half + b) * d : (half + b + 1) * d]
            for p in range(part)
            for b in range(half)
        ],
        0,
    )
    param_grads = (
        late_vec[:, 0],
        late_vec[:, 1],
        late_vec[:, 2],
        late_vec[:, 3],
        qkv_weight_grad,
        qkv_shift_grad,
        dense_sum,
        late_vec[:, 4],
        join_hidden(up_sum, count, r),
        late_vec[:, 8 : 8 + blocks].reshape(-1),
        down_sum,
        late_vec[:, 4],
    )

    normed_one_grad = back.reshape(all_rows, d).astype(F32)
    in_one = norm_back(normed_one_grad, gain_one)
    tokens_grad = (cot_float + in_one + in_two).astype(BF)

    def natural(value):
        return value.reshape(groups, rows, d).transpose(1, 0, 2)

    return (natural(output), natural(tokens_grad)) + tuple(param_grads)


def solution(mesh):
    devices = mesh.devices
    seq_size, ctx_size = devices.shape
    ctx = ("unit", "part")
    tok = P(ctx, "seq", None)
    vec = P(ALL_AXES)
    mat = P(ALL_AXES, None)
    pairs = (vec, vec, vec, vec, mat, vec, mat, vec, mat, vec, mat, vec)

    def run(tokens, *rest):
        units = HEADS // TRIO * (tokens.shape[1] // seq_size)
        split = Mesh(devices.reshape(seq_size, units, ctx_size // units), ALL_AXES)
        mapped = jax.shard_map(
            on_device,
            mesh=split,
            in_specs=(tok, P(ctx, "seq")) + pairs + (tok,),
            out_specs=(tok, tok) + pairs,
            check_vma=False,
        )
        return mapped(tokens, *rest)

    return run
```

```python
import functools
import math

import jax
import jax.numpy as jnp
from jax import lax
from jax.experimental import pallas as pl
from jax.experimental.pallas import tpu as pltpu
from jax.sharding import Mesh, PartitionSpec as P

HEADS = 12
HEAD_DIM = 64
ROT = 16
TRIO = 3
TILE = 128
PACK = 5 * TILE
OPACK = 2 * TILE

EPSILON = 1e-05
NEG_BIG = -1e30
BF = jnp.bfloat16
F32 = jnp.float32
ALL_AXES = ("seq", "unit", "part")
VMEM_BYTES = 56 * 1024 * 1024


def params_of(*semantics):
    return pltpu.CompilerParams(
        dimension_semantics=semantics, vmem_limit_bytes=VMEM_BYTES
    )


def mm(a, b):
    return jnp.dot(a, b, preferred_element_type=F32)


def outer_sum(left_rows, right_rows):
    return lax.dot_general(
        left_rows, right_rows, (((0,), (0,)), ((), ())), preferred_element_type=F32
    )


def inner_back(grad_rows, weight):
    return lax.dot_general(
        grad_rows, weight, (((1,), (1,)), ((), ())), preferred_element_type=F32
    )


def lane_of(shape):
    return lax.broadcasted_iota(jnp.int32, shape, len(shape) - 1)


def turn(tile, cos, sin):
    partner = jnp.where(
        lane_of(tile.shape) % HEAD_DIM < ROT // 2,
        pltpu.roll(tile, TILE - ROT // 2, 1),
        pltpu.roll(tile, ROT // 2, 1),
    )
    return tile * cos + partner * sin


def turn_tables(cos_rows, sin_rows):
    rows = cos_rows.shape[1]
    rest = HEAD_DIM - ROT
    cos_head = [cos_rows, cos_rows, jnp.ones((rest, rows), F32)]
    sin_head = [-sin_rows, sin_rows, jnp.zeros((rest, rows), F32)]
    return jnp.concatenate(cos_head * 2, 0).T, jnp.concatenate(sin_head * 2, 0).T


def first_place(rel):
    return rel % 2 * 4 + rel // 2 % 2 * 2 + rel // 4


def second_place(rel):
    return rel // 2 % 2 * 4 + rel % 2 * 2 + rel // 4


def project_kernel(
    place_ref,
    one_ref,
    two_ref,
    w_ref,
    b_ref,
    gain_ref,
    bias_ref,
    cos_ref,
    sin_ref,
    out_ref,
    kv_ref,
    norm_ref,
    hat_ref,
):
    x = jnp.concatenate([one_ref[0], two_ref[0]], 0).astype(F32)
    centre = x - jnp.mean(x, -1, keepdims=True)
    spread = jnp.mean(centre * centre, -1, keepdims=True)
    hat = centre * lax.rsqrt(spread + EPSILON)
    normed = (hat * gain_ref[...] + bias_ref[...]).astype(BF)
    hat_ref[0] = hat.astype(BF)
    norm_ref[0] = normed
    y = mm(normed, w_ref[...]) + b_ref[...]
    cos, sin = turn_tables(cos_ref[0], sin_ref[0])
    for t in range(5):
        tile = y[:, t * TILE : (t + 1) * TILE]
        if t in (0, 1, 3):
            tile = turn(tile, cos, sin)
        tile = tile.astype(BF)
        out_ref[0, :, t * TILE : (t + 1) * TILE] = tile
        if t > 0:
            kv_ref[0, :, (t - 1) * TILE : t * TILE] = tile


def half_specs(rows, d):
    return [
        pl.BlockSpec((1, rows // 2, d), lambda j, place: (first_place(j ^ place[0]), 0, 0)),
        pl.BlockSpec((1, rows // 2, d), lambda j, place: (second_place(j ^ place[0]), 0, 0)),
    ]


def project(place, toks, weight, bias, gain, offset, cos, sin):
    units, unused, rows = cos.shape
    d = toks[0].shape[2]
    tok_spec = pl.BlockSpec((1, rows, d), lambda j, place: (j, 0, 0))
    row_spec = pl.BlockSpec((1, d), lambda j, place: (0, 0))
    turn_spec = pl.BlockSpec((1, ROT // 2, rows), lambda j, place: (j, 0, 0))
    return pl.pallas_call(
        project_kernel,
        grid_spec=pltpu.PrefetchScalarGridSpec(
            num_scalar_prefetch=1,
            grid=(units,),
            in_specs=half_specs(rows, d)
            + [
                pl.BlockSpec((d, PACK), lambda j, place: (0, 0)),
                pl.BlockSpec((1, PACK), lambda j, place: (0, 0)),
                row_spec,
                row_spec,
                turn_spec,
                turn_spec,
            ],
            out_specs=[
                pl.BlockSpec((1, rows, PACK), lambda j, place: (j, 0, 0)),
                pl.BlockSpec((1, rows, PACK - TILE), lambda j, place: (j, 0, 0)),
                tok_spec,
                tok_spec,
            ],
        ),
        out_shape=[
            jax.ShapeDtypeStruct((units, rows, PACK), BF),
            jax.ShapeDtypeStruct((units, rows, PACK - TILE), BF),
            jax.ShapeDtypeStruct((units, rows, d), BF),
            jax.ShapeDtypeStruct((units, rows, d), BF),
        ],
        compiler_params=params_of("arbitrary"),
        cost_estimate=pl.CostEstimate(
            flops=2 * units * rows * d * PACK,
            bytes_accessed=2 * units * rows * (3 * d + PACK),
            transcendentals=0,
        ),
        name="project",
    )(place, *toks, weight, bias, gain, offset, cos, sin)


def unturn_kernel(place_ref, own_ref, *refs):
    w_ref, cos_ref, sin_ref, out_ref, one_ref, two_ref = refs[-6:]
    others = refs[:-6]
    cos, sin = turn_tables(cos_ref[0], sin_ref[0])
    for t in range(5):
        tile = own_ref[0, :, t * TILE : (t + 1) * TILE].astype(F32)
        if t > 0:
            for other in others:
                tile = tile + other[0, :, (t - 1) * TILE : t * TILE].astype(F32)
        if t in (0, 1, 3):
            tile = turn(tile, cos, -sin)
        out_ref[0, :, t * TILE : (t + 1) * TILE] = tile.astype(BF)
    back = inner_back(out_ref[0], w_ref[...]).astype(BF)
    rows = back.shape[0] // 2
    one_ref[0] = back[:rows]
    two_ref[0] = back[rows:]


def unturn(place, own, others, weight, cos, sin):
    units, rows, unused = own.shape
    d = weight.shape[0]
    turn_spec = pl.BlockSpec((1, ROT // 2, rows), lambda j, place: (j, 0, 0))
    own_spec = pl.BlockSpec((1, rows, PACK), lambda j, place: (j, 0, 0))
    other_spec = pl.BlockSpec((1, rows, PACK - TILE), lambda j, place: (j, 0, 0))
    half = jax.ShapeDtypeStruct((units, rows // 2, d), BF)
    return pl.pallas_call(
        unturn_kernel,
        grid_spec=pltpu.PrefetchScalarGridSpec(
            num_scalar_prefetch=1,
            grid=(units,),
            in_specs=[own_spec]
            + [other_spec] * len(others)
            + [pl.BlockSpec((d, PACK), lambda j, place: (0, 0)), turn_spec, turn_spec],
            out_specs=[own_spec] + half_specs(rows, d),
        ),
        out_shape=[jax.ShapeDtypeStruct(own.shape, BF), half, half],
        compiler_params=params_of("arbitrary"),
        cost_estimate=pl.CostEstimate(flops=0, bytes_accessed=0, transcendentals=0),
        name="unturn",
    )(place, own, *others, weight, cos, sin)


def flip(tile):
    return tile.astype(F32).T


def head_rows(flipped, low):
    row = lax.broadcasted_iota(jnp.int32, flipped.shape, 0)
    keep = row < HEAD_DIM if low else row >= HEAD_DIM
    return jnp.where(keep, flipped, 0.0)


def head_lanes(tile, low):
    lane = lane_of(tile.shape)
    keep = lane < HEAD_DIM if low else lane >= HEAD_DIM
    return jnp.where(keep, tile, 0.0)


def query_sides(q_ref, qb):
    scale = HEAD_DIM ** (-0.5)
    a = flip(q_ref[0, :, 0:TILE]) * scale
    d = flip(q_ref[0, :, 3 * TILE : 4 * TILE]) * scale
    qb[0] = head_rows(a, True).astype(BF)
    qb[1] = head_rows(a, False).astype(BF)
    qb[2] = jnp.concatenate(
        [jnp.zeros((HEAD_DIM, d.shape[1]), F32), d[:HEAD_DIM]], 0
    ).astype(BF)


def live_of(seg_row, unit, query_start, part, rows, c):
    shape = (rows, rows)
    query_pos = query_start + lax.broadcasted_iota(jnp.int32, shape, 1)
    row = lax.broadcasted_iota(jnp.int32, shape, 0)
    pieces = []
    for i in range(part):
        key_pos = (unit * part + lax.rem(c - i + part, part)) * rows + row
        pieces.append((key_pos <= query_pos) & (key_pos >= seg_row))
    return jnp.concatenate(pieces, 0)


def unit_loop(meta, part, units, rows, step):
    j = pl.program_id(0)
    first = meta[j] // (rows * part)
    top_seg = meta[units + j]

    def one(unit, unused):
        masked = (unit == j) | (top_seg > unit * (rows * part))

        @pl.when(masked)
        def _():
            step(unit, True)

        @pl.when(jnp.logical_not(masked))
        def _():
            step(unit, False)

        return unused

    lax.fori_loop(first, j + 1, one, 0)


def join_parts(part, refs, kv_ref):
    rows = refs[0].shape[1]

    def one(unit, unused):
        for i in range(part):
            kv_ref[unit, i * rows : (i + 1) * rows] = refs[i][unit]
        return unused

    lax.fori_loop(0, refs[0].shape[0], one, 0)


def forward_kernel(part, units, meta, q_ref, *refs):
    seg_ref, o_ref, ot_ref, lse_ref, kv_ref, qb, vt, top, total, acc = refs[part:]
    rows = q_ref.shape[1]
    c = meta[2 * units]
    j = pl.program_id(0)

    @pl.when(j == 0)
    def _():
        join_parts(part, refs[:part], kv_ref)

        def turn_values(unit, unused):
            vt[unit, :TILE] = flip(kv_ref[unit, :, TILE : 2 * TILE]).astype(BF)
            vt[unit, TILE:] = flip(kv_ref[unit, :, 3 * TILE :])[:HEAD_DIM].astype(BF)
            return unused

        lax.fori_loop(0, units, turn_values, 0)

    query_sides(q_ref, qb)
    top[...] = jnp.full(top.shape, NEG_BIG, F32)
    total[...] = jnp.zeros(total.shape, F32)
    acc[...] = jnp.zeros(acc.shape, F32)
    seg_row = seg_ref[0]
    query_start = (j * part + c) * rows

    def step(unit, masked):
        k01 = kv_ref[unit, :, 0:TILE]
        k2 = kv_ref[unit, :, 2 * TILE : 3 * TILE]
        if masked:
            live = live_of(seg_row, unit, query_start, part, rows, c)
        scores = [mm(k2 if h == 2 else k01, qb[h]) for h in range(TRIO)]
        if masked:
            scores = [jnp.where(live, score, NEG_BIG) for score in scores]
        old = top[0:TRIO]
        new = jnp.concatenate([jnp.max(score, 0, keepdims=True) for score in scores], 0)
        new = jnp.maximum(old, new)
        factor = jnp.exp(old - new)
        weights = [jnp.exp(scores[h] - new[h : h + 1]) for h in range(TRIO)]
        if masked:
            weights = [jnp.where(live, weight, 0.0) for weight in weights]
        sums = [jnp.sum(weight, 0, keepdims=True) for weight in weights]
        top[0:TRIO] = new
        total[0:TRIO] = total[0:TRIO] * factor + jnp.concatenate(sums, 0)
        for h in range(TRIO):
            vth = vt[unit, h * HEAD_DIM : (h + 1) * HEAD_DIM]
            acc[h] = acc[h] * factor[h : h + 1] + mm(vth, weights[h].astype(BF))

    unit_loop(meta, part, units, rows, step)
    out = [acc[h] / total[h : h + 1] for h in range(TRIO)]
    for h in range(TRIO):
        ot_ref[0, h * HEAD_DIM : (h + 1) * HEAD_DIM] = out[h]
    lse_ref[0, 0:TRIO] = top[0:TRIO] + jnp.log(total[0:TRIO])
    o_ref[0, :, :TILE] = jnp.concatenate(out[:2], 0).T.astype(BF)
    o_ref[0, :, TILE:] = jnp.concatenate([out[2], jnp.zeros_like(out[2])], 0).T.astype(BF)


def backward_kernel(part, units, meta, q_ref, do_ref, ot_ref, lse_ref, *refs):
    seg_ref, own_ref, oth_ref, kv_ref, qb, db, qn, dn, kt, delta, dqt = refs[part : part + 11]
    dk01, dv01, dk2, dv2 = refs[part + 11 :]
    rows = q_ref.shape[1]
    c = meta[2 * units]
    j = pl.program_id(0)

    @pl.when(j == 0)
    def _():
        join_parts(part, refs[:part], kv_ref)

        def turn_keys(unit, unused):
            kt[unit, :TILE] = flip(kv_ref[unit, :, 0:TILE]).astype(BF)
            kt[unit, TILE:] = flip(kv_ref[unit, :, 2 * TILE : 3 * TILE])[HEAD_DIM:].astype(BF)
            return unused

        lax.fori_loop(0, units, turn_keys, 0)
        for ref in (dk01, dv01, dk2, dv2):
            ref[...] = jnp.zeros(ref.shape, F32)

    query_sides(q_ref, qb)
    scale = HEAD_DIM ** (-0.5)
    q01 = q_ref[0, :, 0:TILE].astype(F32) * scale
    q2 = pltpu.roll(q_ref[0, :, 3 * TILE : 4 * TILE].astype(F32), HEAD_DIM, 1) * scale
    qn[0:rows] = head_lanes(q01, True).astype(BF)
    qn[rows : 2 * rows] = head_lanes(q01, False).astype(BF)
    qn[2 * rows :] = head_lanes(q2, False).astype(BF)
    do01 = do_ref[0, :, :TILE].astype(F32)
    do2 = do_ref[0, :, TILE:].astype(F32)
    dn[0:rows] = head_lanes(do01, True).astype(BF)
    dn[rows : 2 * rows] = head_lanes(do01, False).astype(BF)
    dn[2 * rows :] = do2.astype(BF)
    do01t = do01.T
    do2t = do2.T
    db[0] = head_rows(do01t, True).astype(BF)
    db[1] = head_rows(do01t, False).astype(BF)
    db[2] = do2t.astype(BF)
    for h in range(TRIO):
        dot = do2t[:HEAD_DIM] if h == 2 else do01t[h * HEAD_DIM : (h + 1) * HEAD_DIM]
        delta[h : h + 1] = jnp.sum(
            dot * ot_ref[0, h * HEAD_DIM : (h + 1) * HEAD_DIM], 0, keepdims=True
        )
    dqt[...] = jnp.zeros(dqt.shape, F32)
    seg_row = seg_ref[0]
    query_start = (j * part + c) * rows

    def step(unit, masked):
        k01 = kv_ref[unit, :, 0:TILE]
        v01 = kv_ref[unit, :, TILE : 2 * TILE]
        k2 = kv_ref[unit, :, 2 * TILE : 3 * TILE]
        v2 = kv_ref[unit, :, 3 * TILE :]
        if masked:
            live = live_of(seg_row, unit, query_start, part, rows, c)
        scores = [mm(k2 if h == 2 else k01, qb[h]) for h in range(TRIO)]
        dprobs = [mm(v2 if h == 2 else v01, db[h]) for h in range(TRIO)]
        probs = []
        grads = []
        for h in range(TRIO):
            score = scores[h]
            if masked:
                score = jnp.where(live, score, NEG_BIG)
            prob = jnp.exp(score - lse_ref[0, h : h + 1])
            if masked:
                prob = jnp.where(live, prob, 0.0)
            probs.append(prob.astype(BF))
            grads.append((prob * (dprobs[h] - delta[h : h + 1])).astype(BF))
        dv01[unit] += mm(jnp.concatenate(probs[:2], 1), dn[: 2 * rows])
        dk01[unit] += mm(jnp.concatenate(grads[:2], 1), qn[: 2 * rows])
        dv2[unit] += mm(probs[2], dn[2 * rows :])
        dk2[unit] += mm(grads[2], qn[2 * rows :])
        for h in range(TRIO):
            kth = kt[unit, h * HEAD_DIM : (h + 1) * HEAD_DIM]
            dqt[h * HEAD_DIM : (h + 1) * HEAD_DIM] += mm(kth, grads[h])

    unit_loop(meta, part, units, rows, step)
    own_ref[j, :, 0:TILE] = (dqt[:TILE] * scale).T.astype(BF)
    dq2 = dqt[TILE:] * scale
    dk2[j, 0:rows] += jnp.concatenate([dq2, jnp.zeros_like(dq2)], 0).T

    @pl.when(j == units - 1)
    def _():
        for unit in range(units):
            for i in range(part):
                span = slice(i * rows, (i + 1) * rows)
                for t, ref in enumerate((dk01, dv01, dk2, dv2)):
                    tile = ref[unit, span].astype(BF)
                    if i == 0:
                        own_ref[unit, :, (t + 1) * TILE : (t + 2) * TILE] = tile
                    else:
                        oth_ref[i - 1, unit, :, t * TILE : (t + 1) * TILE] = tile


def whole_spec(shape):
    zeros = (0,) * len(shape)
    return pl.BlockSpec(shape, lambda j, meta: zeros)


def attend_forward(meta, packed, kv, seg):
    units, rows, unused = packed.shape
    part = len(kv)
    return pl.pallas_call(
        functools.partial(forward_kernel, part, units),
        grid_spec=pltpu.PrefetchScalarGridSpec(
            num_scalar_prefetch=1,
            grid=(units,),
            in_specs=[
                pl.BlockSpec((1, rows, PACK), lambda j, meta: (j, 0, 0)),
                *[whole_spec(piece.shape) for piece in kv],
                pl.BlockSpec((1, 1, rows), lambda j, meta: (j, 0, 0)),
            ],
            out_specs=[
                pl.BlockSpec((1, rows, OPACK), lambda j, meta: (j, 0, 0)),
                pl.BlockSpec((1, TRIO * HEAD_DIM, rows), lambda j, meta: (j, 0, 0)),
                pl.BlockSpec((1, 8, rows), lambda j, meta: (j, 0, 0)),
            ],
            scratch_shapes=[
                pltpu.VMEM((units, part * rows, PACK - TILE), BF),
                pltpu.VMEM((TRIO, TILE, rows), BF),
                pltpu.VMEM((units, TRIO * HEAD_DIM, part * rows), BF),
                pltpu.VMEM((8, rows), F32),
                pltpu.VMEM((8, rows), F32),
                pltpu.VMEM((TRIO, HEAD_DIM, rows), F32),
            ],
        ),
        out_shape=[
            jax.ShapeDtypeStruct((units, rows, OPACK), BF),
            jax.ShapeDtypeStruct((units, TRIO * HEAD_DIM, rows), F32),
            jax.ShapeDtypeStruct((units, 8, rows), F32),
        ],
        compiler_params=params_of("arbitrary"),
        cost_estimate=pl.CostEstimate(flops=0, bytes_accessed=0, transcendentals=0),
        name="attend_forward",
    )(meta, packed, *kv, seg)


def attend_backward(meta, packed, dout, out_t, lse, kv, seg):
    units, rows, unused = packed.shape
    part = len(kv)
    others = (max(part - 1, 1), units, rows, 4 * TILE)
    grads = pltpu.VMEM((units, part * rows, TILE), F32)
    return pl.pallas_call(
        functools.partial(backward_kernel, part, units),
        grid_spec=pltpu.PrefetchScalarGridSpec(
            num_scalar_prefetch=1,
            grid=(units,),
            in_specs=[
                pl.BlockSpec((1, rows, PACK), lambda j, meta: (j, 0, 0)),
                pl.BlockSpec((1, rows, OPACK), lambda j, meta: (j, 0, 0)),
                pl.BlockSpec((1, TRIO * HEAD_DIM, rows), lambda j, meta: (j, 0, 0)),
                pl.BlockSpec((1, 8, rows), lambda j, meta: (j, 0, 0)),
                *[whole_spec(piece.shape) for piece in kv],
                pl.BlockSpec((1, 1, rows), lambda j, meta: (j, 0, 0)),
            ],
            out_specs=[whole_spec(packed.shape), whole_spec(others)],
            scratch_shapes=[
                pltpu.VMEM((units, part * rows, PACK - TILE), BF),
                pltpu.VMEM((TRIO, TILE, rows), BF),
                pltpu.VMEM((TRIO, TILE, rows), BF),
                pltpu.VMEM((TRIO * rows, TILE), BF),
                pltpu.VMEM((TRIO * rows, TILE), BF),
                pltpu.VMEM((units, TRIO * HEAD_DIM, part * rows), BF),
                pltpu.VMEM((8, rows), F32),
                pltpu.VMEM((TRIO * HEAD_DIM, rows), F32),
                grads,
                grads,
                grads,
                grads,
            ],
        ),
        out_shape=[
            jax.ShapeDtypeStruct(packed.shape, BF),
            jax.ShapeDtypeStruct(others, BF),
        ],
        compiler_params=params_of("arbitrary"),
        cost_estimate=pl.CostEstimate(flops=0, bytes_accessed=0, transcendentals=0),
        name="attend_backward",
    )(meta, packed, dout, out_t, lse, *kv, seg)


def pack_kernel(trios, groups, w_ref, vec_ref, early_ref, local_ref):
    d = w_ref.shape[1] // 3
    w = w_ref[...].astype(F32)
    width = TRIO * HEAD_DIM
    zeros = jnp.zeros((w.shape[0], HEAD_DIM), F32)
    for g in range(trios):
        q, k, v = (w[:, i * d + g * width : i * d + (g + 1) * width] for i in range(3))
        tiles = [q[:, :TILE], k[:, :TILE], v[:, :TILE]]
        tiles.append(jnp.concatenate([q[:, TILE:], k[:, TILE:]], 1))
        tiles.append(jnp.concatenate([v[:, TILE:], zeros], 1))
        for t, tile in enumerate(tiles):
            tile = tile.astype(BF)
            local_ref[:, g * PACK + t * TILE : g * PACK + (t + 1) * TILE] = tile
            for s in range(groups):
                early_ref[s * trios + g, :, t * TILE : (t + 1) * TILE] = tile
        for s in range(groups):
            early_ref[s * trios + g, :, PACK:] = vec_ref[s]


def pack_early(weight, vec, trios):
    r = weight.shape[0]
    groups = vec.shape[0]
    return pl.pallas_call(
        functools.partial(pack_kernel, trios, groups),
        out_shape=[
            jax.ShapeDtypeStruct((trios * groups, r, PACK + TILE), BF),
            jax.ShapeDtypeStruct((r, trios * PACK), BF),
        ],
        name="pack_early",
    )(weight, vec)


def feed_kernel(
    x_ref, cot_ref, up_ref, down_ref, shift_ref, hid_ref, pre_ref, sum_ref, second_ref, back_ref
):
    pre = mm(x_ref[...], up_ref[...]) + shift_ref[...]
    grad = inner_back(cot_ref[...], down_ref[...])
    cdf = 0.5 * (1.0 + lax.erf(pre * math.sqrt(0.5)))
    hidden = (pre * cdf).astype(BF)
    slope = cdf + pre * (jnp.exp(-0.5 * pre * pre) * (1.0 / math.sqrt(2.0 * math.pi)))
    pre_grad = (grad * slope).astype(BF)
    hid_ref[...] = hidden
    pre_ref[...] = pre_grad
    sum_ref[...] = jnp.sum(pre_grad.astype(F32), 0, keepdims=True)
    second = mm(hidden, down_ref[...])
    back = inner_back(pre_grad, up_ref[...])

    @pl.when(pl.program_id(0) == 0)
    def _():
        second_ref[...] = second
        back_ref[...] = back

    @pl.when(pl.program_id(0) > 0)
    def _():
        second_ref[...] += second
        back_ref[...] += back


def feed_forward(x, cot, weights, shift, blocks):
    rows, d = x.shape
    ff = blocks * d
    half = d // 2
    wide = pl.BlockSpec((rows, d), lambda i: (0, 0))
    column = pl.BlockSpec((rows, half), lambda i: (0, i))
    line = pl.BlockSpec((1, half), lambda i: (0, i))
    return pl.pallas_call(
        feed_kernel,
        grid=(2 * blocks,),
        in_specs=[
            wide,
            wide,
            pl.BlockSpec((d, half), lambda i: (0, i)),
            pl.BlockSpec((half, d), lambda i: (i % 2, blocks + i // 2)),
            line,
        ],
        out_specs=[column, column, line, wide, wide],
        out_shape=[
            jax.ShapeDtypeStruct((rows, ff), BF),
            jax.ShapeDtypeStruct((rows, ff), BF),
            jax.ShapeDtypeStruct((1, ff), F32),
            jax.ShapeDtypeStruct((rows, d), F32),
            jax.ShapeDtypeStruct((rows, d), F32),
        ],
        compiler_params=params_of("arbitrary"),
        cost_estimate=pl.CostEstimate(
            flops=8 * rows * d * ff, bytes_accessed=4 * d * ff, transcendentals=2 * rows * ff
        ),
        name="feed_forward",
    )(x, cot, weights, weights, shift)


def gradient_kernel(ups, norm_ref, pre_ref, hidden_ref, cot_ref, out_ref):
    i = pl.program_id(0)

    @pl.when(i < ups)
    def _():
        out_ref[...] = outer_sum(norm_ref[...], pre_ref[...]).astype(BF)

    @pl.when(i >= ups)
    def _():
        out_ref[...] = outer_sum(hidden_ref[...], cot_ref[...]).astype(BF)


def gradients(normed, pre_grad, hidden, cot):
    rows, d = normed.shape
    width = d // 2
    ups = hidden.shape[1] // width

    def down(i):
        return jnp.clip(i - ups, 0, ups - 1)

    return pl.pallas_call(
        functools.partial(gradient_kernel, ups),
        grid=(2 * ups,),
        in_specs=[
            pl.BlockSpec((rows, d), lambda i: (0, 0)),
            pl.BlockSpec((rows, width), lambda i: (0, jnp.minimum(i, ups - 1))),
            pl.BlockSpec((rows, d), lambda i: (0, down(i) // 2)),
            pl.BlockSpec((rows, width), lambda i: (0, down(i) % 2)),
        ],
        out_specs=pl.BlockSpec((d, width), lambda i: (0, i)),
        out_shape=jax.ShapeDtypeStruct((d, 2 * ups * width), BF),
        compiler_params=params_of("arbitrary"),
        cost_estimate=pl.CostEstimate(
            flops=4 * rows * d * ups * width, bytes_accessed=0, transcendentals=0
        ),
        name="gradients",
    )(normed, pre_grad, hidden, cot)


def trio_kernel(norm_ref, hat_ref, grad_ref, w_ref, vec_ref, late_ref, shift_ref, own, hat):
    j = pl.program_id(0)
    d = norm_ref.shape[2]
    grad = grad_ref[...].reshape(-1, PACK)
    own_part = outer_sum(norm_ref[...].reshape(-1, d), grad)
    hat_part = outer_sum(hat_ref[...].reshape(-1, d), grad)
    sums = jnp.sum(grad.astype(F32), 0, keepdims=True)

    @pl.when(j == 0)
    def _():
        own[...] = own_part
        hat[...] = hat_part
        shift_ref[...] = sums

    @pl.when(j > 0)
    def _():
        own[...] += own_part
        hat[...] += hat_part
        shift_ref[...] += sums

    @pl.when(j == pl.num_programs(0) - 1)
    def _():
        late_ref[:, :PACK] = own[...].astype(BF)
        weight = w_ref[...].astype(F32)
        lane = lane_of(vec_ref.shape)
        vec = vec_ref[...]
        vec = jnp.where(lane == 0, jnp.sum(weight * hat[...], 1, keepdims=True), vec)
        vec = jnp.where(lane == 1, jnp.sum(weight * shift_ref[...], 1, keepdims=True), vec)
        late_ref[:, PACK:] = vec.astype(BF)


def trio_gradient(normed, hat, grad, weight, vec):
    units, rows, d = normed.shape
    tok_spec = pl.BlockSpec((2, rows, d), lambda j: (j, 0, 0))
    return pl.pallas_call(
        trio_kernel,
        grid=(units // 2,),
        in_specs=[
            tok_spec,
            tok_spec,
            pl.BlockSpec((2, rows, PACK), lambda j: (j, 0, 0)),
            pl.BlockSpec((d, PACK), lambda j: (0, 0)),
            pl.BlockSpec((d, TILE), lambda j: (0, 0)),
        ],
        out_specs=[
            pl.BlockSpec((d, PACK + TILE), lambda j: (0, 0)),
            pl.BlockSpec((1, PACK), lambda j: (0, 0)),
        ],
        scratch_shapes=[pltpu.VMEM((d, PACK), F32), pltpu.VMEM((d, PACK), F32)],
        out_shape=[
            jax.ShapeDtypeStruct((d, PACK + TILE), BF),
            jax.ShapeDtypeStruct((1, PACK), F32),
        ],
        compiler_params=params_of("arbitrary"),
        cost_estimate=pl.CostEstimate(
            flops=12 * units * rows * d * PACK, bytes_accessed=0, transcendentals=0
        ),
        name="trio_gradient",
    )(normed, hat, grad, weight, vec)


def pack_columns(matrix, trios):
    r = matrix.shape[0]
    q, k, v = (
        part.reshape(r, trios, TRIO * HEAD_DIM) for part in jnp.split(matrix, 3, axis=1)
    )
    zeros = jnp.zeros((r, trios, HEAD_DIM), matrix.dtype)
    pieces = [q[..., :TILE], k[..., :TILE], v[..., :TILE], q[..., TILE:], k[..., TILE:]]
    return jnp.concatenate(pieces + [v[..., TILE:], zeros], -1).reshape(r, trios * PACK)


def unpack_columns(matrix, trios):
    r = matrix.shape[0]
    m = matrix.reshape(r, trios, PACK)
    halves = [
        m[..., 3 * TILE : 3 * TILE + HEAD_DIM],
        m[..., 3 * TILE + HEAD_DIM : 4 * TILE],
        m[..., 4 * TILE : 4 * TILE + HEAD_DIM],
    ]
    return jnp.concatenate(
        [
            jnp.concatenate([m[..., i * TILE : (i + 1) * TILE], halves[i]], -1).reshape(r, -1)
            for i in range(3)
        ],
        -1,
    )


def split_hidden(matrix, count, r):
    lead = matrix.shape[0]
    return matrix.reshape(lead, count, -1, r).transpose(0, 2, 1, 3).reshape(lead, -1)


def join_hidden(matrix, count, r):
    lead = matrix.shape[0]
    return matrix.reshape(lead, -1, count, r).transpose(0, 2, 1, 3).reshape(lead, -1)


def on_device(
    tokens,
    segment,
    ln1_gain,
    ln1_bias,
    ln2_gain,
    ln2_bias,
    qkv_weight,
    qkv_bias,
    dense_weight,
    dense_bias,
    fc1_weight,
    fc1_bias,
    output_feed_weight,
    output_feed_bias,
    cotangent,
):
    rows, groups, d = tokens.shape
    units = lax.axis_size("unit")
    part = lax.axis_size("part")
    count = units * part * lax.axis_size("seq")
    trios = units // groups
    all_rows = rows * groups
    r = qkv_weight.shape[0]
    ff = fc1_weight.shape[1]
    blocks = ff // d
    c = lax.axis_index("part")
    unit = lax.axis_index("unit")

    seq = lax.axis_index("seq")
    seqs = lax.axis_size("seq")
    place = (seq * units + unit) * part + c

    def exchange(blocks_out):
        width = blocks_out.shape[-1]
        return lax.all_to_all(
            blocks_out.reshape(-1, width), "unit", 0, 0, tiled=True
        ).reshape(blocks_out.shape)

    def shift(value, axis, i):
        n = lax.axis_size(axis)
        return lax.ppermute(value, axis, [(p, (p + i) % n) for p in range(n)])

    def flip_unit(value, bit):
        return lax.ppermute(value, "unit", [(u, u ^ bit) for u in range(units)])

    def pick(value, index, axis):
        return lax.dynamic_index_in_dim(value, index, axis, False)

    bits = (unit // trios, unit // 2 % 2, unit % 2)

    def exchange_small(value):
        shape = value.shape
        value = value.reshape((2, 2, 2) + shape[1:])
        for axis, bit in enumerate((trios, 2, 1)):
            keep = pick(value, bits[axis], axis)
            value = jnp.stack([keep, flip_unit(pick(value, 1 - bits[axis], axis), bit)], axis)
        for axis in range(3):
            value = jnp.where(bits[axis] == 0, value, jnp.flip(value, axis))
        return value.reshape(shape)

    def spread_tokens(value):
        keep = pick(value, bits[0], 0)
        both = jnp.stack([keep, flip_unit(pick(value, 1 - bits[0], 0), trios)])
        one, two = both[:, : rows // 2], both[:, rows // 2 :]
        one = jnp.stack([one, flip_unit(one, 2)])
        two = jnp.stack([two, flip_unit(two, 1)])
        one = jnp.stack([one, flip_unit(one, 1)])
        two = jnp.stack([two, flip_unit(two, 2)])
        return one.reshape(units, rows // 2, d), two.reshape(units, rows // 2, d)

    def add(a, b):
        return (a.astype(F32) + b.astype(F32)).astype(BF)

    def natural_order(got, me):
        n = len(got)
        if n == 2:
            return jnp.where(me == 0, jnp.stack(got), jnp.stack(got[::-1]))
        ring = jnp.stack((got + got)[::-1])
        return lax.dynamic_slice_in_dim(ring, n - 1 - me, n, 0)

    def gather_small(value, axis):
        n = lax.axis_size(axis)
        got = [value] + [shift(value, axis, i) for i in range(1, n)]
        return natural_order(got, lax.axis_index(axis))

    def swap_parts(value):
        got = [lax.dynamic_index_in_dim(value, c, 0, False)]
        for i in range(1, part):
            piece = lax.dynamic_index_in_dim(value, (c + i) % part, 0, False)
            got.append(shift(piece, "part", i))
        return natural_order(got, c)

    def all_parts(value):
        return jnp.concatenate([value] + [shift(value, "part", i) for i in range(1, part)], 0)

    def part_pieces(value):
        n = value.shape[0] // part
        return [value[:n]] + [
            shift(value[i * n : (i + 1) * n], "part", part - i) for i in range(1, part)
        ]

    def scatter_small(value, axis):
        n = lax.axis_size(axis)
        me = lax.axis_index(axis)
        total = lax.dynamic_index_in_dim(value, me, 0, False).astype(F32)
        for i in range(1, n):
            piece = lax.dynamic_index_in_dim(value, (me + i) % n, 0, False)
            total = total + shift(piece, axis, i).astype(F32)
        return total.astype(BF)

    vectors = (ln1_gain, ln1_bias, ln2_gain, ln2_bias, dense_bias, output_feed_bias)
    vec = jnp.concatenate(
        [v.reshape(r, 1) for v in vectors] + [qkv_bias.reshape(r, 3), fc1_bias.reshape(r, blocks)],
        1,
    )
    token_rows = tokens.transpose(1, 0, 2)
    seg_rows = segment.T
    seg_lanes = -(-2 * rows // r)
    seg_pack = jnp.concatenate([seg_rows // 64, seg_rows % 64], 1).astype(BF)
    seg_pack = jnp.pad(seg_pack, ((0, 0), (0, seg_lanes * r - 2 * rows)))
    seg_pack = seg_pack.reshape(groups, r, seg_lanes)
    vec = jnp.pad(vec, ((0, 0), (0, 16 - vec.shape[1])))
    vec = jnp.concatenate(
        [
            jnp.broadcast_to(vec, (groups, r, 16)),
            seg_pack,
            jnp.zeros((groups, r, TILE - 16 - seg_lanes), BF),
        ],
        -1,
    )
    early, qkv_local = pack_early(qkv_weight, vec, trios)
    early = exchange_small(early)
    toks = spread_tokens(token_rows)

    seg_mine = early[:, :, PACK + 16 : PACK + 16 + seg_lanes].astype(jnp.int32)
    seg_mine = seg_mine.reshape(units, r * seg_lanes)
    seg_mine = seg_mine[:, :rows] * 64 + seg_mine[:, rows : 2 * rows]
    meta = jnp.concatenate([seg_mine[:, 0], seg_mine[:, -1], c[None]])
    seg_mine = seg_mine[:, None, :]
    trio_full = gather_small(gather_small(early, "seq"), "part")
    trio_full = trio_full.transpose(1, 2, 0, 3, 4).reshape(d, PACK + TILE)
    vec_full = trio_full[:, PACK:].astype(F32)
    vec_rows = vec_full[:, :8].T
    gain_one, bias_one, gain_two, bias_two, dense_shift, down_shift = (
        vec_rows[i : i + 1] for i in range(6)
    )
    qkv_shift = pack_columns(vec_full[:, 6:9].reshape(1, 3 * d), trios).reshape(trios, PACK)
    qkv_shift = lax.dynamic_slice_in_dim(qkv_shift, unit % trios, 1, 0)
    up_shift = split_hidden(vec_full[:, 9 : 9 + blocks].reshape(1, ff), count, r)

    feed_blocks = output_feed_weight.reshape(blocks, r, d)
    half = blocks // part
    up_local = split_hidden(fc1_weight, count, r)
    second_pack = jnp.stack(
        [
            jnp.concatenate(
                [up_local[:, p * half * d : (p + 1) * half * d]]
                + [feed_blocks[b] for b in range(p * half, (p + 1) * half)]
                + [dense_weight],
                1,
            )
            for p in range(part)
        ]
    )
    second_pack = swap_parts(second_pack).reshape(part * r, -1)
    second = lax.all_gather(second_pack, ("seq", "unit"), axis=0, tiled=True)
    dense_pad = jnp.pad(
        second[:, 2 * half * d :].reshape(trios, d // trios, d),
        ((0, 0), (0, OPACK - d // trios), (0, 0)),
    )

    block_start = (jnp.arange(units, dtype=jnp.int32) * part + c) * rows
    positions = block_start[:, None, None] + jnp.arange(rows, dtype=jnp.int32) - seg_mine
    freq = jnp.arange(ROT // 2, dtype=F32)
    inverse = jnp.exp(freq * (-2.0 * math.log(10000.0) / ROT))
    angles = positions.astype(F32) * inverse[None, :, None]
    cos = jnp.cos(angles)
    sin = jnp.sin(angles)

    place_unit = unit[None]
    packed, kv_own, normed_one, hat_one = project(
        place_unit, toks, trio_full, qkv_shift, gain_one, bias_one, cos, sin
    )
    kv = [kv_own] + [shift(kv_own, "part", i) for i in range(1, part)]

    x = token_rows.reshape(all_rows, d).astype(F32)
    cot = cotangent.transpose(1, 0, 2).reshape(all_rows, d)
    centre = x - jnp.mean(x, -1, keepdims=True)
    spread = lax.rsqrt(jnp.mean(centre * centre, -1, keepdims=True) + EPSILON)
    xhat = centre * spread
    normed_two = (xhat * gain_two + bias_two).astype(BF)
    attended_grad = jnp.einsum(
        "sld,gkd->sglk", cot.reshape(groups, rows, d), dense_pad, preferred_element_type=F32
    ).astype(BF)
    dout = exchange(attended_grad.reshape(units, rows, OPACK))
    normed_all = all_parts(normed_two)
    cot_all = all_parts(cot)
    up_shift = lax.dynamic_slice_in_dim(up_shift, c * half * d, half * d, 1)
    hidden_low, pre_grad, up_shift_grad, second_branch, normed_two_grad = feed_forward(
        normed_all, cot_all, second, up_shift, half
    )
    hidden_low, pre_grad, dout = lax.optimization_barrier((hidden_low, pre_grad, dout))
    second_branch = part_pieces(second_branch)
    normed_two_grad = part_pieces(normed_two_grad)
    def norm_back(grad, gain):
        gy = grad * gain
        return spread * (
            gy - jnp.mean(gy, -1, keepdims=True) - xhat * jnp.mean(gy * xhat, -1, keepdims=True)
        )

    mlp_grads = gradients(normed_all, pre_grad, hidden_low, cot_all)
    mlp_grads, meta = lax.optimization_barrier((mlp_grads, meta))
    mlp_sum = lax.psum_scatter(mlp_grads, ("seq", "unit"), scatter_dimension=0, tiled=True)

    out_low, out_t, lse = attend_forward(meta, packed, kv, seg_mine)
    attended = exchange(out_low)

    own, others = attend_backward(meta, packed, dout, out_t, lse, kv, seg_mine)
    others = [shift(others[i - 1], "part", part - i) for i in range(1, part)]
    own, attended = lax.optimization_barrier((own, attended))
    qkv_grad, back_one, back_two = unturn(place_unit, own, others, trio_full, cos, sin)
    back_one = back_one.reshape(2, 2, 2, rows // 2, d)
    back_two = back_two.reshape(2, 2, 2, rows // 2, d)
    swapped = flip_unit(back_one[1], 1), flip_unit(back_two[1], 2)

    attended, second_branch, normed_two_grad, qkv_grad, cot, up_shift_grad = (
        lax.optimization_barrier(
            (attended, second_branch, normed_two_grad, qkv_grad, cot, up_shift_grad)
        )
    )
    cot_float = cot.astype(F32)
    up_shift_grad = lax.dynamic_update_slice_in_dim(
        jnp.zeros((1, ff), F32), up_shift_grad, c * half * d, 1
    )
    second_branch = sum(second_branch)
    normed_two_grad = sum(normed_two_grad)
    attended = attended.reshape(groups, trios, rows, OPACK).transpose(0, 2, 1, 3)
    attended = attended.reshape(all_rows, trios * OPACK)
    dense_grad = outer_sum(attended, cot).reshape(trios, OPACK, d)[:, : d // trios].reshape(d, d)
    branch_one = mm(attended, dense_pad.reshape(trios * OPACK, d)) + dense_shift
    output = (x + branch_one + second_branch + down_shift).astype(BF)
    in_two = norm_back(normed_two_grad, gain_two)
    vec_grads = jnp.concatenate(
        [
            jnp.zeros((2, d), F32),
            jnp.sum(normed_two_grad * xhat, 0)[None],
            jnp.sum(normed_two_grad, 0)[None],
            jnp.sum(cot_float, 0)[None],
            jnp.zeros((3, d), F32),
        ],
        0,
    ).T
    up_shift_grad = join_hidden(up_shift_grad, count, r).reshape(d, blocks)

    vec_grads = jnp.concatenate(
        [vec_grads, up_shift_grad, jnp.zeros((d, TILE - 8 - blocks), F32)], 1
    )
    late, shift_grad = trio_gradient(normed_one, hat_one, qkv_grad, trio_full, vec_grads)
    late = jnp.concatenate([late, dense_grad.astype(BF)], 1)
    swapped, late = lax.optimization_barrier((swapped, late))
    back_one = add(back_one[0], swapped[0])
    back_two = add(back_two[0], swapped[1])
    swapped = flip_unit(back_one[1], 2), flip_unit(back_two[1], 1)
    late = late.reshape(seqs, units, part, r, -1)
    width = late.shape[-1]
    shift_rows = jnp.pad(shift_grad.astype(BF), ((0, 7), (0, width - PACK)))
    late = jnp.concatenate(
        [late, jnp.broadcast_to(shift_rows, (seqs, units, part) + shift_rows.shape)], 3
    )
    late = scatter_small(late.transpose(2, 0, 1, 3, 4), "part")
    swapped, late = lax.optimization_barrier((swapped, late))
    both = jnp.concatenate(
        [add(back_one[0], swapped[0]), add(back_two[0], swapped[1])], 1
    )
    swapped = flip_unit(both[1], trios)
    late = scatter_small(late, "seq")
    swapped, late, mlp_sum = lax.optimization_barrier((swapped, late, mlp_sum))
    back = jnp.where(
        bits[0] == 0, jnp.stack([both[0], swapped]), jnp.stack([swapped, both[0]])
    )
    late = exchange_small(late).astype(F32)
    late = jnp.sum(late.reshape(groups, trios, r + 8, width), 0)
    qkv_weight_grad = unpack_columns(
        late[:, :r, :PACK].transpose(1, 0, 2).reshape(r, trios * PACK), trios
    )
    late_rest = jnp.sum(late[:, :r, PACK:], 0)
    late_vec = late_rest[:, :TILE]
    dense_sum = late_rest[:, TILE:]
    qkv_shift_grad = unpack_columns(late[:, r, :PACK].reshape(1, trios * PACK), trios)[0]
    qkv_shift_grad = lax.dynamic_slice_in_dim(qkv_shift_grad, place * 3 * r, 3 * r)

    mlp_sum = swap_parts(mlp_sum.reshape(part, r, -1)).astype(F32)
    up_sum = jnp.concatenate([mlp_sum[p, :, : half * d] for p in range(part)], 1)
    down_sum = jnp.concatenate(
        [
            mlp_sum[p, :, (half + b) * d : (half + b + 1) * d]
            for p in range(part)
            for b in range(half)
        ],
        0,
    )
    param_grads = (
        late_vec[:, 0],
        late_vec[:, 1],
        late_vec[:, 2],
        late_vec[:, 3],
        qkv_weight_grad,
        qkv_shift_grad,
        dense_sum,
        late_vec[:, 4],
        join_hidden(up_sum, count, r),
        late_vec[:, 8 : 8 + blocks].reshape(-1),
        down_sum,
        late_vec[:, 4],
    )

    normed_one_grad = back.reshape(all_rows, d).astype(F32)
    in_one = norm_back(normed_one_grad, gain_one)
    tokens_grad = (cot_float + in_one + in_two).astype(BF)

    def natural(value):
        return value.reshape(groups, rows, d).transpose(1, 0, 2)

    return (natural(output), natural(tokens_grad)) + tuple(param_grads)


def solution(mesh):
    devices = mesh.devices
    seq_size, ctx_size = devices.shape
    ctx = ("unit", "part")
    tok = P(ctx, "seq", None)
    vec = P(ALL_AXES)
    mat = P(ALL_AXES, None)
    pairs = (vec, vec, vec, vec, mat, vec, mat, vec, mat, vec, mat, vec)

    def run(tokens, *rest):
        units = HEADS // TRIO * (tokens.shape[1] // seq_size)
        split = Mesh(devices.reshape(seq_size, units, ctx_size // units), ALL_AXES)
        mapped = jax.shard_map(
            on_device,
            mesh=split,
            in_specs=(tok, P(ctx, "seq")) + pairs + (tok,),
            out_specs=(tok, tok) + pairs,
            check_vma=False,
        )
        return mapped(tokens, *rest)

    return run
```

```python
import functools
import math

import jax
import jax.numpy as jnp
from jax import lax
from jax.experimental import pallas as pl
from jax.experimental.pallas import tpu as pltpu
from jax.sharding import Mesh, PartitionSpec as P

HEADS = 12
HEAD_DIM = 64
ROT = 16
TRIO = 3
TILE = 128
PACK = 5 * TILE
OPACK = 2 * TILE

EPSILON = 1e-05
NEG_BIG = -1e30
BF = jnp.bfloat16
F32 = jnp.float32
ALL_AXES = ("seq", "unit", "part")
VMEM_BYTES = 56 * 1024 * 1024


def params_of(*semantics):
    return pltpu.CompilerParams(
        dimension_semantics=semantics, vmem_limit_bytes=VMEM_BYTES
    )


def mm(a, b):
    return jnp.dot(a, b, preferred_element_type=F32)


def outer_sum(left_rows, right_rows):
    return lax.dot_general(
        left_rows, right_rows, (((0,), (0,)), ((), ())), preferred_element_type=F32
    )


def inner_back(grad_rows, weight):
    return lax.dot_general(
        grad_rows, weight, (((1,), (1,)), ((), ())), preferred_element_type=F32
    )


def lane_of(shape):
    return lax.broadcasted_iota(jnp.int32, shape, len(shape) - 1)


def turn(tile, cos, sin):
    partner = jnp.where(
        lane_of(tile.shape) % HEAD_DIM < ROT // 2,
        pltpu.roll(tile, TILE - ROT // 2, 1),
        pltpu.roll(tile, ROT // 2, 1),
    )
    return tile * cos + partner * sin


def turn_tables(cos_rows, sin_rows):
    rows = cos_rows.shape[1]
    rest = HEAD_DIM - ROT
    cos_head = [cos_rows, cos_rows, jnp.ones((rest, rows), F32)]
    sin_head = [-sin_rows, sin_rows, jnp.zeros((rest, rows), F32)]
    return jnp.concatenate(cos_head * 2, 0).T, jnp.concatenate(sin_head * 2, 0).T


def first_place(rel):
    return rel % 2 * 4 + rel // 2 % 2 * 2 + rel // 4


def second_place(rel):
    return rel // 2 % 2 * 4 + rel % 2 * 2 + rel // 4


def project_kernel(
    place_ref,
    one_ref,
    two_ref,
    w_ref,
    b_ref,
    gain_ref,
    bias_ref,
    cos_ref,
    sin_ref,
    out_ref,
    kv_ref,
    norm_ref,
    hat_ref,
):
    x = jnp.concatenate([one_ref[0], two_ref[0]], 0).astype(F32)
    centre = x - jnp.mean(x, -1, keepdims=True)
    spread = jnp.mean(centre * centre, -1, keepdims=True)
    hat = centre * lax.rsqrt(spread + EPSILON)
    normed = (hat * gain_ref[...] + bias_ref[...]).astype(BF)
    hat_ref[0] = hat.astype(BF)
    norm_ref[0] = normed
    y = mm(normed, w_ref[...]) + b_ref[...]
    cos, sin = turn_tables(cos_ref[0], sin_ref[0])
    for t in range(5):
        tile = y[:, t * TILE : (t + 1) * TILE]
        if t in (0, 1, 3):
            tile = turn(tile, cos, sin)
        tile = tile.astype(BF)
        out_ref[0, :, t * TILE : (t + 1) * TILE] = tile
        if t > 0:
            kv_ref[0, :, (t - 1) * TILE : t * TILE] = tile


def half_specs(rows, d):
    return [
        pl.BlockSpec((1, rows // 2, d), lambda j, place: (first_place(j ^ place[0]), 0, 0)),
        pl.BlockSpec((1, rows // 2, d), lambda j, place: (second_place(j ^ place[0]), 0, 0)),
    ]


def project(place, toks, weight, bias, gain, offset, cos, sin):
    units, unused, rows = cos.shape
    d = toks[0].shape[2]
    tok_spec = pl.BlockSpec((1, rows, d), lambda j, place: (j, 0, 0))
    row_spec = pl.BlockSpec((1, d), lambda j, place: (0, 0))
    turn_spec = pl.BlockSpec((1, ROT // 2, rows), lambda j, place: (j, 0, 0))
    return pl.pallas_call(
        project_kernel,
        grid_spec=pltpu.PrefetchScalarGridSpec(
            num_scalar_prefetch=1,
            grid=(units,),
            in_specs=half_specs(rows, d)
            + [
                pl.BlockSpec((d, PACK), lambda j, place: (0, 0)),
                pl.BlockSpec((1, PACK), lambda j, place: (0, 0)),
                row_spec,
                row_spec,
                turn_spec,
                turn_spec,
            ],
            out_specs=[
                pl.BlockSpec((1, rows, PACK), lambda j, place: (j, 0, 0)),
                pl.BlockSpec((1, rows, PACK - TILE), lambda j, place: (j, 0, 0)),
                tok_spec,
                tok_spec,
            ],
        ),
        out_shape=[
            jax.ShapeDtypeStruct((units, rows, PACK), BF),
            jax.ShapeDtypeStruct((units, rows, PACK - TILE), BF),
            jax.ShapeDtypeStruct((units, rows, d), BF),
            jax.ShapeDtypeStruct((units, rows, d), BF),
        ],
        compiler_params=params_of("arbitrary"),
        cost_estimate=pl.CostEstimate(
            flops=2 * units * rows * d * PACK,
            bytes_accessed=2 * units * rows * (3 * d + PACK),
            transcendentals=0,
        ),
        name="project",
    )(place, *toks, weight, bias, gain, offset, cos, sin)


def unturn_kernel(place_ref, own_ref, *refs):
    w_ref, cos_ref, sin_ref, out_ref, one_ref, two_ref = refs[-6:]
    others = refs[:-6]
    cos, sin = turn_tables(cos_ref[0], sin_ref[0])
    for t in range(5):
        tile = own_ref[0, :, t * TILE : (t + 1) * TILE].astype(F32)
        if t > 0:
            for other in others:
                tile = tile + other[0, :, (t - 1) * TILE : t * TILE].astype(F32)
        if t in (0, 1, 3):
            tile = turn(tile, cos, -sin)
        out_ref[0, :, t * TILE : (t + 1) * TILE] = tile.astype(BF)
    back = inner_back(out_ref[0], w_ref[...]).astype(BF)
    rows = back.shape[0] // 2
    one_ref[0] = back[:rows]
    two_ref[0] = back[rows:]


def unturn(place, own, others, weight, cos, sin):
    units, rows, unused = own.shape
    d = weight.shape[0]
    turn_spec = pl.BlockSpec((1, ROT // 2, rows), lambda j, place: (j, 0, 0))
    own_spec = pl.BlockSpec((1, rows, PACK), lambda j, place: (j, 0, 0))
    other_spec = pl.BlockSpec((1, rows, PACK - TILE), lambda j, place: (j, 0, 0))
    half = jax.ShapeDtypeStruct((units, rows // 2, d), BF)
    return pl.pallas_call(
        unturn_kernel,
        grid_spec=pltpu.PrefetchScalarGridSpec(
            num_scalar_prefetch=1,
            grid=(units,),
            in_specs=[own_spec]
            + [other_spec] * len(others)
            + [pl.BlockSpec((d, PACK), lambda j, place: (0, 0)), turn_spec, turn_spec],
            out_specs=[own_spec] + half_specs(rows, d),
        ),
        out_shape=[jax.ShapeDtypeStruct(own.shape, BF), half, half],
        compiler_params=params_of("arbitrary"),
        cost_estimate=pl.CostEstimate(flops=0, bytes_accessed=0, transcendentals=0),
        name="unturn",
    )(place, own, *others, weight, cos, sin)


def flip(tile):
    return tile.astype(F32).T


def head_rows(flipped, low):
    row = lax.broadcasted_iota(jnp.int32, flipped.shape, 0)
    keep = row < HEAD_DIM if low else row >= HEAD_DIM
    return jnp.where(keep, flipped, 0.0)


def head_lanes(tile, low):
    lane = lane_of(tile.shape)
    keep = lane < HEAD_DIM if low else lane >= HEAD_DIM
    return jnp.where(keep, tile, 0.0)


def query_sides(q_ref, qb):
    scale = HEAD_DIM ** (-0.5)
    a = flip(q_ref[0, :, 0:TILE]) * scale
    d = flip(q_ref[0, :, 3 * TILE : 4 * TILE]) * scale
    qb[0] = head_rows(a, True).astype(BF)
    qb[1] = head_rows(a, False).astype(BF)
    qb[2] = jnp.concatenate(
        [jnp.zeros((HEAD_DIM, d.shape[1]), F32), d[:HEAD_DIM]], 0
    ).astype(BF)


def live_of(seg_row, unit, query_start, part, rows, c):
    shape = (rows, rows)
    query_pos = query_start + lax.broadcasted_iota(jnp.int32, shape, 1)
    row = lax.broadcasted_iota(jnp.int32, shape, 0)
    pieces = []
    for i in range(part):
        key_pos = (unit * part + lax.rem(c - i + part, part)) * rows + row
        pieces.append((key_pos <= query_pos) & (key_pos >= seg_row))
    return jnp.concatenate(pieces, 0)


def unit_loop(meta, part, units, rows, step):
    j = pl.program_id(0)
    first = meta[j] // (rows * part)
    top_seg = meta[units + j]

    def one(unit, unused):
        masked = (unit == j) | (top_seg > unit * (rows * part))

        @pl.when(masked)
        def _():
            step(unit, True)

        @pl.when(jnp.logical_not(masked))
        def _():
            step(unit, False)

        return unused

    lax.fori_loop(first, j + 1, one, 0)


def join_parts(part, refs, kv_ref):
    rows = refs[0].shape[1]

    def one(unit, unused):
        for i in range(part):
            kv_ref[unit, i * rows : (i + 1) * rows] = refs[i][unit]
        return unused

    lax.fori_loop(0, refs[0].shape[0], one, 0)


def forward_kernel(part, units, meta, q_ref, *refs):
    seg_ref, o_ref, ot_ref, lse_ref, kv_ref, qb, vt, top, total, acc = refs[part:]
    rows = q_ref.shape[1]
    c = meta[2 * units]
    j = pl.program_id(0)

    @pl.when(j == 0)
    def _():
        join_parts(part, refs[:part], kv_ref)

        def turn_values(unit, unused):
            vt[unit, :TILE] = flip(kv_ref[unit, :, TILE : 2 * TILE]).astype(BF)
            vt[unit, TILE:] = flip(kv_ref[unit, :, 3 * TILE :])[:HEAD_DIM].astype(BF)
            return unused

        lax.fori_loop(0, units, turn_values, 0)

    query_sides(q_ref, qb)
    top[...] = jnp.full(top.shape, NEG_BIG, F32)
    total[...] = jnp.zeros(total.shape, F32)
    acc[...] = jnp.zeros(acc.shape, F32)
    seg_row = seg_ref[0]
    query_start = (j * part + c) * rows

    def step(unit, masked):
        k01 = kv_ref[unit, :, 0:TILE]
        k2 = kv_ref[unit, :, 2 * TILE : 3 * TILE]
        if masked:
            live = live_of(seg_row, unit, query_start, part, rows, c)
        scores = [mm(k2 if h == 2 else k01, qb[h]) for h in range(TRIO)]
        if masked:
            scores = [jnp.where(live, score, NEG_BIG) for score in scores]
        old = top[0:TRIO]
        new = jnp.concatenate([jnp.max(score, 0, keepdims=True) for score in scores], 0)
        new = jnp.maximum(old, new)
        factor = jnp.exp(old - new)
        weights = [jnp.exp(scores[h] - new[h : h + 1]) for h in range(TRIO)]
        if masked:
            weights = [jnp.where(live, weight, 0.0) for weight in weights]
        sums = [jnp.sum(weight, 0, keepdims=True) for weight in weights]
        top[0:TRIO] = new
        total[0:TRIO] = total[0:TRIO] * factor + jnp.concatenate(sums, 0)
        for h in range(TRIO):
            vth = vt[unit, h * HEAD_DIM : (h + 1) * HEAD_DIM]
            acc[h] = acc[h] * factor[h : h + 1] + mm(vth, weights[h].astype(BF))

    unit_loop(meta, part, units, rows, step)
    out = [acc[h] / total[h : h + 1] for h in range(TRIO)]
    for h in range(TRIO):
        ot_ref[0, h * HEAD_DIM : (h + 1) * HEAD_DIM] = out[h]
    lse_ref[0, 0:TRIO] = top[0:TRIO] + jnp.log(total[0:TRIO])
    o_ref[0, :, :TILE] = jnp.concatenate(out[:2], 0).T.astype(BF)
    o_ref[0, :, TILE:] = jnp.concatenate([out[2], jnp.zeros_like(out[2])], 0).T.astype(BF)


def backward_kernel(part, units, meta, q_ref, do_ref, ot_ref, lse_ref, *refs):
    seg_ref, own_ref, oth_ref, kv_ref, qb, db, qn, dn, kt, delta, dqt = refs[part : part + 11]
    dk01, dv01, dk2, dv2 = refs[part + 11 :]
    rows = q_ref.shape[1]
    c = meta[2 * units]
    j = pl.program_id(0)

    @pl.when(j == 0)
    def _():
        join_parts(part, refs[:part], kv_ref)

        def turn_keys(unit, unused):
            kt[unit, :TILE] = flip(kv_ref[unit, :, 0:TILE]).astype(BF)
            kt[unit, TILE:] = flip(kv_ref[unit, :, 2 * TILE : 3 * TILE])[HEAD_DIM:].astype(BF)
            return unused

        lax.fori_loop(0, units, turn_keys, 0)
        for ref in (dk01, dv01, dk2, dv2):
            ref[...] = jnp.zeros(ref.shape, F32)

    query_sides(q_ref, qb)
    scale = HEAD_DIM ** (-0.5)
    q01 = q_ref[0, :, 0:TILE].astype(F32) * scale
    q2 = pltpu.roll(q_ref[0, :, 3 * TILE : 4 * TILE].astype(F32), HEAD_DIM, 1) * scale
    qn[0:rows] = head_lanes(q01, True).astype(BF)
    qn[rows : 2 * rows] = head_lanes(q01, False).astype(BF)
    qn[2 * rows :] = head_lanes(q2, False).astype(BF)
    do01 = do_ref[0, :, :TILE].astype(F32)
    do2 = do_ref[0, :, TILE:].astype(F32)
    dn[0:rows] = head_lanes(do01, True).astype(BF)
    dn[rows : 2 * rows] = head_lanes(do01, False).astype(BF)
    dn[2 * rows :] = do2.astype(BF)
    do01t = do01.T
    do2t = do2.T
    db[0] = head_rows(do01t, True).astype(BF)
    db[1] = head_rows(do01t, False).astype(BF)
    db[2] = do2t.astype(BF)
    for h in range(TRIO):
        dot = do2t[:HEAD_DIM] if h == 2 else do01t[h * HEAD_DIM : (h + 1) * HEAD_DIM]
        delta[h : h + 1] = jnp.sum(
            dot * ot_ref[0, h * HEAD_DIM : (h + 1) * HEAD_DIM], 0, keepdims=True
        )
    dqt[...] = jnp.zeros(dqt.shape, F32)
    seg_row = seg_ref[0]
    query_start = (j * part + c) * rows

    def step(unit, masked):
        k01 = kv_ref[unit, :, 0:TILE]
        v01 = kv_ref[unit, :, TILE : 2 * TILE]
        k2 = kv_ref[unit, :, 2 * TILE : 3 * TILE]
        v2 = kv_ref[unit, :, 3 * TILE :]
        if masked:
            live = live_of(seg_row, unit, query_start, part, rows, c)
        scores = [mm(k2 if h == 2 else k01, qb[h]) for h in range(TRIO)]
        dprobs = [mm(v2 if h == 2 else v01, db[h]) for h in range(TRIO)]
        probs = []
        grads = []
        for h in range(TRIO):
            score = scores[h]
            if masked:
                score = jnp.where(live, score, NEG_BIG)
            prob = jnp.exp(score - lse_ref[0, h : h + 1])
            if masked:
                prob = jnp.where(live, prob, 0.0)
            probs.append(prob.astype(BF))
            grads.append((prob * (dprobs[h] - delta[h : h + 1])).astype(BF))
        dv01[unit] += mm(jnp.concatenate(probs[:2], 1), dn[: 2 * rows])
        dk01[unit] += mm(jnp.concatenate(grads[:2], 1), qn[: 2 * rows])
        dv2[unit] += mm(probs[2], dn[2 * rows :])
        dk2[unit] += mm(grads[2], qn[2 * rows :])
        for h in range(TRIO):
            kth = kt[unit, h * HEAD_DIM : (h + 1) * HEAD_DIM]
            dqt[h * HEAD_DIM : (h + 1) * HEAD_DIM] += mm(kth, grads[h])

    unit_loop(meta, part, units, rows, step)
    own_ref[j, :, 0:TILE] = (dqt[:TILE] * scale).T.astype(BF)
    dq2 = dqt[TILE:] * scale
    dk2[j, 0:rows] += jnp.concatenate([dq2, jnp.zeros_like(dq2)], 0).T

    @pl.when(j == units - 1)
    def _():
        for unit in range(units):
            for i in range(part):
                span = slice(i * rows, (i + 1) * rows)
                for t, ref in enumerate((dk01, dv01, dk2, dv2)):
                    tile = ref[unit, span].astype(BF)
                    if i == 0:
                        own_ref[unit, :, (t + 1) * TILE : (t + 2) * TILE] = tile
                    else:
                        oth_ref[i - 1, unit, :, t * TILE : (t + 1) * TILE] = tile


def whole_spec(shape):
    zeros = (0,) * len(shape)
    return pl.BlockSpec(shape, lambda j, meta: zeros)


def attend_forward(meta, packed, kv, seg):
    units, rows, unused = packed.shape
    part = len(kv)
    return pl.pallas_call(
        functools.partial(forward_kernel, part, units),
        grid_spec=pltpu.PrefetchScalarGridSpec(
            num_scalar_prefetch=1,
            grid=(units,),
            in_specs=[
                pl.BlockSpec((1, rows, PACK), lambda j, meta: (j, 0, 0)),
                *[whole_spec(piece.shape) for piece in kv],
                pl.BlockSpec((1, 1, rows), lambda j, meta: (j, 0, 0)),
            ],
            out_specs=[
                pl.BlockSpec((1, rows, OPACK), lambda j, meta: (j, 0, 0)),
                pl.BlockSpec((1, TRIO * HEAD_DIM, rows), lambda j, meta: (j, 0, 0)),
                pl.BlockSpec((1, 8, rows), lambda j, meta: (j, 0, 0)),
            ],
            scratch_shapes=[
                pltpu.VMEM((units, part * rows, PACK - TILE), BF),
                pltpu.VMEM((TRIO, TILE, rows), BF),
                pltpu.VMEM((units, TRIO * HEAD_DIM, part * rows), BF),
                pltpu.VMEM((8, rows), F32),
                pltpu.VMEM((8, rows), F32),
                pltpu.VMEM((TRIO, HEAD_DIM, rows), F32),
            ],
        ),
        out_shape=[
            jax.ShapeDtypeStruct((units, rows, OPACK), BF),
            jax.ShapeDtypeStruct((units, TRIO * HEAD_DIM, rows), F32),
            jax.ShapeDtypeStruct((units, 8, rows), F32),
        ],
        compiler_params=params_of("arbitrary"),
        cost_estimate=pl.CostEstimate(
            flops=48 * units * units * part * rows * rows * HEAD_DIM * TRIO, bytes_accessed=0, transcendentals=0
        ),
        name="attend_forward",
    )(meta, packed, *kv, seg)


def attend_backward(meta, packed, dout, out_t, lse, kv, seg):
    units, rows, unused = packed.shape
    part = len(kv)
    others = (max(part - 1, 1), units, rows, 4 * TILE)
    grads = pltpu.VMEM((units, part * rows, TILE), F32)
    return pl.pallas_call(
        functools.partial(backward_kernel, part, units),
        grid_spec=pltpu.PrefetchScalarGridSpec(
            num_scalar_prefetch=1,
            grid=(units,),
            in_specs=[
                pl.BlockSpec((1, rows, PACK), lambda j, meta: (j, 0, 0)),
                pl.BlockSpec((1, rows, OPACK), lambda j, meta: (j, 0, 0)),
                pl.BlockSpec((1, TRIO * HEAD_DIM, rows), lambda j, meta: (j, 0, 0)),
                pl.BlockSpec((1, 8, rows), lambda j, meta: (j, 0, 0)),
                *[whole_spec(piece.shape) for piece in kv],
                pl.BlockSpec((1, 1, rows), lambda j, meta: (j, 0, 0)),
            ],
            out_specs=[whole_spec(packed.shape), whole_spec(others)],
            scratch_shapes=[
                pltpu.VMEM((units, part * rows, PACK - TILE), BF),
                pltpu.VMEM((TRIO, TILE, rows), BF),
                pltpu.VMEM((TRIO, TILE, rows), BF),
                pltpu.VMEM((TRIO * rows, TILE), BF),
                pltpu.VMEM((TRIO * rows, TILE), BF),
                pltpu.VMEM((units, TRIO * HEAD_DIM, part * rows), BF),
                pltpu.VMEM((8, rows), F32),
                pltpu.VMEM((TRIO * HEAD_DIM, rows), F32),
                grads,
                grads,
                grads,
                grads,
            ],
        ),
        out_shape=[
            jax.ShapeDtypeStruct(packed.shape, BF),
            jax.ShapeDtypeStruct(others, BF),
        ],
        compiler_params=params_of("arbitrary"),
        cost_estimate=pl.CostEstimate(
            flops=63 * units * units * part * rows * rows * HEAD_DIM * TRIO, bytes_accessed=0, transcendentals=0
        ),
        name="attend_backward",
    )(meta, packed, dout, out_t, lse, *kv, seg)


def pack_kernel(trios, groups, w_ref, vec_ref, early_ref, local_ref):
    d = w_ref.shape[1] // 3
    w = w_ref[...].astype(F32)
    width = TRIO * HEAD_DIM
    zeros = jnp.zeros((w.shape[0], HEAD_DIM), F32)
    for g in range(trios):
        q, k, v = (w[:, i * d + g * width : i * d + (g + 1) * width] for i in range(3))
        tiles = [q[:, :TILE], k[:, :TILE], v[:, :TILE]]
        tiles.append(jnp.concatenate([q[:, TILE:], k[:, TILE:]], 1))
        tiles.append(jnp.concatenate([v[:, TILE:], zeros], 1))
        for t, tile in enumerate(tiles):
            tile = tile.astype(BF)
            local_ref[:, g * PACK + t * TILE : g * PACK + (t + 1) * TILE] = tile
            for s in range(groups):
                early_ref[s * trios + g, :, t * TILE : (t + 1) * TILE] = tile
        for s in range(groups):
            early_ref[s * trios + g, :, PACK:] = vec_ref[s]


def pack_early(weight, vec, trios):
    r = weight.shape[0]
    groups = vec.shape[0]
    return pl.pallas_call(
        functools.partial(pack_kernel, trios, groups),
        out_shape=[
            jax.ShapeDtypeStruct((trios * groups, r, PACK + TILE), BF),
            jax.ShapeDtypeStruct((r, trios * PACK), BF),
        ],
        name="pack_early",
    )(weight, vec)


def feed_kernel(
    x_ref, cot_ref, up_ref, down_ref, shift_ref, hid_ref, pre_ref, sum_ref, second_ref, back_ref
):
    pre = mm(x_ref[...], up_ref[...]) + shift_ref[...]
    grad = inner_back(cot_ref[...], down_ref[...])
    cdf = 0.5 * (1.0 + lax.erf(pre * math.sqrt(0.5)))
    hidden = (pre * cdf).astype(BF)
    slope = cdf + pre * (jnp.exp(-0.5 * pre * pre) * (1.0 / math.sqrt(2.0 * math.pi)))
    pre_grad = (grad * slope).astype(BF)
    hid_ref[...] = hidden
    pre_ref[...] = pre_grad
    sum_ref[...] = jnp.sum(pre_grad.astype(F32), 0, keepdims=True)
    second = mm(hidden, down_ref[...])
    back = inner_back(pre_grad, up_ref[...])

    @pl.when(pl.program_id(0) == 0)
    def _():
        second_ref[...] = second
        back_ref[...] = back

    @pl.when(pl.program_id(0) > 0)
    def _():
        second_ref[...] += second
        back_ref[...] += back


def feed_forward(x, cot, weights, shift, blocks):
    rows, d = x.shape
    ff = blocks * d
    half = d // 2
    wide = pl.BlockSpec((rows, d), lambda i: (0, 0))
    column = pl.BlockSpec((rows, half), lambda i: (0, i))
    line = pl.BlockSpec((1, half), lambda i: (0, i))
    return pl.pallas_call(
        feed_kernel,
        grid=(2 * blocks,),
        in_specs=[
            wide,
            wide,
            pl.BlockSpec((d, half), lambda i: (0, i)),
            pl.BlockSpec((half, d), lambda i: (i % 2, blocks + i // 2)),
            line,
        ],
        out_specs=[column, column, line, wide, wide],
        out_shape=[
            jax.ShapeDtypeStruct((rows, ff), BF),
            jax.ShapeDtypeStruct((rows, ff), BF),
            jax.ShapeDtypeStruct((1, ff), F32),
            jax.ShapeDtypeStruct((rows, d), F32),
            jax.ShapeDtypeStruct((rows, d), F32),
        ],
        compiler_params=params_of("arbitrary"),
        cost_estimate=pl.CostEstimate(
            flops=8 * rows * d * ff, bytes_accessed=4 * d * ff, transcendentals=2 * rows * ff
        ),
        name="feed_forward",
    )(x, cot, weights, weights, shift)


def gradient_kernel(ups, norm_ref, pre_ref, hidden_ref, cot_ref, out_ref):
    i = pl.program_id(0)

    @pl.when(i < ups)
    def _():
        out_ref[...] = outer_sum(norm_ref[...], pre_ref[...]).astype(BF)

    @pl.when(i >= ups)
    def _():
        out_ref[...] = outer_sum(hidden_ref[...], cot_ref[...]).astype(BF)


def gradients(normed, pre_grad, hidden, cot):
    rows, d = normed.shape
    width = d // 2
    ups = hidden.shape[1] // width

    def down(i):
        return jnp.clip(i - ups, 0, ups - 1)

    return pl.pallas_call(
        functools.partial(gradient_kernel, ups),
        grid=(2 * ups,),
        in_specs=[
            pl.BlockSpec((rows, d), lambda i: (0, 0)),
            pl.BlockSpec((rows, width), lambda i: (0, jnp.minimum(i, ups - 1))),
            pl.BlockSpec((rows, d), lambda i: (0, down(i) // 2)),
            pl.BlockSpec((rows, width), lambda i: (0, down(i) % 2)),
        ],
        out_specs=pl.BlockSpec((d, width), lambda i: (0, i)),
        out_shape=jax.ShapeDtypeStruct((d, 2 * ups * width), BF),
        compiler_params=params_of("arbitrary"),
        cost_estimate=pl.CostEstimate(
            flops=4 * rows * d * ups * width, bytes_accessed=0, transcendentals=0
        ),
        name="gradients",
    )(normed, pre_grad, hidden, cot)


def trio_kernel(norm_ref, hat_ref, grad_ref, w_ref, vec_ref, late_ref, shift_ref, own, hat):
    j = pl.program_id(0)
    d = norm_ref.shape[2]
    grad = grad_ref[...].reshape(-1, PACK)
    own_part = outer_sum(norm_ref[...].reshape(-1, d), grad)
    hat_part = outer_sum(hat_ref[...].reshape(-1, d), grad)
    sums = jnp.sum(grad.astype(F32), 0, keepdims=True)

    @pl.when(j == 0)
    def _():
        own[...] = own_part
        hat[...] = hat_part
        shift_ref[...] = sums

    @pl.when(j > 0)
    def _():
        own[...] += own_part
        hat[...] += hat_part
        shift_ref[...] += sums

    @pl.when(j == pl.num_programs(0) - 1)
    def _():
        late_ref[:, :PACK] = own[...].astype(BF)
        weight = w_ref[...].astype(F32)
        lane = lane_of(vec_ref.shape)
        vec = vec_ref[...]
        vec = jnp.where(lane == 0, jnp.sum(weight * hat[...], 1, keepdims=True), vec)
        vec = jnp.where(lane == 1, jnp.sum(weight * shift_ref[...], 1, keepdims=True), vec)
        late_ref[:, PACK:] = vec.astype(BF)


def trio_gradient(normed, hat, grad, weight, vec):
    units, rows, d = normed.shape
    tok_spec = pl.BlockSpec((2, rows, d), lambda j: (j, 0, 0))
    return pl.pallas_call(
        trio_kernel,
        grid=(units // 2,),
        in_specs=[
            tok_spec,
            tok_spec,
            pl.BlockSpec((2, rows, PACK), lambda j: (j, 0, 0)),
            pl.BlockSpec((d, PACK), lambda j: (0, 0)),
            pl.BlockSpec((d, TILE), lambda j: (0, 0)),
        ],
        out_specs=[
            pl.BlockSpec((d, PACK + TILE), lambda j: (0, 0)),
            pl.BlockSpec((1, PACK), lambda j: (0, 0)),
        ],
        scratch_shapes=[pltpu.VMEM((d, PACK), F32), pltpu.VMEM((d, PACK), F32)],
        out_shape=[
            jax.ShapeDtypeStruct((d, PACK + TILE), BF),
            jax.ShapeDtypeStruct((1, PACK), F32),
        ],
        compiler_params=params_of("arbitrary"),
        cost_estimate=pl.CostEstimate(
            flops=12 * units * rows * d * PACK, bytes_accessed=0, transcendentals=0
        ),
        name="trio_gradient",
    )(normed, hat, grad, weight, vec)


def pack_columns(matrix, trios):
    r = matrix.shape[0]
    q, k, v = (
        part.reshape(r, trios, TRIO * HEAD_DIM) for part in jnp.split(matrix, 3, axis=1)
    )
    zeros = jnp.zeros((r, trios, HEAD_DIM), matrix.dtype)
    pieces = [q[..., :TILE], k[..., :TILE], v[..., :TILE], q[..., TILE:], k[..., TILE:]]
    return jnp.concatenate(pieces + [v[..., TILE:], zeros], -1).reshape(r, trios * PACK)


def unpack_columns(matrix, trios):
    r = matrix.shape[0]
    m = matrix.reshape(r, trios, PACK)
    halves = [
        m[..., 3 * TILE : 3 * TILE + HEAD_DIM],
        m[..., 3 * TILE + HEAD_DIM : 4 * TILE],
        m[..., 4 * TILE : 4 * TILE + HEAD_DIM],
    ]
    return jnp.concatenate(
        [
            jnp.concatenate([m[..., i * TILE : (i + 1) * TILE], halves[i]], -1).reshape(r, -1)
            for i in range(3)
        ],
        -1,
    )


def split_hidden(matrix, count, r):
    lead = matrix.shape[0]
    return matrix.reshape(lead, count, -1, r).transpose(0, 2, 1, 3).reshape(lead, -1)


def join_hidden(matrix, count, r):
    lead = matrix.shape[0]
    return matrix.reshape(lead, -1, count, r).transpose(0, 2, 1, 3).reshape(lead, -1)


def on_device(
    tokens,
    segment,
    ln1_gain,
    ln1_bias,
    ln2_gain,
    ln2_bias,
    qkv_weight,
    qkv_bias,
    dense_weight,
    dense_bias,
    fc1_weight,
    fc1_bias,
    output_feed_weight,
    output_feed_bias,
    cotangent,
):
    rows, groups, d = tokens.shape
    units = lax.axis_size("unit")
    part = lax.axis_size("part")
    count = units * part * lax.axis_size("seq")
    trios = units // groups
    all_rows = rows * groups
    r = qkv_weight.shape[0]
    ff = fc1_weight.shape[1]
    blocks = ff // d
    c = lax.axis_index("part")
    unit = lax.axis_index("unit")

    seq = lax.axis_index("seq")
    seqs = lax.axis_size("seq")
    place = (seq * units + unit) * part + c

    def exchange(blocks_out):
        width = blocks_out.shape[-1]
        return lax.all_to_all(
            blocks_out.reshape(-1, width), "unit", 0, 0, tiled=True
        ).reshape(blocks_out.shape)

    def shift(value, axis, i):
        n = lax.axis_size(axis)
        return lax.ppermute(value, axis, [(p, (p + i) % n) for p in range(n)])

    def flip_unit(value, bit):
        return lax.ppermute(value, "unit", [(u, u ^ bit) for u in range(units)])

    def pick(value, index, axis):
        return lax.dynamic_index_in_dim(value, index, axis, False)

    bits = (unit // trios, unit // 2 % 2, unit % 2)

    def exchange_small(value):
        shape = value.shape
        value = value.reshape((2, 2, 2) + shape[1:])
        for axis, bit in enumerate((trios, 2, 1)):
            keep = pick(value, bits[axis], axis)
            value = jnp.stack([keep, flip_unit(pick(value, 1 - bits[axis], axis), bit)], axis)
        for axis in range(3):
            value = jnp.where(bits[axis] == 0, value, jnp.flip(value, axis))
        return value.reshape(shape)

    def spread_tokens(value):
        keep = pick(value, bits[0], 0)
        both = jnp.stack([keep, flip_unit(pick(value, 1 - bits[0], 0), trios)])
        one, two = both[:, : rows // 2], both[:, rows // 2 :]
        one = jnp.stack([one, flip_unit(one, 2)])
        two = jnp.stack([two, flip_unit(two, 1)])
        one = jnp.stack([one, flip_unit(one, 1)])
        two = jnp.stack([two, flip_unit(two, 2)])
        return one.reshape(units, rows // 2, d), two.reshape(units, rows // 2, d)

    def add(a, b):
        return (a.astype(F32) + b.astype(F32)).astype(BF)

    def natural_order(got, me):
        n = len(got)
        if n == 2:
            return jnp.where(me == 0, jnp.stack(got), jnp.stack(got[::-1]))
        ring = jnp.stack((got + got)[::-1])
        return lax.dynamic_slice_in_dim(ring, n - 1 - me, n, 0)

    def gather_small(value, axis):
        n = lax.axis_size(axis)
        got = [value] + [shift(value, axis, i) for i in range(1, n)]
        return natural_order(got, lax.axis_index(axis))

    def swap_parts(value):
        got = [lax.dynamic_index_in_dim(value, c, 0, False)]
        for i in range(1, part):
            piece = lax.dynamic_index_in_dim(value, (c + i) % part, 0, False)
            got.append(shift(piece, "part", i))
        return natural_order(got, c)

    def all_parts(value):
        return jnp.concatenate([value] + [shift(value, "part", i) for i in range(1, part)], 0)

    def part_pieces(value):
        n = value.shape[0] // part
        return [value[:n]] + [
            shift(value[i * n : (i + 1) * n], "part", part - i) for i in range(1, part)
        ]

    def halve(value, axis, which):
        if which is None:
            me = lax.axis_index("seq")
            return [pick(value, me, axis)] + [
                shift(pick(value, (me + i) % seqs, axis), "seq", i) for i in range(1, seqs)
            ]
        away = pick(value, 1 - bits[which], axis)
        return [pick(value, bits[which], axis), flip_unit(away, (trios, 2, 1)[which])]

    def add_up(pieces):
        total = pieces[0].astype(F32)
        for piece in pieces[1:]:
            total = total + piece.astype(F32)
        return total.astype(BF)

    def scatter_small(value, axis):
        n = lax.axis_size(axis)
        me = lax.axis_index(axis)
        total = lax.dynamic_index_in_dim(value, me, 0, False).astype(F32)
        for i in range(1, n):
            piece = lax.dynamic_index_in_dim(value, (me + i) % n, 0, False)
            total = total + shift(piece, axis, i).astype(F32)
        return total.astype(BF)

    vectors = (ln1_gain, ln1_bias, ln2_gain, ln2_bias, dense_bias, output_feed_bias)
    vec = jnp.concatenate(
        [v.reshape(r, 1) for v in vectors] + [qkv_bias.reshape(r, 3), fc1_bias.reshape(r, blocks)],
        1,
    )
    token_rows = tokens.transpose(1, 0, 2)
    seg_rows = segment.T
    seg_lanes = -(-2 * rows // r)
    seg_pack = jnp.concatenate([seg_rows // 64, seg_rows % 64], 1).astype(BF)
    seg_pack = jnp.pad(seg_pack, ((0, 0), (0, seg_lanes * r - 2 * rows)))
    seg_pack = seg_pack.reshape(groups, r, seg_lanes)
    vec = jnp.pad(vec, ((0, 0), (0, 16 - vec.shape[1])))
    vec = jnp.concatenate(
        [
            jnp.broadcast_to(vec, (groups, r, 16)),
            seg_pack,
            jnp.zeros((groups, r, TILE - 16 - seg_lanes), BF),
        ],
        -1,
    )
    early, qkv_local = pack_early(qkv_weight, vec, trios)
    early = exchange_small(early)
    toks = spread_tokens(token_rows)

    seg_mine = early[:, :, PACK + 16 : PACK + 16 + seg_lanes].astype(jnp.int32)
    seg_mine = seg_mine.reshape(units, r * seg_lanes)
    seg_mine = seg_mine[:, :rows] * 64 + seg_mine[:, rows : 2 * rows]
    meta = jnp.concatenate([seg_mine[:, 0], seg_mine[:, -1], c[None]])
    seg_mine = seg_mine[:, None, :]
    trio_full = gather_small(gather_small(early, "seq"), "part")
    trio_full = trio_full.transpose(1, 2, 0, 3, 4).reshape(d, PACK + TILE)
    vec_full = trio_full[:, PACK:].astype(F32)
    vec_rows = vec_full[:, :8].T
    gain_one, bias_one, gain_two, bias_two, dense_shift, down_shift = (
        vec_rows[i : i + 1] for i in range(6)
    )
    qkv_shift = pack_columns(vec_full[:, 6:9].reshape(1, 3 * d), trios).reshape(trios, PACK)
    qkv_shift = lax.dynamic_slice_in_dim(qkv_shift, unit % trios, 1, 0)
    up_shift = split_hidden(vec_full[:, 9 : 9 + blocks].reshape(1, ff), count, r)

    feed_blocks = output_feed_weight.reshape(blocks, r, d)
    half = blocks // part
    up_local = split_hidden(fc1_weight, count, r)
    second_pack = jnp.stack(
        [
            jnp.concatenate(
                [up_local[:, p * half * d : (p + 1) * half * d]]
                + [feed_blocks[b] for b in range(p * half, (p + 1) * half)]
                + [dense_weight],
                1,
            )
            for p in range(part)
        ]
    )
    second_pack = swap_parts(second_pack).reshape(part * r, -1)
    second = lax.all_gather(second_pack, ("seq", "unit"), axis=0, tiled=True)
    block_start = (jnp.arange(units, dtype=jnp.int32) * part + c) * rows
    positions = block_start[:, None, None] + jnp.arange(rows, dtype=jnp.int32) - seg_mine
    freq = jnp.arange(ROT // 2, dtype=F32)
    inverse = jnp.exp(freq * (-2.0 * math.log(10000.0) / ROT))
    angles = positions.astype(F32) * inverse[None, :, None]
    cos = jnp.cos(angles)
    sin = jnp.sin(angles)

    place_unit = unit[None]
    packed, kv_own, normed_one, hat_one = project(
        place_unit, toks, trio_full, qkv_shift, gain_one, bias_one, cos, sin
    )
    packed, second = lax.optimization_barrier((packed, second))
    dense_pad = jnp.pad(
        second[:, 2 * half * d :].reshape(trios, d // trios, d),
        ((0, 0), (0, OPACK - d // trios), (0, 0)),
    )
    kv = [kv_own] + [shift(kv_own, "part", i) for i in range(1, part)]

    x = token_rows.reshape(all_rows, d).astype(F32)
    cot = cotangent.transpose(1, 0, 2).reshape(all_rows, d)
    centre = x - jnp.mean(x, -1, keepdims=True)
    spread = lax.rsqrt(jnp.mean(centre * centre, -1, keepdims=True) + EPSILON)
    xhat = centre * spread
    normed_two = (xhat * gain_two + bias_two).astype(BF)
    attended_grad = jnp.einsum(
        "sld,gkd->sglk", cot.reshape(groups, rows, d), dense_pad, preferred_element_type=F32
    ).astype(BF)
    dout = exchange(attended_grad.reshape(units, rows, OPACK))
    normed_all = all_parts(normed_two)
    cot_all = all_parts(cot)
    up_shift = lax.dynamic_slice_in_dim(up_shift, c * half * d, half * d, 1)
    hidden_low, pre_grad, up_shift_grad, second_branch, normed_two_grad = feed_forward(
        normed_all, cot_all, second, up_shift, half
    )
    hidden_low, pre_grad, dout = lax.optimization_barrier((hidden_low, pre_grad, dout))
    second_branch = part_pieces(second_branch)
    normed_two_grad = part_pieces(normed_two_grad)
    def norm_back(grad, gain):
        gy = grad * gain
        return spread * (
            gy - jnp.mean(gy, -1, keepdims=True) - xhat * jnp.mean(gy * xhat, -1, keepdims=True)
        )

    mlp_grads = gradients(normed_all, pre_grad, hidden_low, cot_all)
    split = (seqs, 2, 2, 2, part * r, half * d)
    up_part = halve(mlp_grads[:, : half * d].reshape(split), 0, None)
    down_part = halve(mlp_grads[:, half * d :].reshape(split), 3, 2)
    out_low, out_t, lse = attend_forward(meta, packed, kv, seg_mine)
    up_part, down_part, lse = lax.optimization_barrier((up_part, down_part, lse))
    up_part = halve(add_up(up_part), 2, 2)
    down_part = halve(add_up(down_part), 0, None)
    own, others = attend_backward(meta, packed, dout, out_t, lse, kv, seg_mine)
    others = [shift(others[i - 1], "part", part - i) for i in range(1, part)]
    up_part, down_part, own = lax.optimization_barrier((up_part, down_part, own))
    mlp_part = jnp.concatenate([add_up(up_part), add_up(down_part)], -1)
    mlp_part = halve(mlp_part, 1, 1)
    qkv_grad, back_one, back_two = unturn(place_unit, own, others, trio_full, cos, sin)
    back_one = back_one.reshape(2, 2, 2, rows // 2, d)
    back_two = back_two.reshape(2, 2, 2, rows // 2, d)
    swapped = flip_unit(back_one[1], 1), flip_unit(back_two[1], 2)

    out_low, second_branch, normed_two_grad, qkv_grad, cot, up_shift_grad = (
        lax.optimization_barrier(
            (out_low, second_branch, normed_two_grad, qkv_grad, cot, up_shift_grad)
        )
    )
    attended = exchange(out_low)
    cot_float = cot.astype(F32)
    up_shift_grad = lax.dynamic_update_slice_in_dim(
        jnp.zeros((1, ff), F32), up_shift_grad, c * half * d, 1
    )
    normed_two_grad = sum(normed_two_grad)
    vec_grads = jnp.concatenate(
        [
            jnp.zeros((2, d), F32),
            jnp.sum(normed_two_grad * xhat, 0)[None],
            jnp.sum(normed_two_grad, 0)[None],
            jnp.sum(cot_float, 0)[None],
            jnp.zeros((3, d), F32),
        ],
        0,
    ).T
    up_shift_grad = join_hidden(up_shift_grad, count, r).reshape(d, blocks)

    vec_grads = jnp.concatenate(
        [vec_grads, up_shift_grad, jnp.zeros((d, TILE - 8 - blocks), F32)], 1
    )
    late, shift_grad = trio_gradient(normed_one, hat_one, qkv_grad, trio_full, vec_grads)
    swapped, late, mlp_part = lax.optimization_barrier((swapped, late, mlp_part))
    mlp_part = halve(add_up(mlp_part), 0, 0)
    back_one = add(back_one[0], swapped[0])
    back_two = add(back_two[0], swapped[1])
    swapped = flip_unit(back_one[1], 2), flip_unit(back_two[1], 1)
    late = late.reshape(seqs, units, part, r, -1)
    shift_rows = jnp.pad(shift_grad.astype(BF), ((0, 7), (0, TILE)))
    late = jnp.concatenate(
        [late, jnp.broadcast_to(shift_rows, (seqs, units, part) + shift_rows.shape)], 3
    )
    late = scatter_small(late.transpose(2, 0, 1, 3, 4), "part")
    swapped, late, attended, mlp_part = lax.optimization_barrier(
        (swapped, late, attended, mlp_part)
    )
    mlp_sum = swap_parts(add_up(mlp_part).reshape(part, r, -1))
    both = jnp.concatenate(
        [add(back_one[0], swapped[0]), add(back_two[0], swapped[1])], 1
    )
    swapped = flip_unit(both[1], trios)
    late = scatter_small(late, "seq")
    attended = attended.reshape(groups, trios, rows, OPACK).transpose(0, 2, 1, 3)
    attended = attended.reshape(all_rows, trios * OPACK)
    dense_grad = outer_sum(attended, cot).reshape(trios, OPACK, d)[:, : d // trios]
    dense_grad = dense_grad.astype(BF).reshape(seqs, units, part, r, d)
    dense_grad = scatter_small(dense_grad.transpose(2, 0, 1, 3, 4), "part")
    swapped, late, dense_grad, mlp_sum = lax.optimization_barrier(
        (swapped, late, dense_grad, mlp_sum)
    )
    back = jnp.where(
        bits[0] == 0, jnp.stack([both[0], swapped]), jnp.stack([swapped, both[0]])
    )
    late = exchange_small(late).astype(F32)
    dense_sum = exchange_small(scatter_small(dense_grad, "seq")).astype(F32)
    dense_sum = jnp.sum(dense_sum, 0)
    branch_one = mm(attended, dense_pad.reshape(trios * OPACK, d)) + dense_shift
    output = (x + branch_one + sum(second_branch) + down_shift).astype(BF)
    in_two = norm_back(normed_two_grad, gain_two)
    late = jnp.sum(late.reshape(groups, trios, r + 8, PACK + TILE), 0)
    qkv_weight_grad = unpack_columns(
        late[:, :r, :PACK].transpose(1, 0, 2).reshape(r, trios * PACK), trios
    )
    late_vec = jnp.sum(late[:, :r, PACK:], 0)
    qkv_shift_grad = unpack_columns(late[:, r, :PACK].reshape(1, trios * PACK), trios)[0]
    qkv_shift_grad = lax.dynamic_slice_in_dim(qkv_shift_grad, place * 3 * r, 3 * r)

    mlp_sum = mlp_sum.astype(F32)
    up_sum = jnp.concatenate([mlp_sum[p, :, : half * d] for p in range(part)], 1)
    down_sum = jnp.concatenate(
        [
            mlp_sum[p, :, (half + b) * d : (half + b + 1) * d]
            for p in range(part)
            for b in range(half)
        ],
        0,
    )
    param_grads = (
        late_vec[:, 0],
        late_vec[:, 1],
        late_vec[:, 2],
        late_vec[:, 3],
        qkv_weight_grad,
        qkv_shift_grad,
        dense_sum,
        late_vec[:, 4],
        join_hidden(up_sum, count, r),
        late_vec[:, 8 : 8 + blocks].reshape(-1),
        down_sum,
        late_vec[:, 4],
    )

    normed_one_grad = back.reshape(all_rows, d).astype(F32)
    in_one = norm_back(normed_one_grad, gain_one)
    tokens_grad = (cot_float + in_one + in_two).astype(BF)

    def natural(value):
        return value.reshape(groups, rows, d).transpose(1, 0, 2)

    return (natural(output), natural(tokens_grad)) + tuple(param_grads)


def solution(mesh):
    devices = mesh.devices
    seq_size, ctx_size = devices.shape
    ctx = ("unit", "part")
    tok = P(ctx, "seq", None)
    vec = P(ALL_AXES)
    mat = P(ALL_AXES, None)
    pairs = (vec, vec, vec, vec, mat, vec, mat, vec, mat, vec, mat, vec)

    def run(tokens, *rest):
        units = HEADS // TRIO * (tokens.shape[1] // seq_size)
        split = Mesh(devices.reshape(seq_size, units, ctx_size // units), ALL_AXES)
        mapped = jax.shard_map(
            on_device,
            mesh=split,
            in_specs=(tok, P(ctx, "seq")) + pairs + (tok,),
            out_specs=(tok, tok) + pairs,
            check_vma=False,
        )
        return mapped(tokens, *rest)

    return run
```

```python
import functools
import math

import jax
import jax.numpy as jnp
from jax import lax
from jax.experimental import pallas as pl
from jax.experimental.pallas import tpu as pltpu
from jax.sharding import Mesh, PartitionSpec as P

HEADS = 12
HEAD_DIM = 64
ROT = 16
TRIO = 3
TILE = 128
PACK = 5 * TILE
OPACK = 2 * TILE

EPSILON = 1e-05
NEG_BIG = -1e30
BF = jnp.bfloat16
F32 = jnp.float32
ALL_AXES = ("seq", "unit", "part")
VMEM_BYTES = 56 * 1024 * 1024


def params_of(*semantics):
    return pltpu.CompilerParams(
        dimension_semantics=semantics, vmem_limit_bytes=VMEM_BYTES
    )


def mm(a, b):
    return jnp.dot(a, b, preferred_element_type=F32)


def outer_sum(left_rows, right_rows):
    return lax.dot_general(
        left_rows, right_rows, (((0,), (0,)), ((), ())), preferred_element_type=F32
    )


def inner_back(grad_rows, weight):
    return lax.dot_general(
        grad_rows, weight, (((1,), (1,)), ((), ())), preferred_element_type=F32
    )


def lane_of(shape):
    return lax.broadcasted_iota(jnp.int32, shape, len(shape) - 1)


def turn(tile, cos, sin):
    partner = jnp.where(
        lane_of(tile.shape) % HEAD_DIM < ROT // 2,
        pltpu.roll(tile, TILE - ROT // 2, 1),
        pltpu.roll(tile, ROT // 2, 1),
    )
    return tile * cos + partner * sin


def turn_tables(cos_rows, sin_rows):
    rows = cos_rows.shape[1]
    rest = HEAD_DIM - ROT
    cos_head = [cos_rows, cos_rows, jnp.ones((rest, rows), F32)]
    sin_head = [-sin_rows, sin_rows, jnp.zeros((rest, rows), F32)]
    return jnp.concatenate(cos_head * 2, 0).T, jnp.concatenate(sin_head * 2, 0).T


def first_place(rel):
    return rel % 2 * 4 + rel // 2 % 2 * 2 + rel // 4


def second_place(rel):
    return rel // 2 % 2 * 4 + rel % 2 * 2 + rel // 4


def project_kernel(
    place_ref,
    one_ref,
    two_ref,
    w_ref,
    b_ref,
    gain_ref,
    bias_ref,
    cos_ref,
    sin_ref,
    out_ref,
    kv_ref,
    norm_ref,
    hat_ref,
):
    x = jnp.concatenate([one_ref[0], two_ref[0]], 0).astype(F32)
    centre = x - jnp.mean(x, -1, keepdims=True)
    spread = jnp.mean(centre * centre, -1, keepdims=True)
    hat = centre * lax.rsqrt(spread + EPSILON)
    normed = (hat * gain_ref[...] + bias_ref[...]).astype(BF)
    hat_ref[0] = hat.astype(BF)
    norm_ref[0] = normed
    y = mm(normed, w_ref[...]) + b_ref[...]
    cos, sin = turn_tables(cos_ref[0], sin_ref[0])
    for t in range(5):
        tile = y[:, t * TILE : (t + 1) * TILE]
        if t in (0, 1, 3):
            tile = turn(tile, cos, sin)
        tile = tile.astype(BF)
        out_ref[0, :, t * TILE : (t + 1) * TILE] = tile
        if t > 0:
            kv_ref[0, :, (t - 1) * TILE : t * TILE] = tile


def half_specs(rows, d):
    return [
        pl.BlockSpec((1, rows // 2, d), lambda j, place: (first_place(j ^ place[0]), 0, 0)),
        pl.BlockSpec((1, rows // 2, d), lambda j, place: (second_place(j ^ place[0]), 0, 0)),
    ]


def project(place, toks, weight, bias, gain, offset, cos, sin):
    units, unused, rows = cos.shape
    d = toks[0].shape[2]
    tok_spec = pl.BlockSpec((1, rows, d), lambda j, place: (j, 0, 0))
    row_spec = pl.BlockSpec((1, d), lambda j, place: (0, 0))
    turn_spec = pl.BlockSpec((1, ROT // 2, rows), lambda j, place: (j, 0, 0))
    return pl.pallas_call(
        project_kernel,
        grid_spec=pltpu.PrefetchScalarGridSpec(
            num_scalar_prefetch=1,
            grid=(units,),
            in_specs=half_specs(rows, d)
            + [
                pl.BlockSpec((d, PACK), lambda j, place: (0, 0)),
                pl.BlockSpec((1, PACK), lambda j, place: (0, 0)),
                row_spec,
                row_spec,
                turn_spec,
                turn_spec,
            ],
            out_specs=[
                pl.BlockSpec((1, rows, PACK), lambda j, place: (j, 0, 0)),
                pl.BlockSpec((1, rows, PACK - TILE), lambda j, place: (j, 0, 0)),
                tok_spec,
                tok_spec,
            ],
        ),
        out_shape=[
            jax.ShapeDtypeStruct((units, rows, PACK), BF),
            jax.ShapeDtypeStruct((units, rows, PACK - TILE), BF),
            jax.ShapeDtypeStruct((units, rows, d), BF),
            jax.ShapeDtypeStruct((units, rows, d), BF),
        ],
        compiler_params=params_of("arbitrary"),
        cost_estimate=pl.CostEstimate(flops=0, bytes_accessed=0, transcendentals=0),
        name="project",
    )(place, *toks, weight, bias, gain, offset, cos, sin)


def unturn_kernel(place_ref, own_ref, *refs):
    w_ref, cos_ref, sin_ref, out_ref, one_ref, two_ref = refs[-6:]
    others = refs[:-6]
    cos, sin = turn_tables(cos_ref[0], sin_ref[0])
    for t in range(5):
        tile = own_ref[0, :, t * TILE : (t + 1) * TILE].astype(F32)
        if t > 0:
            for other in others:
                tile = tile + other[0, :, (t - 1) * TILE : t * TILE].astype(F32)
        if t in (0, 1, 3):
            tile = turn(tile, cos, -sin)
        out_ref[0, :, t * TILE : (t + 1) * TILE] = tile.astype(BF)
    back = inner_back(out_ref[0], w_ref[...]).astype(BF)
    rows = back.shape[0] // 2
    one_ref[0] = back[:rows]
    two_ref[0] = back[rows:]


def unturn(place, own, others, weight, cos, sin):
    units, rows, unused = own.shape
    d = weight.shape[0]
    turn_spec = pl.BlockSpec((1, ROT // 2, rows), lambda j, place: (j, 0, 0))
    own_spec = pl.BlockSpec((1, rows, PACK), lambda j, place: (j, 0, 0))
    other_spec = pl.BlockSpec((1, rows, PACK - TILE), lambda j, place: (j, 0, 0))
    half = jax.ShapeDtypeStruct((units, rows // 2, d), BF)
    return pl.pallas_call(
        unturn_kernel,
        grid_spec=pltpu.PrefetchScalarGridSpec(
            num_scalar_prefetch=1,
            grid=(units,),
            in_specs=[own_spec]
            + [other_spec] * len(others)
            + [pl.BlockSpec((d, PACK), lambda j, place: (0, 0)), turn_spec, turn_spec],
            out_specs=[own_spec] + half_specs(rows, d),
        ),
        out_shape=[jax.ShapeDtypeStruct(own.shape, BF), half, half],
        compiler_params=params_of("arbitrary"),
        cost_estimate=pl.CostEstimate(flops=0, bytes_accessed=0, transcendentals=0),
        name="unturn",
    )(place, own, *others, weight, cos, sin)


def flip(tile):
    return tile.astype(F32).T


def head_rows(flipped, low):
    row = lax.broadcasted_iota(jnp.int32, flipped.shape, 0)
    keep = row < HEAD_DIM if low else row >= HEAD_DIM
    return jnp.where(keep, flipped, 0.0)


def head_lanes(tile, low):
    lane = lane_of(tile.shape)
    keep = lane < HEAD_DIM if low else lane >= HEAD_DIM
    return jnp.where(keep, tile, 0.0)


def query_sides(q_ref, qb):
    scale = HEAD_DIM ** (-0.5)
    a = flip(q_ref[0, :, 0:TILE]) * scale
    d = flip(q_ref[0, :, 3 * TILE : 4 * TILE]) * scale
    qb[0] = head_rows(a, True).astype(BF)
    qb[1] = head_rows(a, False).astype(BF)
    qb[2] = jnp.concatenate(
        [jnp.zeros((HEAD_DIM, d.shape[1]), F32), d[:HEAD_DIM]], 0
    ).astype(BF)


def live_of(seg_row, unit, query_start, part, rows, c):
    shape = (rows, rows)
    query_pos = query_start + lax.broadcasted_iota(jnp.int32, shape, 1)
    row = lax.broadcasted_iota(jnp.int32, shape, 0)
    pieces = []
    for i in range(part):
        key_pos = (unit * part + lax.rem(c - i + part, part)) * rows + row
        pieces.append((key_pos <= query_pos) & (key_pos >= seg_row))
    return jnp.concatenate(pieces, 0)


def unit_loop(meta, part, units, rows, step):
    j = pl.program_id(0)
    first = meta[j] // (rows * part)
    top_seg = meta[units + j]

    def one(unit, unused):
        masked = (unit == j) | (top_seg > unit * (rows * part))

        @pl.when(masked)
        def _():
            step(unit, True)

        @pl.when(jnp.logical_not(masked))
        def _():
            step(unit, False)

        return unused

    lax.fori_loop(first, j + 1, one, 0)


def join_parts(part, refs, kv_ref):
    rows = refs[0].shape[1]

    def one(unit, unused):
        for i in range(part):
            kv_ref[unit, i * rows : (i + 1) * rows] = refs[i][unit]
        return unused

    lax.fori_loop(0, refs[0].shape[0], one, 0)


def forward_kernel(part, units, meta, q_ref, *refs):
    seg_ref, o_ref, ot_ref, lse_ref, kv_ref, qb, vt, top, total, acc = refs[part:]
    rows = q_ref.shape[1]
    c = meta[2 * units]
    j = pl.program_id(0)

    @pl.when(j == 0)
    def _():
        join_parts(part, refs[:part], kv_ref)

        def turn_values(unit, unused):
            vt[unit, :TILE] = flip(kv_ref[unit, :, TILE : 2 * TILE]).astype(BF)
            vt[unit, TILE:] = flip(kv_ref[unit, :, 3 * TILE :])[:HEAD_DIM].astype(BF)
            return unused

        lax.fori_loop(0, units, turn_values, 0)

    query_sides(q_ref, qb)
    top[...] = jnp.full(top.shape, NEG_BIG, F32)
    total[...] = jnp.zeros(total.shape, F32)
    acc[...] = jnp.zeros(acc.shape, F32)
    seg_row = seg_ref[0]
    query_start = (j * part + c) * rows

    def step(unit, masked):
        k01 = kv_ref[unit, :, 0:TILE]
        k2 = kv_ref[unit, :, 2 * TILE : 3 * TILE]
        if masked:
            live = live_of(seg_row, unit, query_start, part, rows, c)
        scores = [mm(k2 if h == 2 else k01, qb[h]) for h in range(TRIO)]
        if masked:
            scores = [jnp.where(live, score, NEG_BIG) for score in scores]
        old = top[0:TRIO]
        new = jnp.concatenate([jnp.max(score, 0, keepdims=True) for score in scores], 0)
        new = jnp.maximum(old, new)
        factor = jnp.exp(old - new)
        weights = [jnp.exp(scores[h] - new[h : h + 1]) for h in range(TRIO)]
        if masked:
            weights = [jnp.where(live, weight, 0.0) for weight in weights]
        sums = [jnp.sum(weight, 0, keepdims=True) for weight in weights]
        top[0:TRIO] = new
        total[0:TRIO] = total[0:TRIO] * factor + jnp.concatenate(sums, 0)
        for h in range(TRIO):
            vth = vt[unit, h * HEAD_DIM : (h + 1) * HEAD_DIM]
            acc[h] = acc[h] * factor[h : h + 1] + mm(vth, weights[h].astype(BF))

    unit_loop(meta, part, units, rows, step)
    out = [acc[h] / total[h : h + 1] for h in range(TRIO)]
    for h in range(TRIO):
        ot_ref[0, h * HEAD_DIM : (h + 1) * HEAD_DIM] = out[h]
    lse_ref[0, 0:TRIO] = top[0:TRIO] + jnp.log(total[0:TRIO])
    o_ref[0, :, :TILE] = jnp.concatenate(out[:2], 0).T.astype(BF)
    o_ref[0, :, TILE:] = jnp.concatenate([out[2], jnp.zeros_like(out[2])], 0).T.astype(BF)


def backward_kernel(part, units, meta, q_ref, do_ref, ot_ref, lse_ref, *refs):
    seg_ref, own_ref, oth_ref, kv_ref, qb, db, qn, dn, kt, delta, dqt = refs[part : part + 11]
    dk01, dv01, dk2, dv2 = refs[part + 11 :]
    rows = q_ref.shape[1]
    c = meta[2 * units]
    j = pl.program_id(0)

    @pl.when(j == 0)
    def _():
        join_parts(part, refs[:part], kv_ref)

        def turn_keys(unit, unused):
            kt[unit, :TILE] = flip(kv_ref[unit, :, 0:TILE]).astype(BF)
            kt[unit, TILE:] = flip(kv_ref[unit, :, 2 * TILE : 3 * TILE])[HEAD_DIM:].astype(BF)
            return unused

        lax.fori_loop(0, units, turn_keys, 0)
        for ref in (dk01, dv01, dk2, dv2):
            ref[...] = jnp.zeros(ref.shape, F32)

    query_sides(q_ref, qb)
    scale = HEAD_DIM ** (-0.5)
    q01 = q_ref[0, :, 0:TILE].astype(F32) * scale
    q2 = pltpu.roll(q_ref[0, :, 3 * TILE : 4 * TILE].astype(F32), HEAD_DIM, 1) * scale
    qn[0:rows] = head_lanes(q01, True).astype(BF)
    qn[rows : 2 * rows] = head_lanes(q01, False).astype(BF)
    qn[2 * rows :] = head_lanes(q2, False).astype(BF)
    do01 = do_ref[0, :, :TILE].astype(F32)
    do2 = do_ref[0, :, TILE:].astype(F32)
    dn[0:rows] = head_lanes(do01, True).astype(BF)
    dn[rows : 2 * rows] = head_lanes(do01, False).astype(BF)
    dn[2 * rows :] = do2.astype(BF)
    do01t = do01.T
    do2t = do2.T
    db[0] = head_rows(do01t, True).astype(BF)
    db[1] = head_rows(do01t, False).astype(BF)
    db[2] = do2t.astype(BF)
    for h in range(TRIO):
        dot = do2t[:HEAD_DIM] if h == 2 else do01t[h * HEAD_DIM : (h + 1) * HEAD_DIM]
        delta[h : h + 1] = jnp.sum(
            dot * ot_ref[0, h * HEAD_DIM : (h + 1) * HEAD_DIM], 0, keepdims=True
        )
    dqt[...] = jnp.zeros(dqt.shape, F32)
    seg_row = seg_ref[0]
    query_start = (j * part + c) * rows

    def step(unit, masked):
        k01 = kv_ref[unit, :, 0:TILE]
        v01 = kv_ref[unit, :, TILE : 2 * TILE]
        k2 = kv_ref[unit, :, 2 * TILE : 3 * TILE]
        v2 = kv_ref[unit, :, 3 * TILE :]
        if masked:
            live = live_of(seg_row, unit, query_start, part, rows, c)
        scores = [mm(k2 if h == 2 else k01, qb[h]) for h in range(TRIO)]
        dprobs = [mm(v2 if h == 2 else v01, db[h]) for h in range(TRIO)]
        probs = []
        grads = []
        for h in range(TRIO):
            score = scores[h]
            if masked:
                score = jnp.where(live, score, NEG_BIG)
            prob = jnp.exp(score - lse_ref[0, h : h + 1])
            if masked:
                prob = jnp.where(live, prob, 0.0)
            probs.append(prob.astype(BF))
            grads.append((prob * (dprobs[h] - delta[h : h + 1])).astype(BF))
        dv01[unit] += mm(jnp.concatenate(probs[:2], 1), dn[: 2 * rows])
        dk01[unit] += mm(jnp.concatenate(grads[:2], 1), qn[: 2 * rows])
        dv2[unit] += mm(probs[2], dn[2 * rows :])
        dk2[unit] += mm(grads[2], qn[2 * rows :])
        for h in range(TRIO):
            kth = kt[unit, h * HEAD_DIM : (h + 1) * HEAD_DIM]
            dqt[h * HEAD_DIM : (h + 1) * HEAD_DIM] += mm(kth, grads[h])

    unit_loop(meta, part, units, rows, step)
    own_ref[j, :, 0:TILE] = (dqt[:TILE] * scale).T.astype(BF)
    dq2 = dqt[TILE:] * scale
    dk2[j, 0:rows] += jnp.concatenate([dq2, jnp.zeros_like(dq2)], 0).T

    @pl.when(j == units - 1)
    def _():
        for unit in range(units):
            for i in range(part):
                span = slice(i * rows, (i + 1) * rows)
                for t, ref in enumerate((dk01, dv01, dk2, dv2)):
                    tile = ref[unit, span].astype(BF)
                    if i == 0:
                        own_ref[unit, :, (t + 1) * TILE : (t + 2) * TILE] = tile
                    else:
                        oth_ref[i - 1, unit, :, t * TILE : (t + 1) * TILE] = tile


def whole_spec(shape):
    zeros = (0,) * len(shape)
    return pl.BlockSpec(shape, lambda j, meta: zeros)


def attend_forward(meta, packed, kv, seg):
    units, rows, unused = packed.shape
    part = len(kv)
    return pl.pallas_call(
        functools.partial(forward_kernel, part, units),
        grid_spec=pltpu.PrefetchScalarGridSpec(
            num_scalar_prefetch=1,
            grid=(units,),
            in_specs=[
                pl.BlockSpec((1, rows, PACK), lambda j, meta: (j, 0, 0)),
                *[whole_spec(piece.shape) for piece in kv],
                pl.BlockSpec((1, 1, rows), lambda j, meta: (j, 0, 0)),
            ],
            out_specs=[
                pl.BlockSpec((1, rows, OPACK), lambda j, meta: (j, 0, 0)),
                pl.BlockSpec((1, TRIO * HEAD_DIM, rows), lambda j, meta: (j, 0, 0)),
                pl.BlockSpec((1, 8, rows), lambda j, meta: (j, 0, 0)),
            ],
            scratch_shapes=[
                pltpu.VMEM((units, part * rows, PACK - TILE), BF),
                pltpu.VMEM((TRIO, TILE, rows), BF),
                pltpu.VMEM((units, TRIO * HEAD_DIM, part * rows), BF),
                pltpu.VMEM((8, rows), F32),
                pltpu.VMEM((8, rows), F32),
                pltpu.VMEM((TRIO, HEAD_DIM, rows), F32),
            ],
        ),
        out_shape=[
            jax.ShapeDtypeStruct((units, rows, OPACK), BF),
            jax.ShapeDtypeStruct((units, TRIO * HEAD_DIM, rows), F32),
            jax.ShapeDtypeStruct((units, 8, rows), F32),
        ],
        compiler_params=params_of("arbitrary"),
        cost_estimate=pl.CostEstimate(flops=0, bytes_accessed=0, transcendentals=0),
        name="attend_forward",
    )(meta, packed, *kv, seg)


def attend_backward(meta, packed, dout, out_t, lse, kv, seg):
    units, rows, unused = packed.shape
    part = len(kv)
    others = (max(part - 1, 1), units, rows, 4 * TILE)
    grads = pltpu.VMEM((units, part * rows, TILE), F32)
    return pl.pallas_call(
        functools.partial(backward_kernel, part, units),
        grid_spec=pltpu.PrefetchScalarGridSpec(
            num_scalar_prefetch=1,
            grid=(units,),
            in_specs=[
                pl.BlockSpec((1, rows, PACK), lambda j, meta: (j, 0, 0)),
                pl.BlockSpec((1, rows, OPACK), lambda j, meta: (j, 0, 0)),
                pl.BlockSpec((1, TRIO * HEAD_DIM, rows), lambda j, meta: (j, 0, 0)),
                pl.BlockSpec((1, 8, rows), lambda j, meta: (j, 0, 0)),
                *[whole_spec(piece.shape) for piece in kv],
                pl.BlockSpec((1, 1, rows), lambda j, meta: (j, 0, 0)),
            ],
            out_specs=[whole_spec(packed.shape), whole_spec(others)],
            scratch_shapes=[
                pltpu.VMEM((units, part * rows, PACK - TILE), BF),
                pltpu.VMEM((TRIO, TILE, rows), BF),
                pltpu.VMEM((TRIO, TILE, rows), BF),
                pltpu.VMEM((TRIO * rows, TILE), BF),
                pltpu.VMEM((TRIO * rows, TILE), BF),
                pltpu.VMEM((units, TRIO * HEAD_DIM, part * rows), BF),
                pltpu.VMEM((8, rows), F32),
                pltpu.VMEM((TRIO * HEAD_DIM, rows), F32),
                grads,
                grads,
                grads,
                grads,
            ],
        ),
        out_shape=[
            jax.ShapeDtypeStruct(packed.shape, BF),
            jax.ShapeDtypeStruct(others, BF),
        ],
        compiler_params=params_of("arbitrary"),
        cost_estimate=pl.CostEstimate(
            flops=63 * units * units * part * rows * rows * HEAD_DIM * TRIO, bytes_accessed=0, transcendentals=0
        ),
        name="attend_backward",
    )(meta, packed, dout, out_t, lse, *kv, seg)


def pack_kernel(trios, groups, w_ref, vec_ref, early_ref, local_ref):
    d = w_ref.shape[1] // 3
    w = w_ref[...].astype(F32)
    width = TRIO * HEAD_DIM
    zeros = jnp.zeros((w.shape[0], HEAD_DIM), F32)
    for g in range(trios):
        q, k, v = (w[:, i * d + g * width : i * d + (g + 1) * width] for i in range(3))
        tiles = [q[:, :TILE], k[:, :TILE], v[:, :TILE]]
        tiles.append(jnp.concatenate([q[:, TILE:], k[:, TILE:]], 1))
        tiles.append(jnp.concatenate([v[:, TILE:], zeros], 1))
        for t, tile in enumerate(tiles):
            tile = tile.astype(BF)
            local_ref[:, g * PACK + t * TILE : g * PACK + (t + 1) * TILE] = tile
            for s in range(groups):
                early_ref[s * trios + g, :, t * TILE : (t + 1) * TILE] = tile
        for s in range(groups):
            early_ref[s * trios + g, :, PACK:] = vec_ref[s]


def pack_early(weight, vec, trios):
    r = weight.shape[0]
    groups = vec.shape[0]
    return pl.pallas_call(
        functools.partial(pack_kernel, trios, groups),
        out_shape=[
            jax.ShapeDtypeStruct((trios * groups, r, PACK + TILE), BF),
            jax.ShapeDtypeStruct((r, trios * PACK), BF),
        ],
        name="pack_early",
    )(weight, vec)


def feed_kernel(
    x_ref, cot_ref, up_ref, down_ref, shift_ref, hid_ref, pre_ref, sum_ref, second_ref, back_ref
):
    pre = mm(x_ref[...], up_ref[...]) + shift_ref[...]
    grad = inner_back(cot_ref[...], down_ref[...])
    cdf = 0.5 * (1.0 + lax.erf(pre * math.sqrt(0.5)))
    hidden = (pre * cdf).astype(BF)
    slope = cdf + pre * (jnp.exp(-0.5 * pre * pre) * (1.0 / math.sqrt(2.0 * math.pi)))
    pre_grad = (grad * slope).astype(BF)
    hid_ref[...] = hidden
    pre_ref[...] = pre_grad
    sum_ref[...] = jnp.sum(pre_grad.astype(F32), 0, keepdims=True)
    second = mm(hidden, down_ref[...])
    back = inner_back(pre_grad, up_ref[...])

    @pl.when(pl.program_id(0) == 0)
    def _():
        second_ref[...] = second
        back_ref[...] = back

    @pl.when(pl.program_id(0) > 0)
    def _():
        second_ref[...] += second
        back_ref[...] += back


def feed_forward(x, cot, weights, shift, blocks):
    rows, d = x.shape
    ff = blocks * d
    half = d // 2
    wide = pl.BlockSpec((rows, d), lambda i: (0, 0))
    column = pl.BlockSpec((rows, half), lambda i: (0, i))
    line = pl.BlockSpec((1, half), lambda i: (0, i))
    return pl.pallas_call(
        feed_kernel,
        grid=(2 * blocks,),
        in_specs=[
            wide,
            wide,
            pl.BlockSpec((d, half), lambda i: (0, i)),
            pl.BlockSpec((half, d), lambda i: (i % 2, blocks + i // 2)),
            line,
        ],
        out_specs=[column, column, line, wide, wide],
        out_shape=[
            jax.ShapeDtypeStruct((rows, ff), BF),
            jax.ShapeDtypeStruct((rows, ff), BF),
            jax.ShapeDtypeStruct((1, ff), F32),
            jax.ShapeDtypeStruct((rows, d), F32),
            jax.ShapeDtypeStruct((rows, d), F32),
        ],
        compiler_params=params_of("arbitrary"),
        cost_estimate=pl.CostEstimate(
            flops=8 * rows * d * ff, bytes_accessed=4 * d * ff, transcendentals=2 * rows * ff
        ),
        name="feed_forward",
    )(x, cot, weights, weights, shift)


def gradient_kernel(ups, norm_ref, pre_ref, hidden_ref, cot_ref, out_ref):
    i = pl.program_id(0)

    @pl.when(i < ups)
    def _():
        out_ref[...] = outer_sum(norm_ref[...], pre_ref[...]).astype(BF)

    @pl.when(i >= ups)
    def _():
        out_ref[...] = outer_sum(hidden_ref[...], cot_ref[...]).astype(BF)


def gradients(normed, pre_grad, hidden, cot):
    rows, d = normed.shape
    width = d // 2
    ups = hidden.shape[1] // width

    def down(i):
        return jnp.clip(i - ups, 0, ups - 1)

    return pl.pallas_call(
        functools.partial(gradient_kernel, ups),
        grid=(2 * ups,),
        in_specs=[
            pl.BlockSpec((rows, d), lambda i: (0, 0)),
            pl.BlockSpec((rows, width), lambda i: (0, jnp.minimum(i, ups - 1))),
            pl.BlockSpec((rows, d), lambda i: (0, down(i) // 2)),
            pl.BlockSpec((rows, width), lambda i: (0, down(i) % 2)),
        ],
        out_specs=pl.BlockSpec((d, width), lambda i: (0, i)),
        out_shape=jax.ShapeDtypeStruct((d, 2 * ups * width), BF),
        compiler_params=params_of("arbitrary"),
        cost_estimate=pl.CostEstimate(
            flops=4 * rows * d * ups * width, bytes_accessed=0, transcendentals=0
        ),
        name="gradients",
    )(normed, pre_grad, hidden, cot)


def trio_kernel(norm_ref, hat_ref, grad_ref, w_ref, late_ref, shift_ref, own, hat):
    j = pl.program_id(0)
    d = norm_ref.shape[2]
    grad = grad_ref[...].reshape(-1, PACK)
    own_part = outer_sum(norm_ref[...].reshape(-1, d), grad)
    hat_part = outer_sum(hat_ref[...].reshape(-1, d), grad)
    sums = jnp.sum(grad.astype(F32), 0, keepdims=True)

    @pl.when(j == 0)
    def _():
        own[...] = own_part
        hat[...] = hat_part
        shift_ref[...] = sums

    @pl.when(j > 0)
    def _():
        own[...] += own_part
        hat[...] += hat_part
        shift_ref[...] += sums

    @pl.when(j == pl.num_programs(0) - 1)
    def _():
        late_ref[:, :PACK] = own[...].astype(BF)
        weight = w_ref[...].astype(F32)
        lane = lane_of((d, TILE))
        vec = jnp.where(lane == 0, jnp.sum(weight * hat[...], 1, keepdims=True), 0.0)
        vec = jnp.where(lane == 1, jnp.sum(weight * shift_ref[...], 1, keepdims=True), vec)
        late_ref[:, PACK:] = vec.astype(BF)


def trio_gradient(normed, hat, grad, weight):
    units, rows, d = normed.shape
    tok_spec = pl.BlockSpec((2, rows, d), lambda j: (j, 0, 0))
    return pl.pallas_call(
        trio_kernel,
        grid=(units // 2,),
        in_specs=[
            tok_spec,
            tok_spec,
            pl.BlockSpec((2, rows, PACK), lambda j: (j, 0, 0)),
            pl.BlockSpec((d, PACK), lambda j: (0, 0)),
        ],
        out_specs=[
            pl.BlockSpec((d, PACK + TILE), lambda j: (0, 0)),
            pl.BlockSpec((1, PACK), lambda j: (0, 0)),
        ],
        scratch_shapes=[pltpu.VMEM((d, PACK), F32), pltpu.VMEM((d, PACK), F32)],
        out_shape=[
            jax.ShapeDtypeStruct((d, PACK + TILE), BF),
            jax.ShapeDtypeStruct((1, PACK), F32),
        ],
        compiler_params=params_of("arbitrary"),
        cost_estimate=pl.CostEstimate(
            flops=12 * units * rows * d * PACK, bytes_accessed=0, transcendentals=0
        ),
        name="trio_gradient",
    )(normed, hat, grad, weight)


def pack_columns(matrix, trios):
    r = matrix.shape[0]
    q, k, v = (
        part.reshape(r, trios, TRIO * HEAD_DIM) for part in jnp.split(matrix, 3, axis=1)
    )
    zeros = jnp.zeros((r, trios, HEAD_DIM), matrix.dtype)
    pieces = [q[..., :TILE], k[..., :TILE], v[..., :TILE], q[..., TILE:], k[..., TILE:]]
    return jnp.concatenate(pieces + [v[..., TILE:], zeros], -1).reshape(r, trios * PACK)


def unpack_columns(matrix, trios):
    r = matrix.shape[0]
    m = matrix.reshape(r, trios, PACK)
    halves = [
        m[..., 3 * TILE : 3 * TILE + HEAD_DIM],
        m[..., 3 * TILE + HEAD_DIM : 4 * TILE],
        m[..., 4 * TILE : 4 * TILE + HEAD_DIM],
    ]
    return jnp.concatenate(
        [
            jnp.concatenate([m[..., i * TILE : (i + 1) * TILE], halves[i]], -1).reshape(r, -1)
            for i in range(3)
        ],
        -1,
    )


def split_hidden(matrix, count, r):
    lead = matrix.shape[0]
    return matrix.reshape(lead, count, -1, r).transpose(0, 2, 1, 3).reshape(lead, -1)


def join_hidden(matrix, count, r):
    lead = matrix.shape[0]
    return matrix.reshape(lead, -1, count, r).transpose(0, 2, 1, 3).reshape(lead, -1)


def on_device(
    tokens,
    segment,
    ln1_gain,
    ln1_bias,
    ln2_gain,
    ln2_bias,
    qkv_weight,
    qkv_bias,
    dense_weight,
    dense_bias,
    fc1_weight,
    fc1_bias,
    output_feed_weight,
    output_feed_bias,
    cotangent,
):
    rows, groups, d = tokens.shape
    units = lax.axis_size("unit")
    part = lax.axis_size("part")
    count = units * part * lax.axis_size("seq")
    trios = units // groups
    all_rows = rows * groups
    r = qkv_weight.shape[0]
    ff = fc1_weight.shape[1]
    blocks = ff // d
    c = lax.axis_index("part")
    unit = lax.axis_index("unit")

    seq = lax.axis_index("seq")
    seqs = lax.axis_size("seq")
    place = (seq * units + unit) * part + c

    def exchange(blocks_out):
        width = blocks_out.shape[-1]
        return lax.all_to_all(
            blocks_out.reshape(-1, width), "unit", 0, 0, tiled=True
        ).reshape(blocks_out.shape)

    def shift(value, axis, i):
        n = lax.axis_size(axis)
        return lax.ppermute(value, axis, [(p, (p + i) % n) for p in range(n)])

    def flip_unit(value, bit):
        return lax.ppermute(value, "unit", [(u, u ^ bit) for u in range(units)])

    def pick(value, index, axis):
        return lax.dynamic_index_in_dim(value, index, axis, False)

    bits = (unit // trios, unit // 2 % 2, unit % 2)

    def exchange_small(value):
        shape = value.shape
        value = value.reshape((2, 2, 2) + shape[1:])
        for axis, bit in enumerate((trios, 2, 1)):
            keep = pick(value, bits[axis], axis)
            value = jnp.stack([keep, flip_unit(pick(value, 1 - bits[axis], axis), bit)], axis)
        for axis in range(3):
            value = jnp.where(bits[axis] == 0, value, jnp.flip(value, axis))
        return value.reshape(shape)

    def spread_tokens(value, beside):
        keep = pick(value, bits[0], 0)
        both = jnp.stack([keep, flip_unit(pick(value, 1 - bits[0], 0), trios)])
        one, two = both[:, : rows // 2], both[:, rows // 2 :]
        one = jnp.stack([one, flip_unit(one, 2)])
        two = jnp.stack([two, flip_unit(two, 1)])
        one, two, beside = lax.optimization_barrier((one, two, beside))
        one = jnp.stack([one, flip_unit(one, 1)])
        two = jnp.stack([two, flip_unit(two, 2)])
        return (one.reshape(units, rows // 2, d), two.reshape(units, rows // 2, d)), beside

    def add(a, b):
        return (a.astype(F32) + b.astype(F32)).astype(BF)

    def natural_order(got, me):
        n = len(got)
        if n == 2:
            return jnp.where(me == 0, jnp.stack(got), jnp.stack(got[::-1]))
        ring = jnp.stack((got + got)[::-1])
        return lax.dynamic_slice_in_dim(ring, n - 1 - me, n, 0)

    def gather_small(value, axis):
        n = lax.axis_size(axis)
        got = [value] + [shift(value, axis, i) for i in range(1, n)]
        return natural_order(got, lax.axis_index(axis))

    def swap_parts(value):
        got = [lax.dynamic_index_in_dim(value, c, 0, False)]
        for i in range(1, part):
            piece = lax.dynamic_index_in_dim(value, (c + i) % part, 0, False)
            got.append(shift(piece, "part", i))
        return natural_order(got, c)

    def all_parts(value):
        return jnp.concatenate([value] + [shift(value, "part", i) for i in range(1, part)], 0)

    def part_pieces(value):
        n = value.shape[0] // part
        return [value[:n]] + [
            shift(value[i * n : (i + 1) * n], "part", part - i) for i in range(1, part)
        ]

    def halve(value, axis, which):
        if isinstance(which, str):
            n = lax.axis_size(which)
            me = lax.axis_index(which)
            return [pick(value, me, axis)] + [
                shift(pick(value, (me + i) % n, axis), which, i) for i in range(1, n)
            ]
        away = pick(value, 1 - bits[which], axis)
        return [pick(value, bits[which], axis), flip_unit(away, (trios, 2, 1)[which])]

    def add_up(pieces):
        total = pieces[0].astype(F32)
        for piece in pieces[1:]:
            total = total + piece.astype(F32)
        return total.astype(BF)

    vectors = (ln1_gain, ln1_bias, ln2_gain, ln2_bias, dense_bias, output_feed_bias)
    vec = jnp.concatenate(
        [v.reshape(r, 1) for v in vectors] + [qkv_bias.reshape(r, 3), fc1_bias.reshape(r, blocks)],
        1,
    )
    token_rows = tokens.transpose(1, 0, 2)
    seg_rows = segment.T
    seg_lanes = -(-2 * rows // r)
    seg_pack = jnp.concatenate([seg_rows // 64, seg_rows % 64], 1).astype(BF)
    seg_pack = jnp.pad(seg_pack, ((0, 0), (0, seg_lanes * r - 2 * rows)))
    seg_pack = seg_pack.reshape(groups, r, seg_lanes)
    vec = jnp.pad(vec, ((0, 0), (0, 16 - vec.shape[1])))
    vec = jnp.concatenate(
        [
            jnp.broadcast_to(vec, (groups, r, 16)),
            seg_pack,
            jnp.zeros((groups, r, TILE - 16 - seg_lanes), BF),
        ],
        -1,
    )
    early, qkv_local = pack_early(qkv_weight, vec, trios)
    early = exchange_small(early)
    feed_blocks = output_feed_weight.reshape(blocks, r, d)
    half = blocks // part
    up_local = split_hidden(fc1_weight, count, r)
    second_pack = jnp.stack(
        [
            jnp.concatenate(
                [up_local[:, p * half * d : (p + 1) * half * d]]
                + [feed_blocks[b] for b in range(p * half, (p + 1) * half)]
                + [dense_weight],
                1,
            )
            for p in range(part)
        ]
    )
    second_pack = swap_parts(second_pack).reshape(part * r, -1)
    toks, second_pack = spread_tokens(token_rows, second_pack)
    second = lax.all_gather(second_pack, ("seq", "unit"), axis=0, tiled=True)

    seg_mine = early[:, :, PACK + 16 : PACK + 16 + seg_lanes].astype(jnp.int32)
    seg_mine = seg_mine.reshape(units, r * seg_lanes)
    seg_mine = seg_mine[:, :rows] * 64 + seg_mine[:, rows : 2 * rows]
    meta = jnp.concatenate([seg_mine[:, 0], seg_mine[:, -1], c[None]])
    seg_mine = seg_mine[:, None, :]
    trio_full = gather_small(gather_small(early, "seq"), "part")
    trio_full = trio_full.transpose(1, 2, 0, 3, 4).reshape(d, PACK + TILE)
    vec_full = trio_full[:, PACK:].astype(F32)
    vec_rows = vec_full[:, :8].T
    gain_one, bias_one, gain_two, bias_two, dense_shift, down_shift = (
        vec_rows[i : i + 1] for i in range(6)
    )
    qkv_shift = pack_columns(vec_full[:, 6:9].reshape(1, 3 * d), trios).reshape(trios, PACK)
    qkv_shift = lax.dynamic_slice_in_dim(qkv_shift, unit % trios, 1, 0)
    up_shift = split_hidden(vec_full[:, 9 : 9 + blocks].reshape(1, ff), count, r)

    block_start = (jnp.arange(units, dtype=jnp.int32) * part + c) * rows
    positions = block_start[:, None, None] + jnp.arange(rows, dtype=jnp.int32) - seg_mine
    freq = jnp.arange(ROT // 2, dtype=F32)
    inverse = jnp.exp(freq * (-2.0 * math.log(10000.0) / ROT))
    angles = positions.astype(F32) * inverse[None, :, None]
    cos = jnp.cos(angles)
    sin = jnp.sin(angles)

    place_unit = unit[None]
    packed, kv_own, normed_one, hat_one = project(
        place_unit, toks, trio_full, qkv_shift, gain_one, bias_one, cos, sin
    )
    kv = [kv_own] + [shift(kv_own, "part", i) for i in range(1, part)]
    out_low, out_t, lse = attend_forward(meta, packed, kv, seg_mine)
    second, out_low = lax.optimization_barrier((second, out_low))
    attended = exchange(out_low)
    dense_pad = jnp.pad(
        second[:, 2 * half * d :].reshape(trios, d // trios, d),
        ((0, 0), (0, OPACK - d // trios), (0, 0)),
    )

    x = token_rows.reshape(all_rows, d).astype(F32)
    cot = cotangent.transpose(1, 0, 2).reshape(all_rows, d)
    centre = x - jnp.mean(x, -1, keepdims=True)
    spread = lax.rsqrt(jnp.mean(centre * centre, -1, keepdims=True) + EPSILON)
    xhat = centre * spread
    normed_two = (xhat * gain_two + bias_two).astype(BF)
    attended_grad = jnp.einsum(
        "sld,gkd->sglk", cot.reshape(groups, rows, d), dense_pad, preferred_element_type=F32
    ).astype(BF)
    dout = exchange(attended_grad.reshape(units, rows, OPACK))
    normed_all = all_parts(normed_two)
    cot_all = all_parts(cot)
    up_shift = lax.dynamic_slice_in_dim(up_shift, c * half * d, half * d, 1)
    hidden_low, pre_grad, up_shift_grad, second_branch, normed_two_grad = feed_forward(
        normed_all, cot_all, second, up_shift, half
    )
    hidden_low, pre_grad, attended = lax.optimization_barrier((hidden_low, pre_grad, attended))
    second_branch = part_pieces(second_branch)
    normed_two_grad = part_pieces(normed_two_grad)
    def norm_back(grad, gain):
        gy = grad * gain
        return spread * (
            gy - jnp.mean(gy, -1, keepdims=True) - xhat * jnp.mean(gy * xhat, -1, keepdims=True)
        )

    mlp_grads = gradients(normed_all, pre_grad, hidden_low, cot_all)
    mlp_grads, dout = lax.optimization_barrier((mlp_grads, dout))

    split = (seqs, 2, 2, 2, part * r, half * d)
    up_part = halve(mlp_grads[:, : half * d].reshape(split), 0, "seq")
    down_part = halve(mlp_grads[:, half * d :].reshape(split), 3, 2)

    attended = attended.reshape(groups, trios, rows, OPACK).transpose(0, 2, 1, 3)
    attended = attended.reshape(all_rows, trios * OPACK)
    dense_grad = outer_sum(attended, cot).reshape(trios, OPACK, d)[:, : d // trios].reshape(d, d)
    normed_two_grad = sum(normed_two_grad)
    vec_grads = jnp.concatenate(
        [
            jnp.zeros((2, d), F32),
            jnp.sum(normed_two_grad * xhat, 0)[None],
            jnp.sum(normed_two_grad, 0)[None],
            jnp.sum(cot.astype(F32), 0)[None],
            jnp.zeros((3, d), F32),
        ],
        0,
    ).T
    up_shift_grad = lax.dynamic_update_slice_in_dim(
        jnp.zeros((1, ff), F32), up_shift_grad, c * half * d, 1
    )
    up_shift_grad = join_hidden(up_shift_grad, count, r).reshape(d, blocks)
    dense_part = jnp.concatenate(
        [dense_grad, vec_grads, up_shift_grad, jnp.zeros((d, TILE - 8 - blocks), F32)], 1
    ).astype(BF)
    dense_part, lse = lax.optimization_barrier((dense_part, lse))
    dense_part = halve(dense_part.reshape(seqs, units, part, r, d + TILE), 2, "part")

    own, others = attend_backward(meta, packed, dout, out_t, lse, kv, seg_mine)
    others = [shift(others[i - 1], "part", part - i) for i in range(1, part)]
    up_part, down_part, dense_part, own = lax.optimization_barrier(
        (up_part, down_part, dense_part, own)
    )
    up_part = halve(add_up(up_part), 2, 2)
    down_part = halve(add_up(down_part), 0, "seq")
    dense_part = halve(add_up(dense_part), 0, "seq")
    qkv_grad, back_one, back_two = unturn(place_unit, own, others, trio_full, cos, sin)
    back_one = back_one.reshape(2, 2, 2, rows // 2, d)
    back_two = back_two.reshape(2, 2, 2, rows // 2, d)
    swapped = flip_unit(back_one[1], 1), flip_unit(back_two[1], 2)

    late, shift_grad = trio_gradient(normed_one, hat_one, qkv_grad, trio_full)
    swapped, late, up_part, down_part, dense_part = lax.optimization_barrier(
        (swapped, late, up_part, down_part, dense_part)
    )
    back_one = add(back_one[0], swapped[0])
    back_two = add(back_two[0], swapped[1])
    swapped = flip_unit(back_one[1], 2), flip_unit(back_two[1], 1)
    mlp_part = jnp.concatenate([add_up(up_part), add_up(down_part)], -1)
    mlp_part = halve(mlp_part, 1, 1)
    late = late.reshape(seqs, units, part, r, -1)
    shift_rows = jnp.pad(shift_grad.astype(BF), ((0, 7), (0, TILE)))
    late = jnp.concatenate(
        [late, jnp.broadcast_to(shift_rows, (seqs, units, part) + shift_rows.shape)], 3
    )
    late = halve(late, 2, "part")
    swapped, late, mlp_part = lax.optimization_barrier((swapped, late, mlp_part))
    both = jnp.concatenate(
        [add(back_one[0], swapped[0]), add(back_two[0], swapped[1])], 1
    )
    swapped = flip_unit(both[1], trios)
    mlp_part = halve(add_up(mlp_part), 0, 0)
    late = halve(add_up(late), 0, "seq")
    swapped, late, mlp_part = lax.optimization_barrier((swapped, late, mlp_part))
    mlp_sum = swap_parts(add_up(mlp_part).reshape(part, r, -1)).astype(F32)
    dense_part = jnp.pad(add_up(dense_part), ((0, 0), (0, 8), (0, 0)))
    late = exchange_small(jnp.concatenate([add_up(late), dense_part], -1)).astype(F32)
    rest = jnp.sum(late[:, :r, PACK + TILE :], 0)
    dense_sum = rest[:, :d]
    back = jnp.where(
        bits[0] == 0, jnp.stack([both[0], swapped]), jnp.stack([swapped, both[0]])
    )
    branch_one = mm(attended, dense_pad.reshape(trios * OPACK, d)) + dense_shift
    output = (x + branch_one + sum(second_branch) + down_shift).astype(BF)
    in_two = norm_back(normed_two_grad, gain_two)
    late = jnp.sum(late[:, :, : PACK + TILE].reshape(groups, trios, r + 8, PACK + TILE), 0)
    qkv_weight_grad = unpack_columns(
        late[:, :r, :PACK].transpose(1, 0, 2).reshape(r, trios * PACK), trios
    )
    late_vec = jnp.sum(late[:, :r, PACK:], 0) + rest[:, d:]
    qkv_shift_grad = unpack_columns(late[:, r, :PACK].reshape(1, trios * PACK), trios)[0]
    qkv_shift_grad = lax.dynamic_slice_in_dim(qkv_shift_grad, place * 3 * r, 3 * r)

    up_sum = jnp.concatenate([mlp_sum[p, :, : half * d] for p in range(part)], 1)
    down_sum = jnp.concatenate(
        [
            mlp_sum[p, :, (half + b) * d : (half + b + 1) * d]
            for p in range(part)
            for b in range(half)
        ],
        0,
    )
    param_grads = (
        late_vec[:, 0],
        late_vec[:, 1],
        late_vec[:, 2],
        late_vec[:, 3],
        qkv_weight_grad,
        qkv_shift_grad,
        dense_sum,
        late_vec[:, 4],
        join_hidden(up_sum, count, r),
        late_vec[:, 8 : 8 + blocks].reshape(-1),
        down_sum,
        late_vec[:, 4],
    )

    normed_one_grad = back.reshape(all_rows, d).astype(F32)
    in_one = norm_back(normed_one_grad, gain_one)
    tokens_grad = (cot.astype(F32) + in_one + in_two).astype(BF)

    def natural(value):
        return value.reshape(groups, rows, d).transpose(1, 0, 2)

    return (natural(output), natural(tokens_grad)) + tuple(param_grads)


def solution(mesh):
    devices = mesh.devices
    seq_size, ctx_size = devices.shape
    ctx = ("unit", "part")
    tok = P(ctx, "seq", None)
    vec = P(ALL_AXES)
    mat = P(ALL_AXES, None)
    pairs = (vec, vec, vec, vec, mat, vec, mat, vec, mat, vec, mat, vec)

    def run(tokens, *rest):
        units = HEADS // TRIO * (tokens.shape[1] // seq_size)
        split = Mesh(devices.reshape(seq_size, units, ctx_size // units), ALL_AXES)
        mapped = jax.shard_map(
            on_device,
            mesh=split,
            in_specs=(tok, P(ctx, "seq")) + pairs + (tok,),
            out_specs=(tok, tok) + pairs,
            check_vma=False,
        )
        return mapped(tokens, *rest)

    return run
```

```python
import functools
import math

import jax
import jax.numpy as jnp
from jax import lax
from jax.experimental import pallas as pl
from jax.experimental.pallas import tpu as pltpu
from jax.sharding import Mesh, PartitionSpec as P

HEADS = 12
HEAD_DIM = 64
ROT = 16
TRIO = 3
TILE = 128
PACK = 5 * TILE
OPACK = 2 * TILE

EPSILON = 1e-05
NEG_BIG = -1e30
BF = jnp.bfloat16
F32 = jnp.float32
ALL_AXES = ("seq", "unit", "part")
VMEM_BYTES = 56 * 1024 * 1024


def params_of(*semantics):
    return pltpu.CompilerParams(
        dimension_semantics=semantics, vmem_limit_bytes=VMEM_BYTES
    )


def mm(a, b):
    return jnp.dot(a, b, preferred_element_type=F32)


def outer_sum(left_rows, right_rows):
    return lax.dot_general(
        left_rows, right_rows, (((0,), (0,)), ((), ())), preferred_element_type=F32
    )


def inner_back(grad_rows, weight):
    return lax.dot_general(
        grad_rows, weight, (((1,), (1,)), ((), ())), preferred_element_type=F32
    )


def lane_of(shape):
    return lax.broadcasted_iota(jnp.int32, shape, len(shape) - 1)


def turn(tile, cos, sin):
    partner = jnp.where(
        lane_of(tile.shape) % HEAD_DIM < ROT // 2,
        pltpu.roll(tile, TILE - ROT // 2, 1),
        pltpu.roll(tile, ROT // 2, 1),
    )
    return tile * cos + partner * sin


def turn_tables(cos_rows, sin_rows):
    rows = cos_rows.shape[1]
    rest = HEAD_DIM - ROT
    cos_head = [cos_rows, cos_rows, jnp.ones((rest, rows), F32)]
    sin_head = [-sin_rows, sin_rows, jnp.zeros((rest, rows), F32)]
    return jnp.concatenate(cos_head * 2, 0).T, jnp.concatenate(sin_head * 2, 0).T


def first_place(rel):
    return rel % 2 * 4 + rel // 2 % 2 * 2 + rel // 4


def second_place(rel):
    return rel // 2 % 2 * 4 + rel % 2 * 2 + rel // 4


def project_kernel(
    place_ref,
    one_ref,
    two_ref,
    w_ref,
    b_ref,
    gain_ref,
    bias_ref,
    cos_ref,
    sin_ref,
    out_ref,
    kv_ref,
    norm_ref,
    hat_ref,
):
    x = jnp.concatenate([one_ref[0], two_ref[0]], 0).astype(F32)
    centre = x - jnp.mean(x, -1, keepdims=True)
    spread = jnp.mean(centre * centre, -1, keepdims=True)
    hat = centre * lax.rsqrt(spread + EPSILON)
    normed = (hat * gain_ref[...] + bias_ref[...]).astype(BF)
    hat_ref[0] = hat.astype(BF)
    norm_ref[0] = normed
    y = mm(normed, w_ref[...]) + b_ref[...]
    cos, sin = turn_tables(cos_ref[0], sin_ref[0])
    for t in range(5):
        tile = y[:, t * TILE : (t + 1) * TILE]
        if t in (0, 1, 3):
            tile = turn(tile, cos, sin)
        tile = tile.astype(BF)
        out_ref[0, :, t * TILE : (t + 1) * TILE] = tile
        if t > 0:
            kv_ref[0, :, (t - 1) * TILE : t * TILE] = tile


def half_specs(rows, d):
    return [
        pl.BlockSpec((1, rows // 2, d), lambda j, place: (first_place(j ^ place[0]), 0, 0)),
        pl.BlockSpec((1, rows // 2, d), lambda j, place: (second_place(j ^ place[0]), 0, 0)),
    ]


def project(place, toks, weight, bias, gain, offset, cos, sin):
    units, unused, rows = cos.shape
    d = toks[0].shape[2]
    tok_spec = pl.BlockSpec((1, rows, d), lambda j, place: (j, 0, 0))
    row_spec = pl.BlockSpec((1, d), lambda j, place: (0, 0))
    turn_spec = pl.BlockSpec((1, ROT // 2, rows), lambda j, place: (j, 0, 0))
    return pl.pallas_call(
        project_kernel,
        grid_spec=pltpu.PrefetchScalarGridSpec(
            num_scalar_prefetch=1,
            grid=(units,),
            in_specs=half_specs(rows, d)
            + [
                pl.BlockSpec((d, PACK), lambda j, place: (0, 0)),
                pl.BlockSpec((1, PACK), lambda j, place: (0, 0)),
                row_spec,
                row_spec,
                turn_spec,
                turn_spec,
            ],
            out_specs=[
                pl.BlockSpec((1, rows, PACK), lambda j, place: (j, 0, 0)),
                pl.BlockSpec((1, rows, PACK - TILE), lambda j, place: (j, 0, 0)),
                tok_spec,
                tok_spec,
            ],
        ),
        out_shape=[
            jax.ShapeDtypeStruct((units, rows, PACK), BF),
            jax.ShapeDtypeStruct((units, rows, PACK - TILE), BF),
            jax.ShapeDtypeStruct((units, rows, d), BF),
            jax.ShapeDtypeStruct((units, rows, d), BF),
        ],
        compiler_params=params_of("arbitrary"),
        cost_estimate=pl.CostEstimate(flops=0, bytes_accessed=0, transcendentals=0),
        name="project",
    )(place, *toks, weight, bias, gain, offset, cos, sin)


def unturn_kernel(place_ref, own_ref, *refs):
    w_ref, cos_ref, sin_ref, out_ref, one_ref, two_ref = refs[-6:]
    others = refs[:-6]
    cos, sin = turn_tables(cos_ref[0], sin_ref[0])
    for t in range(5):
        tile = own_ref[0, :, t * TILE : (t + 1) * TILE].astype(F32)
        if t > 0:
            for other in others:
                tile = tile + other[0, :, (t - 1) * TILE : t * TILE].astype(F32)
        if t in (0, 1, 3):
            tile = turn(tile, cos, -sin)
        out_ref[0, :, t * TILE : (t + 1) * TILE] = tile.astype(BF)
    back = inner_back(out_ref[0], w_ref[...]).astype(BF)
    rows = back.shape[0] // 2
    one_ref[0] = back[:rows]
    two_ref[0] = back[rows:]


def unturn(place, own, others, weight, cos, sin):
    units, rows, unused = own.shape
    d = weight.shape[0]
    turn_spec = pl.BlockSpec((1, ROT // 2, rows), lambda j, place: (j, 0, 0))
    own_spec = pl.BlockSpec((1, rows, PACK), lambda j, place: (j, 0, 0))
    other_spec = pl.BlockSpec((1, rows, PACK - TILE), lambda j, place: (j, 0, 0))
    half = jax.ShapeDtypeStruct((units, rows // 2, d), BF)
    return pl.pallas_call(
        unturn_kernel,
        grid_spec=pltpu.PrefetchScalarGridSpec(
            num_scalar_prefetch=1,
            grid=(units,),
            in_specs=[own_spec]
            + [other_spec] * len(others)
            + [pl.BlockSpec((d, PACK), lambda j, place: (0, 0)), turn_spec, turn_spec],
            out_specs=[own_spec] + half_specs(rows, d),
        ),
        out_shape=[jax.ShapeDtypeStruct(own.shape, BF), half, half],
        compiler_params=params_of("arbitrary"),
        cost_estimate=pl.CostEstimate(flops=0, bytes_accessed=0, transcendentals=0),
        name="unturn",
    )(place, own, *others, weight, cos, sin)


def flip(tile):
    return tile.astype(F32).T


def head_rows(flipped, low):
    row = lax.broadcasted_iota(jnp.int32, flipped.shape, 0)
    keep = row < HEAD_DIM if low else row >= HEAD_DIM
    return jnp.where(keep, flipped, 0.0)


def head_lanes(tile, low):
    lane = lane_of(tile.shape)
    keep = lane < HEAD_DIM if low else lane >= HEAD_DIM
    return jnp.where(keep, tile, 0.0)


def query_sides(q_ref, qb):
    scale = HEAD_DIM ** (-0.5)
    a = flip(q_ref[0, :, 0:TILE]) * scale
    d = flip(q_ref[0, :, 3 * TILE : 4 * TILE]) * scale
    qb[0] = head_rows(a, True).astype(BF)
    qb[1] = head_rows(a, False).astype(BF)
    qb[2] = jnp.concatenate(
        [jnp.zeros((HEAD_DIM, d.shape[1]), F32), d[:HEAD_DIM]], 0
    ).astype(BF)


def live_of(seg_row, unit, query_start, part, rows, c):
    shape = (rows, rows)
    query_pos = query_start + lax.broadcasted_iota(jnp.int32, shape, 1)
    row = lax.broadcasted_iota(jnp.int32, shape, 0)
    pieces = []
    for i in range(part):
        key_pos = (unit * part + lax.rem(c - i + part, part)) * rows + row
        pieces.append((key_pos <= query_pos) & (key_pos >= seg_row))
    return jnp.concatenate(pieces, 0)


def unit_loop(meta, part, units, rows, step):
    j = pl.program_id(0)
    first = meta[j] // (rows * part)
    top_seg = meta[units + j]

    def one(unit, unused):
        masked = (unit == j) | (top_seg > unit * (rows * part))

        @pl.when(masked)
        def _():
            step(unit, True)

        @pl.when(jnp.logical_not(masked))
        def _():
            step(unit, False)

        return unused

    lax.fori_loop(first, j + 1, one, 0)


def join_parts(part, refs, kv_ref):
    rows = refs[0].shape[1]

    def one(unit, unused):
        for i in range(part):
            kv_ref[unit, i * rows : (i + 1) * rows] = refs[i][unit]
        return unused

    lax.fori_loop(0, refs[0].shape[0], one, 0)


def forward_kernel(part, units, meta, q_ref, *refs):
    seg_ref, o_ref, ot_ref, lse_ref, kv_ref, qb, vt, top, total, acc = refs[part:]
    rows = q_ref.shape[1]
    c = meta[2 * units]
    j = pl.program_id(0)

    @pl.when(j == 0)
    def _():
        join_parts(part, refs[:part], kv_ref)

        def turn_values(unit, unused):
            vt[unit, :TILE] = flip(kv_ref[unit, :, TILE : 2 * TILE]).astype(BF)
            vt[unit, TILE:] = flip(kv_ref[unit, :, 3 * TILE :])[:HEAD_DIM].astype(BF)
            return unused

        lax.fori_loop(0, units, turn_values, 0)

    query_sides(q_ref, qb)
    top[...] = jnp.full(top.shape, NEG_BIG, F32)
    total[...] = jnp.zeros(total.shape, F32)
    acc[...] = jnp.zeros(acc.shape, F32)
    seg_row = seg_ref[0]
    query_start = (j * part + c) * rows

    def step(unit, masked):
        k01 = kv_ref[unit, :, 0:TILE]
        k2 = kv_ref[unit, :, 2 * TILE : 3 * TILE]
        if masked:
            live = live_of(seg_row, unit, query_start, part, rows, c)
        scores = [mm(k2 if h == 2 else k01, qb[h]) for h in range(TRIO)]
        if masked:
            scores = [jnp.where(live, score, NEG_BIG) for score in scores]
        old = top[0:TRIO]
        new = jnp.concatenate([jnp.max(score, 0, keepdims=True) for score in scores], 0)
        new = jnp.maximum(old, new)
        factor = jnp.exp(old - new)
        weights = [jnp.exp(scores[h] - new[h : h + 1]) for h in range(TRIO)]
        if masked:
            weights = [jnp.where(live, weight, 0.0) for weight in weights]
        sums = [jnp.sum(weight, 0, keepdims=True) for weight in weights]
        top[0:TRIO] = new
        total[0:TRIO] = total[0:TRIO] * factor + jnp.concatenate(sums, 0)
        for h in range(TRIO):
            vth = vt[unit, h * HEAD_DIM : (h + 1) * HEAD_DIM]
            acc[h] = acc[h] * factor[h : h + 1] + mm(vth, weights[h].astype(BF))

    unit_loop(meta, part, units, rows, step)
    out = [acc[h] / total[h : h + 1] for h in range(TRIO)]
    for h in range(TRIO):
        ot_ref[0, h * HEAD_DIM : (h + 1) * HEAD_DIM] = out[h]
    lse_ref[0, 0:TRIO] = top[0:TRIO] + jnp.log(total[0:TRIO])
    o_ref[0, :, :TILE] = jnp.concatenate(out[:2], 0).T.astype(BF)
    o_ref[0, :, TILE:] = jnp.concatenate([out[2], jnp.zeros_like(out[2])], 0).T.astype(BF)


def backward_kernel(part, units, meta, q_ref, do_ref, ot_ref, lse_ref, *refs):
    seg_ref, own_ref, oth_ref, kv_ref, qb, db, qn, dn, kt, delta, dqt = refs[part : part + 11]
    dk01, dv01, dk2, dv2 = refs[part + 11 :]
    rows = q_ref.shape[1]
    c = meta[2 * units]
    j = pl.program_id(0)

    @pl.when(j == 0)
    def _():
        join_parts(part, refs[:part], kv_ref)

        def turn_keys(unit, unused):
            kt[unit, :TILE] = flip(kv_ref[unit, :, 0:TILE]).astype(BF)
            kt[unit, TILE:] = flip(kv_ref[unit, :, 2 * TILE : 3 * TILE])[HEAD_DIM:].astype(BF)
            return unused

        lax.fori_loop(0, units, turn_keys, 0)
        for ref in (dk01, dv01, dk2, dv2):
            ref[...] = jnp.zeros(ref.shape, F32)

    query_sides(q_ref, qb)
    scale = HEAD_DIM ** (-0.5)
    q01 = q_ref[0, :, 0:TILE].astype(F32) * scale
    q2 = pltpu.roll(q_ref[0, :, 3 * TILE : 4 * TILE].astype(F32), HEAD_DIM, 1) * scale
    qn[0:rows] = head_lanes(q01, True).astype(BF)
    qn[rows : 2 * rows] = head_lanes(q01, False).astype(BF)
    qn[2 * rows :] = head_lanes(q2, False).astype(BF)
    do01 = do_ref[0, :, :TILE].astype(F32)
    do2 = do_ref[0, :, TILE:].astype(F32)
    dn[0:rows] = head_lanes(do01, True).astype(BF)
    dn[rows : 2 * rows] = head_lanes(do01, False).astype(BF)
    dn[2 * rows :] = do2.astype(BF)
    do01t = do01.T
    do2t = do2.T
    db[0] = head_rows(do01t, True).astype(BF)
    db[1] = head_rows(do01t, False).astype(BF)
    db[2] = do2t.astype(BF)
    for h in range(TRIO):
        dot = do2t[:HEAD_DIM] if h == 2 else do01t[h * HEAD_DIM : (h + 1) * HEAD_DIM]
        delta[h : h + 1] = jnp.sum(
            dot * ot_ref[0, h * HEAD_DIM : (h + 1) * HEAD_DIM], 0, keepdims=True
        )
    dqt[...] = jnp.zeros(dqt.shape, F32)
    seg_row = seg_ref[0]
    query_start = (j * part + c) * rows

    def step(unit, masked):
        k01 = kv_ref[unit, :, 0:TILE]
        v01 = kv_ref[unit, :, TILE : 2 * TILE]
        k2 = kv_ref[unit, :, 2 * TILE : 3 * TILE]
        v2 = kv_ref[unit, :, 3 * TILE :]
        if masked:
            live = live_of(seg_row, unit, query_start, part, rows, c)
        scores = [mm(k2 if h == 2 else k01, qb[h]) for h in range(TRIO)]
        dprobs = [mm(v2 if h == 2 else v01, db[h]) for h in range(TRIO)]
        probs = []
        grads = []
        for h in range(TRIO):
            score = scores[h]
            if masked:
                score = jnp.where(live, score, NEG_BIG)
            prob = jnp.exp(score - lse_ref[0, h : h + 1])
            if masked:
                prob = jnp.where(live, prob, 0.0)
            probs.append(prob.astype(BF))
            grads.append((prob * (dprobs[h] - delta[h : h + 1])).astype(BF))
        dv01[unit] += mm(jnp.concatenate(probs[:2], 1), dn[: 2 * rows])
        dk01[unit] += mm(jnp.concatenate(grads[:2], 1), qn[: 2 * rows])
        dv2[unit] += mm(probs[2], dn[2 * rows :])
        dk2[unit] += mm(grads[2], qn[2 * rows :])
        for h in range(TRIO):
            kth = kt[unit, h * HEAD_DIM : (h + 1) * HEAD_DIM]
            dqt[h * HEAD_DIM : (h + 1) * HEAD_DIM] += mm(kth, grads[h])

    unit_loop(meta, part, units, rows, step)
    own_ref[j, :, 0:TILE] = (dqt[:TILE] * scale).T.astype(BF)
    dq2 = dqt[TILE:] * scale
    dk2[j, 0:rows] += jnp.concatenate([dq2, jnp.zeros_like(dq2)], 0).T

    @pl.when(j == units - 1)
    def _():
        for unit in range(units):
            for i in range(part):
                span = slice(i * rows, (i + 1) * rows)
                for t, ref in enumerate((dk01, dv01, dk2, dv2)):
                    tile = ref[unit, span].astype(BF)
                    if i == 0:
                        own_ref[unit, :, (t + 1) * TILE : (t + 2) * TILE] = tile
                    else:
                        oth_ref[i - 1, unit, :, t * TILE : (t + 1) * TILE] = tile


def whole_spec(shape):
    zeros = (0,) * len(shape)
    return pl.BlockSpec(shape, lambda j, meta: zeros)


def attend_forward(meta, packed, kv, seg):
    units, rows, unused = packed.shape
    part = len(kv)
    return pl.pallas_call(
        functools.partial(forward_kernel, part, units),
        grid_spec=pltpu.PrefetchScalarGridSpec(
            num_scalar_prefetch=1,
            grid=(units,),
            in_specs=[
                pl.BlockSpec((1, rows, PACK), lambda j, meta: (j, 0, 0)),
                *[whole_spec(piece.shape) for piece in kv],
                pl.BlockSpec((1, 1, rows), lambda j, meta: (j, 0, 0)),
            ],
            out_specs=[
                pl.BlockSpec((1, rows, OPACK), lambda j, meta: (j, 0, 0)),
                pl.BlockSpec((1, TRIO * HEAD_DIM, rows), lambda j, meta: (j, 0, 0)),
                pl.BlockSpec((1, 8, rows), lambda j, meta: (j, 0, 0)),
            ],
            scratch_shapes=[
                pltpu.VMEM((units, part * rows, PACK - TILE), BF),
                pltpu.VMEM((TRIO, TILE, rows), BF),
                pltpu.VMEM((units, TRIO * HEAD_DIM, part * rows), BF),
                pltpu.VMEM((8, rows), F32),
                pltpu.VMEM((8, rows), F32),
                pltpu.VMEM((TRIO, HEAD_DIM, rows), F32),
            ],
        ),
        out_shape=[
            jax.ShapeDtypeStruct((units, rows, OPACK), BF),
            jax.ShapeDtypeStruct((units, TRIO * HEAD_DIM, rows), F32),
            jax.ShapeDtypeStruct((units, 8, rows), F32),
        ],
        compiler_params=params_of("arbitrary"),
        cost_estimate=pl.CostEstimate(flops=0, bytes_accessed=0, transcendentals=0),
        name="attend_forward",
    )(meta, packed, *kv, seg)


def attend_backward(meta, packed, dout, out_t, lse, kv, seg):
    units, rows, unused = packed.shape
    part = len(kv)
    others = (max(part - 1, 1), units, rows, 4 * TILE)
    grads = pltpu.VMEM((units, part * rows, TILE), F32)
    return pl.pallas_call(
        functools.partial(backward_kernel, part, units),
        grid_spec=pltpu.PrefetchScalarGridSpec(
            num_scalar_prefetch=1,
            grid=(units,),
            in_specs=[
                pl.BlockSpec((1, rows, PACK), lambda j, meta: (j, 0, 0)),
                pl.BlockSpec((1, rows, OPACK), lambda j, meta: (j, 0, 0)),
                pl.BlockSpec((1, TRIO * HEAD_DIM, rows), lambda j, meta: (j, 0, 0)),
                pl.BlockSpec((1, 8, rows), lambda j, meta: (j, 0, 0)),
                *[whole_spec(piece.shape) for piece in kv],
                pl.BlockSpec((1, 1, rows), lambda j, meta: (j, 0, 0)),
            ],
            out_specs=[whole_spec(packed.shape), whole_spec(others)],
            scratch_shapes=[
                pltpu.VMEM((units, part * rows, PACK - TILE), BF),
                pltpu.VMEM((TRIO, TILE, rows), BF),
                pltpu.VMEM((TRIO, TILE, rows), BF),
                pltpu.VMEM((TRIO * rows, TILE), BF),
                pltpu.VMEM((TRIO * rows, TILE), BF),
                pltpu.VMEM((units, TRIO * HEAD_DIM, part * rows), BF),
                pltpu.VMEM((8, rows), F32),
                pltpu.VMEM((TRIO * HEAD_DIM, rows), F32),
                grads,
                grads,
                grads,
                grads,
            ],
        ),
        out_shape=[
            jax.ShapeDtypeStruct(packed.shape, BF),
            jax.ShapeDtypeStruct(others, BF),
        ],
        compiler_params=params_of("arbitrary"),
        cost_estimate=pl.CostEstimate(
            flops=63 * units * units * part * rows * rows * HEAD_DIM * TRIO, bytes_accessed=0, transcendentals=0
        ),
        name="attend_backward",
    )(meta, packed, dout, out_t, lse, *kv, seg)


def pack_kernel(trios, groups, w_ref, vec_ref, early_ref, local_ref):
    d = w_ref.shape[1] // 3
    w = w_ref[...].astype(F32)
    width = TRIO * HEAD_DIM
    zeros = jnp.zeros((w.shape[0], HEAD_DIM), F32)
    for g in range(trios):
        q, k, v = (w[:, i * d + g * width : i * d + (g + 1) * width] for i in range(3))
        tiles = [q[:, :TILE], k[:, :TILE], v[:, :TILE]]
        tiles.append(jnp.concatenate([q[:, TILE:], k[:, TILE:]], 1))
        tiles.append(jnp.concatenate([v[:, TILE:], zeros], 1))
        for t, tile in enumerate(tiles):
            tile = tile.astype(BF)
            local_ref[:, g * PACK + t * TILE : g * PACK + (t + 1) * TILE] = tile
            for s in range(groups):
                early_ref[s * trios + g, :, t * TILE : (t + 1) * TILE] = tile
        for s in range(groups):
            early_ref[s * trios + g, :, PACK:] = vec_ref[s]


def pack_early(weight, vec, trios):
    r = weight.shape[0]
    groups = vec.shape[0]
    return pl.pallas_call(
        functools.partial(pack_kernel, trios, groups),
        out_shape=[
            jax.ShapeDtypeStruct((trios * groups, r, PACK + TILE), BF),
            jax.ShapeDtypeStruct((r, trios * PACK), BF),
        ],
        name="pack_early",
    )(weight, vec)


def feed_kernel(
    x_ref, cot_ref, up_ref, down_ref, shift_ref, hid_ref, pre_ref, sum_ref, second_ref, back_ref
):
    pre = mm(x_ref[...], up_ref[...]) + shift_ref[...]
    grad = inner_back(cot_ref[...], down_ref[...])
    cdf = 0.5 * (1.0 + lax.erf(pre * math.sqrt(0.5)))
    hidden = (pre * cdf).astype(BF)
    slope = cdf + pre * (jnp.exp(-0.5 * pre * pre) * (1.0 / math.sqrt(2.0 * math.pi)))
    pre_grad = (grad * slope).astype(BF)
    hid_ref[...] = hidden
    pre_ref[...] = pre_grad
    sum_ref[...] = jnp.sum(pre_grad.astype(F32), 0, keepdims=True)
    second = mm(hidden, down_ref[...])
    back = inner_back(pre_grad, up_ref[...])

    @pl.when(pl.program_id(0) == 0)
    def _():
        second_ref[...] = second
        back_ref[...] = back

    @pl.when(pl.program_id(0) > 0)
    def _():
        second_ref[...] += second
        back_ref[...] += back


def feed_forward(x, cot, weights, shift, blocks):
    rows, d = x.shape
    ff = blocks * d
    half = d // 2
    wide = pl.BlockSpec((rows, d), lambda i: (0, 0))
    column = pl.BlockSpec((rows, half), lambda i: (0, i))
    line = pl.BlockSpec((1, half), lambda i: (0, i))
    return pl.pallas_call(
        feed_kernel,
        grid=(2 * blocks,),
        in_specs=[
            wide,
            wide,
            pl.BlockSpec((d, half), lambda i: (0, i)),
            pl.BlockSpec((half, d), lambda i: (i % 2, blocks + i // 2)),
            line,
        ],
        out_specs=[column, column, line, wide, wide],
        out_shape=[
            jax.ShapeDtypeStruct((rows, ff), BF),
            jax.ShapeDtypeStruct((rows, ff), BF),
            jax.ShapeDtypeStruct((1, ff), F32),
            jax.ShapeDtypeStruct((rows, d), F32),
            jax.ShapeDtypeStruct((rows, d), F32),
        ],
        compiler_params=params_of("arbitrary"),
        cost_estimate=pl.CostEstimate(
            flops=8 * rows * d * ff, bytes_accessed=4 * d * ff, transcendentals=2 * rows * ff
        ),
        name="feed_forward",
    )(x, cot, weights, weights, shift)


def gradient_kernel(ups, norm_ref, pre_ref, hidden_ref, cot_ref, out_ref):
    i = pl.program_id(0)

    @pl.when(i < ups)
    def _():
        out_ref[...] = outer_sum(norm_ref[...], pre_ref[...]).astype(BF)

    @pl.when(i >= ups)
    def _():
        out_ref[...] = outer_sum(hidden_ref[...], cot_ref[...]).astype(BF)


def gradients(normed, pre_grad, hidden, cot):
    rows, d = normed.shape
    width = d // 2
    ups = hidden.shape[1] // width

    def down(i):
        return jnp.clip(i - ups, 0, ups - 1)

    return pl.pallas_call(
        functools.partial(gradient_kernel, ups),
        grid=(2 * ups,),
        in_specs=[
            pl.BlockSpec((rows, d), lambda i: (0, 0)),
            pl.BlockSpec((rows, width), lambda i: (0, jnp.minimum(i, ups - 1))),
            pl.BlockSpec((rows, d), lambda i: (0, down(i) // 2)),
            pl.BlockSpec((rows, width), lambda i: (0, down(i) % 2)),
        ],
        out_specs=pl.BlockSpec((d, width), lambda i: (0, i)),
        out_shape=jax.ShapeDtypeStruct((d, 2 * ups * width), BF),
        compiler_params=params_of("arbitrary"),
        cost_estimate=pl.CostEstimate(
            flops=4 * rows * d * ups * width, bytes_accessed=0, transcendentals=0
        ),
        name="gradients",
    )(normed, pre_grad, hidden, cot)


def trio_kernel(norm_ref, hat_ref, grad_ref, w_ref, late_ref, shift_ref, own, hat):
    j = pl.program_id(0)
    d = norm_ref.shape[2]
    grad = grad_ref[...].reshape(-1, PACK)
    own_part = outer_sum(norm_ref[...].reshape(-1, d), grad)
    hat_part = outer_sum(hat_ref[...].reshape(-1, d), grad)
    sums = jnp.sum(grad.astype(F32), 0, keepdims=True)

    @pl.when(j == 0)
    def _():
        own[...] = own_part
        hat[...] = hat_part
        shift_ref[...] = sums

    @pl.when(j > 0)
    def _():
        own[...] += own_part
        hat[...] += hat_part
        shift_ref[...] += sums

    @pl.when(j == pl.num_programs(0) - 1)
    def _():
        late_ref[:, :PACK] = own[...].astype(BF)
        weight = w_ref[...].astype(F32)
        lane = lane_of((d, TILE))
        vec = jnp.where(lane == 0, jnp.sum(weight * hat[...], 1, keepdims=True), 0.0)
        vec = jnp.where(lane == 1, jnp.sum(weight * shift_ref[...], 1, keepdims=True), vec)
        late_ref[:, PACK:] = vec.astype(BF)


def trio_gradient(normed, hat, grad, weight):
    units, rows, d = normed.shape
    tok_spec = pl.BlockSpec((2, rows, d), lambda j: (j, 0, 0))
    return pl.pallas_call(
        trio_kernel,
        grid=(units // 2,),
        in_specs=[
            tok_spec,
            tok_spec,
            pl.BlockSpec((2, rows, PACK), lambda j: (j, 0, 0)),
            pl.BlockSpec((d, PACK), lambda j: (0, 0)),
        ],
        out_specs=[
            pl.BlockSpec((d, PACK + TILE), lambda j: (0, 0)),
            pl.BlockSpec((1, PACK), lambda j: (0, 0)),
        ],
        scratch_shapes=[pltpu.VMEM((d, PACK), F32), pltpu.VMEM((d, PACK), F32)],
        out_shape=[
            jax.ShapeDtypeStruct((d, PACK + TILE), BF),
            jax.ShapeDtypeStruct((1, PACK), F32),
        ],
        compiler_params=params_of("arbitrary"),
        cost_estimate=pl.CostEstimate(
            flops=12 * units * rows * d * PACK, bytes_accessed=0, transcendentals=0
        ),
        name="trio_gradient",
    )(normed, hat, grad, weight)


def vector_kernel(half, part_ref, hat_ref, cot_ref, up_ref, *refs):
    out_ref = refs[-1]
    total = refs[0][...]
    for ref in refs[1:-1]:
        total = total + ref[...]
    d = total.shape[1]
    row = lax.broadcasted_iota(jnp.int32, (16, d), 0)
    sums = jnp.where(row == 2, jnp.sum(total * hat_ref[...], 0, keepdims=True), 0.0)
    sums = jnp.where(row == 3, jnp.sum(total, 0, keepdims=True), sums)
    sums = jnp.where(row == 4, jnp.sum(cot_ref[...].astype(F32), 0, keepdims=True), sums)
    for b in range(half):
        here = row == 8 + part_ref[0] * half + b
        sums = jnp.where(here, up_ref[:, b * d : (b + 1) * d], sums)
    sums = jnp.concatenate([sums, jnp.zeros((TILE - 16, d), F32)], 0)
    out_ref[...] = sums.T.astype(BF)


def vector_sums(c, hat, cot, up_sums, pieces):
    d = hat.shape[1]
    whole = pl.BlockSpec(memory_space=pltpu.VMEM)
    return pl.pallas_call(
        functools.partial(vector_kernel, up_sums.shape[1] // d),
        in_specs=[pl.BlockSpec(memory_space=pltpu.SMEM)] + [whole] * (3 + len(pieces)),
        out_specs=whole,
        out_shape=jax.ShapeDtypeStruct((d, TILE), BF),
        compiler_params=pltpu.CompilerParams(vmem_limit_bytes=VMEM_BYTES),
        name="vector_sums",
    )(c[None], hat, cot, up_sums, *pieces)


def pack_columns(matrix, trios):
    r = matrix.shape[0]
    q, k, v = (
        part.reshape(r, trios, TRIO * HEAD_DIM) for part in jnp.split(matrix, 3, axis=1)
    )
    zeros = jnp.zeros((r, trios, HEAD_DIM), matrix.dtype)
    pieces = [q[..., :TILE], k[..., :TILE], v[..., :TILE], q[..., TILE:], k[..., TILE:]]
    return jnp.concatenate(pieces + [v[..., TILE:], zeros], -1).reshape(r, trios * PACK)


def unpack_columns(matrix, trios):
    r = matrix.shape[0]
    m = matrix.reshape(r, trios, PACK)
    halves = [
        m[..., 3 * TILE : 3 * TILE + HEAD_DIM],
        m[..., 3 * TILE + HEAD_DIM : 4 * TILE],
        m[..., 4 * TILE : 4 * TILE + HEAD_DIM],
    ]
    return jnp.concatenate(
        [
            jnp.concatenate([m[..., i * TILE : (i + 1) * TILE], halves[i]], -1).reshape(r, -1)
            for i in range(3)
        ],
        -1,
    )


def split_hidden(matrix, count, r):
    lead = matrix.shape[0]
    return matrix.reshape(lead, count, -1, r).transpose(0, 2, 1, 3).reshape(lead, -1)


def join_hidden(matrix, count, r):
    lead = matrix.shape[0]
    return matrix.reshape(lead, -1, count, r).transpose(0, 2, 1, 3).reshape(lead, -1)


def on_device(
    tokens,
    segment,
    ln1_gain,
    ln1_bias,
    ln2_gain,
    ln2_bias,
    qkv_weight,
    qkv_bias,
    dense_weight,
    dense_bias,
    fc1_weight,
    fc1_bias,
    output_feed_weight,
    output_feed_bias,
    cotangent,
):
    rows, groups, d = tokens.shape
    units = lax.axis_size("unit")
    part = lax.axis_size("part")
    count = units * part * lax.axis_size("seq")
    trios = units // groups
    all_rows = rows * groups
    r = qkv_weight.shape[0]
    ff = fc1_weight.shape[1]
    blocks = ff // d
    c = lax.axis_index("part")
    unit = lax.axis_index("unit")

    seq = lax.axis_index("seq")
    seqs = lax.axis_size("seq")
    place = (seq * units + unit) * part + c

    def exchange(blocks_out):
        width = blocks_out.shape[-1]
        return lax.all_to_all(
            blocks_out.reshape(-1, width), "unit", 0, 0, tiled=True
        ).reshape(blocks_out.shape)

    def shift(value, axis, i):
        n = lax.axis_size(axis)
        return lax.ppermute(value, axis, [(p, (p + i) % n) for p in range(n)])

    def flip_unit(value, bit):
        return lax.ppermute(value, "unit", [(u, u ^ bit) for u in range(units)])

    def pick(value, index, axis):
        return lax.dynamic_index_in_dim(value, index, axis, False)

    bits = (unit // trios, unit // 2 % 2, unit % 2)

    def exchange_small(value):
        shape = value.shape
        value = value.reshape((2, 2, 2) + shape[1:])
        for axis, bit in enumerate((trios, 2, 1)):
            keep = pick(value, bits[axis], axis)
            value = jnp.stack([keep, flip_unit(pick(value, 1 - bits[axis], axis), bit)], axis)
        for axis in range(3):
            value = jnp.where(bits[axis] == 0, value, jnp.flip(value, axis))
        return value.reshape(shape)

    def exchange_trio(value):
        for axis in range(2):
            bit = bits[axis + 1]
            away = flip_unit(pick(value, 1 - bit, axis), (2, 1)[axis])
            value = jnp.stack([pick(value, bit, axis), away], axis)
        for axis in range(2):
            value = jnp.where(bits[axis + 1] == 0, value, jnp.flip(value, axis))
        return value.reshape((trios,) + value.shape[2:])

    def spread_tokens(value, beside):
        keep = pick(value, bits[0], 0)
        both = jnp.stack([keep, flip_unit(pick(value, 1 - bits[0], 0), trios)])
        one, two = both[:, : rows // 2], both[:, rows // 2 :]
        one = jnp.stack([one, flip_unit(one, 2)])
        two = jnp.stack([two, flip_unit(two, 1)])
        one, two, beside = lax.optimization_barrier((one, two, beside))
        one = jnp.stack([one, flip_unit(one, 1)])
        two = jnp.stack([two, flip_unit(two, 2)])
        return (one.reshape(units, rows // 2, d), two.reshape(units, rows // 2, d)), beside

    def add(a, b):
        return (a.astype(F32) + b.astype(F32)).astype(BF)

    def natural_order(got, me):
        n = len(got)
        if n == 2:
            return jnp.where(me == 0, jnp.stack(got), jnp.stack(got[::-1]))
        ring = jnp.stack((got + got)[::-1])
        return lax.dynamic_slice_in_dim(ring, n - 1 - me, n, 0)

    def gather_small(value, axis):
        n = lax.axis_size(axis)
        got = [value] + [shift(value, axis, i) for i in range(1, n)]
        return natural_order(got, lax.axis_index(axis))

    def swap_parts(value):
        got = [lax.dynamic_index_in_dim(value, c, 0, False)]
        for i in range(1, part):
            piece = lax.dynamic_index_in_dim(value, (c + i) % part, 0, False)
            got.append(shift(piece, "part", i))
        return natural_order(got, c)

    def all_parts(value):
        return jnp.concatenate([value] + [shift(value, "part", i) for i in range(1, part)], 0)

    def part_pieces(value):
        n = value.shape[0] // part
        return [value[:n]] + [
            shift(value[i * n : (i + 1) * n], "part", part - i) for i in range(1, part)
        ]

    def halve(value, axis, which):
        if isinstance(which, str):
            n = lax.axis_size(which)
            me = lax.axis_index(which)
            return [pick(value, me, axis)] + [
                shift(pick(value, (me + i) % n, axis), which, i) for i in range(1, n)
            ]
        away = pick(value, 1 - bits[which], axis)
        return [pick(value, bits[which], axis), flip_unit(away, (trios, 2, 1)[which])]

    def add_up(pieces):
        total = pieces[0].astype(F32)
        for piece in pieces[1:]:
            total = total + piece.astype(F32)
        return total.astype(BF)

    vectors = (ln1_gain, ln1_bias, ln2_gain, ln2_bias, dense_bias, output_feed_bias)
    vec = jnp.concatenate(
        [v.reshape(r, 1) for v in vectors] + [qkv_bias.reshape(r, 3), fc1_bias.reshape(r, blocks)],
        1,
    )
    token_rows = tokens.transpose(1, 0, 2)
    seg_rows = segment.T
    seg_lanes = -(-2 * rows // r)
    seg_pack = jnp.concatenate([seg_rows // 64, seg_rows % 64], 1).astype(BF)
    seg_pack = jnp.pad(seg_pack, ((0, 0), (0, seg_lanes * r - 2 * rows)))
    seg_pack = seg_pack.reshape(groups, r, seg_lanes)
    vec = jnp.pad(vec, ((0, 0), (0, 16 - vec.shape[1])))
    vec = jnp.concatenate(
        [
            jnp.broadcast_to(vec, (groups, r, 16)),
            seg_pack,
            jnp.zeros((groups, r, TILE - 16 - seg_lanes), BF),
        ],
        -1,
    )
    early, qkv_local = pack_early(qkv_weight, vec, trios)
    early = exchange_small(early)
    feed_blocks = output_feed_weight.reshape(blocks, r, d)
    half = blocks // part
    up_local = split_hidden(fc1_weight, count, r)
    second_pack = jnp.stack(
        [
            jnp.concatenate(
                [up_local[:, p * half * d : (p + 1) * half * d]]
                + [feed_blocks[b] for b in range(p * half, (p + 1) * half)]
                + [dense_weight],
                1,
            )
            for p in range(part)
        ]
    )
    second_pack = swap_parts(second_pack).reshape(part * r, -1)
    toks, (second_pack, early) = spread_tokens(token_rows, (second_pack, early))
    second = lax.all_gather(second_pack, ("seq", "unit"), axis=0, tiled=True)

    seg_mine = early[:, :, PACK + 16 : PACK + 16 + seg_lanes].astype(jnp.int32)
    seg_mine = seg_mine.reshape(units, r * seg_lanes)
    seg_mine = seg_mine[:, :rows] * 64 + seg_mine[:, rows : 2 * rows]
    meta = jnp.concatenate([seg_mine[:, 0], seg_mine[:, -1], c[None]])
    seg_mine = seg_mine[:, None, :]
    trio_full = gather_small(gather_small(early, "seq"), "part")
    trio_full = trio_full.transpose(1, 2, 0, 3, 4).reshape(d, PACK + TILE)
    vec_full = trio_full[:, PACK:].astype(F32)
    vec_rows = vec_full[:, :8].T
    gain_one, bias_one, gain_two, bias_two, dense_shift, down_shift = (
        vec_rows[i : i + 1] for i in range(6)
    )
    qkv_shift = pack_columns(vec_full[:, 6:9].reshape(1, 3 * d), trios).reshape(trios, PACK)
    qkv_shift = lax.dynamic_slice_in_dim(qkv_shift, unit % trios, 1, 0)
    up_shift = split_hidden(vec_full[:, 9 : 9 + blocks].reshape(1, ff), count, r)

    block_start = (jnp.arange(units, dtype=jnp.int32) * part + c) * rows
    positions = block_start[:, None, None] + jnp.arange(rows, dtype=jnp.int32) - seg_mine
    freq = jnp.arange(ROT // 2, dtype=F32)
    inverse = jnp.exp(freq * (-2.0 * math.log(10000.0) / ROT))
    angles = positions.astype(F32) * inverse[None, :, None]
    cos = jnp.cos(angles)
    sin = jnp.sin(angles)

    place_unit = unit[None]
    packed, kv_own, normed_one, hat_one = project(
        place_unit, toks, trio_full, qkv_shift, gain_one, bias_one, cos, sin
    )
    kv = [kv_own] + [shift(kv_own, "part", i) for i in range(1, part)]
    out_low, out_t, lse = attend_forward(meta, packed, kv, seg_mine)
    second, out_low = lax.optimization_barrier((second, out_low))
    attended = exchange(out_low)
    dense_pad = jnp.pad(
        second[:, 2 * half * d :].reshape(trios, d // trios, d),
        ((0, 0), (0, OPACK - d // trios), (0, 0)),
    )

    x = token_rows.reshape(all_rows, d).astype(F32)
    cot = cotangent.transpose(1, 0, 2).reshape(all_rows, d)
    centre = x - jnp.mean(x, -1, keepdims=True)
    spread = lax.rsqrt(jnp.mean(centre * centre, -1, keepdims=True) + EPSILON)
    xhat = centre * spread
    normed_two = (xhat * gain_two + bias_two).astype(BF)
    attended_grad = jnp.einsum(
        "sld,gkd->sglk", cot.reshape(groups, rows, d), dense_pad, preferred_element_type=F32
    ).astype(BF)
    dout = exchange(attended_grad.reshape(units, rows, OPACK))
    normed_all = all_parts(normed_two)
    cot_all = all_parts(cot)
    up_shift = lax.dynamic_slice_in_dim(up_shift, c * half * d, half * d, 1)
    hidden_low, pre_grad, up_shift_grad, second_branch, normed_two_grad = feed_forward(
        normed_all, cot_all, second, up_shift, half
    )
    hidden_low, pre_grad, attended = lax.optimization_barrier((hidden_low, pre_grad, attended))
    second_branch = part_pieces(second_branch)
    normed_two_grad = part_pieces(normed_two_grad)
    def norm_back(grad, gain):
        gy = grad * gain
        return spread * (
            gy - jnp.mean(gy, -1, keepdims=True) - xhat * jnp.mean(gy * xhat, -1, keepdims=True)
        )

    mlp_grads = gradients(normed_all, pre_grad, hidden_low, cot_all)
    mlp_grads, dout = lax.optimization_barrier((mlp_grads, dout))

    split = (seqs, 2, 2, 2, part * r, half * d)
    up_part = halve(mlp_grads[:, : half * d].reshape(split), 0, "seq")
    down_part = halve(mlp_grads[:, half * d :].reshape(split), 3, 2)

    attended = attended.reshape(groups, trios, rows, OPACK).transpose(0, 2, 1, 3)
    attended = attended.reshape(all_rows, trios * OPACK)
    dense_grad = outer_sum(attended, cot).reshape(trios, OPACK, d)[:, : d // trios].reshape(d, d)
    vec_grads = vector_sums(c, xhat, cot, up_shift_grad, normed_two_grad)
    dense_part = jnp.concatenate([dense_grad.astype(BF), vec_grads], 1)
    dense_part, lse = lax.optimization_barrier((dense_part, lse))
    dense_part = halve(dense_part.reshape(seqs, units, part, r, d + TILE), 2, "part")

    own, others = attend_backward(meta, packed, dout, out_t, lse, kv, seg_mine)
    others = [shift(others[i - 1], "part", part - i) for i in range(1, part)]
    up_part, down_part, dense_part, own = lax.optimization_barrier(
        (up_part, down_part, dense_part, own)
    )
    up_part = halve(add_up(up_part), 2, 2)
    down_part = halve(add_up(down_part), 0, "seq")
    dense_part = halve(add_up(dense_part), 0, "seq")
    qkv_grad, back_one, back_two = unturn(place_unit, own, others, trio_full, cos, sin)
    back_one = back_one.reshape(2, 2, 2, rows // 2, d)
    back_two = back_two.reshape(2, 2, 2, rows // 2, d)
    swapped = flip_unit(back_one[1], 1), flip_unit(back_two[1], 2)

    late, shift_grad = trio_gradient(normed_one, hat_one, qkv_grad, trio_full)
    swapped, late, up_part, down_part, dense_part = lax.optimization_barrier(
        (swapped, late, up_part, down_part, dense_part)
    )
    back_one = add(back_one[0], swapped[0])
    back_two = add(back_two[0], swapped[1])
    swapped = flip_unit(back_one[1], 2), flip_unit(back_two[1], 1)
    mlp_part = jnp.concatenate([add_up(up_part), add_up(down_part)], -1)
    mlp_part = halve(mlp_part, 1, 1)
    dense_part = add_up(dense_part).reshape(2, 2, 2, r, d + TILE)
    dense_part = halve(dense_part, 2, 2)
    late = late.reshape(seqs, units, part, r, -1)
    shift_rows = jnp.pad(shift_grad.astype(BF), ((0, 7), (0, TILE)))
    late = jnp.concatenate(
        [late, jnp.broadcast_to(shift_rows, (seqs, units, part) + shift_rows.shape)], 3
    )
    late = halve(late, 2, "part")
    swapped, late, mlp_part, dense_part = lax.optimization_barrier(
        (swapped, late, mlp_part, dense_part)
    )
    dense_part = halve(add_up(dense_part), 1, 1)
    both = jnp.concatenate(
        [add(back_one[0], swapped[0]), add(back_two[0], swapped[1])], 1
    )
    swapped = flip_unit(both[1], trios)
    mlp_part = halve(add_up(mlp_part), 0, 0)
    late = halve(add_up(late), 0, "seq")
    swapped, late, mlp_part, dense_part = lax.optimization_barrier(
        (swapped, late, mlp_part, dense_part)
    )
    mlp_sum = swap_parts(add_up(mlp_part).reshape(part, r, -1)).astype(F32)
    rest = add_up(halve(add_up(dense_part), 0, 0)).astype(F32)
    dense_sum = rest[:, :d]
    late = add_up(halve(add_up(late).reshape(2, 2, 2, r + 8, PACK + TILE), 0, 0))
    late = exchange_trio(late).astype(F32)
    back = jnp.where(
        bits[0] == 0, jnp.stack([both[0], swapped]), jnp.stack([swapped, both[0]])
    )
    branch_one = mm(attended, dense_pad.reshape(trios * OPACK, d)) + dense_shift
    output = (x + branch_one + sum(second_branch) + down_shift).astype(BF)
    in_two = norm_back(sum(normed_two_grad), gain_two)
    qkv_weight_grad = unpack_columns(
        late[:, :r, :PACK].transpose(1, 0, 2).reshape(r, trios * PACK), trios
    )
    late_vec = jnp.sum(late[:, :r, PACK:], 0) + rest[:, d:]
    qkv_shift_grad = unpack_columns(late[:, r, :PACK].reshape(1, trios * PACK), trios)[0]
    qkv_shift_grad = lax.dynamic_slice_in_dim(qkv_shift_grad, place * 3 * r, 3 * r)

    up_sum = jnp.concatenate([mlp_sum[p, :, : half * d] for p in range(part)], 1)
    down_sum = jnp.concatenate(
        [
            mlp_sum[p, :, (half + b) * d : (half + b + 1) * d]
            for p in range(part)
            for b in range(half)
        ],
        0,
    )
    param_grads = (
        late_vec[:, 0],
        late_vec[:, 1],
        late_vec[:, 2],
        late_vec[:, 3],
        qkv_weight_grad,
        qkv_shift_grad,
        dense_sum,
        late_vec[:, 4],
        join_hidden(up_sum, count, r),
        late_vec[:, 8 : 8 + blocks].T.reshape(-1),
        down_sum,
        late_vec[:, 4],
    )

    normed_one_grad = back.reshape(all_rows, d).astype(F32)
    in_one = norm_back(normed_one_grad, gain_one)
    tokens_grad = (cot.astype(F32) + in_one + in_two).astype(BF)

    def natural(value):
        return value.reshape(groups, rows, d).transpose(1, 0, 2)

    return (natural(output), natural(tokens_grad)) + tuple(param_grads)


def solution(mesh):
    devices = mesh.devices
    seq_size, ctx_size = devices.shape
    ctx = ("unit", "part")
    tok = P(ctx, "seq", None)
    vec = P(ALL_AXES)
    mat = P(ALL_AXES, None)
    pairs = (vec, vec, vec, vec, mat, vec, mat, vec, mat, vec, mat, vec)

    def run(tokens, *rest):
        units = HEADS // TRIO * (tokens.shape[1] // seq_size)
        split = Mesh(devices.reshape(seq_size, units, ctx_size // units), ALL_AXES)
        mapped = jax.shard_map(
            on_device,
            mesh=split,
            in_specs=(tok, P(ctx, "seq")) + pairs + (tok,),
            out_specs=(tok, tok) + pairs,
            check_vma=False,
        )
        return mapped(tokens, *rest)

    return run
```

```python
import functools
import math

import jax
import jax.numpy as jnp
from jax import lax
from jax.experimental import pallas as pl
from jax.experimental.pallas import tpu as pltpu
from jax.sharding import Mesh, PartitionSpec as P

HEADS = 12
HEAD_DIM = 64
ROT = 16
TRIO = 3
TILE = 128
PACK = 5 * TILE
OPACK = 2 * TILE

EPSILON = 1e-05
NEG_BIG = -1e30
BF = jnp.bfloat16
F32 = jnp.float32
ALL_AXES = ("seq", "unit", "part")
VMEM_BYTES = 56 * 1024 * 1024


def params_of(*semantics):
    return pltpu.CompilerParams(
        dimension_semantics=semantics, vmem_limit_bytes=VMEM_BYTES
    )


def mm(a, b):
    return jnp.dot(a, b, preferred_element_type=F32)


def outer_sum(left_rows, right_rows):
    return lax.dot_general(
        left_rows, right_rows, (((0,), (0,)), ((), ())), preferred_element_type=F32
    )


def inner_back(grad_rows, weight):
    return lax.dot_general(
        grad_rows, weight, (((1,), (1,)), ((), ())), preferred_element_type=F32
    )


def lane_of(shape):
    return lax.broadcasted_iota(jnp.int32, shape, len(shape) - 1)


def turn(tile, cos, sin):
    partner = jnp.where(
        lane_of(tile.shape) % HEAD_DIM < ROT // 2,
        pltpu.roll(tile, TILE - ROT // 2, 1),
        pltpu.roll(tile, ROT // 2, 1),
    )
    return tile * cos + partner * sin


def turn_tables(cos_rows, sin_rows):
    rows = cos_rows.shape[1]
    rest = HEAD_DIM - ROT
    cos_head = [cos_rows, cos_rows, jnp.ones((rest, rows), F32)]
    sin_head = [-sin_rows, sin_rows, jnp.zeros((rest, rows), F32)]
    return jnp.concatenate(cos_head * 2, 0).T, jnp.concatenate(sin_head * 2, 0).T


def first_place(rel):
    return rel % 2 * 4 + rel // 2 % 2 * 2 + rel // 4


def second_place(rel):
    return rel // 2 % 2 * 4 + rel % 2 * 2 + rel // 4


def project_kernel(
    place_ref,
    one_ref,
    two_ref,
    w_ref,
    b_ref,
    gain_ref,
    bias_ref,
    cos_ref,
    sin_ref,
    out_ref,
    kv_ref,
    norm_ref,
    hat_ref,
):
    x = jnp.concatenate([one_ref[0], two_ref[0]], 0).astype(F32)
    centre = x - jnp.mean(x, -1, keepdims=True)
    spread = jnp.mean(centre * centre, -1, keepdims=True)
    hat = centre * lax.rsqrt(spread + EPSILON)
    normed = (hat * gain_ref[...] + bias_ref[...]).astype(BF)
    hat_ref[0] = hat.astype(BF)
    norm_ref[0] = normed
    y = mm(normed, w_ref[...]) + b_ref[...]
    cos, sin = turn_tables(cos_ref[0], sin_ref[0])
    for t in range(5):
        tile = y[:, t * TILE : (t + 1) * TILE]
        if t in (0, 1, 3):
            tile = turn(tile, cos, sin)
        tile = tile.astype(BF)
        out_ref[0, :, t * TILE : (t + 1) * TILE] = tile
        if t > 0:
            kv_ref[0, :, (t - 1) * TILE : t * TILE] = tile


def half_specs(rows, d):
    return [
        pl.BlockSpec((1, rows // 2, d), lambda j, place: (first_place(j ^ place[0]), 0, 0)),
        pl.BlockSpec((1, rows // 2, d), lambda j, place: (second_place(j ^ place[0]), 0, 0)),
    ]


def project(place, toks, weight, bias, gain, offset, cos, sin):
    units, unused, rows = cos.shape
    d = toks[0].shape[2]
    tok_spec = pl.BlockSpec((1, rows, d), lambda j, place: (j, 0, 0))
    row_spec = pl.BlockSpec((1, d), lambda j, place: (0, 0))
    turn_spec = pl.BlockSpec((1, ROT // 2, rows), lambda j, place: (j, 0, 0))
    return pl.pallas_call(
        project_kernel,
        grid_spec=pltpu.PrefetchScalarGridSpec(
            num_scalar_prefetch=1,
            grid=(units,),
            in_specs=half_specs(rows, d)
            + [
                pl.BlockSpec((d, PACK), lambda j, place: (0, 0)),
                pl.BlockSpec((1, PACK), lambda j, place: (0, 0)),
                row_spec,
                row_spec,
                turn_spec,
                turn_spec,
            ],
            out_specs=[
                pl.BlockSpec((1, rows, PACK), lambda j, place: (j, 0, 0)),
                pl.BlockSpec((1, rows, PACK - TILE), lambda j, place: (j, 0, 0)),
                tok_spec,
                tok_spec,
            ],
        ),
        out_shape=[
            jax.ShapeDtypeStruct((units, rows, PACK), BF),
            jax.ShapeDtypeStruct((units, rows, PACK - TILE), BF),
            jax.ShapeDtypeStruct((units, rows, d), BF),
            jax.ShapeDtypeStruct((units, rows, d), BF),
        ],
        compiler_params=params_of("arbitrary"),
        cost_estimate=pl.CostEstimate(flops=0, bytes_accessed=0, transcendentals=0),
        name="project",
    )(place, *toks, weight, bias, gain, offset, cos, sin)


def unturn_kernel(place_ref, own_ref, *refs):
    w_ref, cos_ref, sin_ref, out_ref, one_ref, two_ref = refs[-6:]
    others = refs[:-6]
    cos, sin = turn_tables(cos_ref[0], sin_ref[0])
    for t in range(5):
        tile = own_ref[0, :, t * TILE : (t + 1) * TILE].astype(F32)
        if t > 0:
            for other in others:
                tile = tile + other[0, :, (t - 1) * TILE : t * TILE].astype(F32)
        if t in (0, 1, 3):
            tile = turn(tile, cos, -sin)
        out_ref[0, :, t * TILE : (t + 1) * TILE] = tile.astype(BF)
    back = inner_back(out_ref[0], w_ref[...]).astype(BF)
    rows = back.shape[0] // 2
    one_ref[0] = back[:rows]
    two_ref[0] = back[rows:]


def unturn(place, own, others, weight, cos, sin):
    units, rows, unused = own.shape
    d = weight.shape[0]
    turn_spec = pl.BlockSpec((1, ROT // 2, rows), lambda j, place: (j, 0, 0))
    own_spec = pl.BlockSpec((1, rows, PACK), lambda j, place: (j, 0, 0))
    other_spec = pl.BlockSpec((1, rows, PACK - TILE), lambda j, place: (j, 0, 0))
    half = jax.ShapeDtypeStruct((units, rows // 2, d), BF)
    return pl.pallas_call(
        unturn_kernel,
        grid_spec=pltpu.PrefetchScalarGridSpec(
            num_scalar_prefetch=1,
            grid=(units,),
            in_specs=[own_spec]
            + [other_spec] * len(others)
            + [pl.BlockSpec((d, PACK), lambda j, place: (0, 0)), turn_spec, turn_spec],
            out_specs=[own_spec] + half_specs(rows, d),
        ),
        out_shape=[jax.ShapeDtypeStruct(own.shape, BF), half, half],
        compiler_params=params_of("arbitrary"),
        cost_estimate=pl.CostEstimate(flops=0, bytes_accessed=0, transcendentals=0),
        name="unturn",
    )(place, own, *others, weight, cos, sin)


def flip(tile):
    return tile.astype(F32).T


def head_rows(flipped, low):
    row = lax.broadcasted_iota(jnp.int32, flipped.shape, 0)
    keep = row < HEAD_DIM if low else row >= HEAD_DIM
    return jnp.where(keep, flipped, 0.0)


def head_lanes(tile, low):
    lane = lane_of(tile.shape)
    keep = lane < HEAD_DIM if low else lane >= HEAD_DIM
    return jnp.where(keep, tile, 0.0)


def query_sides(q_ref, qb):
    scale = HEAD_DIM ** (-0.5)
    a = flip(q_ref[0, :, 0:TILE]) * scale
    d = flip(q_ref[0, :, 3 * TILE : 4 * TILE]) * scale
    qb[0] = head_rows(a, True).astype(BF)
    qb[1] = head_rows(a, False).astype(BF)
    qb[2] = jnp.concatenate(
        [jnp.zeros((HEAD_DIM, d.shape[1]), F32), d[:HEAD_DIM]], 0
    ).astype(BF)


def live_of(seg_row, unit, query_start, part, rows, c):
    shape = (rows, rows)
    query_pos = query_start + lax.broadcasted_iota(jnp.int32, shape, 1)
    row = lax.broadcasted_iota(jnp.int32, shape, 0)
    pieces = []
    for i in range(part):
        key_pos = (unit * part + lax.rem(c - i + part, part)) * rows + row
        pieces.append((key_pos <= query_pos) & (key_pos >= seg_row))
    return jnp.concatenate(pieces, 0)


def unit_loop(meta, part, units, rows, step):
    j = pl.program_id(0)
    first = meta[j] // (rows * part)
    top_seg = meta[units + j]

    def one(unit, unused):
        masked = (unit == j) | (top_seg > unit * (rows * part))

        @pl.when(masked)
        def _():
            step(unit, True)

        @pl.when(jnp.logical_not(masked))
        def _():
            step(unit, False)

        return unused

    lax.fori_loop(first, j + 1, one, 0)


def join_parts(part, refs, kv_ref):
    rows = refs[0].shape[1]

    def one(unit, unused):
        for i in range(part):
            kv_ref[unit, i * rows : (i + 1) * rows] = refs[i][unit]
        return unused

    lax.fori_loop(0, refs[0].shape[0], one, 0)


def forward_kernel(part, units, meta, q_ref, *refs):
    seg_ref, o_ref, ot_ref, lse_ref, kv_ref, qb, vt, top, total, acc = refs[part:]
    rows = q_ref.shape[1]
    c = meta[2 * units]
    j = pl.program_id(0)

    @pl.when(j == 0)
    def _():
        join_parts(part, refs[:part], kv_ref)

        def turn_values(unit, unused):
            vt[unit, :TILE] = flip(kv_ref[unit, :, TILE : 2 * TILE]).astype(BF)
            vt[unit, TILE:] = flip(kv_ref[unit, :, 3 * TILE :])[:HEAD_DIM].astype(BF)
            return unused

        lax.fori_loop(0, units, turn_values, 0)

    query_sides(q_ref, qb)
    top[...] = jnp.full(top.shape, NEG_BIG, F32)
    total[...] = jnp.zeros(total.shape, F32)
    acc[...] = jnp.zeros(acc.shape, F32)
    seg_row = seg_ref[0]
    query_start = (j * part + c) * rows

    def step(unit, masked):
        k01 = kv_ref[unit, :, 0:TILE]
        k2 = kv_ref[unit, :, 2 * TILE : 3 * TILE]
        if masked:
            live = live_of(seg_row, unit, query_start, part, rows, c)
        scores = [mm(k2 if h == 2 else k01, qb[h]) for h in range(TRIO)]
        if masked:
            scores = [jnp.where(live, score, NEG_BIG) for score in scores]
        old = top[0:TRIO]
        new = jnp.concatenate([jnp.max(score, 0, keepdims=True) for score in scores], 0)
        new = jnp.maximum(old, new)
        factor = jnp.exp(old - new)
        weights = [jnp.exp(scores[h] - new[h : h + 1]) for h in range(TRIO)]
        if masked:
            weights = [jnp.where(live, weight, 0.0) for weight in weights]
        sums = [jnp.sum(weight, 0, keepdims=True) for weight in weights]
        top[0:TRIO] = new
        total[0:TRIO] = total[0:TRIO] * factor + jnp.concatenate(sums, 0)
        for h in range(TRIO):
            vth = vt[unit, h * HEAD_DIM : (h + 1) * HEAD_DIM]
            acc[h] = acc[h] * factor[h : h + 1] + mm(vth, weights[h].astype(BF))

    unit_loop(meta, part, units, rows, step)
    out = [acc[h] / total[h : h + 1] for h in range(TRIO)]
    for h in range(TRIO):
        ot_ref[0, h * HEAD_DIM : (h + 1) * HEAD_DIM] = out[h]
    lse_ref[0, 0:TRIO] = top[0:TRIO] + jnp.log(total[0:TRIO])
    o_ref[0, :, :TILE] = jnp.concatenate(out[:2], 0).T.astype(BF)
    o_ref[0, :, TILE:] = jnp.concatenate([out[2], jnp.zeros_like(out[2])], 0).T.astype(BF)


def backward_kernel(part, units, meta, q_ref, do_ref, ot_ref, lse_ref, *refs):
    seg_ref, own_ref, oth_ref, kv_ref, qb, db, qn, dn, kt, delta, dqt = refs[part : part + 11]
    dk01, dv01, dk2, dv2 = refs[part + 11 :]
    rows = q_ref.shape[1]
    c = meta[2 * units]
    j = pl.program_id(0)

    @pl.when(j == 0)
    def _():
        join_parts(part, refs[:part], kv_ref)

        def turn_keys(unit, unused):
            kt[unit, :TILE] = flip(kv_ref[unit, :, 0:TILE]).astype(BF)
            kt[unit, TILE:] = flip(kv_ref[unit, :, 2 * TILE : 3 * TILE])[HEAD_DIM:].astype(BF)
            return unused

        lax.fori_loop(0, units, turn_keys, 0)
        for ref in (dk01, dv01, dk2, dv2):
            ref[...] = jnp.zeros(ref.shape, F32)

    query_sides(q_ref, qb)
    scale = HEAD_DIM ** (-0.5)
    q01 = q_ref[0, :, 0:TILE].astype(F32) * scale
    q2 = pltpu.roll(q_ref[0, :, 3 * TILE : 4 * TILE].astype(F32), HEAD_DIM, 1) * scale
    qn[0:rows] = head_lanes(q01, True).astype(BF)
    qn[rows : 2 * rows] = head_lanes(q01, False).astype(BF)
    qn[2 * rows :] = head_lanes(q2, False).astype(BF)
    do01 = do_ref[0, :, :TILE].astype(F32)
    do2 = do_ref[0, :, TILE:].astype(F32)
    dn[0:rows] = head_lanes(do01, True).astype(BF)
    dn[rows : 2 * rows] = head_lanes(do01, False).astype(BF)
    dn[2 * rows :] = do2.astype(BF)
    do01t = do01.T
    do2t = do2.T
    db[0] = head_rows(do01t, True).astype(BF)
    db[1] = head_rows(do01t, False).astype(BF)
    db[2] = do2t.astype(BF)
    for h in range(TRIO):
        dot = do2t[:HEAD_DIM] if h == 2 else do01t[h * HEAD_DIM : (h + 1) * HEAD_DIM]
        delta[h : h + 1] = jnp.sum(
            dot * ot_ref[0, h * HEAD_DIM : (h + 1) * HEAD_DIM], 0, keepdims=True
        )
    dqt[...] = jnp.zeros(dqt.shape, F32)
    seg_row = seg_ref[0]
    query_start = (j * part + c) * rows

    def step(unit, masked):
        k01 = kv_ref[unit, :, 0:TILE]
        v01 = kv_ref[unit, :, TILE : 2 * TILE]
        k2 = kv_ref[unit, :, 2 * TILE : 3 * TILE]
        v2 = kv_ref[unit, :, 3 * TILE :]
        if masked:
            live = live_of(seg_row, unit, query_start, part, rows, c)
        scores = [mm(k2 if h == 2 else k01, qb[h]) for h in range(TRIO)]
        dprobs = [mm(v2 if h == 2 else v01, db[h]) for h in range(TRIO)]
        probs = []
        grads = []
        for h in range(TRIO):
            score = scores[h]
            if masked:
                score = jnp.where(live, score, NEG_BIG)
            prob = jnp.exp(score - lse_ref[0, h : h + 1])
            if masked:
                prob = jnp.where(live, prob, 0.0)
            probs.append(prob.astype(BF))
            grads.append((prob * (dprobs[h] - delta[h : h + 1])).astype(BF))
        dv01[unit] += mm(jnp.concatenate(probs[:2], 1), dn[: 2 * rows])
        dk01[unit] += mm(jnp.concatenate(grads[:2], 1), qn[: 2 * rows])
        dv2[unit] += mm(probs[2], dn[2 * rows :])
        dk2[unit] += mm(grads[2], qn[2 * rows :])
        for h in range(TRIO):
            kth = kt[unit, h * HEAD_DIM : (h + 1) * HEAD_DIM]
            dqt[h * HEAD_DIM : (h + 1) * HEAD_DIM] += mm(kth, grads[h])

    unit_loop(meta, part, units, rows, step)
    own_ref[j, :, 0:TILE] = (dqt[:TILE] * scale).T.astype(BF)
    dq2 = dqt[TILE:] * scale
    dk2[j, 0:rows] += jnp.concatenate([dq2, jnp.zeros_like(dq2)], 0).T

    @pl.when(j == units - 1)
    def _():
        for unit in range(units):
            for i in range(part):
                span = slice(i * rows, (i + 1) * rows)
                for t, ref in enumerate((dk01, dv01, dk2, dv2)):
                    tile = ref[unit, span].astype(BF)
                    if i == 0:
                        own_ref[unit, :, (t + 1) * TILE : (t + 2) * TILE] = tile
                    else:
                        oth_ref[i - 1, unit, :, t * TILE : (t + 1) * TILE] = tile


def whole_spec(shape):
    zeros = (0,) * len(shape)
    return pl.BlockSpec(shape, lambda j, meta: zeros)


def attend_forward(meta, packed, kv, seg):
    units, rows, unused = packed.shape
    part = len(kv)
    return pl.pallas_call(
        functools.partial(forward_kernel, part, units),
        grid_spec=pltpu.PrefetchScalarGridSpec(
            num_scalar_prefetch=1,
            grid=(units,),
            in_specs=[
                pl.BlockSpec((1, rows, PACK), lambda j, meta: (j, 0, 0)),
                *[whole_spec(piece.shape) for piece in kv],
                pl.BlockSpec((1, 1, rows), lambda j, meta: (j, 0, 0)),
            ],
            out_specs=[
                pl.BlockSpec((1, rows, OPACK), lambda j, meta: (j, 0, 0)),
                pl.BlockSpec((1, TRIO * HEAD_DIM, rows), lambda j, meta: (j, 0, 0)),
                pl.BlockSpec((1, 8, rows), lambda j, meta: (j, 0, 0)),
            ],
            scratch_shapes=[
                pltpu.VMEM((units, part * rows, PACK - TILE), BF),
                pltpu.VMEM((TRIO, TILE, rows), BF),
                pltpu.VMEM((units, TRIO * HEAD_DIM, part * rows), BF),
                pltpu.VMEM((8, rows), F32),
                pltpu.VMEM((8, rows), F32),
                pltpu.VMEM((TRIO, HEAD_DIM, rows), F32),
            ],
        ),
        out_shape=[
            jax.ShapeDtypeStruct((units, rows, OPACK), BF),
            jax.ShapeDtypeStruct((units, TRIO * HEAD_DIM, rows), F32),
            jax.ShapeDtypeStruct((units, 8, rows), F32),
        ],
        compiler_params=params_of("arbitrary"),
        cost_estimate=pl.CostEstimate(flops=0, bytes_accessed=0, transcendentals=0),
        name="attend_forward",
    )(meta, packed, *kv, seg)


def attend_backward(meta, packed, dout, out_t, lse, kv, seg):
    units, rows, unused = packed.shape
    part = len(kv)
    others = (max(part - 1, 1), units, rows, 4 * TILE)
    grads = pltpu.VMEM((units, part * rows, TILE), F32)
    return pl.pallas_call(
        functools.partial(backward_kernel, part, units),
        grid_spec=pltpu.PrefetchScalarGridSpec(
            num_scalar_prefetch=1,
            grid=(units,),
            in_specs=[
                pl.BlockSpec((1, rows, PACK), lambda j, meta: (j, 0, 0)),
                pl.BlockSpec((1, rows, OPACK), lambda j, meta: (j, 0, 0)),
                pl.BlockSpec((1, TRIO * HEAD_DIM, rows), lambda j, meta: (j, 0, 0)),
                pl.BlockSpec((1, 8, rows), lambda j, meta: (j, 0, 0)),
                *[whole_spec(piece.shape) for piece in kv],
                pl.BlockSpec((1, 1, rows), lambda j, meta: (j, 0, 0)),
            ],
            out_specs=[whole_spec(packed.shape), whole_spec(others)],
            scratch_shapes=[
                pltpu.VMEM((units, part * rows, PACK - TILE), BF),
                pltpu.VMEM((TRIO, TILE, rows), BF),
                pltpu.VMEM((TRIO, TILE, rows), BF),
                pltpu.VMEM((TRIO * rows, TILE), BF),
                pltpu.VMEM((TRIO * rows, TILE), BF),
                pltpu.VMEM((units, TRIO * HEAD_DIM, part * rows), BF),
                pltpu.VMEM((8, rows), F32),
                pltpu.VMEM((TRIO * HEAD_DIM, rows), F32),
                grads,
                grads,
                grads,
                grads,
            ],
        ),
        out_shape=[
            jax.ShapeDtypeStruct(packed.shape, BF),
            jax.ShapeDtypeStruct(others, BF),
        ],
        compiler_params=params_of("arbitrary"),
        cost_estimate=pl.CostEstimate(
            flops=63 * units * units * part * rows * rows * HEAD_DIM * TRIO, bytes_accessed=0, transcendentals=0
        ),
        name="attend_backward",
    )(meta, packed, dout, out_t, lse, *kv, seg)


def pack_kernel(trios, groups, w_ref, vec_ref, early_ref, local_ref):
    d = w_ref.shape[1] // 3
    w = w_ref[...].astype(F32)
    width = TRIO * HEAD_DIM
    zeros = jnp.zeros((w.shape[0], HEAD_DIM), F32)
    for g in range(trios):
        q, k, v = (w[:, i * d + g * width : i * d + (g + 1) * width] for i in range(3))
        tiles = [q[:, :TILE], k[:, :TILE], v[:, :TILE]]
        tiles.append(jnp.concatenate([q[:, TILE:], k[:, TILE:]], 1))
        tiles.append(jnp.concatenate([v[:, TILE:], zeros], 1))
        for t, tile in enumerate(tiles):
            tile = tile.astype(BF)
            local_ref[:, g * PACK + t * TILE : g * PACK + (t + 1) * TILE] = tile
            for s in range(groups):
                early_ref[s * trios + g, :, t * TILE : (t + 1) * TILE] = tile
        for s in range(groups):
            early_ref[s * trios + g, :, PACK:] = vec_ref[s]


def pack_early(weight, vec, trios):
    r = weight.shape[0]
    groups = vec.shape[0]
    return pl.pallas_call(
        functools.partial(pack_kernel, trios, groups),
        out_shape=[
            jax.ShapeDtypeStruct((trios * groups, r, PACK + TILE), BF),
            jax.ShapeDtypeStruct((r, trios * PACK), BF),
        ],
        name="pack_early",
    )(weight, vec)


def feed_kernel(
    x_ref, cot_ref, up_ref, down_ref, shift_ref, hid_ref, pre_ref, sum_ref, second_ref, back_ref
):
    pre = mm(x_ref[...], up_ref[...]) + shift_ref[...]
    grad = inner_back(cot_ref[...], down_ref[...])
    cdf = 0.5 * (1.0 + lax.erf(pre * math.sqrt(0.5)))
    hidden = (pre * cdf).astype(BF)
    slope = cdf + pre * (jnp.exp(-0.5 * pre * pre) * (1.0 / math.sqrt(2.0 * math.pi)))
    pre_grad = (grad * slope).astype(BF)
    hid_ref[...] = hidden
    pre_ref[...] = pre_grad
    sum_ref[...] = jnp.sum(pre_grad.astype(F32), 0, keepdims=True)
    second = mm(hidden, down_ref[...])
    back = inner_back(pre_grad, up_ref[...])

    @pl.when(pl.program_id(0) == 0)
    def _():
        second_ref[...] = second
        back_ref[...] = back

    @pl.when(pl.program_id(0) > 0)
    def _():
        second_ref[...] += second
        back_ref[...] += back


def feed_forward(x, cot, weights, shift, blocks):
    rows, d = x.shape
    ff = blocks * d
    half = d // 2
    wide = pl.BlockSpec((rows, d), lambda i: (0, 0))
    column = pl.BlockSpec((rows, half), lambda i: (0, i))
    line = pl.BlockSpec((1, half), lambda i: (0, i))
    return pl.pallas_call(
        feed_kernel,
        grid=(2 * blocks,),
        in_specs=[
            wide,
            wide,
            pl.BlockSpec((d, half), lambda i: (0, i)),
            pl.BlockSpec((half, d), lambda i: (i % 2, blocks + i // 2)),
            line,
        ],
        out_specs=[column, column, line, wide, wide],
        out_shape=[
            jax.ShapeDtypeStruct((rows, ff), BF),
            jax.ShapeDtypeStruct((rows, ff), BF),
            jax.ShapeDtypeStruct((1, ff), F32),
            jax.ShapeDtypeStruct((rows, d), F32),
            jax.ShapeDtypeStruct((rows, d), F32),
        ],
        compiler_params=params_of("arbitrary"),
        cost_estimate=pl.CostEstimate(
            flops=8 * rows * d * ff, bytes_accessed=4 * d * ff, transcendentals=2 * rows * ff
        ),
        name="feed_forward",
    )(x, cot, weights, weights, shift)


def gradient_kernel(ups, norm_ref, pre_ref, hidden_ref, cot_ref, out_ref):
    i = pl.program_id(0)

    @pl.when(i < ups)
    def _():
        out_ref[...] = outer_sum(norm_ref[...], pre_ref[...]).astype(BF)

    @pl.when(i >= ups)
    def _():
        out_ref[...] = outer_sum(hidden_ref[...], cot_ref[...]).astype(BF)


def gradients(normed, pre_grad, hidden, cot):
    rows, d = normed.shape
    width = d // 2
    ups = hidden.shape[1] // width

    def down(i):
        return jnp.clip(i - ups, 0, ups - 1)

    return pl.pallas_call(
        functools.partial(gradient_kernel, ups),
        grid=(2 * ups,),
        in_specs=[
            pl.BlockSpec((rows, d), lambda i: (0, 0)),
            pl.BlockSpec((rows, width), lambda i: (0, jnp.minimum(i, ups - 1))),
            pl.BlockSpec((rows, d), lambda i: (0, down(i) // 2)),
            pl.BlockSpec((rows, width), lambda i: (0, down(i) % 2)),
        ],
        out_specs=pl.BlockSpec((d, width), lambda i: (0, i)),
        out_shape=jax.ShapeDtypeStruct((d, 2 * ups * width), BF),
        compiler_params=params_of("arbitrary"),
        cost_estimate=pl.CostEstimate(
            flops=4 * rows * d * ups * width, bytes_accessed=0, transcendentals=0
        ),
        name="gradients",
    )(normed, pre_grad, hidden, cot)


def trio_kernel(norm_ref, hat_ref, grad_ref, w_ref, late_ref, shift_ref, own, hat):
    j = pl.program_id(0)
    d = norm_ref.shape[2]
    grad = grad_ref[...].reshape(-1, PACK)
    own_part = outer_sum(norm_ref[...].reshape(-1, d), grad)
    hat_part = outer_sum(hat_ref[...].reshape(-1, d), grad)
    sums = jnp.sum(grad.astype(F32), 0, keepdims=True)

    @pl.when(j == 0)
    def _():
        own[...] = own_part
        hat[...] = hat_part
        shift_ref[...] = sums

    @pl.when(j > 0)
    def _():
        own[...] += own_part
        hat[...] += hat_part
        shift_ref[...] += sums

    @pl.when(j == pl.num_programs(0) - 1)
    def _():
        late_ref[:, :PACK] = own[...].astype(BF)
        weight = w_ref[...].astype(F32)
        lane = lane_of((d, TILE))
        vec = jnp.where(lane == 0, jnp.sum(weight * hat[...], 1, keepdims=True), 0.0)
        vec = jnp.where(lane == 1, jnp.sum(weight * shift_ref[...], 1, keepdims=True), vec)
        late_ref[:, PACK:] = vec.astype(BF)


def trio_gradient(normed, hat, grad, weight):
    units, rows, d = normed.shape
    tok_spec = pl.BlockSpec((2, rows, d), lambda j: (j, 0, 0))
    return pl.pallas_call(
        trio_kernel,
        grid=(units // 2,),
        in_specs=[
            tok_spec,
            tok_spec,
            pl.BlockSpec((2, rows, PACK), lambda j: (j, 0, 0)),
            pl.BlockSpec((d, PACK), lambda j: (0, 0)),
        ],
        out_specs=[
            pl.BlockSpec((d, PACK + TILE), lambda j: (0, 0)),
            pl.BlockSpec((1, PACK), lambda j: (0, 0)),
        ],
        scratch_shapes=[pltpu.VMEM((d, PACK), F32), pltpu.VMEM((d, PACK), F32)],
        out_shape=[
            jax.ShapeDtypeStruct((d, PACK + TILE), BF),
            jax.ShapeDtypeStruct((1, PACK), F32),
        ],
        compiler_params=params_of("arbitrary"),
        cost_estimate=pl.CostEstimate(
            flops=12 * units * rows * d * PACK, bytes_accessed=0, transcendentals=0
        ),
        name="trio_gradient",
    )(normed, hat, grad, weight)


def vector_kernel(half, part_ref, hat_ref, cot_ref, up_ref, *refs):
    out_ref = refs[-1]
    total = refs[0][...]
    for ref in refs[1:-1]:
        total = total + ref[...]
    d = total.shape[1]
    row = lax.broadcasted_iota(jnp.int32, (16, d), 0)
    sums = jnp.where(row == 2, jnp.sum(total * hat_ref[...], 0, keepdims=True), 0.0)
    sums = jnp.where(row == 3, jnp.sum(total, 0, keepdims=True), sums)
    sums = jnp.where(row == 4, jnp.sum(cot_ref[...].astype(F32), 0, keepdims=True), sums)
    for b in range(half):
        here = row == 8 + part_ref[0] * half + b
        sums = jnp.where(here, up_ref[:, b * d : (b + 1) * d], sums)
    sums = jnp.concatenate([sums, jnp.zeros((TILE - 16, d), F32)], 0)
    out_ref[...] = sums.T.astype(BF)


def vector_sums(c, hat, cot, up_sums, pieces):
    d = hat.shape[1]
    whole = pl.BlockSpec(memory_space=pltpu.VMEM)
    return pl.pallas_call(
        functools.partial(vector_kernel, up_sums.shape[1] // d),
        in_specs=[pl.BlockSpec(memory_space=pltpu.SMEM)] + [whole] * (3 + len(pieces)),
        out_specs=whole,
        out_shape=jax.ShapeDtypeStruct((d, TILE), BF),
        compiler_params=pltpu.CompilerParams(vmem_limit_bytes=VMEM_BYTES),
        name="vector_sums",
    )(c[None], hat, cot, up_sums, *pieces)


def pack_columns(matrix, trios):
    r = matrix.shape[0]
    q, k, v = (
        part.reshape(r, trios, TRIO * HEAD_DIM) for part in jnp.split(matrix, 3, axis=1)
    )
    zeros = jnp.zeros((r, trios, HEAD_DIM), matrix.dtype)
    pieces = [q[..., :TILE], k[..., :TILE], v[..., :TILE], q[..., TILE:], k[..., TILE:]]
    return jnp.concatenate(pieces + [v[..., TILE:], zeros], -1).reshape(r, trios * PACK)


def unpack_columns(matrix, trios):
    r = matrix.shape[0]
    m = matrix.reshape(r, trios, PACK)
    halves = [
        m[..., 3 * TILE : 3 * TILE + HEAD_DIM],
        m[..., 3 * TILE + HEAD_DIM : 4 * TILE],
        m[..., 4 * TILE : 4 * TILE + HEAD_DIM],
    ]
    return jnp.concatenate(
        [
            jnp.concatenate([m[..., i * TILE : (i + 1) * TILE], halves[i]], -1).reshape(r, -1)
            for i in range(3)
        ],
        -1,
    )


def split_hidden(matrix, count, r):
    lead = matrix.shape[0]
    return matrix.reshape(lead, count, -1, r).transpose(0, 2, 1, 3).reshape(lead, -1)


def join_hidden(matrix, count, r):
    lead = matrix.shape[0]
    return matrix.reshape(lead, -1, count, r).transpose(0, 2, 1, 3).reshape(lead, -1)


def on_device(
    tokens,
    segment,
    ln1_gain,
    ln1_bias,
    ln2_gain,
    ln2_bias,
    qkv_weight,
    qkv_bias,
    dense_weight,
    dense_bias,
    fc1_weight,
    fc1_bias,
    output_feed_weight,
    output_feed_bias,
    cotangent,
):
    rows, groups, d = tokens.shape
    units = lax.axis_size("unit")
    part = lax.axis_size("part")
    count = units * part * lax.axis_size("seq")
    trios = units // groups
    all_rows = rows * groups
    r = qkv_weight.shape[0]
    ff = fc1_weight.shape[1]
    blocks = ff // d
    c = lax.axis_index("part")
    unit = lax.axis_index("unit")

    seq = lax.axis_index("seq")
    seqs = lax.axis_size("seq")
    place = (seq * units + unit) * part + c

    def exchange(blocks_out):
        width = blocks_out.shape[-1]
        return lax.all_to_all(
            blocks_out.reshape(-1, width), "unit", 0, 0, tiled=True
        ).reshape(blocks_out.shape)

    def shift(value, axis, i):
        n = lax.axis_size(axis)
        return lax.ppermute(value, axis, [(p, (p + i) % n) for p in range(n)])

    def flip_unit(value, bit):
        return lax.ppermute(value, "unit", [(u, u ^ bit) for u in range(units)])

    def pick(value, index, axis):
        return lax.dynamic_index_in_dim(value, index, axis, False)

    bits = (unit // trios, unit // 2 % 2, unit % 2)

    def exchange_small(value):
        shape = value.shape
        value = value.reshape((2, 2, 2) + shape[1:])
        for axis, bit in enumerate((trios, 2, 1)):
            keep = pick(value, bits[axis], axis)
            value = jnp.stack([keep, flip_unit(pick(value, 1 - bits[axis], axis), bit)], axis)
        for axis in range(3):
            value = jnp.where(bits[axis] == 0, value, jnp.flip(value, axis))
        return value.reshape(shape)

    def exchange_trio(value):
        for axis in range(2):
            bit = bits[axis + 1]
            away = flip_unit(pick(value, 1 - bit, axis), (2, 1)[axis])
            value = jnp.stack([pick(value, bit, axis), away], axis)
        for axis in range(2):
            value = jnp.where(bits[axis + 1] == 0, value, jnp.flip(value, axis))
        return value.reshape((trios,) + value.shape[2:])

    def spread_tokens(value, beside):
        keep = pick(value, bits[0], 0)
        both = jnp.stack([keep, flip_unit(pick(value, 1 - bits[0], 0), trios)])
        one, two = both[:, : rows // 2], both[:, rows // 2 :]
        one = jnp.stack([one, flip_unit(one, 2)])
        two = jnp.stack([two, flip_unit(two, 1)])
        one, two, beside = lax.optimization_barrier((one, two, beside))
        one = jnp.stack([one, flip_unit(one, 1)])
        two = jnp.stack([two, flip_unit(two, 2)])
        return (one.reshape(units, rows // 2, d), two.reshape(units, rows // 2, d)), beside

    def add(a, b):
        return (a.astype(F32) + b.astype(F32)).astype(BF)

    def natural_order(got, me):
        n = len(got)
        if n == 2:
            return jnp.where(me == 0, jnp.stack(got), jnp.stack(got[::-1]))
        ring = jnp.stack((got + got)[::-1])
        return lax.dynamic_slice_in_dim(ring, n - 1 - me, n, 0)

    def gather_small(value, axis):
        n = lax.axis_size(axis)
        got = [value] + [shift(value, axis, i) for i in range(1, n)]
        return natural_order(got, lax.axis_index(axis))

    def swap_parts(value):
        got = [lax.dynamic_index_in_dim(value, c, 0, False)]
        for i in range(1, part):
            piece = lax.dynamic_index_in_dim(value, (c + i) % part, 0, False)
            got.append(shift(piece, "part", i))
        return natural_order(got, c)

    def all_parts(value):
        return jnp.concatenate([value] + [shift(value, "part", i) for i in range(1, part)], 0)

    def part_pieces(value):
        n = value.shape[0] // part
        return [value[:n]] + [
            shift(value[i * n : (i + 1) * n], "part", part - i) for i in range(1, part)
        ]

    def halve(value, axis, which):
        if isinstance(which, str):
            n = lax.axis_size(which)
            me = lax.axis_index(which)
            return [pick(value, me, axis)] + [
                shift(pick(value, (me + i) % n, axis), which, i) for i in range(1, n)
            ]
        away = pick(value, 1 - bits[which], axis)
        return [pick(value, bits[which], axis), flip_unit(away, (trios, 2, 1)[which])]

    def add_up(pieces):
        total = pieces[0].astype(F32)
        for piece in pieces[1:]:
            total = total + piece.astype(F32)
        return total.astype(BF)

    vectors = (ln1_gain, ln1_bias, ln2_gain, ln2_bias, dense_bias, output_feed_bias)
    vec = jnp.concatenate(
        [v.reshape(r, 1) for v in vectors] + [qkv_bias.reshape(r, 3), fc1_bias.reshape(r, blocks)],
        1,
    )
    token_rows = tokens.transpose(1, 0, 2)
    seg_rows = segment.T
    seg_lanes = -(-2 * rows // r)
    seg_pack = jnp.concatenate([seg_rows // 64, seg_rows % 64], 1).astype(BF)
    seg_pack = jnp.pad(seg_pack, ((0, 0), (0, seg_lanes * r - 2 * rows)))
    seg_pack = seg_pack.reshape(groups, r, seg_lanes)
    vec = jnp.pad(vec, ((0, 0), (0, 16 - vec.shape[1])))
    vec = jnp.concatenate(
        [
            jnp.broadcast_to(vec, (groups, r, 16)),
            seg_pack,
            jnp.zeros((groups, r, TILE - 16 - seg_lanes), BF),
        ],
        -1,
    )
    early, qkv_local = pack_early(qkv_weight, vec, trios)
    early = exchange_small(early)
    feed_blocks = output_feed_weight.reshape(blocks, r, d)
    half = blocks // part
    up_local = split_hidden(fc1_weight, count, r)
    second_pack = jnp.stack(
        [
            jnp.concatenate(
                [up_local[:, p * half * d : (p + 1) * half * d]]
                + [feed_blocks[b] for b in range(p * half, (p + 1) * half)]
                + [dense_weight],
                1,
            )
            for p in range(part)
        ]
    )
    second_pack = swap_parts(second_pack).reshape(part * r, -1)
    toks, (second_pack, early) = spread_tokens(token_rows, (second_pack, early))
    second = lax.all_gather(second_pack, ("seq", "unit"), axis=0, tiled=True)

    seg_mine = early[:, :, PACK + 16 : PACK + 16 + seg_lanes].astype(jnp.int32)
    seg_mine = seg_mine.reshape(units, r * seg_lanes)
    seg_mine = seg_mine[:, :rows] * 64 + seg_mine[:, rows : 2 * rows]
    meta = jnp.concatenate([seg_mine[:, 0], seg_mine[:, -1], c[None]])
    seg_mine = seg_mine[:, None, :]
    trio_full = gather_small(gather_small(early, "seq"), "part")
    trio_full = trio_full.transpose(1, 2, 0, 3, 4).reshape(d, PACK + TILE)
    vec_full = trio_full[:, PACK:].astype(F32)
    vec_rows = vec_full[:, :8].T
    gain_one, bias_one, gain_two, bias_two, dense_shift, down_shift = (
        vec_rows[i : i + 1] for i in range(6)
    )
    qkv_shift = pack_columns(vec_full[:, 6:9].reshape(1, 3 * d), trios).reshape(trios, PACK)
    qkv_shift = lax.dynamic_slice_in_dim(qkv_shift, unit % trios, 1, 0)
    up_shift = split_hidden(vec_full[:, 9 : 9 + blocks].reshape(1, ff), count, r)

    block_start = (jnp.arange(units, dtype=jnp.int32) * part + c) * rows
    positions = block_start[:, None, None] + jnp.arange(rows, dtype=jnp.int32) - seg_mine
    freq = jnp.arange(ROT // 2, dtype=F32)
    inverse = jnp.exp(freq * (-2.0 * math.log(10000.0) / ROT))
    angles = positions.astype(F32) * inverse[None, :, None]
    cos = jnp.cos(angles)
    sin = jnp.sin(angles)

    place_unit = unit[None]
    packed, kv_own, normed_one, hat_one = project(
        place_unit, toks, trio_full, qkv_shift, gain_one, bias_one, cos, sin
    )
    kv = [kv_own] + [shift(kv_own, "part", i) for i in range(1, part)]
    out_low, out_t, lse = attend_forward(meta, packed, kv, seg_mine)
    second, out_low = lax.optimization_barrier((second, out_low))
    attended = exchange(out_low)
    dense_pad = jnp.pad(
        second[:, 2 * half * d :].reshape(trios, d // trios, d),
        ((0, 0), (0, OPACK - d // trios), (0, 0)),
    )

    x = token_rows.reshape(all_rows, d).astype(F32)
    cot = cotangent.transpose(1, 0, 2).reshape(all_rows, d)
    centre = x - jnp.mean(x, -1, keepdims=True)
    spread = lax.rsqrt(jnp.mean(centre * centre, -1, keepdims=True) + EPSILON)
    xhat = centre * spread
    normed_two = (xhat * gain_two + bias_two).astype(BF)
    attended_grad = jnp.einsum(
        "sld,gkd->sglk", cot.reshape(groups, rows, d), dense_pad, preferred_element_type=F32
    ).astype(BF)
    normed_all = all_parts(normed_two)
    cot_all = all_parts(cot)
    up_shift = lax.dynamic_slice_in_dim(up_shift, c * half * d, half * d, 1)
    hidden_low, pre_grad, up_shift_grad, second_branch, normed_two_grad = feed_forward(
        normed_all, cot_all, second, up_shift, half
    )
    hidden_low, pre_grad, attended, attended_grad = lax.optimization_barrier(
        (hidden_low, pre_grad, attended, attended_grad)
    )
    dout = exchange(attended_grad.reshape(units, rows, OPACK))
    second_branch = part_pieces(second_branch)
    normed_two_grad = part_pieces(normed_two_grad)
    def norm_back(grad, gain):
        gy = grad * gain
        return spread * (
            gy - jnp.mean(gy, -1, keepdims=True) - xhat * jnp.mean(gy * xhat, -1, keepdims=True)
        )

    mlp_grads = gradients(normed_all, pre_grad, hidden_low, cot_all)
    mlp_grads, dout = lax.optimization_barrier((mlp_grads, dout))

    split = (seqs, 2, 2, 2, part * r, half * d)
    up_part = halve(mlp_grads[:, : half * d].reshape(split), 0, "seq")
    down_part = halve(mlp_grads[:, half * d :].reshape(split), 1, 0)

    attended = attended.reshape(groups, trios, rows, OPACK).transpose(0, 2, 1, 3)
    attended = attended.reshape(all_rows, trios * OPACK)
    dense_grad = outer_sum(attended, cot).reshape(trios, OPACK, d)[:, : d // trios].reshape(d, d)
    vec_grads = vector_sums(c, xhat, cot, up_shift_grad, normed_two_grad)
    dense_part = jnp.concatenate([dense_grad.astype(BF), vec_grads], 1)
    dense_part, lse = lax.optimization_barrier((dense_part, lse))
    dense_part = halve(dense_part.reshape(seqs, units, part, r, d + TILE), 2, "part")

    own, others = attend_backward(meta, packed, dout, out_t, lse, kv, seg_mine)
    others = [shift(others[i - 1], "part", part - i) for i in range(1, part)]
    up_part, down_part, dense_part, own = lax.optimization_barrier(
        (up_part, down_part, dense_part, own)
    )
    up_part = halve(add_up(up_part), 0, 0)
    down_part = halve(add_up(down_part), 0, "seq")
    dense_part = halve(add_up(dense_part), 0, "seq")
    qkv_grad, back_one, back_two = unturn(place_unit, own, others, trio_full, cos, sin)
    back_one = back_one.reshape(2, 2, 2, rows // 2, d)
    back_two = back_two.reshape(2, 2, 2, rows // 2, d)
    swapped = flip_unit(back_one[1], 1), flip_unit(back_two[1], 2)

    late, shift_grad = trio_gradient(normed_one, hat_one, qkv_grad, trio_full)
    swapped, late, up_part, down_part, dense_part = lax.optimization_barrier(
        (swapped, late, up_part, down_part, dense_part)
    )
    back_one = add(back_one[0], swapped[0])
    back_two = add(back_two[0], swapped[1])
    swapped = flip_unit(back_one[1], 2), flip_unit(back_two[1], 1)
    mlp_part = jnp.concatenate([add_up(up_part), add_up(down_part)], -1)
    mlp_part = halve(mlp_part, 1, 2)
    dense_part = add_up(dense_part).reshape(2, 2, 2, r, d + TILE)
    dense_part = halve(dense_part, 2, 2)
    late = late.reshape(seqs, units, part, r, -1)
    shift_rows = jnp.pad(shift_grad.astype(BF), ((0, 7), (0, TILE)))
    late = jnp.concatenate(
        [late, jnp.broadcast_to(shift_rows, (seqs, units, part) + shift_rows.shape)], 3
    )
    late = halve(late, 2, "part")
    swapped, late, mlp_part, dense_part = lax.optimization_barrier(
        (swapped, late, mlp_part, dense_part)
    )
    dense_part = halve(add_up(dense_part), 1, 1)
    both = jnp.concatenate(
        [add(back_one[0], swapped[0]), add(back_two[0], swapped[1])], 1
    )
    swapped = flip_unit(both[1], trios)
    mlp_part = halve(add_up(mlp_part), 0, 1)
    late = halve(add_up(late), 0, "seq")
    swapped, late, mlp_part, dense_part = lax.optimization_barrier(
        (swapped, late, mlp_part, dense_part)
    )
    mlp_sum = swap_parts(add_up(mlp_part).reshape(part, r, -1)).astype(F32)
    rest = add_up(halve(add_up(dense_part), 0, 0)).astype(F32)
    dense_sum = rest[:, :d]
    late = add_up(halve(add_up(late).reshape(2, 2, 2, r + 8, PACK + TILE), 0, 0))
    late = exchange_trio(late).astype(F32)
    back = jnp.where(
        bits[0] == 0, jnp.stack([both[0], swapped]), jnp.stack([swapped, both[0]])
    )
    branch_one = mm(attended, dense_pad.reshape(trios * OPACK, d)) + dense_shift
    output = (x + branch_one + sum(second_branch) + down_shift).astype(BF)
    in_two = norm_back(sum(normed_two_grad), gain_two)
    qkv_weight_grad = unpack_columns(
        late[:, :r, :PACK].transpose(1, 0, 2).reshape(r, trios * PACK), trios
    )
    late_vec = jnp.sum(late[:, :r, PACK:], 0) + rest[:, d:]
    qkv_shift_grad = unpack_columns(late[:, r, :PACK].reshape(1, trios * PACK), trios)[0]
    qkv_shift_grad = lax.dynamic_slice_in_dim(qkv_shift_grad, place * 3 * r, 3 * r)

    up_sum = jnp.concatenate([mlp_sum[p, :, : half * d] for p in range(part)], 1)
    down_sum = jnp.concatenate(
        [
            mlp_sum[p, :, (half + b) * d : (half + b + 1) * d]
            for p in range(part)
            for b in range(half)
        ],
        0,
    )
    param_grads = (
        late_vec[:, 0],
        late_vec[:, 1],
        late_vec[:, 2],
        late_vec[:, 3],
        qkv_weight_grad,
        qkv_shift_grad,
        dense_sum,
        late_vec[:, 4],
        join_hidden(up_sum, count, r),
        late_vec[:, 8 : 8 + blocks].T.reshape(-1),
        down_sum,
        late_vec[:, 4],
    )

    normed_one_grad = back.reshape(all_rows, d).astype(F32)
    in_one = norm_back(normed_one_grad, gain_one)
    tokens_grad = (cot.astype(F32) + in_one + in_two).astype(BF)

    def natural(value):
        return value.reshape(groups, rows, d).transpose(1, 0, 2)

    return (natural(output), natural(tokens_grad)) + tuple(param_grads)


def solution(mesh):
    devices = mesh.devices
    seq_size, ctx_size = devices.shape
    ctx = ("unit", "part")
    tok = P(ctx, "seq", None)
    vec = P(ALL_AXES)
    mat = P(ALL_AXES, None)
    pairs = (vec, vec, vec, vec, mat, vec, mat, vec, mat, vec, mat, vec)

    def run(tokens, *rest):
        units = HEADS // TRIO * (tokens.shape[1] // seq_size)
        split = Mesh(devices.reshape(seq_size, units, ctx_size // units), ALL_AXES)
        mapped = jax.shard_map(
            on_device,
            mesh=split,
            in_specs=(tok, P(ctx, "seq")) + pairs + (tok,),
            out_specs=(tok, tok) + pairs,
            check_vma=False,
        )
        return mapped(tokens, *rest)

    return run
```

```python
import functools
import math

import jax
import jax.numpy as jnp
from jax import lax
from jax.experimental import pallas as pl
from jax.experimental.pallas import tpu as pltpu
from jax.sharding import Mesh, PartitionSpec as P

HEADS = 12
HEAD_DIM = 64
ROT = 16
TRIO = 3
TILE = 128
PACK = 5 * TILE
OPACK = 2 * TILE

EPSILON = 1e-05
NEG_BIG = -1e30
BF = jnp.bfloat16
F32 = jnp.float32
ALL_AXES = ("seq", "unit", "part")
VMEM_BYTES = 56 * 1024 * 1024


def params_of(*semantics):
    return pltpu.CompilerParams(
        dimension_semantics=semantics, vmem_limit_bytes=VMEM_BYTES
    )


def mm(a, b):
    return jnp.dot(a, b, preferred_element_type=F32)


def outer_sum(left_rows, right_rows):
    return lax.dot_general(
        left_rows, right_rows, (((0,), (0,)), ((), ())), preferred_element_type=F32
    )


def inner_back(grad_rows, weight):
    return lax.dot_general(
        grad_rows, weight, (((1,), (1,)), ((), ())), preferred_element_type=F32
    )


def lane_of(shape):
    return lax.broadcasted_iota(jnp.int32, shape, len(shape) - 1)


def turn(tile, cos, sin):
    partner = jnp.where(
        lane_of(tile.shape) % HEAD_DIM < ROT // 2,
        pltpu.roll(tile, TILE - ROT // 2, 1),
        pltpu.roll(tile, ROT // 2, 1),
    )
    return tile * cos + partner * sin


def turn_tables(cos_rows, sin_rows):
    rows = cos_rows.shape[1]
    rest = HEAD_DIM - ROT
    cos_head = [cos_rows, cos_rows, jnp.ones((rest, rows), F32)]
    sin_head = [-sin_rows, sin_rows, jnp.zeros((rest, rows), F32)]
    return jnp.concatenate(cos_head * 2, 0).T, jnp.concatenate(sin_head * 2, 0).T


def first_place(rel):
    return rel % 2 * 4 + rel // 2 % 2 * 2 + rel // 4


def second_place(rel):
    return rel // 2 % 2 * 4 + rel % 2 * 2 + rel // 4


def project_kernel(
    place_ref,
    one_ref,
    two_ref,
    w_ref,
    b_ref,
    gain_ref,
    bias_ref,
    cos_ref,
    sin_ref,
    out_ref,
    kv_ref,
    norm_ref,
    hat_ref,
):
    x = jnp.concatenate([one_ref[0], two_ref[0]], 0).astype(F32)
    centre = x - jnp.mean(x, -1, keepdims=True)
    spread = jnp.mean(centre * centre, -1, keepdims=True)
    hat = centre * lax.rsqrt(spread + EPSILON)
    normed = (hat * gain_ref[...] + bias_ref[...]).astype(BF)
    hat_ref[0] = hat.astype(BF)
    norm_ref[0] = normed
    y = mm(normed, w_ref[...]) + b_ref[...]
    cos, sin = turn_tables(cos_ref[0], sin_ref[0])
    for t in range(5):
        tile = y[:, t * TILE : (t + 1) * TILE]
        if t in (0, 1, 3):
            tile = turn(tile, cos, sin)
        tile = tile.astype(BF)
        out_ref[0, :, t * TILE : (t + 1) * TILE] = tile
        if t > 0:
            kv_ref[0, :, (t - 1) * TILE : t * TILE] = tile


def half_specs(rows, d):
    return [
        pl.BlockSpec((1, rows // 2, d), lambda j, place: (first_place(j ^ place[0]), 0, 0)),
        pl.BlockSpec((1, rows // 2, d), lambda j, place: (second_place(j ^ place[0]), 0, 0)),
    ]


def project(place, toks, weight, bias, gain, offset, cos, sin):
    units, unused, rows = cos.shape
    d = toks[0].shape[2]
    tok_spec = pl.BlockSpec((1, rows, d), lambda j, place: (j, 0, 0))
    row_spec = pl.BlockSpec((1, d), lambda j, place: (0, 0))
    turn_spec = pl.BlockSpec((1, ROT // 2, rows), lambda j, place: (j, 0, 0))
    return pl.pallas_call(
        project_kernel,
        grid_spec=pltpu.PrefetchScalarGridSpec(
            num_scalar_prefetch=1,
            grid=(units,),
            in_specs=half_specs(rows, d)
            + [
                pl.BlockSpec((d, PACK), lambda j, place: (0, 0)),
                pl.BlockSpec((1, PACK), lambda j, place: (0, 0)),
                row_spec,
                row_spec,
                turn_spec,
                turn_spec,
            ],
            out_specs=[
                pl.BlockSpec((1, rows, PACK), lambda j, place: (j, 0, 0)),
                pl.BlockSpec((1, rows, PACK - TILE), lambda j, place: (j, 0, 0)),
                tok_spec,
                tok_spec,
            ],
        ),
        out_shape=[
            jax.ShapeDtypeStruct((units, rows, PACK), BF),
            jax.ShapeDtypeStruct((units, rows, PACK - TILE), BF),
            jax.ShapeDtypeStruct((units, rows, d), BF),
            jax.ShapeDtypeStruct((units, rows, d), BF),
        ],
        compiler_params=params_of("arbitrary"),
        cost_estimate=pl.CostEstimate(flops=0, bytes_accessed=0, transcendentals=0),
        name="project",
    )(place, *toks, weight, bias, gain, offset, cos, sin)


def unturn_kernel(place_ref, own_ref, *refs):
    w_ref, cos_ref, sin_ref, out_ref, one_ref, two_ref = refs[-6:]
    others = refs[:-6]
    cos, sin = turn_tables(cos_ref[0], sin_ref[0])
    for t in range(5):
        tile = own_ref[0, :, t * TILE : (t + 1) * TILE].astype(F32)
        if t > 0:
            for other in others:
                tile = tile + other[0, :, (t - 1) * TILE : t * TILE].astype(F32)
        if t in (0, 1, 3):
            tile = turn(tile, cos, -sin)
        out_ref[0, :, t * TILE : (t + 1) * TILE] = tile.astype(BF)
    back = inner_back(out_ref[0], w_ref[...]).astype(BF)
    rows = back.shape[0] // 2
    one_ref[0] = back[:rows]
    two_ref[0] = back[rows:]


def unturn(place, own, others, weight, cos, sin):
    units, rows, unused = own.shape
    d = weight.shape[0]
    turn_spec = pl.BlockSpec((1, ROT // 2, rows), lambda j, place: (j, 0, 0))
    own_spec = pl.BlockSpec((1, rows, PACK), lambda j, place: (j, 0, 0))
    other_spec = pl.BlockSpec((1, rows, PACK - TILE), lambda j, place: (j, 0, 0))
    half = jax.ShapeDtypeStruct((units, rows // 2, d), BF)
    return pl.pallas_call(
        unturn_kernel,
        grid_spec=pltpu.PrefetchScalarGridSpec(
            num_scalar_prefetch=1,
            grid=(units,),
            in_specs=[own_spec]
            + [other_spec] * len(others)
            + [pl.BlockSpec((d, PACK), lambda j, place: (0, 0)), turn_spec, turn_spec],
            out_specs=[own_spec] + half_specs(rows, d),
        ),
        out_shape=[jax.ShapeDtypeStruct(own.shape, BF), half, half],
        compiler_params=params_of("arbitrary"),
        cost_estimate=pl.CostEstimate(flops=0, bytes_accessed=0, transcendentals=0),
        name="unturn",
    )(place, own, *others, weight, cos, sin)


def flip(tile):
    return tile.astype(F32).T


def head_rows(flipped, low):
    row = lax.broadcasted_iota(jnp.int32, flipped.shape, 0)
    keep = row < HEAD_DIM if low else row >= HEAD_DIM
    return jnp.where(keep, flipped, 0.0)


def head_lanes(tile, low):
    lane = lane_of(tile.shape)
    keep = lane < HEAD_DIM if low else lane >= HEAD_DIM
    return jnp.where(keep, tile, 0.0)


def query_sides(q_ref, qb):
    scale = HEAD_DIM ** (-0.5)
    a = flip(q_ref[0, :, 0:TILE]) * scale
    d = flip(q_ref[0, :, 3 * TILE : 4 * TILE]) * scale
    qb[0] = head_rows(a, True).astype(BF)
    qb[1] = head_rows(a, False).astype(BF)
    qb[2] = jnp.concatenate(
        [jnp.zeros((HEAD_DIM, d.shape[1]), F32), d[:HEAD_DIM]], 0
    ).astype(BF)


def live_of(seg_row, unit, query_start, part, rows, c):
    shape = (rows, rows)
    query_pos = query_start + lax.broadcasted_iota(jnp.int32, shape, 1)
    row = lax.broadcasted_iota(jnp.int32, shape, 0)
    pieces = []
    for i in range(part):
        key_pos = (unit * part + lax.rem(c - i + part, part)) * rows + row
        pieces.append((key_pos <= query_pos) & (key_pos >= seg_row))
    return jnp.concatenate(pieces, 0)


def unit_loop(meta, part, units, rows, step):
    j = pl.program_id(0)
    first = meta[j] // (rows * part)
    top_seg = meta[units + j]

    def one(unit, unused):
        masked = (unit == j) | (top_seg > unit * (rows * part))

        @pl.when(masked)
        def _():
            step(unit, True)

        @pl.when(jnp.logical_not(masked))
        def _():
            step(unit, False)

        return unused

    lax.fori_loop(first, j + 1, one, 0)


def join_parts(part, refs, kv_ref):
    rows = refs[0].shape[1]

    def one(unit, unused):
        for i in range(part):
            kv_ref[unit, i * rows : (i + 1) * rows] = refs[i][unit]
        return unused

    lax.fori_loop(0, refs[0].shape[0], one, 0)


def forward_kernel(part, units, meta, q_ref, *refs):
    seg_ref, o_ref, ot_ref, lse_ref, kv_ref, qb, vt, top, total, acc = refs[part:]
    rows = q_ref.shape[1]
    c = meta[2 * units]
    j = pl.program_id(0)

    @pl.when(j == 0)
    def _():
        join_parts(part, refs[:part], kv_ref)

        def turn_values(unit, unused):
            vt[unit, :TILE] = flip(kv_ref[unit, :, TILE : 2 * TILE]).astype(BF)
            vt[unit, TILE:] = flip(kv_ref[unit, :, 3 * TILE :])[:HEAD_DIM].astype(BF)
            return unused

        lax.fori_loop(0, units, turn_values, 0)

    query_sides(q_ref, qb)
    top[...] = jnp.full(top.shape, NEG_BIG, F32)
    total[...] = jnp.zeros(total.shape, F32)
    acc[...] = jnp.zeros(acc.shape, F32)
    seg_row = seg_ref[0]
    query_start = (j * part + c) * rows

    def step(unit, masked):
        k01 = kv_ref[unit, :, 0:TILE]
        k2 = kv_ref[unit, :, 2 * TILE : 3 * TILE]
        if masked:
            live = live_of(seg_row, unit, query_start, part, rows, c)
        scores = [mm(k2 if h == 2 else k01, qb[h]) for h in range(TRIO)]
        if masked:
            scores = [jnp.where(live, score, NEG_BIG) for score in scores]
        old = top[0:TRIO]
        new = jnp.concatenate([jnp.max(score, 0, keepdims=True) for score in scores], 0)
        new = jnp.maximum(old, new)
        factor = jnp.exp(old - new)
        weights = [jnp.exp(scores[h] - new[h : h + 1]) for h in range(TRIO)]
        if masked:
            weights = [jnp.where(live, weight, 0.0) for weight in weights]
        sums = [jnp.sum(weight, 0, keepdims=True) for weight in weights]
        top[0:TRIO] = new
        total[0:TRIO] = total[0:TRIO] * factor + jnp.concatenate(sums, 0)
        for h in range(TRIO):
            vth = vt[unit, h * HEAD_DIM : (h + 1) * HEAD_DIM]
            acc[h] = acc[h] * factor[h : h + 1] + mm(vth, weights[h].astype(BF))

    unit_loop(meta, part, units, rows, step)
    out = [acc[h] / total[h : h + 1] for h in range(TRIO)]
    for h in range(TRIO):
        ot_ref[0, h * HEAD_DIM : (h + 1) * HEAD_DIM] = out[h]
    lse_ref[0, 0:TRIO] = top[0:TRIO] + jnp.log(total[0:TRIO])
    o_ref[0, :, :TILE] = jnp.concatenate(out[:2], 0).T.astype(BF)
    o_ref[0, :, TILE:] = jnp.concatenate([out[2], jnp.zeros_like(out[2])], 0).T.astype(BF)


def backward_kernel(part, units, meta, q_ref, do_ref, ot_ref, lse_ref, *refs):
    seg_ref, own_ref, oth_ref, kv_ref, qb, db, qn, dn, kt, delta, dqt = refs[part : part + 11]
    dk01, dv01, dk2, dv2 = refs[part + 11 :]
    rows = q_ref.shape[1]
    c = meta[2 * units]
    j = pl.program_id(0)

    @pl.when(j == 0)
    def _():
        join_parts(part, refs[:part], kv_ref)

        def turn_keys(unit, unused):
            kt[unit, :TILE] = flip(kv_ref[unit, :, 0:TILE]).astype(BF)
            kt[unit, TILE:] = flip(kv_ref[unit, :, 2 * TILE : 3 * TILE])[HEAD_DIM:].astype(BF)
            return unused

        lax.fori_loop(0, units, turn_keys, 0)
        for ref in (dk01, dv01, dk2, dv2):
            ref[...] = jnp.zeros(ref.shape, F32)

    query_sides(q_ref, qb)
    scale = HEAD_DIM ** (-0.5)
    q01 = q_ref[0, :, 0:TILE].astype(F32) * scale
    q2 = pltpu.roll(q_ref[0, :, 3 * TILE : 4 * TILE].astype(F32), HEAD_DIM, 1) * scale
    qn[0:rows] = head_lanes(q01, True).astype(BF)
    qn[rows : 2 * rows] = head_lanes(q01, False).astype(BF)
    qn[2 * rows :] = head_lanes(q2, False).astype(BF)
    do01 = do_ref[0, :, :TILE].astype(F32)
    do2 = do_ref[0, :, TILE:].astype(F32)
    dn[0:rows] = head_lanes(do01, True).astype(BF)
    dn[rows : 2 * rows] = head_lanes(do01, False).astype(BF)
    dn[2 * rows :] = do2.astype(BF)
    do01t = do01.T
    do2t = do2.T
    db[0] = head_rows(do01t, True).astype(BF)
    db[1] = head_rows(do01t, False).astype(BF)
    db[2] = do2t.astype(BF)
    for h in range(TRIO):
        dot = do2t[:HEAD_DIM] if h == 2 else do01t[h * HEAD_DIM : (h + 1) * HEAD_DIM]
        delta[h : h + 1] = jnp.sum(
            dot * ot_ref[0, h * HEAD_DIM : (h + 1) * HEAD_DIM], 0, keepdims=True
        )
    dqt[...] = jnp.zeros(dqt.shape, F32)
    seg_row = seg_ref[0]
    query_start = (j * part + c) * rows

    def step(unit, masked):
        k01 = kv_ref[unit, :, 0:TILE]
        v01 = kv_ref[unit, :, TILE : 2 * TILE]
        k2 = kv_ref[unit, :, 2 * TILE : 3 * TILE]
        v2 = kv_ref[unit, :, 3 * TILE :]
        if masked:
            live = live_of(seg_row, unit, query_start, part, rows, c)
        scores = [mm(k2 if h == 2 else k01, qb[h]) for h in range(TRIO)]
        dprobs = [mm(v2 if h == 2 else v01, db[h]) for h in range(TRIO)]
        probs = []
        grads = []
        for h in range(TRIO):
            score = scores[h]
            if masked:
                score = jnp.where(live, score, NEG_BIG)
            prob = jnp.exp(score - lse_ref[0, h : h + 1])
            if masked:
                prob = jnp.where(live, prob, 0.0)
            probs.append(prob.astype(BF))
            grads.append((prob * (dprobs[h] - delta[h : h + 1])).astype(BF))
        dv01[unit] += mm(jnp.concatenate(probs[:2], 1), dn[: 2 * rows])
        dk01[unit] += mm(jnp.concatenate(grads[:2], 1), qn[: 2 * rows])
        dv2[unit] += mm(probs[2], dn[2 * rows :])
        dk2[unit] += mm(grads[2], qn[2 * rows :])
        for h in range(TRIO):
            kth = kt[unit, h * HEAD_DIM : (h + 1) * HEAD_DIM]
            dqt[h * HEAD_DIM : (h + 1) * HEAD_DIM] += mm(kth, grads[h])

    unit_loop(meta, part, units, rows, step)
    own_ref[j, :, 0:TILE] = (dqt[:TILE] * scale).T.astype(BF)
    dq2 = dqt[TILE:] * scale
    dk2[j, 0:rows] += jnp.concatenate([dq2, jnp.zeros_like(dq2)], 0).T

    @pl.when(j == units - 1)
    def _():
        for unit in range(units):
            for i in range(part):
                span = slice(i * rows, (i + 1) * rows)
                for t, ref in enumerate((dk01, dv01, dk2, dv2)):
                    tile = ref[unit, span].astype(BF)
                    if i == 0:
                        own_ref[unit, :, (t + 1) * TILE : (t + 2) * TILE] = tile
                    else:
                        oth_ref[i - 1, unit, :, t * TILE : (t + 1) * TILE] = tile


def whole_spec(shape):
    zeros = (0,) * len(shape)
    return pl.BlockSpec(shape, lambda j, meta: zeros)


def attend_forward(meta, packed, kv, seg):
    units, rows, unused = packed.shape
    part = len(kv)
    return pl.pallas_call(
        functools.partial(forward_kernel, part, units),
        grid_spec=pltpu.PrefetchScalarGridSpec(
            num_scalar_prefetch=1,
            grid=(units,),
            in_specs=[
                pl.BlockSpec((1, rows, PACK), lambda j, meta: (j, 0, 0)),
                *[whole_spec(piece.shape) for piece in kv],
                pl.BlockSpec((1, 1, rows), lambda j, meta: (j, 0, 0)),
            ],
            out_specs=[
                pl.BlockSpec((1, rows, OPACK), lambda j, meta: (j, 0, 0)),
                pl.BlockSpec((1, TRIO * HEAD_DIM, rows), lambda j, meta: (j, 0, 0)),
                pl.BlockSpec((1, 8, rows), lambda j, meta: (j, 0, 0)),
            ],
            scratch_shapes=[
                pltpu.VMEM((units, part * rows, PACK - TILE), BF),
                pltpu.VMEM((TRIO, TILE, rows), BF),
                pltpu.VMEM((units, TRIO * HEAD_DIM, part * rows), BF),
                pltpu.VMEM((8, rows), F32),
                pltpu.VMEM((8, rows), F32),
                pltpu.VMEM((TRIO, HEAD_DIM, rows), F32),
            ],
        ),
        out_shape=[
            jax.ShapeDtypeStruct((units, rows, OPACK), BF),
            jax.ShapeDtypeStruct((units, TRIO * HEAD_DIM, rows), F32),
            jax.ShapeDtypeStruct((units, 8, rows), F32),
        ],
        compiler_params=params_of("arbitrary"),
        cost_estimate=pl.CostEstimate(flops=0, bytes_accessed=0, transcendentals=0),
        name="attend_forward",
    )(meta, packed, *kv, seg)


def attend_backward(meta, packed, dout, out_t, lse, kv, seg):
    units, rows, unused = packed.shape
    part = len(kv)
    others = (max(part - 1, 1), units, rows, 4 * TILE)
    grads = pltpu.VMEM((units, part * rows, TILE), F32)
    return pl.pallas_call(
        functools.partial(backward_kernel, part, units),
        grid_spec=pltpu.PrefetchScalarGridSpec(
            num_scalar_prefetch=1,
            grid=(units,),
            in_specs=[
                pl.BlockSpec((1, rows, PACK), lambda j, meta: (j, 0, 0)),
                pl.BlockSpec((1, rows, OPACK), lambda j, meta: (j, 0, 0)),
                pl.BlockSpec((1, TRIO * HEAD_DIM, rows), lambda j, meta: (j, 0, 0)),
                pl.BlockSpec((1, 8, rows), lambda j, meta: (j, 0, 0)),
                *[whole_spec(piece.shape) for piece in kv],
                pl.BlockSpec((1, 1, rows), lambda j, meta: (j, 0, 0)),
            ],
            out_specs=[whole_spec(packed.shape), whole_spec(others)],
            scratch_shapes=[
                pltpu.VMEM((units, part * rows, PACK - TILE), BF),
                pltpu.VMEM((TRIO, TILE, rows), BF),
                pltpu.VMEM((TRIO, TILE, rows), BF),
                pltpu.VMEM((TRIO * rows, TILE), BF),
                pltpu.VMEM((TRIO * rows, TILE), BF),
                pltpu.VMEM((units, TRIO * HEAD_DIM, part * rows), BF),
                pltpu.VMEM((8, rows), F32),
                pltpu.VMEM((TRIO * HEAD_DIM, rows), F32),
                grads,
                grads,
                grads,
                grads,
            ],
        ),
        out_shape=[
            jax.ShapeDtypeStruct(packed.shape, BF),
            jax.ShapeDtypeStruct(others, BF),
        ],
        compiler_params=params_of("arbitrary"),
        cost_estimate=pl.CostEstimate(
            flops=63 * units * units * part * rows * rows * HEAD_DIM * TRIO, bytes_accessed=0, transcendentals=0
        ),
        name="attend_backward",
    )(meta, packed, dout, out_t, lse, *kv, seg)


def pack_kernel(trios, groups, w_ref, vec_ref, early_ref, local_ref):
    d = w_ref.shape[1] // 3
    w = w_ref[...].astype(F32)
    width = TRIO * HEAD_DIM
    zeros = jnp.zeros((w.shape[0], HEAD_DIM), F32)
    for g in range(trios):
        q, k, v = (w[:, i * d + g * width : i * d + (g + 1) * width] for i in range(3))
        tiles = [q[:, :TILE], k[:, :TILE], v[:, :TILE]]
        tiles.append(jnp.concatenate([q[:, TILE:], k[:, TILE:]], 1))
        tiles.append(jnp.concatenate([v[:, TILE:], zeros], 1))
        for t, tile in enumerate(tiles):
            tile = tile.astype(BF)
            local_ref[:, g * PACK + t * TILE : g * PACK + (t + 1) * TILE] = tile
            for s in range(groups):
                early_ref[s * trios + g, :, t * TILE : (t + 1) * TILE] = tile
        for s in range(groups):
            early_ref[s * trios + g, :, PACK:] = vec_ref[s]


def pack_early(weight, vec, trios):
    r = weight.shape[0]
    groups = vec.shape[0]
    return pl.pallas_call(
        functools.partial(pack_kernel, trios, groups),
        out_shape=[
            jax.ShapeDtypeStruct((trios * groups, r, PACK + TILE), BF),
            jax.ShapeDtypeStruct((r, trios * PACK), BF),
        ],
        name="pack_early",
    )(weight, vec)


def feed_kernel(
    x_ref, cot_ref, up_ref, down_ref, shift_ref, hid_ref, pre_ref, sum_ref, second_ref, back_ref
):
    pre = mm(x_ref[...], up_ref[...]) + shift_ref[...]
    grad = inner_back(cot_ref[...], down_ref[...])
    cdf = 0.5 * (1.0 + lax.erf(pre * math.sqrt(0.5)))
    hidden = (pre * cdf).astype(BF)
    slope = cdf + pre * (jnp.exp(-0.5 * pre * pre) * (1.0 / math.sqrt(2.0 * math.pi)))
    pre_grad = (grad * slope).astype(BF)
    hid_ref[...] = hidden
    pre_ref[...] = pre_grad
    sum_ref[...] = jnp.sum(pre_grad.astype(F32), 0, keepdims=True)
    second = mm(hidden, down_ref[...])
    back = inner_back(pre_grad, up_ref[...])

    @pl.when(pl.program_id(0) == 0)
    def _():
        second_ref[...] = second
        back_ref[...] = back

    @pl.when(pl.program_id(0) > 0)
    def _():
        second_ref[...] += second
        back_ref[...] += back


def feed_forward(x, cot, weights, shift, blocks):
    rows, d = x.shape
    ff = blocks * d
    half = d // 2
    wide = pl.BlockSpec((rows, d), lambda i: (0, 0))
    column = pl.BlockSpec((rows, half), lambda i: (0, i))
    line = pl.BlockSpec((1, half), lambda i: (0, i))
    return pl.pallas_call(
        feed_kernel,
        grid=(2 * blocks,),
        in_specs=[
            wide,
            wide,
            pl.BlockSpec((d, half), lambda i: (0, i)),
            pl.BlockSpec((half, d), lambda i: (i % 2, blocks + i // 2)),
            line,
        ],
        out_specs=[column, column, line, wide, wide],
        out_shape=[
            jax.ShapeDtypeStruct((rows, ff), BF),
            jax.ShapeDtypeStruct((rows, ff), BF),
            jax.ShapeDtypeStruct((1, ff), F32),
            jax.ShapeDtypeStruct((rows, d), F32),
            jax.ShapeDtypeStruct((rows, d), F32),
        ],
        compiler_params=params_of("arbitrary"),
        cost_estimate=pl.CostEstimate(
            flops=8 * rows * d * ff, bytes_accessed=4 * d * ff, transcendentals=2 * rows * ff
        ),
        name="feed_forward",
    )(x, cot, weights, weights, shift)


def gradient_kernel(ups, norm_ref, pre_ref, hidden_ref, cot_ref, out_ref):
    i = pl.program_id(0)

    @pl.when(i < ups)
    def _():
        out_ref[...] = outer_sum(norm_ref[...], pre_ref[...]).astype(BF)

    @pl.when(i >= ups)
    def _():
        out_ref[...] = outer_sum(hidden_ref[...], cot_ref[...]).astype(BF)


def gradients(normed, pre_grad, hidden, cot):
    rows, d = normed.shape
    width = d // 2
    ups = hidden.shape[1] // width

    def down(i):
        return jnp.clip(i - ups, 0, ups - 1)

    return pl.pallas_call(
        functools.partial(gradient_kernel, ups),
        grid=(2 * ups,),
        in_specs=[
            pl.BlockSpec((rows, d), lambda i: (0, 0)),
            pl.BlockSpec((rows, width), lambda i: (0, jnp.minimum(i, ups - 1))),
            pl.BlockSpec((rows, d), lambda i: (0, down(i) // 2)),
            pl.BlockSpec((rows, width), lambda i: (0, down(i) % 2)),
        ],
        out_specs=pl.BlockSpec((d, width), lambda i: (0, i)),
        out_shape=jax.ShapeDtypeStruct((d, 2 * ups * width), BF),
        compiler_params=params_of("arbitrary"),
        cost_estimate=pl.CostEstimate(
            flops=4 * rows * d * ups * width, bytes_accessed=0, transcendentals=0
        ),
        name="gradients",
    )(normed, pre_grad, hidden, cot)


def trio_kernel(norm_ref, hat_ref, grad_ref, w_ref, late_ref, shift_ref, own, hat):
    j = pl.program_id(0)
    d = norm_ref.shape[2]
    grad = grad_ref[...].reshape(-1, PACK)
    own_part = outer_sum(norm_ref[...].reshape(-1, d), grad)
    hat_part = outer_sum(hat_ref[...].reshape(-1, d), grad)
    sums = jnp.sum(grad.astype(F32), 0, keepdims=True)

    @pl.when(j == 0)
    def _():
        own[...] = own_part
        hat[...] = hat_part
        shift_ref[...] = sums

    @pl.when(j > 0)
    def _():
        own[...] += own_part
        hat[...] += hat_part
        shift_ref[...] += sums

    @pl.when(j == pl.num_programs(0) - 1)
    def _():
        late_ref[:, :PACK] = own[...].astype(BF)
        weight = w_ref[...].astype(F32)
        lane = lane_of((d, TILE))
        vec = jnp.where(lane == 0, jnp.sum(weight * hat[...], 1, keepdims=True), 0.0)
        vec = jnp.where(lane == 1, jnp.sum(weight * shift_ref[...], 1, keepdims=True), vec)
        late_ref[:, PACK:] = vec.astype(BF)


def trio_gradient(normed, hat, grad, weight):
    units, rows, d = normed.shape
    tok_spec = pl.BlockSpec((2, rows, d), lambda j: (j, 0, 0))
    return pl.pallas_call(
        trio_kernel,
        grid=(units // 2,),
        in_specs=[
            tok_spec,
            tok_spec,
            pl.BlockSpec((2, rows, PACK), lambda j: (j, 0, 0)),
            pl.BlockSpec((d, PACK), lambda j: (0, 0)),
        ],
        out_specs=[
            pl.BlockSpec((d, PACK + TILE), lambda j: (0, 0)),
            pl.BlockSpec((1, PACK), lambda j: (0, 0)),
        ],
        scratch_shapes=[pltpu.VMEM((d, PACK), F32), pltpu.VMEM((d, PACK), F32)],
        out_shape=[
            jax.ShapeDtypeStruct((d, PACK + TILE), BF),
            jax.ShapeDtypeStruct((1, PACK), F32),
        ],
        compiler_params=params_of("arbitrary"),
        cost_estimate=pl.CostEstimate(
            flops=12 * units * rows * d * PACK, bytes_accessed=0, transcendentals=0
        ),
        name="trio_gradient",
    )(normed, hat, grad, weight)


def vector_kernel(half, part_ref, hat_ref, cot_ref, up_ref, *refs):
    out_ref = refs[-1]
    total = refs[0][...]
    for ref in refs[1:-1]:
        total = total + ref[...]
    d = total.shape[1]
    row = lax.broadcasted_iota(jnp.int32, (16, d), 0)
    sums = jnp.where(row == 2, jnp.sum(total * hat_ref[...], 0, keepdims=True), 0.0)
    sums = jnp.where(row == 3, jnp.sum(total, 0, keepdims=True), sums)
    sums = jnp.where(row == 4, jnp.sum(cot_ref[...].astype(F32), 0, keepdims=True), sums)
    for b in range(half):
        here = row == 8 + part_ref[0] * half + b
        sums = jnp.where(here, up_ref[:, b * d : (b + 1) * d], sums)
    sums = jnp.concatenate([sums, jnp.zeros((TILE - 16, d), F32)], 0)
    out_ref[...] = sums.T.astype(BF)


def vector_sums(c, hat, cot, up_sums, pieces):
    d = hat.shape[1]
    whole = pl.BlockSpec(memory_space=pltpu.VMEM)
    return pl.pallas_call(
        functools.partial(vector_kernel, up_sums.shape[1] // d),
        in_specs=[pl.BlockSpec(memory_space=pltpu.SMEM)] + [whole] * (3 + len(pieces)),
        out_specs=whole,
        out_shape=jax.ShapeDtypeStruct((d, TILE), BF),
        compiler_params=pltpu.CompilerParams(vmem_limit_bytes=VMEM_BYTES),
        name="vector_sums",
    )(c[None], hat, cot, up_sums, *pieces)


def pack_columns(matrix, trios):
    r = matrix.shape[0]
    q, k, v = (
        part.reshape(r, trios, TRIO * HEAD_DIM) for part in jnp.split(matrix, 3, axis=1)
    )
    zeros = jnp.zeros((r, trios, HEAD_DIM), matrix.dtype)
    pieces = [q[..., :TILE], k[..., :TILE], v[..., :TILE], q[..., TILE:], k[..., TILE:]]
    return jnp.concatenate(pieces + [v[..., TILE:], zeros], -1).reshape(r, trios * PACK)


def unpack_columns(matrix, trios):
    r = matrix.shape[0]
    m = matrix.reshape(r, trios, PACK)
    halves = [
        m[..., 3 * TILE : 3 * TILE + HEAD_DIM],
        m[..., 3 * TILE + HEAD_DIM : 4 * TILE],
        m[..., 4 * TILE : 4 * TILE + HEAD_DIM],
    ]
    return jnp.concatenate(
        [
            jnp.concatenate([m[..., i * TILE : (i + 1) * TILE], halves[i]], -1).reshape(r, -1)
            for i in range(3)
        ],
        -1,
    )


def split_hidden(matrix, count, r):
    lead = matrix.shape[0]
    return matrix.reshape(lead, count, -1, r).transpose(0, 2, 1, 3).reshape(lead, -1)


def join_hidden(matrix, count, r):
    lead = matrix.shape[0]
    return matrix.reshape(lead, -1, count, r).transpose(0, 2, 1, 3).reshape(lead, -1)


def on_device(
    tokens,
    segment,
    ln1_gain,
    ln1_bias,
    ln2_gain,
    ln2_bias,
    qkv_weight,
    qkv_bias,
    dense_weight,
    dense_bias,
    fc1_weight,
    fc1_bias,
    output_feed_weight,
    output_feed_bias,
    cotangent,
):
    rows, groups, d = tokens.shape
    units = lax.axis_size("unit")
    part = lax.axis_size("part")
    count = units * part * lax.axis_size("seq")
    trios = units // groups
    all_rows = rows * groups
    r = qkv_weight.shape[0]
    ff = fc1_weight.shape[1]
    blocks = ff // d
    c = lax.axis_index("part")
    unit = lax.axis_index("unit")

    seq = lax.axis_index("seq")
    seqs = lax.axis_size("seq")
    place = (seq * units + unit) * part + c

    def exchange(blocks_out):
        width = blocks_out.shape[-1]
        return lax.all_to_all(
            blocks_out.reshape(-1, width), "unit", 0, 0, tiled=True
        ).reshape(blocks_out.shape)

    def shift(value, axis, i):
        n = lax.axis_size(axis)
        return lax.ppermute(value, axis, [(p, (p + i) % n) for p in range(n)])

    def flip_unit(value, bit):
        return lax.ppermute(value, "unit", [(u, u ^ bit) for u in range(units)])

    def pick(value, index, axis):
        return lax.dynamic_index_in_dim(value, index, axis, False)

    bits = (unit // trios, unit // 2 % 2, unit % 2)

    def exchange_small(value):
        shape = value.shape
        value = value.reshape((2, 2, 2) + shape[1:])
        for axis, bit in enumerate((trios, 2, 1)):
            keep = pick(value, bits[axis], axis)
            value = jnp.stack([keep, flip_unit(pick(value, 1 - bits[axis], axis), bit)], axis)
        for axis in range(3):
            value = jnp.where(bits[axis] == 0, value, jnp.flip(value, axis))
        return value.reshape(shape)

    def exchange_trio(value):
        for axis in range(2):
            bit = bits[axis + 1]
            away = flip_unit(pick(value, 1 - bit, axis), (2, 1)[axis])
            value = jnp.stack([pick(value, bit, axis), away], axis)
        for axis in range(2):
            value = jnp.where(bits[axis + 1] == 0, value, jnp.flip(value, axis))
        return value.reshape((trios,) + value.shape[2:])

    def spread_tokens(value, beside):
        keep = pick(value, bits[0], 0)
        both = jnp.stack([keep, flip_unit(pick(value, 1 - bits[0], 0), trios)])
        one, two = both[:, : rows // 2], both[:, rows // 2 :]
        one = jnp.stack([one, flip_unit(one, 2)])
        two = jnp.stack([two, flip_unit(two, 1)])
        one, two, beside = lax.optimization_barrier((one, two, beside))
        one = jnp.stack([one, flip_unit(one, 1)])
        two = jnp.stack([two, flip_unit(two, 2)])
        return (one.reshape(units, rows // 2, d), two.reshape(units, rows // 2, d)), beside

    def add(a, b):
        return (a.astype(F32) + b.astype(F32)).astype(BF)

    def natural_order(got, me):
        n = len(got)
        if n == 2:
            return jnp.where(me == 0, jnp.stack(got), jnp.stack(got[::-1]))
        ring = jnp.stack((got + got)[::-1])
        return lax.dynamic_slice_in_dim(ring, n - 1 - me, n, 0)

    def gather_small(value, axis):
        n = lax.axis_size(axis)
        got = [value] + [shift(value, axis, i) for i in range(1, n)]
        return natural_order(got, lax.axis_index(axis))

    def swap_parts(value):
        got = [lax.dynamic_index_in_dim(value, c, 0, False)]
        for i in range(1, part):
            piece = lax.dynamic_index_in_dim(value, (c + i) % part, 0, False)
            got.append(shift(piece, "part", i))
        return natural_order(got, c)

    def all_parts(value):
        return jnp.concatenate([value] + [shift(value, "part", i) for i in range(1, part)], 0)

    def part_pieces(value):
        n = value.shape[0] // part
        return [value[:n]] + [
            shift(value[i * n : (i + 1) * n], "part", part - i) for i in range(1, part)
        ]

    def halve(value, axis, which):
        if isinstance(which, str):
            n = lax.axis_size(which)
            me = lax.axis_index(which)
            return [pick(value, me, axis)] + [
                shift(pick(value, (me + i) % n, axis), which, i) for i in range(1, n)
            ]
        away = pick(value, 1 - bits[which], axis)
        return [pick(value, bits[which], axis), flip_unit(away, (trios, 2, 1)[which])]

    def add_up(pieces):
        total = pieces[0].astype(F32)
        for piece in pieces[1:]:
            total = total + piece.astype(F32)
        return total.astype(BF)

    vectors = (ln1_gain, ln1_bias, ln2_gain, ln2_bias, dense_bias, output_feed_bias)
    vec = jnp.concatenate(
        [v.reshape(r, 1) for v in vectors] + [qkv_bias.reshape(r, 3), fc1_bias.reshape(r, blocks)],
        1,
    )
    token_rows = tokens.transpose(1, 0, 2)
    seg_rows = segment.T
    seg_lanes = -(-2 * rows // r)
    seg_pack = jnp.concatenate([seg_rows // 64, seg_rows % 64], 1).astype(BF)
    seg_pack = jnp.pad(seg_pack, ((0, 0), (0, seg_lanes * r - 2 * rows)))
    seg_pack = seg_pack.reshape(groups, r, seg_lanes)
    vec = jnp.pad(vec, ((0, 0), (0, 16 - vec.shape[1])))
    vec = jnp.concatenate(
        [
            jnp.broadcast_to(vec, (groups, r, 16)),
            seg_pack,
            jnp.zeros((groups, r, TILE - 16 - seg_lanes), BF),
        ],
        -1,
    )
    early, qkv_local = pack_early(qkv_weight, vec, trios)
    early = exchange_small(early)
    feed_blocks = output_feed_weight.reshape(blocks, r, d)
    half = blocks // part
    up_local = split_hidden(fc1_weight, count, r)
    second_pack = jnp.stack(
        [
            jnp.concatenate(
                [up_local[:, p * half * d : (p + 1) * half * d]]
                + [feed_blocks[b] for b in range(p * half, (p + 1) * half)]
                + [dense_weight],
                1,
            )
            for p in range(part)
        ]
    )
    second_pack = swap_parts(second_pack).reshape(part * r, -1)
    toks, (second_pack, early) = spread_tokens(token_rows, (second_pack, early))
    second = lax.all_gather(second_pack, ("seq", "unit"), axis=0, tiled=True)

    seg_mine = early[:, :, PACK + 16 : PACK + 16 + seg_lanes].astype(jnp.int32)
    seg_mine = seg_mine.reshape(units, r * seg_lanes)
    seg_mine = seg_mine[:, :rows] * 64 + seg_mine[:, rows : 2 * rows]
    meta = jnp.concatenate([seg_mine[:, 0], seg_mine[:, -1], c[None]])
    seg_mine = seg_mine[:, None, :]
    trio_full = gather_small(gather_small(early, "seq"), "part")
    trio_full = trio_full.transpose(1, 2, 0, 3, 4).reshape(d, PACK + TILE)
    vec_full = trio_full[:, PACK:].astype(F32)
    vec_rows = vec_full[:, :8].T
    gain_one, bias_one, gain_two, bias_two, dense_shift, down_shift = (
        vec_rows[i : i + 1] for i in range(6)
    )
    qkv_shift = pack_columns(vec_full[:, 6:9].reshape(1, 3 * d), trios).reshape(trios, PACK)
    qkv_shift = lax.dynamic_slice_in_dim(qkv_shift, unit % trios, 1, 0)
    up_shift = split_hidden(vec_full[:, 9 : 9 + blocks].reshape(1, ff), count, r)

    block_start = (jnp.arange(units, dtype=jnp.int32) * part + c) * rows
    positions = block_start[:, None, None] + jnp.arange(rows, dtype=jnp.int32) - seg_mine
    freq = jnp.arange(ROT // 2, dtype=F32)
    inverse = jnp.exp(freq * (-2.0 * math.log(10000.0) / ROT))
    angles = positions.astype(F32) * inverse[None, :, None]
    cos = jnp.cos(angles)
    sin = jnp.sin(angles)

    place_unit = unit[None]
    packed, kv_own, normed_one, hat_one = project(
        place_unit, toks, trio_full, qkv_shift, gain_one, bias_one, cos, sin
    )
    kv = [kv_own] + [shift(kv_own, "part", i) for i in range(1, part)]
    out_low, out_t, lse = attend_forward(meta, packed, kv, seg_mine)
    second, out_low = lax.optimization_barrier((second, out_low))
    attended = exchange(out_low)
    dense_pad = jnp.pad(
        second[:, 2 * half * d :].reshape(trios, d // trios, d),
        ((0, 0), (0, OPACK - d // trios), (0, 0)),
    )

    x = token_rows.reshape(all_rows, d).astype(F32)
    cot = cotangent.transpose(1, 0, 2).reshape(all_rows, d)
    centre = x - jnp.mean(x, -1, keepdims=True)
    spread = lax.rsqrt(jnp.mean(centre * centre, -1, keepdims=True) + EPSILON)
    xhat = centre * spread
    normed_two = (xhat * gain_two + bias_two).astype(BF)
    attended_grad = jnp.einsum(
        "sld,gkd->sglk", cot.reshape(groups, rows, d), dense_pad, preferred_element_type=F32
    ).astype(BF)
    normed_all = all_parts(normed_two)
    cot_all = all_parts(cot)
    up_shift = lax.dynamic_slice_in_dim(up_shift, c * half * d, half * d, 1)
    hidden_low, pre_grad, up_shift_grad, second_branch, normed_two_grad = feed_forward(
        normed_all, cot_all, second, up_shift, half
    )
    hidden_low, pre_grad, attended, attended_grad = lax.optimization_barrier(
        (hidden_low, pre_grad, attended, attended_grad)
    )
    dout = exchange(attended_grad.reshape(units, rows, OPACK))
    second_branch = part_pieces(second_branch)
    normed_two_grad = part_pieces(normed_two_grad)
    def norm_back(grad, gain):
        gy = grad * gain
        return spread * (
            gy - jnp.mean(gy, -1, keepdims=True) - xhat * jnp.mean(gy * xhat, -1, keepdims=True)
        )

    mlp_grads = gradients(normed_all, pre_grad, hidden_low, cot_all)
    mlp_grads, dout = lax.optimization_barrier((mlp_grads, dout))

    split = (seqs, 2, 2, 2, part * r, half * d)
    up_part = halve(mlp_grads[:, : half * d].reshape(split), 0, "seq")
    down_part = halve(mlp_grads[:, half * d :].reshape(split), 1, 0)

    own, others = attend_backward(meta, packed, dout, out_t, lse, kv, seg_mine)
    others = [shift(others[i - 1], "part", part - i) for i in range(1, part)]
    up_part, down_part, own = lax.optimization_barrier((up_part, down_part, own))
    up_part = halve(add_up(up_part), 0, 0)
    down_part = halve(add_up(down_part), 0, "seq")
    qkv_grad, back_one, back_two = unturn(place_unit, own, others, trio_full, cos, sin)
    back_one = back_one.reshape(2, 2, 2, rows // 2, d)
    back_two = back_two.reshape(2, 2, 2, rows // 2, d)
    swapped = flip_unit(back_one[1], 1), flip_unit(back_two[1], 2)

    attended, normed_two_grad, up_shift_grad, qkv_grad = lax.optimization_barrier(
        (attended, normed_two_grad, up_shift_grad, qkv_grad)
    )
    attended = attended.reshape(groups, trios, rows, OPACK).transpose(0, 2, 1, 3)
    attended = attended.reshape(all_rows, trios * OPACK)
    dense_grad = outer_sum(attended, cot).reshape(trios, OPACK, d)[:, : d // trios].reshape(d, d)
    vec_grads = vector_sums(c, xhat, cot, up_shift_grad, normed_two_grad)
    dense_part = jnp.concatenate([dense_grad.astype(BF), vec_grads], 1)
    late, shift_grad = trio_gradient(normed_one, hat_one, qkv_grad, trio_full)
    swapped, late, up_part, down_part, dense_part = lax.optimization_barrier(
        (swapped, late, up_part, down_part, dense_part)
    )
    back_one = add(back_one[0], swapped[0])
    back_two = add(back_two[0], swapped[1])
    swapped = flip_unit(back_one[1], 2), flip_unit(back_two[1], 1)
    mlp_part = jnp.concatenate([add_up(up_part), add_up(down_part)], -1)
    mlp_part = halve(mlp_part, 1, 2)
    dense_part = halve(dense_part.reshape(seqs, units, part, r, d + TILE), 2, "part")
    late = late.reshape(seqs, units, part, r, -1)
    shift_rows = jnp.pad(shift_grad.astype(BF), ((0, 7), (0, TILE)))
    late = jnp.concatenate(
        [late, jnp.broadcast_to(shift_rows, (seqs, units, part) + shift_rows.shape)], 3
    )
    late = halve(late, 2, "part")
    swapped, late, mlp_part, dense_part = lax.optimization_barrier(
        (swapped, late, mlp_part, dense_part)
    )
    dense_part = halve(add_up(dense_part), 0, "seq")
    both = jnp.concatenate(
        [add(back_one[0], swapped[0]), add(back_two[0], swapped[1])], 1
    )
    swapped = flip_unit(both[1], trios)
    mlp_part = halve(add_up(mlp_part), 0, 1)
    late = halve(add_up(late), 0, "seq")
    swapped, late, mlp_part, dense_part = lax.optimization_barrier(
        (swapped, late, mlp_part, dense_part)
    )
    mlp_sum = swap_parts(add_up(mlp_part).reshape(part, r, -1)).astype(F32)
    dense_part = add_up(dense_part).reshape(2, 2, 2, r, d + TILE)
    for axis in (2, 1, 0):
        dense_part = add_up(halve(dense_part, axis, axis))
    rest = dense_part.astype(F32)
    dense_sum = rest[:, :d]
    late = add_up(halve(add_up(late).reshape(2, 2, 2, r + 8, PACK + TILE), 0, 0))
    late = exchange_trio(late).astype(F32)
    back = jnp.where(
        bits[0] == 0, jnp.stack([both[0], swapped]), jnp.stack([swapped, both[0]])
    )
    branch_one = mm(attended, dense_pad.reshape(trios * OPACK, d)) + dense_shift
    output = (x + branch_one + sum(second_branch) + down_shift).astype(BF)
    in_two = norm_back(sum(normed_two_grad), gain_two)
    qkv_weight_grad = unpack_columns(
        late[:, :r, :PACK].transpose(1, 0, 2).reshape(r, trios * PACK), trios
    )
    late_vec = jnp.sum(late[:, :r, PACK:], 0) + rest[:, d:]
    qkv_shift_grad = unpack_columns(late[:, r, :PACK].reshape(1, trios * PACK), trios)[0]
    qkv_shift_grad = lax.dynamic_slice_in_dim(qkv_shift_grad, place * 3 * r, 3 * r)

    up_sum = jnp.concatenate([mlp_sum[p, :, : half * d] for p in range(part)], 1)
    down_sum = jnp.concatenate(
        [
            mlp_sum[p, :, (half + b) * d : (half + b + 1) * d]
            for p in range(part)
            for b in range(half)
        ],
        0,
    )
    param_grads = (
        late_vec[:, 0],
        late_vec[:, 1],
        late_vec[:, 2],
        late_vec[:, 3],
        qkv_weight_grad,
        qkv_shift_grad,
        dense_sum,
        late_vec[:, 4],
        join_hidden(up_sum, count, r),
        late_vec[:, 8 : 8 + blocks].T.reshape(-1),
        down_sum,
        late_vec[:, 4],
    )

    normed_one_grad = back.reshape(all_rows, d).astype(F32)
    in_one = norm_back(normed_one_grad, gain_one)
    tokens_grad = (cot.astype(F32) + in_one + in_two).astype(BF)

    def natural(value):
        return value.reshape(groups, rows, d).transpose(1, 0, 2)

    return (natural(output), natural(tokens_grad)) + tuple(param_grads)


def solution(mesh):
    devices = mesh.devices
    seq_size, ctx_size = devices.shape
    ctx = ("unit", "part")
    tok = P(ctx, "seq", None)
    vec = P(ALL_AXES)
    mat = P(ALL_AXES, None)
    pairs = (vec, vec, vec, vec, mat, vec, mat, vec, mat, vec, mat, vec)

    def run(tokens, *rest):
        units = HEADS // TRIO * (tokens.shape[1] // seq_size)
        split = Mesh(devices.reshape(seq_size, units, ctx_size // units), ALL_AXES)
        mapped = jax.shard_map(
            on_device,
            mesh=split,
            in_specs=(tok, P(ctx, "seq")) + pairs + (tok,),
            out_specs=(tok, tok) + pairs,
            check_vma=False,
        )
        return mapped(tokens, *rest)

    return run
```
